32 devices in a mesh: dp: 4 (over y, x), fsdp: 8 (over z, core).
Axes of the slice: x: 2, y: 2, z: 4, core: 2. Of those that a mesh axis runs over, the one named last changes fastest.
Arguments:
- tokens: bfloat16 [32, 1024, 768], P(('dp', 'fsdp')), may hold values from -6 to 6
- cotangent: bfloat16 [32, 1024, 768], P(('dp', 'fsdp')), may hold values from -6 to 6
- row_flag: int32 [32], P(('dp', 'fsdp')), may hold values from 0 to 1
- sentence_mask: int32 [32, 1024], P(('dp', 'fsdp')), may hold values 0 or 1
- token_mask: int32 [32, 1024], P(('dp', 'fsdp')), may hold values 0 or 1
- lengths: int32 [32], P(('dp', 'fsdp')), may hold values from 512 to 1024, as said below
- mix_weight: float32 [768, 2304], P('fsdp'), may hold values from -0.21875 to 0.21875
- proj_weight: float32 [768, 768], P('fsdp'), may hold values from -2 to 2
- expand_weight: float32 [768, 3072], P('fsdp'), may hold values from -0.21875 to 0.21875
- shrink_weight: float32 [3072, 768], P('fsdp'), may hold values from -0.109375 to 0.109375
- norm_vectors: float32 [6, 768], P(None, 'fsdp')
- mix_rows: float32 [768], P('fsdp'), may hold values from 6553.6 to 26214.4
- proj_rows: float32 [768], P('fsdp'), may hold values from 98.304 to 393.216
- expand_rows: float32 [768], P('fsdp'), may hold values from 557.056 to 2293.76
- shrink_rows: float32 [3072], P('fsdp'), may hold values from 2293.76 to 8847.36
- mix_cols: float32 [2304], replicated, may hold values from 6553.6 to 26214.4
- proj_cols: float32 [768], replicated, may hold values from 98.304 to 393.216
- expand_cols: float32 [3072], replicated, may hold values from 557.056 to 2293.76
- shrink_cols: float32 [768], replicated, may hold values from 2293.76 to 8847.36
- vector_moment: float32 [6, 768], P(None, 'fsdp'), may hold values from 3276.8 to 32768
Outputs:
- block_output: bfloat16 [32, 1024, 768], P(('dp', 'fsdp'))
- input_grad: float32 [32, 1024, 768], P(('dp', 'fsdp'))
- mix_grad: float32 [768, 2304], P('fsdp')
- proj_grad: float32 [768, 768], P('fsdp')
- expand_grad: float32 [768, 3072], P('fsdp')
- shrink_grad: float32 [3072, 768], P('fsdp')
- vector_grad: float32 [6, 768], P(None, 'fsdp')
- mix_new: float32 [768, 2304], P('fsdp')
- proj_new: float32 [768, 768], P('fsdp')
- expand_new: float32 [768, 3072], P('fsdp')
- shrink_new: float32 [3072, 768], P('fsdp')
- vector_new: float32 [6, 768], P(None, 'fsdp')
- mix_rows_new: float32 [768], P('fsdp')
- proj_rows_new: float32 [768], P('fsdp')
- expand_rows_new: float32 [768], P('fsdp')
- shrink_rows_new: float32 [3072], P('fsdp')
- mix_cols_new: float32 [2304], replicated
- proj_cols_new: float32 [768], replicated
- expand_cols_new: float32 [3072], replicated
- shrink_cols_new: float32 [768], replicated
- moment_new: float32 [6, 768], P(None, 'fsdp')
The draws below stay inside these ranges and needn't reach their ends.
Inputs may be any that keep to these rules, and one draw needn't show every extreme that they name: `lengths`: one sequence has exactly 1024 tokens and another exactly 512.
All inputs are finite; a program needn't handle non-finite values. No bound on the sum of `sentence_mask` or of `token_mask` on one device may be relied on, other than what follows from the above.
Results may differ from the reference program's by a relative error of at most 0.01.
The reference program's roundings to bfloat16 on the way count: a program that leaves them out, or rounds other values in their place, can miss the bound.
Values may be sent and summed in bfloat16 or wider, within the bound.
A program may use at most 256 MiB of HBM per device.

```python
import math
import jax
import jax.numpy as jnp
from jax import lax

D = 768
FF = 3072
HEADS = 12
SEQ = 1024
STEP = 10
BATCH = 32


def draw_norm_vectors(key, part):
    key = jax.random.fold_in(key, 11)
    keys = jax.random.split(key, 3)
    ramp = jnp.arange(D, dtype=jnp.float32) / (D - 1)
    gains = (0.5 + ramp)[None, :] * jax.random.uniform(keys[0], (2, D), jnp.float32, 0.8, 1.2)
    shifts = 0.3 * jax.random.normal(keys[1], (2, D), jnp.float32)
    marks = jax.random.normal(keys[2], (2, D), jnp.float32)
    return jnp.stack([gains[0], shifts[0], gains[1], shifts[1], marks[0], marks[1]])


def draw_lengths(key, part):
    key = jax.random.fold_in(key, 23)
    keys = jax.random.split(key, 3)
    values = jax.random.randint(keys[0], (BATCH,), SEQ // 2, SEQ + 1)
    first = jax.random.randint(keys[1], (), 0, BATCH)
    second = (first + jax.random.randint(keys[2], (), 1, BATCH)) % BATCH
    values = values.at[first].set(SEQ).at[second].set(SEQ // 2)
    return values.astype(jnp.int32)


def plant(array, rng, low, largest):
    place = [jax.random.randint(jax.random.fold_in(rng, axis), (), 0, length) for axis, length in enumerate(array.shape)]
    main_axis = array.shape.index(max(array.shape))
    beside = place[:main_axis] + [(place[main_axis] + 1) % array.shape[main_axis]] + place[main_axis + 1:]
    return array.at[tuple(place)].set(low).at[tuple(beside)].set(largest)


def steps_of(stream_key, extent, pieces, least, largest):
    level = 1.0
    for axis_at, shards_of in pieces:
        draws = jax.random.uniform(jax.random.fold_in(jax.random.fold_in(stream_key, 6), axis_at), (shards_of,), jnp.float32, least / len(pieces), largest / len(pieces))
        level = level * jnp.repeat(jnp.exp(draws), extent[axis_at] // shards_of).reshape((-1,) + (1,) * (len(extent) - 1 - axis_at))
    return level


def gaussian(key, extent, scale, most, pieces=(), kind=jnp.bfloat16):
    entries = jax.random.normal(key, extent, jnp.float32) * scale
    if len(pieces) > 0:
        entries = steps_of(key, extent, pieces, -0.22, 0.18) * entries
    return jnp.clip(entries, min=-most, max=most).astype(kind)


def setup_inputs(seed: int = 0) -> dict:
    seeds = jax.random.split(jax.random.key(seed), 21)
    return {
        "tokens": gaussian(seeds[0], (BATCH, SEQ, D), 1.0, 6.0, ((0, 32),)),
        "cotangent": gaussian(seeds[1], (BATCH, SEQ, D), 1.0, 6.0, ((0, 32),)),
        "row_flag": plant(jax.random.randint(seeds[2], (BATCH,), 0, 2), jax.random.fold_in(seeds[2], 1), 0, 1).astype(jnp.int32),
        "sentence_mask": plant((jax.random.randint(seeds[3], (BATCH, SEQ), 0, 10) < 3).astype(jnp.int32), jax.random.fold_in(seeds[3], 1), 0, 1),
        "token_mask": plant((jax.random.randint(seeds[4], (BATCH, SEQ), 0, 20) < 3).astype(jnp.int32), jax.random.fold_in(seeds[4], 1), 0, 1),
        "lengths": draw_lengths(jax.random.fold_in(seeds[20], 71), 0),
        "mix_weight": gaussian(seeds[6], (D, 3 * D), D ** -0.5, 0.21875, ((0, 8),), jnp.float32),
        "proj_weight": gaussian(seeds[7], (D, D), (max(D * 10 // SEQ, 1)) ** -0.5, 2.0, ((0, 8),), jnp.float32),
        "expand_weight": gaussian(seeds[8], (D, FF), D ** -0.5, 0.21875, ((0, 8),), jnp.float32),
        "shrink_weight": gaussian(seeds[9], (FF, D), FF ** -0.5, 0.109375, ((0, 8),), jnp.float32),
        "norm_vectors": draw_norm_vectors(jax.random.fold_in(seeds[20], 71), 0),
        "mix_rows": jnp.clip(jnp.exp(math.log(26214.4) - 1.3862944 * jax.random.uniform(seeds[11], (D,), jnp.float32) ** steps_of(seeds[11], (D,), ((0, 8),), -0.2, 0.2)), 6553.6, 26214.4),
        "proj_rows": jnp.clip(jnp.exp(math.log(393.216) - 1.3862944 * jax.random.uniform(seeds[12], (D,), jnp.float32) ** steps_of(seeds[12], (D,), ((0, 8),), -0.2, 0.2)), 98.304, 393.216),
        "expand_rows": jnp.clip(jnp.exp(math.log(2293.76) - 1.41528185 * jax.random.uniform(seeds[13], (D,), jnp.float32) ** steps_of(seeds[13], (D,), ((0, 8),), -0.2, 0.2)), 557.056, 2293.76),
        "shrink_rows": jnp.clip(jnp.exp(math.log(8847.36) - 1.34992675 * jax.random.uniform(seeds[14], (FF,), jnp.float32) ** steps_of(seeds[14], (FF,), ((0, 8),), -0.2, 0.2)), 2293.76, 8847.36),
        "mix_cols": jnp.clip(jnp.exp(jax.random.uniform(seeds[15], (3 * D,), jnp.float32, math.log(6553.6), math.log(26214.4))), 6553.6, 26214.4),
        "proj_cols": jnp.clip(jnp.exp(jax.random.uniform(seeds[16], (D,), jnp.float32, math.log(98.304), math.log(393.216))), 98.304, 393.216),
        "expand_cols": jnp.clip(jnp.exp(jax.random.uniform(seeds[17], (FF,), jnp.float32, math.log(557.056), math.log(2293.76))), 557.056, 2293.76),
        "shrink_cols": jnp.clip(jnp.exp(jax.random.uniform(seeds[18], (D,), jnp.float32, math.log(2293.76), math.log(8847.36))), 2293.76, 8847.36),
        "vector_moment": jnp.clip(jnp.exp(math.log(32768.0) - 2.3025851 * jax.random.uniform(seeds[19], (6, D), jnp.float32) ** steps_of(seeds[19], (6, D), ((1, 8),), -0.2, 0.2)), 3276.8, 32768.0),
    }


@jax.custom_vjp
def low(v):
    return lax.optimization_barrier(v.astype(jnp.bfloat16)).astype(jnp.float32)

@jax.custom_vjp
def low_back(v):
    return v

def low_keep(v):
    return (low(v), None)

def low_pass(kept, grad):
    return (grad,)

def back_keep(v):
    return (v, None)

def back_low(kept, grad):
    return (low(grad),)
low.defvjp(low_keep, low_pass)
low_back.defvjp(back_keep, back_low)
highest = lax.Precision.HIGHEST
RATE = 0.5
CLIP = 1.0

def layer_norm(h, gain, shift):
    mean = lax.optimization_barrier(jnp.mean(h, axis=-1, keepdims=True))
    centered = h - mean
    spread = lax.optimization_barrier(jnp.mean(centered * centered, axis=-1, keepdims=True))
    return centered * lax.rsqrt(spread + 1e-06) * gain + shift

def attend_block(query, keys, values, valid):
    width = query.shape[-1]
    scores = jnp.einsum('qhd,khd->hqk', query, keys, precision=highest) * width ** (-0.5)
    scores = low_back(scores)
    scores = jnp.where(valid[None, None, :], scores, -jnp.inf)
    probs = jax.nn.softmax(scores, axis=-1)
    return jnp.einsum('hqk,khd->qhd', low(probs), values, precision=highest)

def attend(mixed, valid):
    length = mixed.shape[0]
    width = mixed.shape[1] // 3
    head_dim = width // HEADS
    queries = mixed[:, :width].reshape(length, HEADS, head_dim)
    keys = mixed[:, width:2 * width].reshape(length, HEADS, head_dim)
    values = mixed[:, 2 * width:].reshape(length, HEADS, head_dim)
    block = min(512, length)
    blocks = queries.reshape(length // block, block, HEADS, head_dim)
    stepper = jax.checkpoint(attend_block)
    context = lax.map(lambda query: stepper(query, keys, values, valid), blocks)
    return context.reshape(length, width)

def layer_forward(params, inputs, valid, marked, flags):
    mix, proj, expand, shrink, vectors = (low(p) for p in params)
    embed = jnp.where(flags[:, None] == 1, vectors[5][None, :], vectors[4][None, :])
    start = inputs + marked[:, :, None] * embed[:, None, :]
    normed1 = low(layer_norm(start, vectors[0], vectors[1]))
    mixed = low(low_back(jnp.einsum('bsd,dc->bsc', normed1, mix, precision=highest)))
    context = low(low_back(jax.vmap(attend)(mixed, valid)))
    middle = start + low_back(jnp.einsum('bsi,id->bsd', context, proj, precision=highest))
    normed2 = low(layer_norm(middle, vectors[2], vectors[3]))
    inner = low_back(jnp.einsum('bsd,df->bsf', normed2, expand, precision=highest))
    active = low(jax.nn.gelu(inner, approximate=False))
    return middle + jnp.einsum('bsf,fd->bsd', active, shrink, precision=highest)

def factored_update(weight, grad, rows, cols, beta):
    square = grad * grad + 1e-30
    rows_new = beta * rows + (1.0 - beta) * lax.optimization_barrier(jnp.mean(square, axis=1))
    cols_new = beta * cols + (1.0 - beta) * lax.optimization_barrier(jnp.mean(square, axis=0))
    approx = rows_new[:, None] * cols_new[None, :] / jnp.mean(rows_new)
    update = grad * lax.rsqrt(approx)
    update = update / jnp.maximum(1.0, jnp.sqrt(jnp.mean(update * update)) / CLIP)
    rate = RATE * jnp.maximum(0.001, jnp.sqrt(jnp.mean(weight * weight)))
    return (weight - rate * update, rows_new, cols_new)

def vector_update(vectors, grad, moment, beta):
    moment_new = beta * moment + (1.0 - beta) * (grad * grad + 1e-30)
    update = grad * lax.rsqrt(moment_new)
    update = update / jnp.maximum(1.0, jnp.sqrt(lax.optimization_barrier(jnp.mean(update * update, axis=1, keepdims=True))) / CLIP)
    rate = RATE * jnp.maximum(0.001, jnp.sqrt(lax.optimization_barrier(jnp.mean(vectors * vectors, axis=1, keepdims=True))))
    return (vectors - rate * update, moment_new)

def reference(tokens, cotangent, row_flag, sentence_mask, token_mask, lengths, mix_weight, proj_weight, expand_weight, shrink_weight, norm_vectors, mix_rows, proj_rows, expand_rows, shrink_rows, mix_cols, proj_cols, expand_cols, shrink_cols, vector_moment):
    group = min(BATCH, max(1, 4096 // SEQ))
    count = BATCH // group
    positions = jnp.arange(SEQ, dtype=jnp.int32)[None, :]
    valid = positions < lengths[:, None]
    chosen = jnp.where(row_flag[:, None] == 1, token_mask, sentence_mask)
    marked = (chosen * valid.astype(jnp.int32)).astype(jnp.float32)
    bound = cotangent.astype(jnp.float32) * valid.astype(jnp.float32)[:, :, None]
    params = (mix_weight, proj_weight, expand_weight, shrink_weight, norm_vectors)

    def grouped(v):
        return v.reshape((count, group) + v.shape[1:])

    def step(totals, item):
        inputs, valid_group, marked_group, flag_group, bound_group = item

        def run(p, x):
            return layer_forward(p, x, valid_group, marked_group, flag_group)
        output, pull = jax.vjp(run, params, inputs.astype(jnp.float32))
        grads, input_back = pull(bound_group)
        totals = jax.tree.map(lambda a, b: a + b, totals, grads)
        return (totals, (output.astype(jnp.bfloat16), input_back))
    zeros = tuple((jnp.zeros_like(p) for p in params))
    totals, (outputs, input_backs) = lax.scan(step, zeros, (grouped(tokens), grouped(valid), grouped(marked), grouped(row_flag), grouped(bound)))
    block_output = outputs.reshape(BATCH, SEQ, -1)
    input_grad = input_backs.reshape(BATCH, SEQ, -1)
    mix_grad, proj_grad, expand_grad, shrink_grad, vector_grad = totals
    beta = 1.0 - STEP ** (-0.8)
    mix_new, mix_rows_new, mix_cols_new = factored_update(mix_weight, mix_grad, mix_rows, mix_cols, beta)
    proj_new, proj_rows_new, proj_cols_new = factored_update(proj_weight, proj_grad, proj_rows, proj_cols, beta)
    expand_new, expand_rows_new, expand_cols_new = factored_update(expand_weight, expand_grad, expand_rows, expand_cols, beta)
    shrink_new, shrink_rows_new, shrink_cols_new = factored_update(shrink_weight, shrink_grad, shrink_rows, shrink_cols, beta)
    vector_new, moment_new = vector_update(norm_vectors, vector_grad, vector_moment, beta)
    return (block_output, input_grad, mix_grad, proj_grad, expand_grad, shrink_grad, vector_grad, mix_new, proj_new, expand_new, shrink_new, vector_new, mix_rows_new, proj_rows_new, expand_rows_new, shrink_rows_new, mix_cols_new, proj_cols_new, expand_cols_new, shrink_cols_new, moment_new)
```

```python
import functools

import jax
import jax.numpy as jnp
from jax import lax
from jax.experimental import pallas as pl
from jax.experimental.pallas import tpu as pltpu
from jax.sharding import PartitionSpec as P

HEADS = 12
STEP = 10
RATE = 0.5
CLIP = 1.0
F32 = jnp.float32
BF = jnp.bfloat16
VMEM_LIMIT = 60 * 1024 * 1024
AXES = ("dp", "fsdp")


def nn(a, b):
    return lax.dot_general(a, b, (((1,), (0,)), ((), ())), preferred_element_type=F32)


def nt(a, b):
    return lax.dot_general(a, b, (((1,), (1,)), ((), ())), preferred_element_type=F32)


def tn(a, b):
    return lax.dot_general(a, b, (((0,), (0,)), ((), ())), preferred_element_type=F32)


def normalise(h):
    mean = jnp.mean(h, axis=-1, keepdims=True)
    centered = h - mean
    inverse = lax.rsqrt(jnp.mean(centered * centered, axis=-1, keepdims=True) + 1e-06)
    return centered * inverse, inverse


def norm_back(grad, normal, inverse, gain):
    scaled = grad * gain
    first = jnp.mean(scaled, axis=-1, keepdims=True)
    second = jnp.mean(scaled * normal, axis=-1, keepdims=True)
    return inverse * (scaled - first - normal * second)


def params(**kw):
    return pltpu.CompilerParams(vmem_limit_bytes=VMEM_LIMIT, **kw)


def rows_of(ref):
    value = ref[...]
    return value.reshape(-1, value.shape[-1])


def mixed_kernel(tokens, marks, vectors, weight, normed, mixed):
    start = tokens[...].astype(F32) + tn(marks[...], vectors[...].astype(BF))
    normal, _ = normalise(start)
    low = (normal * vectors[0:1, :] + vectors[1:2, :]).astype(BF)
    normed[...] = low
    result = nn(low, weight[...]).astype(BF)
    for k in range(mixed.shape[0]):
        mixed[k] = result[:, k * 128 : (k + 1) * 128]


def run_mixed(tokens, marks, vectors, weight):
    rows, width = tokens.shape
    cols = weight.shape[1]
    tile = 256
    return pl.pallas_call(
        mixed_kernel,
        grid=(rows // tile,),
        in_specs=[
            pl.BlockSpec((tile, width), lambda i: (i, 0)),
            pl.BlockSpec((16, tile), lambda i: (0, i)),
            pl.BlockSpec((16, width), lambda i: (0, 0)),
            pl.BlockSpec((width, cols), lambda i: (0, 0)),
        ],
        out_specs=[
            pl.BlockSpec((tile, width), lambda i: (i, 0)),
            pl.BlockSpec((cols // 128, tile, 128), lambda i: (0, i, 0)),
        ],
        out_shape=[
            jax.ShapeDtypeStruct((rows, width), BF),
            jax.ShapeDtypeStruct((cols // 128, rows, 128), BF),
        ],
        compiler_params=params(),
        name="mixed",
    )(tokens, marks, vectors, weight)


def lane_iota(rows):
    return lax.broadcasted_iota(jnp.int32, (rows, 128), 1)


def key_extra(rows, length, base):
    lane = lane_iota(rows)
    row = lax.broadcasted_iota(jnp.int32, (rows, 128), 0)
    mask = jnp.where(row < length, 0.0, -1e30)
    ones = jnp.where((lane > base) & (lane < base + 4), 1.0, 0.0)
    return jnp.where(lane == base, mask, ones).astype(BF)


def attend_pair(length, query, key, value, context, kept, tile):
    rows = query.shape[0]
    lane = lane_iota(tile)
    lane_all = lane_iota(rows)
    count = rows // tile
    keys = [
        jnp.where(lane_all < 64, key[...], key_extra(rows, length, 64)),
        jnp.where(lane_all >= 64, key[...], key_extra(rows, length, 0)),
    ]
    values = value[...]

    def first(head, t):
        base = 64 - 64 * head
        mine = (lane < 64) if head == 0 else (lane >= 64)
        one = jnp.where(lane == base, 1.0, 0.0).astype(BF)
        q = jnp.where(mine, query[pl.ds(t * tile, tile), :] * BF(0.125), one)
        return q, nt(q, keys[head])

    def second(head, t, q, score):
        base = 64 - 64 * head
        mine = (lane < 64) if head == 0 else (lane >= 64)
        top = jnp.max(score, axis=-1, keepdims=True)
        expo = jnp.exp(score - top)
        total = jnp.sum(expo, axis=-1, keepdims=True)
        probs = (expo * (1.0 / total)).astype(BF)
        lse = top + jnp.log(total)
        high = lse.astype(BF).astype(F32)
        rest = lse - high
        mid = rest.astype(BF).astype(F32)
        extra = jnp.where(lane == base, 1.0, 0.0)
        extra = jnp.where(lane == base + 1, -high, extra)
        extra = jnp.where(lane == base + 2, -mid, extra)
        extra = jnp.where(lane == base + 3, mid - rest, extra)
        kept[head, pl.ds(t * tile, tile), :] = jnp.where(mine, q, extra.astype(BF))
        return probs

    order = [(head, t) for head in range(2) for t in range(count)]
    outs = {}
    ahead = first(*order[0])
    waiting = None
    for n, spot in enumerate(order):
        now = ahead
        if n + 1 < len(order):
            ahead = first(*order[n + 1])
        if waiting is not None:
            outs[waiting[0]] = nn(waiting[1], values)
        waiting = (spot, second(*spot, *now))
    outs[waiting[0]] = nn(waiting[1], values)
    for t in range(count):
        context[pl.ds(t * tile, tile), :] = jnp.where(lane < 64, outs[0, t], outs[1, t]).astype(BF)


def attend_kernel(length, query, key, value, context, kept, *, tile):
    attend_pair(length[0], query.at[0], key.at[0], value.at[0], context, kept, tile)


def run_attend(length, mixed, tile=256):
    groups, rows, _ = mixed.shape
    pairs = groups // 3
    return pl.pallas_call(
        functools.partial(attend_kernel, tile=tile),
        grid=(pairs,),
        in_specs=[
            pl.BlockSpec(memory_space=pltpu.SMEM),
            pl.BlockSpec((1, rows, 128), lambda p: (p, 0, 0)),
            pl.BlockSpec((1, rows, 128), lambda p: (pairs + p, 0, 0)),
            pl.BlockSpec((1, rows, 128), lambda p: (2 * pairs + p, 0, 0)),
        ],
        out_specs=[
            pl.BlockSpec((rows, 128), lambda p: (0, p)),
            pl.BlockSpec((2, rows, 128), lambda p: (p, 0, 0)),
        ],
        out_shape=[
            jax.ShapeDtypeStruct((rows, pairs * 128), BF),
            jax.ShapeDtypeStruct((2 * pairs, rows, 128), BF),
        ],
        compiler_params=params(),
        name="attend",
    )(length, mixed, mixed, mixed)


class Spot:
    def __init__(self):
        fs = lax.axis_index("fsdp")
        dp = lax.axis_index("dp")
        self.fs, self.dp = fs, dp
        self.c, self.z = fs % 2, fs // 2
        z0, z1 = self.z % 2, self.z // 2
        near, far = z1 * 2 + (1 - z0), (1 - z1) * 2 + z0
        self.zs = (self.z, near, far, (1 - z1) * 2 + (1 - z0))
        x, y = dp % 2, dp // 2
        turn_x, turn_y = 1 - 2 * x, 1 - 2 * y
        first = (y + turn_y * self.c) * 2 + x + turn_x * (1 - self.c)
        second = (y + turn_y * (1 - self.c)) * 2 + x + turn_x * self.c
        self.qs = (dp, first, second, (1 - y) * 2 + 1 - x)
        self.near = (dp, near * 2 + self.c)
        self.far = (dp, far * 2 + self.c)
        self.first = (first, fs)
        self.second = (second, fs)
        self.core = (dp, self.z * 2 + 1 - self.c)

    def row(self, k):
        return (self.dp, (self.fs + k) % 8)


MESH = pl.DeviceIdType.MESH


def front_kernel(
    length, tokens, marks, share, mix_w, proj_w, expand_w, shrink_w,
    a_out, b_out, c_out, vectors_out, normed_out, mixed_out, context, kept,
    stage, own, w_a, vec_in, vectors, normed, mixed, send, recv, vec_send, vec_recv, local, *, tile
):
    step = pl.program_id(0)
    spot = Spot()
    c, dp = spot.c, spot.dp

    def block(g, z, cc, q):
        if g == 0:
            return w_a.at[q, z, cc]
        if g == 1:
            return b_out.at[q, z, cc]
        return c_out.at[z, cc, q]

    def remote(g, z, cc, q, kind, target, mine=False):
        dst = block(g, z, cc, q)
        return pltpu.make_async_remote_copy(
            src_ref=own.at[g - 1] if mine and g > 0 else dst,
            dst_ref=dst,
            send_sem=send.at[g, kind],
            recv_sem=recv.at[g, (z * 2 + cc) * 4 + q],
            device_id=target,
            device_id_type=MESH,
        )

    def push(g, z, q, kind, target, mine=False):
        remote(g, z, c, q, kind, target, mine).start()

    def arrive(g, z, cc, q):
        remote(g, z, cc, q, 0, spot.core).wait_recv()

    def phase0(g):
        push(g, spot.z, dp, 0, spot.far, True)
        push(g, spot.z, dp, 1, spot.near, True)
        push(g, spot.z, dp, 7, spot.second, True)
        push(g, spot.z, dp, 3, spot.first, True)
        push(g, spot.z, dp, 15, spot.core, True)

    def spread(g, k):
        push(g, spot.zs[k], dp, 7 + k, spot.second)
        push(g, spot.zs[k], dp, 3 + k, spot.first)
        push(g, spot.zs[k], dp, 15 + k, spot.core)

    def phase1(g):
        arrive(g, spot.zs[2], c, dp)
        push(g, spot.zs[2], dp, 2, spot.near)
        spread(g, 2)

    def phase2(g):
        arrive(g, spot.zs[1], c, dp)
        spread(g, 1)
        arrive(g, spot.zs[3], c, dp)
        spread(g, 3)

    def phase3(g):
        for k in range(4):
            arrive(g, spot.zs[k], c, spot.qs[1])
            push(g, spot.zs[k], spot.qs[1], 11 + k, spot.second)
            push(g, spot.zs[k], spot.qs[1], 19 + k, spot.core)

    def phase4(g):
        for m in (2, 3):
            for k in range(4):
                arrive(g, spot.zs[k], c, spot.qs[m])
                push(g, spot.zs[k], spot.qs[m], 15 + 4 * m + k, spot.core)

    def phase5(g):
        for q in range(4):
            for z in range(4):
                arrive(g, z, 1 - c, q)

    def phase6(g):
        for kind in range(31):
            remote(g, spot.z, c, dp, kind, spot.core, True).wait_send()

    def vec_copy(k):
        return pltpu.make_async_remote_copy(
            src_ref=vec_in.at[spot.fs],
            dst_ref=vec_in.at[spot.fs],
            send_sem=vec_send.at[k],
            recv_sem=vec_recv.at[spot.fs],
            device_id=spot.row(k),
            device_id_type=MESH,
        )

    def vec_arrive(k):
        other = (spot.fs + k) % 8
        pltpu.make_async_remote_copy(
            src_ref=vec_in.at[other],
            dst_ref=vec_in.at[other],
            send_sem=vec_send.at[k],
            recv_sem=vec_recv.at[other],
            device_id=spot.row(k),
            device_id_type=MESH,
        ).wait_recv()

    def keep_copies():
        return (
            pltpu.make_async_copy(w_a, a_out, local.at[3]),
            pltpu.make_async_copy(own.at[0], b_out.at[dp, spot.z, c], local.at[4]),
            pltpu.make_async_copy(own.at[1], c_out.at[spot.z, c, dp], local.at[5]),
            pltpu.make_async_copy(normed, normed_out, local.at[6]),
            pltpu.make_async_copy(mixed, mixed_out, local.at[7]),
        )

    @pl.when(step == 0)
    def _():
        barrier = pltpu.get_barrier_semaphore()
        peers = [spot.row(k) for k in range(1, 8)] + [spot.first, spot.second]
        for peer in peers:
            pl.semaphore_signal(barrier, inc=1, device_id=peer, device_id_type=MESH)

        @pl.when(dp < 3)
        def _():
            columns = pl.ds(pl.multiple_of(dp * 768, 128), 768)
            pltpu.make_async_copy(mix_w.at[:, columns], stage.at[0], local.at[0]).start()

        @pl.when(dp == 3)
        def _():
            pltpu.make_async_copy(proj_w, stage.at[0], local.at[0]).start()

        columns = pl.ds(pl.multiple_of(dp * 768, 128), 768)
        second = pltpu.make_async_copy(expand_w.at[:, columns], stage.at[1], local.at[1])
        second.start()
        third = pltpu.make_async_copy(
            shrink_w.at[pl.ds(pl.multiple_of(dp * 96, 8), 96), :], stage.at[2], local.at[2]
        )
        third.start()
        vec_in[spot.fs] = share[...]
        pltpu.make_async_copy(proj_w, stage.at[0], local.at[0]).wait()
        w_a[dp, spot.z, c] = stage[0].astype(BF)
        pl.semaphore_wait(barrier, len(peers))
        phase0(0)
        for k in range(1, 8):
            vec_copy(k).start()
        second.wait()
        own[0] = stage[1].astype(BF)
        third.wait()
        own[1] = stage[2].astype(BF)
        copies = keep_copies()
        copies[1].start()
        copies[2].start()
        for k in range(1, 8):
            vec_arrive(k)
        total = jnp.zeros((16, 768), F32)
        for f in range(8):
            row = lax.broadcasted_iota(jnp.int32, (128, 768), 0)
            lane = lax.broadcasted_iota(jnp.int32, (128, 768), 1)
            pick = jnp.where((lane - 96 * f == row) & (row < 96), 1.0, 0.0).astype(BF)
            total += nn(vec_in[f], pick)
        vectors[...] = total
        vectors_out[...] = total

        def norm(t):
            part = pl.ds(t * 256, 256)
            start = tokens[part, :].astype(F32) + tn(marks[:, part], total.astype(BF))
            normal, _ = normalise(start)
            normed[part, :] = (normal * total[0:1, :] + total[1:2, :]).astype(BF)

        norm(0)
        phase1(0)
        norm(1)
        phase2(0)
        norm(2)
        norm(3)
        phase3(0)
        phase0(1)
        phase0(2)
        phase4(0)
        phase5(0)
        copies[0].start()
        copies[3].start()
        for q in range(3):
            weight = rows_of(w_a.at[q])
            for t in range(4):
                part = pl.ds(t * 256, 256)
                result = nn(normed[part, :], weight).astype(BF)
                for k in range(6):
                    mixed[q * 6 + k, part, :] = result[:, k * 128 : (k + 1) * 128]
            if q == 0:
                phase1(1)
                phase1(2)
            if q == 2:
                phase2(1)
                phase2(2)
        copies[4].start()

    @pl.when(step > 0)
    def _():
        p = step - 1
        attend_pair(length[0], mixed.at[p], mixed.at[6 + p], mixed.at[12 + p], context, kept, tile)

    for at, phase, g in ((1, phase3, 1), (2, phase3, 2), (5, phase4, 1), (6, phase4, 2)):

        @pl.when(step == at)
        def _():
            phase(g)

    @pl.when(step == 6)
    def _():
        phase5(1)
        phase5(2)
        for g in range(3):
            phase6(g)
        for k in range(1, 8):
            vec_copy(k).wait_send()
        for copy in keep_copies():
            copy.wait()


def run_front(length, tokens, marks, share, mix_w, proj_w, expand_w, shrink_w, tile=256):
    rows, width = tokens.shape
    anywhere = pl.BlockSpec(memory_space=pl.ANY)
    once = pl.Buffered(1)

    def whole(*shape):
        return pl.BlockSpec(shape, lambda i: (0,) * len(shape), pipeline_mode=once)

    return pl.pallas_call(
        functools.partial(front_kernel, tile=tile),
        grid=(7,),
        in_specs=[
            pl.BlockSpec(memory_space=pltpu.SMEM),
            whole(rows, width),
            whole(16, rows),
            whole(16, 128),
            anywhere,
            anywhere,
            anywhere,
            anywhere,
        ],
        out_specs=[
            anywhere,
            anywhere,
            anywhere,
            whole(16, width),
            anywhere,
            anywhere,
            pl.BlockSpec((rows, 128), lambda i: (0, jnp.maximum(i - 1, 0))),
            pl.BlockSpec((2, rows, 128), lambda i: (jnp.maximum(i - 1, 0), 0, 0)),
        ],
        out_shape=[
            jax.ShapeDtypeStruct((4, 4, 2, 96, 768), BF),
            jax.ShapeDtypeStruct((4, 4, 2, 96, 768), BF),
            jax.ShapeDtypeStruct((4, 2, 4, 96, 768), BF),
            jax.ShapeDtypeStruct((16, width), F32),
            jax.ShapeDtypeStruct((rows, width), BF),
            jax.ShapeDtypeStruct((18, rows, 128), BF),
            jax.ShapeDtypeStruct((rows, width), BF),
            jax.ShapeDtypeStruct((12, rows, 128), BF),
        ],
        scratch_shapes=[
            pltpu.VMEM((3, 96, 768), F32),
            pltpu.VMEM((2, 96, 768), BF),
            pltpu.VMEM((4, 4, 2, 96, 768), BF),
            pltpu.VMEM((8, 16, 128), BF),
            pltpu.VMEM((16, width), F32),
            pltpu.VMEM((rows, width), BF),
            pltpu.VMEM((18, rows, 128), BF),
            pltpu.SemaphoreType.DMA((3, 31)),
            pltpu.SemaphoreType.DMA((3, 32)),
            pltpu.SemaphoreType.DMA((8,)),
            pltpu.SemaphoreType.DMA((8,)),
            pltpu.SemaphoreType.DMA((8,)),
        ],
        compiler_params=params(collective_id=0, has_side_effects=True),
        name="front",
    )(length, tokens, marks, share, mix_w, proj_w, expand_w, shrink_w)


def attend_back_kernel(length, kept, key, value, ctx_grad, dq, dk, dv, *, tile):
    key, value = key.at[0], value.at[0]
    rows = key.shape[0]
    lane = lane_iota(tile)
    lane_all = lane_iota(rows)
    count = rows // tile
    plain, plain_values = key[...], value[...]
    keys = [
        jnp.where(lane_all < 64, plain, key_extra(rows, length[0], 64)),
        jnp.where(lane_all >= 64, plain, key_extra(rows, length[0], 0)),
    ]
    zero = jnp.zeros_like(plain_values)
    values = [
        jnp.where(lane_all < 64, plain_values, zero),
        jnp.where(lane_all >= 64, plain_values, zero),
    ]

    def first(head, t):
        q = kept[head, pl.ds(t * tile, tile), :]
        grad = ctx_grad[pl.ds(t * tile, tile), :]
        return q, grad, nt(keys[head], q), nt(values[head], grad)

    sums = {}

    def second(head, t, q, grad, score, prob_back):
        probs = jnp.exp(score)
        product = probs * prob_back
        delta = jnp.sum(product, axis=0, keepdims=True)
        score_back = (product - probs * delta).astype(BF)
        dv_part = nn(probs.astype(BF), grad)
        dk_part = nn(score_back, q)
        sums[head, "v"] = dv_part if t == 0 else sums[head, "v"] + dv_part
        sums[head, "k"] = dk_part if t == 0 else sums[head, "k"] + dk_part
        sums[head, t] = tn(score_back, plain)

    order = [(head, t) for head in range(2) for t in range(count)]
    ahead = first(*order[0])
    for n, spot in enumerate(order):
        now = ahead
        if n + 1 < len(order):
            ahead = first(*order[n + 1])
        second(*spot, *now)
    dk[...] = jnp.where(lane_all < 64, sums[0, "k"], sums[1, "k"]).astype(BF)
    dv[...] = jnp.where(lane_all < 64, sums[0, "v"], sums[1, "v"]).astype(BF)
    for t in range(count):
        both = jnp.where(lane < 64, sums[0, t], sums[1, t]) * 0.125
        dq[pl.ds(t * tile, tile), :] = both.astype(BF)


def run_attend_back(length, kept, mixed, ctx_grad, tile=128):
    groups, rows, _ = mixed.shape
    pairs = groups // 3
    width = pairs * 128
    spec = pl.BlockSpec((rows, 128), lambda p: (0, p))
    return pl.pallas_call(
        functools.partial(attend_back_kernel, tile=tile),
        grid=(pairs,),
        in_specs=[
            pl.BlockSpec(memory_space=pltpu.SMEM),
            pl.BlockSpec((2, rows, 128), lambda p: (p, 0, 0)),
            pl.BlockSpec((1, rows, 128), lambda p: (pairs + p, 0, 0)),
            pl.BlockSpec((1, rows, 128), lambda p: (2 * pairs + p, 0, 0)),
            spec,
        ],
        out_specs=[spec, spec, spec],
        out_shape=[jax.ShapeDtypeStruct((rows, width), BF)] * 3,
        compiler_params=params(),
        name="attend_back",
    )(length, kept, mixed, mixed, ctx_grad)


def gelu_pair(v):
    cdf = 0.5 * (1.0 + lax.erf(v * 0.7071067811865476))
    return v * cdf, cdf + v * jnp.exp(-0.5 * v * v) * 0.3989422804014327


def feed_kernel(
    place, length, context, tokens, marks, vectors, proj, expand, shrink, cotangent,
    output, middle_back, ctx_back, gain_grads, *rest, tile, blocked
):
    if blocked:
        (proj_keep, proj_send, expand_keep, expand_send, shrink_keep, shrink_send,
         middle, normed, bound, out_sum, back_sum, active, inner_back) = rest
    else:
        (proj_grad, expand_grad, shrink_grad,
         middle, normed, bound, out_sum, back_sum, active, inner_back) = rest
    rows = tokens.shape[0]
    j = pl.program_id(0)
    parts = [pl.ds(t * tile, tile) for t in range(rows // tile)]
    expand_now, shrink_now = rows_of(expand), rows_of(shrink)

    @pl.when(j == 0)
    def _():
        for t, part in enumerate(parts):
            start = tokens[part, :].astype(F32) + tn(marks[:, part], vectors[...].astype(BF))
            mid = start + nn(context[part, :], rows_of(proj))
            middle[part, :] = mid
            normal, _ = normalise(mid)
            normed[part, :] = (normal * vectors[2:3, :] + vectors[3:4, :]).astype(BF)
            row = t * tile + lax.broadcasted_iota(jnp.int32, (tile, 1), 0)
            bound[part, :] = jnp.where(row < length[0], cotangent[part, :].astype(F32), 0.0).astype(BF)

    for part in parts:
        inner = nn(normed[part, :], expand_now)
        act_back = nt(bound[part, :], shrink_now)
        act, slope = gelu_pair(inner)
        act = act.astype(BF)
        active[part, :] = act
        back = (act_back * slope).astype(BF)
        inner_back[part, :] = back
        out_part = nn(act, shrink_now)
        back_part = nt(back, expand_now)

        @pl.when(j == 0)
        def _():
            out_sum[part, :] = out_part
            back_sum[part, :] = back_part

        @pl.when(j > 0)
        def _():
            out_sum[part, :] += out_part
            back_sum[part, :] += back_part

    grad_e = tn(normed[...], inner_back[...])
    grad_s = tn(active[...], bound[...])
    if blocked:
        core = place[0]
        here = place[1]
        for z in range(4):
            r = place[2 + z]
            for c in range(2):
                piece = grad_e[(2 * z + c) * 96 : (2 * z + c + 1) * 96, :].astype(BF)

                @pl.when(core == c)
                def _():
                    expand_keep[0, r] = piece

                @pl.when(core != c)
                def _():
                    expand_send[0, r] = piece
        for c in range(2):
            for q in range(4):
                piece = grad_s[(c * 4 + q) * 96 : (c * 4 + q + 1) * 96, :].astype(BF)

                @pl.when(core == c)
                def _():
                    shrink_keep[place[6 + q], 0] = piece

                @pl.when(core != c)
                def _():
                    shrink_send[place[10 + q], 0] = piece
    else:
        expand_grad[...] = grad_e
        shrink_grad[...] = grad_s

    @pl.when(j == pl.num_programs(0) - 1)
    def _():
        gain = jnp.zeros((1, tokens.shape[1]), F32)
        shift = jnp.zeros((1, tokens.shape[1]), F32)
        for part in parts:
            mid = middle[part, :]
            output[part, :] = (mid + out_sum[part, :]).astype(BF)
            normal, inverse = normalise(mid)
            grad = back_sum[part, :]
            gain += jnp.sum(grad * normal, axis=0, keepdims=True)
            shift += jnp.sum(grad, axis=0, keepdims=True)
            back = bound[part, :].astype(F32) + norm_back(grad, normal, inverse, vectors[2:3, :])
            middle_back[part, :] = back
            low = back.astype(BF)
            normed[part, :] = low
            ctx_back[part, :] = nt(low, rows_of(proj)).astype(BF)
        gain_grads[...] = jnp.concatenate([gain, shift, jnp.zeros((6, gain.shape[1]), F32)], axis=0)
        grad_p = tn(context[...], normed[...])
        if blocked:
            core = place[0]
            for z in range(4):
                r = place[2 + z]
                for c in range(2):
                    piece = grad_p[(2 * z + c) * 96 : (2 * z + c + 1) * 96, :].astype(BF)

                    @pl.when(core == c)
                    def _():
                        proj_keep[r] = piece

                    @pl.when(core != c)
                    def _():
                        proj_send[r] = piece
        else:
            proj_grad[...] = grad_p


def run_feed(place, length, context, tokens, marks, vectors, proj, expand, shrink, cotangent,
             blocked, tile=256):
    rows, width = tokens.shape
    inner = 4 * width
    chunk = width
    steps = inner // chunk
    once = pl.Buffered(1)

    def whole(*shape):
        return pl.BlockSpec(shape, lambda j, pl_: (0,) * len(shape), pipeline_mode=once)

    in_specs = [
        pl.BlockSpec(memory_space=pltpu.SMEM),
        whole(rows, width),
        whole(rows, width),
        whole(16, rows),
        whole(16, width),
        whole(width, width),
        pl.BlockSpec((width, chunk), lambda j, pl_: (0, j)),
        pl.BlockSpec((chunk, width), lambda j, pl_: (j, 0)),
        whole(rows, width),
    ]
    if blocked:
        in_specs[5:8] = [
            pl.BlockSpec((1, 4, 2, 96, 768), lambda j, pl_: (3, 0, 0, 0, 0), pipeline_mode=once),
            pl.BlockSpec((1, 4, 2, 96, 768), lambda j, pl_: (j, 0, 0, 0, 0)),
            pl.BlockSpec((1, 2, 4, 96, 768), lambda j, pl_: (j, 0, 0, 0, 0)),
        ]
    out_specs = [whole(rows, width), whole(rows, width), whole(rows, width), whole(8, width)]
    out_shape = [
        jax.ShapeDtypeStruct((rows, width), BF),
        jax.ShapeDtypeStruct((rows, width), F32),
        jax.ShapeDtypeStruct((rows, width), BF),
        jax.ShapeDtypeStruct((8, width), F32),
    ]
    if blocked:
        out_specs += [whole(4, 96, 768)] * 2
        out_shape += [jax.ShapeDtypeStruct((4, 96, 768), BF)] * 2
        out_specs += [
            pl.BlockSpec((1, 4, 96, 768), lambda j, pl_: (pl_[6 + j], 0, 0, 0)),
            pl.BlockSpec((1, 4, 96, 768), lambda j, pl_: (pl_[10 + j], 0, 0, 0)),
            pl.BlockSpec((4, 1, 96, 768), lambda j, pl_: (0, pl_[2 + j], 0, 0)),
            pl.BlockSpec((4, 1, 96, 768), lambda j, pl_: (0, pl_[2 + j], 0, 0)),
        ]
        out_shape += [jax.ShapeDtypeStruct((4, 4, 96, 768), BF)] * 4
    else:
        out_specs += [
            whole(width, width),
            pl.BlockSpec((width, chunk), lambda j, pl_: (0, j)),
            pl.BlockSpec((chunk, width), lambda j, pl_: (j, 0)),
        ]
        out_shape += [
            jax.ShapeDtypeStruct((width, width), F32),
            jax.ShapeDtypeStruct((width, inner), F32),
            jax.ShapeDtypeStruct((inner, width), F32),
        ]
    grid_spec = pltpu.PrefetchScalarGridSpec(
        num_scalar_prefetch=1,
        grid=(steps,),
        in_specs=in_specs,
        out_specs=out_specs,
        scratch_shapes=[
            pltpu.VMEM((rows, width), F32),
            pltpu.VMEM((rows, width), BF),
            pltpu.VMEM((rows, width), BF),
            pltpu.VMEM((rows, width), F32),
            pltpu.VMEM((rows, width), F32),
            pltpu.VMEM((rows, chunk), BF),
            pltpu.VMEM((rows, chunk), BF),
        ],
    )
    return pl.pallas_call(
        functools.partial(feed_kernel, tile=tile, blocked=blocked),
        grid_spec=grid_spec,
        out_shape=out_shape,
        compiler_params=params(),
        name="feed",
    )(place, length, context, tokens, marks, vectors, proj, expand, shrink, cotangent)


def mix_grad_kernel(place, normed, dq, dk, dv, *rest, blocked):
    if blocked:
        proj_keep, proj_send, keep, send = rest
    else:
        (grad_out,) = rest
    j = pl.program_id(0)
    for index, source in enumerate((dq, dk, dv)):

        @pl.when(j == index)
        def _():
            grad = tn(normed[...], source[...])
            if not blocked:
                grad_out[...] = grad
                return
            core = place[0]
            for z in range(4):
                r = place[2 + z]
                for c in range(2):
                    piece = grad[(2 * z + c) * 96 : (2 * z + c + 1) * 96, :].astype(BF)

                    @pl.when(core == c)
                    def _():
                        keep[0, r] = piece

                    @pl.when(core != c)
                    def _():
                        send[0, r] = piece

    if blocked:

        @pl.when(j == 3)
        def _():
            keep[0] = proj_keep[...]
            send[0] = proj_send[...]


def run_mix_grad(place, normed, dq, dk, dv, blocked, proj_keep=None, proj_send=None):
    rows, width = normed.shape
    once = pl.Buffered(1)

    def whole(*shape):
        return pl.BlockSpec(shape, lambda j, pl_: (0,) * len(shape), pipeline_mode=once)

    in_specs = [whole(rows, width)] * 4
    ins = [normed, dq, dk, dv]
    if blocked:
        in_specs += [whole(4, 96, 768)] * 2
        ins += [proj_keep, proj_send]
        out_specs = [
            pl.BlockSpec((1, 4, 96, 768), lambda j, pl_: (pl_[6 + j], 0, 0, 0)),
            pl.BlockSpec((1, 4, 96, 768), lambda j, pl_: (pl_[10 + j], 0, 0, 0)),
        ]
        out_shape = [jax.ShapeDtypeStruct((4, 4, 96, 768), BF)] * 2
        steps = 4
    else:
        out_specs = [pl.BlockSpec((width, width), lambda j, pl_: (0, j))]
        out_shape = [jax.ShapeDtypeStruct((width, 3 * width), F32)]
        steps = 3
    return pl.pallas_call(
        functools.partial(mix_grad_kernel, blocked=blocked),
        grid_spec=pltpu.PrefetchScalarGridSpec(
            num_scalar_prefetch=1, grid=(steps,), in_specs=in_specs, out_specs=out_specs
        ),
        out_shape=out_shape,
        compiler_params=params(),
        name="mix_grad",
    )(place, *ins)


def input_kernel(tokens, marks, vectors, weight, dq, dk, dv, middle_back, input_grad, sums):
    i = pl.program_id(0)
    width = tokens.shape[1]
    start = tokens[...].astype(F32) + tn(marks[...], vectors[...].astype(BF))
    normal, inverse = normalise(start)
    grad = jnp.zeros(start.shape, F32)
    for k, source in enumerate((dq, dk, dv)):
        if len(weight.shape) == 2:
            part = weight[:, k * width : (k + 1) * width]
        else:
            part = rows_of(weight.at[k])
        grad += nt(source[...], part)
    gain = jnp.sum(grad * normal, axis=0, keepdims=True)
    shift = jnp.sum(grad, axis=0, keepdims=True)
    result = middle_back[...] + norm_back(grad, normal, inverse, vectors[0:1, :])
    input_grad[...] = result
    spread = tn(marks[...], jnp.ones((16, width), BF))
    mark = jnp.sum(spread * result, axis=0, keepdims=True)
    both = jnp.concatenate([gain, shift, mark, jnp.zeros((5, width), F32)], axis=0)

    @pl.when(i == 0)
    def _():
        sums[...] = both

    @pl.when(i > 0)
    def _():
        sums[...] += both


def run_input(tokens, marks, vectors, weight, dq, dk, dv, middle_back, tile=256):
    rows, width = tokens.shape
    spec = pl.BlockSpec((tile, width), lambda i: (i, 0))
    if len(weight.shape) == 2:
        shape = (width, 3 * width)
    else:
        shape = (3,) + weight.shape[1:]
    weight_spec = pl.BlockSpec(shape, lambda i: (0,) * len(shape), pipeline_mode=pl.Buffered(1))
    return pl.pallas_call(
        input_kernel,
        grid=(rows // tile,),
        in_specs=[
            spec,
            pl.BlockSpec((16, tile), lambda i: (0, i)),
            pl.BlockSpec((16, width), lambda i: (0, 0)),
            weight_spec,
            spec,
            spec,
            spec,
            spec,
        ],
        out_specs=[spec, pl.BlockSpec((8, width), lambda i: (0, 0))],
        out_shape=[jax.ShapeDtypeStruct((rows, width), F32), jax.ShapeDtypeStruct((8, width), F32)],
        compiler_params=params(),
        name="input_grad",
    )(tokens, marks, vectors, weight, dq, dk, dv, middle_back)


def partners(change):
    pairs = []
    for dp in range(4):
        for fs in range(8):
            to_dp, to_fs = change(dp, fs)
            pairs.append((dp * 8 + fs, to_dp * 8 + to_fs))
    return pairs


CORE = partners(lambda dp, fs: (dp, fs ^ 1))
FIRST = partners(lambda dp, fs: (dp ^ (2 if fs & 1 else 1), fs))
SECOND = partners(lambda dp, fs: (dp ^ (1 if fs & 1 else 2), fs))
NEAR = partners(lambda dp, fs: (dp, fs ^ 2))
FAR = partners(lambda dp, fs: (dp, fs ^ 4))
ALONG_X = partners(lambda dp, fs: (dp ^ 1, fs))
ALONG_Y = partners(lambda dp, fs: (dp ^ 2, fs))
ALONG_XY = partners(lambda dp, fs: (dp ^ 3, fs))


def move(value, pairs):
    return lax.ppermute(value, AXES, pairs)


def add(a, b):
    return (a.astype(F32) + b.astype(F32)).astype(BF)


def places():
    dp = lax.axis_index("dp")
    fs = lax.axis_index("fsdp")
    core = fs & 1
    z = fs >> 1

    def rel_z(other):
        bits = z ^ other
        return (bits & 1) * 2 + (bits >> 1)

    def rel_q(other, which):
        bits = dp ^ other
        swapped = (bits & 1) * 2 + (bits >> 1)
        return jnp.where(which == 0, swapped, bits)

    values = [core, dp] + [rel_z(k) for k in range(4)]
    values += [rel_q(k, core) for k in range(4)] + [rel_q(k, 1 - core) for k in range(4)]
    return jnp.stack([v.astype(jnp.int32) for v in values])


def reduce_blocks(keep, send):
    got = move(send, CORE)
    near, far = add(keep[:2], got[:2]), add(keep[2:], got[2:])
    got = move(far, FIRST)
    near, far = add(near[0], got[0]), add(near[1], got[1])
    got = move(far, SECOND)
    near, far = add(near[:2], got[:2]), add(near[2:], got[2:])
    got = move(far, NEAR)
    near, far = add(near[0], got[0]), add(near[1], got[1])
    got = move(far, FAR)
    return add(near, got)


def gather_quarters(own):
    pieces = jnp.stack([own, move(own, ALONG_X), move(own, ALONG_Y), move(own, ALONG_XY)])
    dp = lax.axis_index("dp")
    return [lax.dynamic_index_in_dim(pieces, dp ^ q, 0, keepdims=False).astype(F32) for q in range(4)]


def sum_all(value, stages):
    for pairs in stages:
        value = value + move(value, pairs)
    return value


def body(
    tokens, cotangent, row_flag, sentence_mask, token_mask, lengths,
    mix_weight, proj_weight, expand_weight, shrink_weight, norm_vectors,
    mix_rows, proj_rows, expand_rows, shrink_rows,
    mix_cols, proj_cols, expand_cols, shrink_cols, vector_moment,
):
    length, width = tokens.shape[1:]
    tokens = tokens.reshape(length, width)
    cotangent = cotangent.reshape(length, width)
    owners = lax.axis_size("fsdp")
    blocked = owners == 8 and lax.axis_size("dp") == 4
    fs = lax.axis_index("fsdp")

    valid = (lax.broadcasted_iota(jnp.int32, (1, length), 1) < lengths[:, None]).astype(jnp.int32)
    is_token = (row_flag == 1).astype(jnp.int32)[:, None]
    marks = jnp.concatenate(
        [
            jnp.zeros((4, length), jnp.int32),
            sentence_mask * valid * (1 - is_token),
            token_mask * valid * is_token,
            jnp.zeros((10, length), jnp.int32),
        ]
    ).astype(BF)

    share = norm_vectors.shape[1]
    if blocked:
        place = places()
        packed = jnp.pad(norm_vectors, ((0, 10), (0, 128 - share))).astype(BF)
        mix_full, expand_full, shrink_full, vectors, normed, mixed, context, kept = run_front(
            lengths, tokens, marks, packed, mix_weight, proj_weight, expand_weight, shrink_weight
        )
        proj_full = mix_full
    else:
        mix_full = lax.all_gather(mix_weight.astype(BF), "fsdp", axis=0, tiled=True)
        proj_full = lax.all_gather(proj_weight.astype(BF), "fsdp", axis=0, tiled=True)
        expand_full = lax.all_gather(expand_weight.astype(BF), "fsdp", axis=0, tiled=True)
        shrink_full = lax.all_gather(shrink_weight.astype(BF), "fsdp", axis=0, tiled=True)
        vectors = lax.all_gather(norm_vectors.astype(BF), "fsdp", axis=1, tiled=True).astype(F32)
        vectors = jnp.concatenate([vectors, jnp.zeros((10, width), F32)])
        place = jnp.zeros((14,), jnp.int32)
        normed, mixed = run_mixed(tokens, marks, vectors, mix_full)
        context, kept = run_attend(lengths, mixed)
    fed = run_feed(
        place, lengths, context, tokens, marks, vectors,
        proj_full, expand_full, shrink_full, cotangent, blocked,
    )
    block_output, middle_back, ctx_back, gain2 = fed[:4]
    dq, dk, dv = run_attend_back(lengths, kept, mixed, ctx_back)
    if blocked:
        mix_parts = run_mix_grad(place, normed, dq, dk, dv, True, fed[4], fed[5])
    else:
        mix_parts = run_mix_grad(place, normed, dq, dk, dv, False)
    input_grad, gain1 = run_input(
        tokens, marks, vectors, mix_full, dq, dk, dv, middle_back
    )
    token_row = is_token.astype(F32)
    vector_local = jnp.concatenate(
        [gain1[0:2], gain2[0:2], gain1[2:3] * (1.0 - token_row), gain1[2:3] * token_row]
    )

    if blocked:
        quarters = gather_quarters(reduce_blocks(fed[6], fed[7]))
        expand_grad = jnp.concatenate(quarters, axis=1)
        quarters = gather_quarters(reduce_blocks(fed[8], fed[9]))
        shrink_grad = jnp.concatenate(quarters, axis=0)
        quarters = gather_quarters(reduce_blocks(*mix_parts))
        mix_grad = jnp.concatenate(quarters[:3], axis=1)
        proj_grad = quarters[3]
        vector_grad = sum_all(vector_local, (CORE, FIRST, SECOND, NEAR, FAR))
        vector_grad = lax.dynamic_slice(vector_grad, (0, fs * share), (6, share))
    else:
        local = (mix_parts[0], fed[4], fed[5], fed[6])
        shards = [lax.psum_scatter(g, "fsdp", scatter_dimension=0, tiled=True) for g in local]
        shards.append(lax.psum_scatter(vector_local, "fsdp", scatter_dimension=1, tiled=True))
        mix_grad, proj_grad, expand_grad, shrink_grad, vector_grad = lax.psum(tuple(shards), "dp")

    beta = 1.0 - STEP ** (-0.8)
    grads = (mix_grad, proj_grad, expand_grad, shrink_grad)
    weights = (mix_weight, proj_weight, expand_weight, shrink_weight)
    old_rows = (mix_rows, proj_rows, expand_rows, shrink_rows)
    old_cols = (mix_cols, proj_cols, expand_cols, shrink_cols)
    rows_new, col_parts, scaled_parts = [], [], []
    for g, r in zip(grads, old_rows):
        square = g * g + 1e-30
        row = beta * r + (1.0 - beta) * jnp.mean(square, axis=1)
        rows_new.append(row)
        col_parts.append(jnp.sum(square, axis=0))
        scaled_parts.append(jnp.sum(g * g * (1.0 / row)[:, None], axis=0))
    moment_new = beta * vector_moment + (1.0 - beta) * (vector_grad * vector_grad + 1e-30)
    vector_step = vector_grad * lax.rsqrt(moment_new)
    small = jnp.concatenate(
        [
            jnp.stack([jnp.sum(r) for r in rows_new]),
            jnp.stack([jnp.sum(w * w) for w in weights]),
            jnp.sum(vector_step * vector_step, axis=1),
            jnp.sum(norm_vectors * norm_vectors, axis=1),
        ]
    )
    packed = jnp.concatenate(col_parts + scaled_parts + [small])
    if blocked:
        packed = jnp.pad(packed, (0, -packed.shape[0] % 1024)).reshape(-1, 128)
        packed = sum_all(packed, (CORE, NEAR, FAR)).reshape(-1)
    else:
        packed = lax.psum(packed, "fsdp")
    offset = 0
    total_cols = sum(c.shape[0] for c in old_cols)
    small = packed[2 * total_cols :]
    cols_new, new_weights = [], []
    for index in range(4):
        count = grads[index].shape[0] * owners
        wide = old_cols[index].shape[0]
        entries = count * wide
        col = beta * old_cols[index] + (1.0 - beta) * packed[offset : offset + wide] / count
        scaled = packed[total_cols + offset : total_cols + offset + wide]
        offset += wide
        cols_new.append(col)
        row_mean = small[index] / count
        update_square = row_mean * jnp.sum(scaled / col)
        clip_factor = jnp.maximum(1.0, jnp.sqrt(update_square / entries) / CLIP)
        rate = RATE * jnp.maximum(0.001, jnp.sqrt(small[4 + index] / entries))
        approx = rows_new[index][:, None] * col[None, :] / row_mean
        step = grads[index] * lax.rsqrt(approx)
        new_weights.append(weights[index] - (rate / clip_factor) * step)
    vector_clip = jnp.maximum(1.0, jnp.sqrt(small[8:14] / width) / CLIP)
    vector_rate = RATE * jnp.maximum(0.001, jnp.sqrt(small[14:20] / width))
    vector_new = norm_vectors - vector_rate[:, None] * (vector_step / vector_clip[:, None])
    return (
        block_output.reshape(1, length, width),
        input_grad.reshape(1, length, width),
        mix_grad, proj_grad, expand_grad, shrink_grad, vector_grad,
        *new_weights, vector_new, *rows_new, *cols_new, moment_new,
    )


def solution(mesh):
    sequence = P(AXES, None, None)
    ins = (
        sequence, sequence, P(AXES), P(AXES, None), P(AXES, None), P(AXES),
        P("fsdp", None), P("fsdp", None), P("fsdp", None), P("fsdp", None), P(None, "fsdp"),
        P("fsdp"), P("fsdp"), P("fsdp"), P("fsdp"), P(), P(), P(), P(), P(None, "fsdp"),
    )
    outs = (
        sequence, sequence,
        P("fsdp", None), P("fsdp", None), P("fsdp", None), P("fsdp", None), P(None, "fsdp"),
        P("fsdp", None), P("fsdp", None), P("fsdp", None), P("fsdp", None), P(None, "fsdp"),
        P("fsdp"), P("fsdp"), P("fsdp"), P("fsdp"), P(), P(), P(), P(), P(None, "fsdp"),
    )
    return jax.shard_map(body, mesh=mesh, in_specs=ins, out_specs=outs, check_vma=False)
```

```python
import functools

import jax
import jax.numpy as jnp
from jax import lax
from jax.experimental import pallas as pl
from jax.experimental.pallas import tpu as pltpu
from jax.sharding import PartitionSpec as P

HEADS = 12
STEP = 10
RATE = 0.5
CLIP = 1.0
F32 = jnp.float32
BF = jnp.bfloat16
VMEM_LIMIT = 60 * 1024 * 1024
AXES = ("dp", "fsdp")


def nn(a, b):
    return lax.dot_general(a, b, (((1,), (0,)), ((), ())), preferred_element_type=F32)


def nt(a, b):
    return lax.dot_general(a, b, (((1,), (1,)), ((), ())), preferred_element_type=F32)


def tn(a, b):
    return lax.dot_general(a, b, (((0,), (0,)), ((), ())), preferred_element_type=F32)


def normalise(h):
    mean = jnp.mean(h, axis=-1, keepdims=True)
    centered = h - mean
    inverse = lax.rsqrt(jnp.mean(centered * centered, axis=-1, keepdims=True) + 1e-06)
    return centered * inverse, inverse


def norm_back(grad, normal, inverse, gain):
    scaled = grad * gain
    first = jnp.mean(scaled, axis=-1, keepdims=True)
    second = jnp.mean(scaled * normal, axis=-1, keepdims=True)
    return inverse * (scaled - first - normal * second)


def params(**kw):
    return pltpu.CompilerParams(vmem_limit_bytes=VMEM_LIMIT, **kw)


def fixed(*shape):
    return pl.BlockSpec(shape, lambda *_: (0,) * len(shape), pipeline_mode=pl.Buffered(1))


ANYWHERE = pl.BlockSpec(memory_space=pl.ANY)
SCALARS = pl.BlockSpec(memory_space=pltpu.SMEM)


def shapes(*items):
    return [jax.ShapeDtypeStruct(shape, kind) for shape, kind in items]


def rows_of(ref):
    value = ref[...]
    return value.reshape(-1, value.shape[-1])


def mixed_kernel(tokens, marks, vectors, weight, normed, mixed):
    start = tokens[...].astype(F32) + tn(marks[...], vectors[...].astype(BF))
    normal, _ = normalise(start)
    low = (normal * vectors[0:1, :] + vectors[1:2, :]).astype(BF)
    normed[...] = low
    result = nn(low, weight[...]).astype(BF)
    for k in range(mixed.shape[0]):
        mixed[k] = result[:, k * 128 : (k + 1) * 128]


def run_mixed(tokens, marks, vectors, weight):
    rows, width = tokens.shape
    cols = weight.shape[1]
    tile = 256
    return pl.pallas_call(
        mixed_kernel,
        grid=(rows // tile,),
        in_specs=[
            pl.BlockSpec((tile, width), lambda i: (i, 0)),
            pl.BlockSpec((16, tile), lambda i: (0, i)),
            pl.BlockSpec((16, width), lambda i: (0, 0)),
            pl.BlockSpec((width, cols), lambda i: (0, 0)),
        ],
        out_specs=[
            pl.BlockSpec((tile, width), lambda i: (i, 0)),
            pl.BlockSpec((cols // 128, tile, 128), lambda i: (0, i, 0)),
        ],
        out_shape=[
            jax.ShapeDtypeStruct((rows, width), BF),
            jax.ShapeDtypeStruct((cols // 128, rows, 128), BF),
        ],
        compiler_params=params(),
        name="mixed",
    )(tokens, marks, vectors, weight)


def lane_iota(rows):
    return lax.broadcasted_iota(jnp.int32, (rows, 128), 1)


def key_extra(rows, length, base):
    lane = lane_iota(rows)
    row = lax.broadcasted_iota(jnp.int32, (rows, 128), 0)
    mask = jnp.where(row < length, 0.0, -1e30)
    ones = jnp.where((lane > base) & (lane < base + 4), 1.0, 0.0)
    return jnp.where(lane == base, mask, ones).astype(BF)


def attend_pair(length, query, key, value, context, kept, tile):
    rows = query.shape[0]
    lane = lane_iota(tile)
    lane_all = lane_iota(rows)
    count = rows // tile
    keys = [
        jnp.where(lane_all < 64, key[...], key_extra(rows, length, 64)),
        jnp.where(lane_all >= 64, key[...], key_extra(rows, length, 0)),
    ]
    values = value[...]

    def first(head, t):
        base = 64 - 64 * head
        mine = (lane < 64) if head == 0 else (lane >= 64)
        one = jnp.where(lane == base, 1.0, 0.0).astype(BF)
        q = jnp.where(mine, query[pl.ds(t * tile, tile), :] * BF(0.125), one)
        return q, nt(q, keys[head])

    def second(head, t, q, score):
        base = 64 - 64 * head
        mine = (lane < 64) if head == 0 else (lane >= 64)
        top = jnp.max(score, axis=-1, keepdims=True)
        expo = jnp.exp(score - top)
        total = jnp.sum(expo, axis=-1, keepdims=True)
        probs = (expo * (1.0 / total)).astype(BF)
        lse = top + jnp.log(total)
        high = lse.astype(BF).astype(F32)
        rest = lse - high
        mid = rest.astype(BF).astype(F32)
        extra = jnp.where(lane == base, 1.0, 0.0)
        extra = jnp.where(lane == base + 1, -high, extra)
        extra = jnp.where(lane == base + 2, -mid, extra)
        extra = jnp.where(lane == base + 3, mid - rest, extra)
        kept[head, pl.ds(t * tile, tile), :] = jnp.where(mine, q, extra.astype(BF))
        return probs

    order = [(head, t) for head in range(2) for t in range(count)]
    outs = {}
    ahead = first(*order[0])
    waiting = None
    for n, spot in enumerate(order):
        now = ahead
        if n + 1 < len(order):
            ahead = first(*order[n + 1])
        if waiting is not None:
            outs[waiting[0]] = nn(waiting[1], values)
        waiting = (spot, second(*spot, *now))
    outs[waiting[0]] = nn(waiting[1], values)
    for t in range(count):
        context[pl.ds(t * tile, tile), :] = jnp.where(lane < 64, outs[0, t], outs[1, t]).astype(BF)


def attend_kernel(length, query, key, value, context, kept, *, tile):
    attend_pair(length[0], query.at[0], key.at[0], value.at[0], context, kept, tile)


def run_attend(length, mixed, tile=256):
    groups, rows, _ = mixed.shape
    pairs = groups // 3
    return pl.pallas_call(
        functools.partial(attend_kernel, tile=tile),
        grid=(pairs,),
        in_specs=[
            pl.BlockSpec(memory_space=pltpu.SMEM),
            pl.BlockSpec((1, rows, 128), lambda p: (p, 0, 0)),
            pl.BlockSpec((1, rows, 128), lambda p: (pairs + p, 0, 0)),
            pl.BlockSpec((1, rows, 128), lambda p: (2 * pairs + p, 0, 0)),
        ],
        out_specs=[
            pl.BlockSpec((rows, 128), lambda p: (0, p)),
            pl.BlockSpec((2, rows, 128), lambda p: (p, 0, 0)),
        ],
        out_shape=[
            jax.ShapeDtypeStruct((rows, pairs * 128), BF),
            jax.ShapeDtypeStruct((2 * pairs, rows, 128), BF),
        ],
        compiler_params=params(),
        name="attend",
    )(length, mixed, mixed, mixed)


class Spot:
    def __init__(self):
        fs = lax.axis_index("fsdp")
        dp = lax.axis_index("dp")
        self.fs, self.dp = fs, dp
        self.c, self.z = fs % 2, fs // 2
        z0, z1 = self.z % 2, self.z // 2
        near, far = z1 * 2 + (1 - z0), (1 - z1) * 2 + z0
        self.zs = (self.z, near, far, (1 - z1) * 2 + (1 - z0))
        x, y = dp % 2, dp // 2
        turn_x, turn_y = 1 - 2 * x, 1 - 2 * y
        first = (y + turn_y * self.c) * 2 + x + turn_x * (1 - self.c)
        second = (y + turn_y * (1 - self.c)) * 2 + x + turn_x * self.c
        self.qs = (dp, first, second, (1 - y) * 2 + 1 - x)
        self.near = (dp, near * 2 + self.c)
        self.far = (dp, far * 2 + self.c)
        self.first = (first, fs)
        self.second = (second, fs)
        self.core = (dp, self.z * 2 + 1 - self.c)

        self.diag = (self.qs[3], fs)
        self.bits = (x, y, z0, z1)

    def row(self, k):
        return (self.dp, (self.fs + k) % 8)

    def rel_z(self, z):
        near = 1 - self.bits[2] if z % 2 else self.bits[2]
        far = 1 - self.bits[3] if z // 2 else self.bits[3]
        return near * 2 + far

    def rel_q(self, q):
        x = 1 - self.bits[0] if q % 2 else self.bits[0]
        y = 1 - self.bits[1] if q // 2 else self.bits[1]
        return x + (y - x) * self.c, y + (x - y) * self.c


def greet(peers):
    barrier = pltpu.get_barrier_semaphore()
    for peer in peers:
        pl.semaphore_signal(barrier, inc=1, device_id=peer, device_id_type=MESH)
    pl.semaphore_wait(barrier, len(peers))


def link(src, dst, send_sem, recv_sem, target):
    return pltpu.make_async_remote_copy(
        src_ref=src, dst_ref=dst, send_sem=send_sem, recv_sem=recv_sem,
        device_id=target, device_id_type=MESH,
    )


def total_of(*parts):
    value = parts[0].astype(F32)
    for part in parts[1:]:
        value = value + part.astype(F32)
    return value


MESH = pl.DeviceIdType.MESH


def front_kernel(
    length, tokens, marks, share, mix_w, proj_w, expand_w, shrink_w,
    a_out, b_out, c_out, vectors_out, normed_out, mixed_out, context, kept,
    stage, own, w_a, vec_in, vectors, normed, mixed, send, recv, vec_send, vec_recv, local, *, tile
):
    step = pl.program_id(0)
    spot = Spot()
    c, dp = spot.c, spot.dp

    def block(g, z, cc, q):
        if g == 0:
            return w_a.at[q, z, cc]
        if g == 1:
            return b_out.at[q, z, cc]
        return c_out.at[z, cc, q]

    def remote(g, z, cc, q, kind, target, mine=False):
        dst = block(g, z, cc, q)
        return pltpu.make_async_remote_copy(
            src_ref=own.at[g - 1] if mine and g > 0 else dst,
            dst_ref=dst,
            send_sem=send.at[g, kind],
            recv_sem=recv.at[g, (z * 2 + cc) * 4 + q],
            device_id=target,
            device_id_type=MESH,
        )

    def push(g, z, q, kind, target, mine=False):
        remote(g, z, c, q, kind, target, mine).start()

    def arrive(g, z, cc, q):
        remote(g, z, cc, q, 0, spot.core).wait_recv()

    def phase0(g):
        push(g, spot.z, dp, 0, spot.far, True)
        push(g, spot.z, dp, 1, spot.near, True)
        push(g, spot.z, dp, 7, spot.second, True)
        push(g, spot.z, dp, 3, spot.first, True)
        push(g, spot.z, dp, 15, spot.core, True)

    def spread(g, k):
        push(g, spot.zs[k], dp, 7 + k, spot.second)
        push(g, spot.zs[k], dp, 3 + k, spot.first)
        push(g, spot.zs[k], dp, 15 + k, spot.core)

    def phase1(g):
        arrive(g, spot.zs[2], c, dp)
        push(g, spot.zs[2], dp, 2, spot.near)
        spread(g, 2)

    def phase2(g):
        arrive(g, spot.zs[1], c, dp)
        spread(g, 1)
        arrive(g, spot.zs[3], c, dp)
        spread(g, 3)

    def phase3(g):
        for k in range(4):
            arrive(g, spot.zs[k], c, spot.qs[1])
            push(g, spot.zs[k], spot.qs[1], 11 + k, spot.second)
            push(g, spot.zs[k], spot.qs[1], 19 + k, spot.core)

    def phase4(g):
        for m in (2, 3):
            for k in range(4):
                arrive(g, spot.zs[k], c, spot.qs[m])
                push(g, spot.zs[k], spot.qs[m], 15 + 4 * m + k, spot.core)

    def phase5(g):
        for q in range(4):
            for z in range(4):
                arrive(g, z, 1 - c, q)

    def phase6(g):
        for kind in range(31):
            remote(g, spot.z, c, dp, kind, spot.core, True).wait_send()

    def vec_copy(k):
        return pltpu.make_async_remote_copy(
            src_ref=vec_in.at[spot.fs],
            dst_ref=vec_in.at[spot.fs],
            send_sem=vec_send.at[k],
            recv_sem=vec_recv.at[spot.fs],
            device_id=spot.row(k),
            device_id_type=MESH,
        )

    def vec_arrive(k):
        other = (spot.fs + k) % 8
        pltpu.make_async_remote_copy(
            src_ref=vec_in.at[other],
            dst_ref=vec_in.at[other],
            send_sem=vec_send.at[k],
            recv_sem=vec_recv.at[other],
            device_id=spot.row(k),
            device_id_type=MESH,
        ).wait_recv()

    def keep_copies():
        return (
            pltpu.make_async_copy(w_a, a_out, local.at[3]),
            pltpu.make_async_copy(own.at[0], b_out.at[dp, spot.z, c], local.at[4]),
            pltpu.make_async_copy(own.at[1], c_out.at[spot.z, c, dp], local.at[5]),
            pltpu.make_async_copy(normed, normed_out, local.at[6]),
            pltpu.make_async_copy(mixed, mixed_out, local.at[7]),
        )

    @pl.when(step == 0)
    def _():
        barrier = pltpu.get_barrier_semaphore()
        peers = [spot.row(k) for k in range(1, 8)] + [spot.first, spot.second]
        for peer in peers:
            pl.semaphore_signal(barrier, inc=1, device_id=peer, device_id_type=MESH)

        @pl.when(dp < 3)
        def _():
            columns = pl.ds(pl.multiple_of(dp * 768, 128), 768)
            pltpu.make_async_copy(mix_w.at[:, columns], stage.at[0], local.at[0]).start()

        @pl.when(dp == 3)
        def _():
            pltpu.make_async_copy(proj_w, stage.at[0], local.at[0]).start()

        columns = pl.ds(pl.multiple_of(dp * 768, 128), 768)
        second = pltpu.make_async_copy(expand_w.at[:, columns], stage.at[1], local.at[1])
        second.start()
        third = pltpu.make_async_copy(
            shrink_w.at[pl.ds(pl.multiple_of(dp * 96, 8), 96), :], stage.at[2], local.at[2]
        )
        third.start()
        vec_in[spot.fs] = share[...]
        pltpu.make_async_copy(proj_w, stage.at[0], local.at[0]).wait()
        w_a[dp, spot.z, c] = stage[0].astype(BF)
        pl.semaphore_wait(barrier, len(peers))
        phase0(0)
        for k in range(1, 8):
            vec_copy(k).start()
        second.wait()
        own[0] = stage[1].astype(BF)
        third.wait()
        own[1] = stage[2].astype(BF)
        copies = keep_copies()
        copies[1].start()
        copies[2].start()
        for k in range(1, 8):
            vec_arrive(k)
        total = jnp.zeros((16, 768), F32)
        for f in range(8):
            row = lax.broadcasted_iota(jnp.int32, (128, 768), 0)
            lane = lax.broadcasted_iota(jnp.int32, (128, 768), 1)
            pick = jnp.where((lane - 96 * f == row) & (row < 96), 1.0, 0.0).astype(BF)
            total += nn(vec_in[f], pick)
        vectors[...] = total
        vectors_out[...] = total

        def norm(t):
            part = pl.ds(t * 256, 256)
            start = tokens[part, :].astype(F32) + tn(marks[:, part], total.astype(BF))
            normal, _ = normalise(start)
            normed[part, :] = (normal * total[0:1, :] + total[1:2, :]).astype(BF)

        norm(0)
        phase1(0)
        norm(1)
        phase2(0)
        norm(2)
        norm(3)
        phase3(0)
        phase0(1)
        phase0(2)
        phase4(0)
        phase5(0)
        copies[0].start()
        copies[3].start()
        for q in range(3):
            weight = rows_of(w_a.at[q])
            for t in range(4):
                part = pl.ds(t * 256, 256)
                result = nn(normed[part, :], weight).astype(BF)
                for k in range(6):
                    mixed[q * 6 + k, part, :] = result[:, k * 128 : (k + 1) * 128]
            if q == 0:
                phase1(1)
                phase1(2)
            if q == 2:
                phase2(1)
                phase2(2)
        copies[4].start()

    @pl.when(step > 0)
    def _():
        p = step - 1
        attend_pair(length[0], mixed.at[p], mixed.at[6 + p], mixed.at[12 + p], context, kept, tile)

    for at, phase, g in ((1, phase3, 1), (2, phase3, 2), (5, phase4, 1), (6, phase4, 2)):

        @pl.when(step == at)
        def _():
            phase(g)

    @pl.when(step == 6)
    def _():
        phase5(1)
        phase5(2)
        for g in range(3):
            phase6(g)
        for k in range(1, 8):
            vec_copy(k).wait_send()
        for copy in keep_copies():
            copy.wait()


def run_front(length, tokens, marks, share, mix_w, proj_w, expand_w, shrink_w, tile=256):
    rows, width = tokens.shape
    anywhere = pl.BlockSpec(memory_space=pl.ANY)
    once = pl.Buffered(1)

    def whole(*shape):
        return pl.BlockSpec(shape, lambda i: (0,) * len(shape), pipeline_mode=once)

    return pl.pallas_call(
        functools.partial(front_kernel, tile=tile),
        grid=(7,),
        in_specs=[
            pl.BlockSpec(memory_space=pltpu.SMEM),
            whole(rows, width),
            whole(16, rows),
            whole(16, 128),
            anywhere,
            anywhere,
            anywhere,
            anywhere,
        ],
        out_specs=[
            anywhere,
            anywhere,
            anywhere,
            whole(16, width),
            anywhere,
            anywhere,
            pl.BlockSpec((rows, 128), lambda i: (0, jnp.maximum(i - 1, 0))),
            pl.BlockSpec((2, rows, 128), lambda i: (jnp.maximum(i - 1, 0), 0, 0)),
        ],
        out_shape=[
            jax.ShapeDtypeStruct((4, 4, 2, 96, 768), BF),
            jax.ShapeDtypeStruct((4, 4, 2, 96, 768), BF),
            jax.ShapeDtypeStruct((4, 2, 4, 96, 768), BF),
            jax.ShapeDtypeStruct((16, width), F32),
            jax.ShapeDtypeStruct((rows, width), BF),
            jax.ShapeDtypeStruct((18, rows, 128), BF),
            jax.ShapeDtypeStruct((rows, width), BF),
            jax.ShapeDtypeStruct((12, rows, 128), BF),
        ],
        scratch_shapes=[
            pltpu.VMEM((3, 96, 768), F32),
            pltpu.VMEM((2, 96, 768), BF),
            pltpu.VMEM((4, 4, 2, 96, 768), BF),
            pltpu.VMEM((8, 16, 128), BF),
            pltpu.VMEM((16, width), F32),
            pltpu.VMEM((rows, width), BF),
            pltpu.VMEM((18, rows, 128), BF),
            pltpu.SemaphoreType.DMA((3, 31)),
            pltpu.SemaphoreType.DMA((3, 32)),
            pltpu.SemaphoreType.DMA((8,)),
            pltpu.SemaphoreType.DMA((8,)),
            pltpu.SemaphoreType.DMA((8,)),
        ],
        compiler_params=params(collective_id=0, has_side_effects=True),
        name="front",
    )(length, tokens, marks, share, mix_w, proj_w, expand_w, shrink_w)


def attend_back_pair(length, kept, key, value, ctx_grad, dq, dk, dv, tile):
    rows = key.shape[0]
    lane = lane_iota(tile)
    lane_all = lane_iota(rows)
    count = rows // tile
    plain, plain_values = key[...], value[...]
    keys = [
        jnp.where(lane_all < 64, plain, key_extra(rows, length, 64)),
        jnp.where(lane_all >= 64, plain, key_extra(rows, length, 0)),
    ]
    zero = jnp.zeros_like(plain_values)
    values = [
        jnp.where(lane_all < 64, plain_values, zero),
        jnp.where(lane_all >= 64, plain_values, zero),
    ]

    def first(head, t):
        q = kept[head, pl.ds(t * tile, tile), :]
        grad = ctx_grad[pl.ds(t * tile, tile), :]
        return q, grad, nt(keys[head], q), nt(values[head], grad)

    sums = {}

    def second(head, t, q, grad, score, prob_back):
        probs = jnp.exp(score)
        product = probs * prob_back
        delta = jnp.sum(product, axis=0, keepdims=True)
        score_back = (product - probs * delta).astype(BF)
        dv_part = nn(probs.astype(BF), grad)
        dk_part = nn(score_back, q)
        sums[head, "v"] = dv_part if t == 0 else sums[head, "v"] + dv_part
        sums[head, "k"] = dk_part if t == 0 else sums[head, "k"] + dk_part
        sums[head, t] = tn(score_back, plain)

    order = [(head, t) for head in range(2) for t in range(count)]
    ahead = first(*order[0])
    for n, spot in enumerate(order):
        now = ahead
        if n + 1 < len(order):
            ahead = first(*order[n + 1])
        second(*spot, *now)
    dk[...] = jnp.where(lane_all < 64, sums[0, "k"], sums[1, "k"]).astype(BF)
    dv[...] = jnp.where(lane_all < 64, sums[0, "v"], sums[1, "v"]).astype(BF)
    for t in range(count):
        both = jnp.where(lane < 64, sums[0, t], sums[1, t]) * 0.125
        dq[pl.ds(t * tile, tile), :] = both.astype(BF)


def attend_back_kernel(length, kept, key, value, ctx_grad, dq, dk, dv, *, tile):
    attend_back_pair(length[0], kept, key.at[0], value.at[0], ctx_grad, dq, dk, dv, tile)


def attend_back_send_kernel(
    length, kept, key, value, ctx_grad, near_e, got_e, near_s, got_s,
    dq, dk, dv, fin_e, fin_s,
    out2, in2, out3, in3, out4, in4, hold, sent, landed, *, tile
):
    step = pl.program_id(0)
    spot = Spot()
    near, got, fin = (near_e, near_s), (got_e, got_s), (fin_e, fin_s)

    def copy(stage, g):
        src, dst, target = (
            (out2, in2, spot.second), (out3, in3, spot.near), (out4, in4, spot.far),
        )[stage]
        return link(src.at[g], dst.at[g], sent.at[stage, g], landed.at[stage, g], target)

    def stage2(g):
        for r in range(4):
            out2[g, r] = total_of(near[g][1, r], got[g][1, r]).astype(BF)
        copy(0, g).start()

    def stage3(g):
        copy(0, g).wait_recv()
        for r in range(2):
            out3[g, r] = total_of(near[g][0, 2 + r], got[g][0, 2 + r], in2[g, 2 + r]).astype(BF)
        copy(1, g).start()
        for r in range(2):
            hold[g, r] = total_of(near[g][0, r], got[g][0, r], in2[g, r])

    def stage4(g):
        copy(1, g).wait_recv()
        out4[g] = total_of(hold[g, 1], in3[g, 1]).astype(BF)
        copy(2, g).start()
        hold[g, 0] = total_of(hold[g, 0], in3[g, 0])

    def stage5(g):
        copy(2, g).wait_recv()
        fin[g][...] = total_of(hold[g, 0], in4[g]).astype(BF)
        for stage in range(3):
            copy(stage, g).wait_send()

    @pl.when(step == 0)
    def _():
        greet([spot.second, spot.near, spot.far])
        stage2(0)
        stage2(1)

    attend_back_pair(length[0], kept, key.at[0], value.at[0], ctx_grad, dq, dk, dv, tile)
    for at, stage, g in ((1, stage3, 0), (2, stage3, 1), (3, stage4, 0), (4, stage4, 1), (5, stage5, 0), (5, stage5, 1)):

        @pl.when(step == at)
        def _():
            stage(g)


def run_attend_back_send(length, kept, mixed, ctx_grad, near_e, got_e, near_s, got_s, tile=128):
    groups, rows, _ = mixed.shape
    pairs = groups // 3
    spec = pl.BlockSpec((rows, 128), lambda p: (0, p))
    block = (96, 768)
    return pl.pallas_call(
        functools.partial(attend_back_send_kernel, tile=tile),
        grid=(pairs,),
        in_specs=[
            SCALARS,
            pl.BlockSpec((2, rows, 128), lambda p: (p, 0, 0)),
            pl.BlockSpec((1, rows, 128), lambda p: (pairs + p, 0, 0)),
            pl.BlockSpec((1, rows, 128), lambda p: (2 * pairs + p, 0, 0)),
            spec,
            *[fixed(2, 4, *block)] * 4,
        ],
        out_specs=[spec, spec, spec, fixed(*block), fixed(*block)],
        out_shape=shapes(*[((rows, pairs * 128), BF)] * 3, (block, BF), (block, BF)),
        scratch_shapes=[
            pltpu.VMEM((2, 4) + block, BF),
            pltpu.VMEM((2, 4) + block, BF),
            pltpu.VMEM((2, 2) + block, BF),
            pltpu.VMEM((2, 2) + block, BF),
            pltpu.VMEM((2,) + block, BF),
            pltpu.VMEM((2,) + block, BF),
            pltpu.VMEM((2, 2) + block, F32),
            pltpu.SemaphoreType.DMA((3, 2)),
            pltpu.SemaphoreType.DMA((3, 2)),
        ],
        compiler_params=params(collective_id=2, has_side_effects=True),
        name="attend_back",
    )(length, kept, mixed, mixed, ctx_grad, near_e, got_e, near_s, got_s)


def run_attend_back(length, kept, mixed, ctx_grad, tile=128):
    groups, rows, _ = mixed.shape
    pairs = groups // 3
    width = pairs * 128
    spec = pl.BlockSpec((rows, 128), lambda p: (0, p))
    return pl.pallas_call(
        functools.partial(attend_back_kernel, tile=tile),
        grid=(pairs,),
        in_specs=[
            pl.BlockSpec(memory_space=pltpu.SMEM),
            pl.BlockSpec((2, rows, 128), lambda p: (p, 0, 0)),
            pl.BlockSpec((1, rows, 128), lambda p: (pairs + p, 0, 0)),
            pl.BlockSpec((1, rows, 128), lambda p: (2 * pairs + p, 0, 0)),
            spec,
        ],
        out_specs=[spec, spec, spec],
        out_shape=[jax.ShapeDtypeStruct((rows, width), BF)] * 3,
        compiler_params=params(),
        name="attend_back",
    )(length, kept, mixed, mixed, ctx_grad)


def gelu_pair(v):
    cdf = 0.5 * (1.0 + lax.erf(v * 0.7071067811865476))
    return v * cdf, cdf + v * jnp.exp(-0.5 * v * v) * 0.3989422804014327


def feed_start(length, context, tokens, marks, vectors, proj, cotangent, middle, normed, bound, parts):
    for part in parts:
        start = tokens[part, :].astype(F32) + tn(marks[:, part], vectors[...].astype(BF))
        mid = start + nn(context[part, :], proj)
        middle[part, :] = mid
        normal, _ = normalise(mid)
        normed[part, :] = (normal * vectors[2:3, :] + vectors[3:4, :]).astype(BF)
        row = part.start + lax.broadcasted_iota(jnp.int32, (part.size, 1), 0)
        kept = jnp.where(row < length, cotangent[part, :].astype(F32), 0.0)
        bound[part, :] = kept.astype(BF)


def feed_chunk(j, expand, shrink, normed, bound, active, inner_back, out_sum, back_sum, parts):
    for part in parts:
        inner = nn(normed[part, :], expand)
        act_back = nt(bound[part, :], shrink)
        act, slope = gelu_pair(inner)
        act = act.astype(BF)
        active[part, :] = act
        back = (act_back * slope).astype(BF)
        inner_back[part, :] = back
        out_part = nn(act, shrink)
        back_part = nt(back, expand)

        @pl.when(j == 0)
        def _():
            out_sum[part, :] = out_part
            back_sum[part, :] = back_part

        @pl.when(j > 0)
        def _():
            out_sum[part, :] += out_part
            back_sum[part, :] += back_part


def feed_finish(vectors, proj, middle, normed, bound, out_sum, back_sum, output, middle_back, ctx_back, gain_grads, parts):
    gain = jnp.zeros((1, middle.shape[1]), F32)
    shift = jnp.zeros((1, middle.shape[1]), F32)
    for part in parts:
        mid = middle[part, :]
        output[part, :] = (mid + out_sum[part, :]).astype(BF)
        normal, inverse = normalise(mid)
        grad = back_sum[part, :]
        gain += jnp.sum(grad * normal, axis=0, keepdims=True)
        shift += jnp.sum(grad, axis=0, keepdims=True)
        back = bound[part, :].astype(F32) + norm_back(grad, normal, inverse, vectors[2:3, :])
        middle_back[part, :] = back
        low = back.astype(BF)
        normed[part, :] = low
        ctx_back[part, :] = nt(low, proj).astype(BF)
    gain_grads[...] = jnp.concatenate([gain, shift, jnp.zeros((6, gain.shape[1]), F32)], axis=0)


def feed_kernel(
    length, context, tokens, marks, vectors, proj, expand, shrink, cotangent,
    output, middle_back, ctx_back, gain_grads, proj_grad, expand_grad, shrink_grad,
    middle, normed, bound, out_sum, active, inner_back, *, tile
):
    j = pl.program_id(0)
    parts = [pl.ds(t * tile, tile) for t in range(tokens.shape[0] // tile)]

    @pl.when(j == 0)
    def _():
        feed_start(
            length[0], context, tokens, marks, vectors, proj[...], cotangent, middle, normed, bound, parts
        )

    feed_chunk(
        j, expand[...], shrink[...], normed, bound, active, inner_back, out_sum, middle_back, parts
    )
    expand_grad[...] = tn(normed[...], inner_back[...])
    shrink_grad[...] = tn(active[...], bound[...])

    @pl.when(j == pl.num_programs(0) - 1)
    def _():
        feed_finish(
            vectors, proj[...], middle, normed, bound, out_sum, middle_back,
            output, middle_back, ctx_back, gain_grads, parts,
        )
        proj_grad[...] = tn(context[...], normed[...])


def run_feed(length, context, tokens, marks, vectors, proj, expand, shrink, cotangent, tile=256):
    rows, width = tokens.shape
    inner = expand.shape[1]
    chunk = width
    wide = pl.BlockSpec((width, chunk), lambda j: (0, j))
    tall = pl.BlockSpec((chunk, width), lambda j: (j, 0))
    return pl.pallas_call(
        functools.partial(feed_kernel, tile=tile),
        grid=(inner // chunk,),
        in_specs=[
            SCALARS, fixed(rows, width), fixed(rows, width), fixed(16, rows), fixed(16, width),
            fixed(width, width), wide, tall, fixed(rows, width),
        ],
        out_specs=[
            fixed(rows, width), fixed(rows, width), fixed(rows, width), fixed(8, width),
            fixed(width, width), wide, tall,
        ],
        out_shape=shapes(
            ((rows, width), BF), ((rows, width), F32), ((rows, width), BF), ((8, width), F32),
            ((width, width), F32), ((width, inner), F32), ((inner, width), F32),
        ),
        scratch_shapes=[
            pltpu.VMEM((rows, width), F32),
            pltpu.VMEM((rows, width), BF),
            pltpu.VMEM((rows, width), BF),
            pltpu.VMEM((rows, width), F32),
            pltpu.VMEM((rows, chunk), BF),
            pltpu.VMEM((rows, chunk), BF),
        ],
        compiler_params=params(),
        name="feed",
    )(length, context, tokens, marks, vectors, proj, expand, shrink, cotangent)


def feed_send_kernel(
    length, context, tokens, marks, vectors, proj, expand, shrink, cotangent,
    output, middle_back, ctx_back, gain_grads, proj_keep, proj_send, near_e, near_s, got_e, got_s,
    middle, normed, bound, out_sum, active, inner_back,
    keep_e, keep_s, send_e, send_s, pair_e, pair_s, out_e, out_s,
    pair_sem, pair_got, first_e_sem, first_e_got, first_s_sem, first_s_got, *, tile
):
    j = pl.program_id(0)
    spot = Spot()
    c = spot.c
    parts = [pl.ds(t * tile, tile) for t in range(tokens.shape[0] // tile)]

    def pair_copy(step, g):
        slot = step % 2
        src, dst = (send_e, pair_e) if g == 0 else (send_s, pair_s)
        return link(
            src.at[slot], dst.at[step], pair_sem.at[g, slot], pair_got.at[g, step], spot.core
        )

    def first_e(p2):
        return link(
            out_e.at[p2], got_e.at[p2], first_e_sem.at[p2], first_e_got.at[p2], spot.first
        )

    def first_s(p2, r):
        return link(
            out_s.at[p2, r], got_s.at[p2, r], first_s_sem.at[p2, r], first_s_got.at[p2, r], spot.first
        )

    def to_first(step):
        slot = step % 2
        pair_copy(step, 0).wait_recv()
        p1, p2 = spot.rel_q(step)

        @pl.when(p1 == 1)
        def _():
            for r in range(4):
                out_e[p2, r] = total_of(keep_e[slot, r], pair_e[step, r]).astype(BF)
            first_e(p2).start()

        @pl.when(p1 == 0)
        def _():
            for r in range(4):
                near_e[p2, r] = total_of(keep_e[slot, r], pair_e[step, r]).astype(BF)

        pair_copy(step, 1).wait_recv()
        r = spot.rel_z(step)
        for p2, q in enumerate((spot.qs[1], spot.qs[3])):
            out_s[p2, r] = total_of(keep_s[slot, q], pair_s[step, q]).astype(BF)
            first_s(p2, r).start()
        for p2, q in enumerate((spot.qs[0], spot.qs[2])):
            near_s[p2, r] = total_of(keep_s[slot, q], pair_s[step, q]).astype(BF)

    @pl.when(j == 0)
    def _():
        greet([spot.core, spot.first])
        feed_start(
            length[0], context, tokens, marks, vectors, rows_of(proj), cotangent,
            middle, normed, bound, parts,
        )

    feed_chunk(
        j, rows_of(expand), rows_of(shrink), normed, bound, active, inner_back,
        out_sum, middle_back, parts,
    )
    for step in range(3):

        @pl.when(j == step + 1)
        def _():
            to_first(step)

    slot = j % 2

    @pl.when(j >= 2)
    def _():
        pair_copy(j - 2, 0).wait_send()
        pair_copy(j - 2, 1).wait_send()

    grad_e = tn(normed[...], inner_back[...])
    for z in range(4):
        r = spot.rel_z(z)
        for cc in range(2):
            piece = grad_e[(2 * z + cc) * 96 : (2 * z + cc + 1) * 96, :].astype(BF)

            @pl.when(c == cc)
            def _():
                keep_e[slot, r] = piece

            @pl.when(c != cc)
            def _():
                send_e[slot, r] = piece

    pair_copy(j, 0).start()
    grad_s = tn(active[...], bound[...])
    for cc in range(2):
        for q in range(4):
            piece = grad_s[(cc * 4 + q) * 96 : (cc * 4 + q + 1) * 96, :].astype(BF)

            @pl.when(c == cc)
            def _():
                keep_s[slot, q] = piece

            @pl.when(c != cc)
            def _():
                send_s[slot, q] = piece

    pair_copy(j, 1).start()

    @pl.when(j == 3)
    def _():
        feed_finish(
            vectors, rows_of(proj), middle, normed, bound, out_sum, middle_back,
            output, middle_back, ctx_back, gain_grads, parts,
        )
        to_first(3)
        grad_p = tn(context[...], normed[...])
        for z in range(4):
            r = spot.rel_z(z)
            for cc in range(2):
                piece = grad_p[(2 * z + cc) * 96 : (2 * z + cc + 1) * 96, :].astype(BF)

                @pl.when(c == cc)
                def _():
                    proj_keep[r] = piece

                @pl.when(c != cc)
                def _():
                    proj_send[r] = piece

        for step in (2, 3):
            for g in range(2):
                pair_copy(step, g).wait_send()
        for p2 in range(2):
            first_e(p2).wait_send()
            first_e(p2).wait_recv()
            for r in range(4):
                first_s(p2, r).wait_send()
                first_s(p2, r).wait_recv()


def run_feed_send(length, context, tokens, marks, vectors, a_full, b_full, c_full, cotangent, tile=256):
    rows, width = tokens.shape
    block = (96, 768)
    return pl.pallas_call(
        functools.partial(feed_send_kernel, tile=tile),
        grid=(4,),
        in_specs=[
            SCALARS, fixed(rows, width), fixed(rows, width), fixed(16, rows), fixed(16, width),
            pl.BlockSpec((1, 4, 2) + block, lambda j: (3, 0, 0, 0, 0), pipeline_mode=pl.Buffered(1)),
            pl.BlockSpec((1, 4, 2) + block, lambda j: (j, 0, 0, 0, 0)),
            pl.BlockSpec((1, 2, 4) + block, lambda j: (j, 0, 0, 0, 0)),
            fixed(rows, width),
        ],
        out_specs=[
            fixed(rows, width), fixed(rows, width), fixed(rows, width), fixed(8, width),
            fixed(4, *block), fixed(4, *block), fixed(2, 4, *block), fixed(2, 4, *block),
            ANYWHERE, ANYWHERE,
        ],
        out_shape=shapes(
            ((rows, width), BF), ((rows, width), F32), ((rows, width), BF), ((8, width), F32),
            ((4,) + block, BF), ((4,) + block, BF),
            *[((2, 4) + block, BF)] * 4,
        ),
        scratch_shapes=[
            pltpu.VMEM((rows, width), F32),
            pltpu.VMEM((rows, width), BF),
            pltpu.VMEM((rows, width), BF),
            pltpu.VMEM((rows, width), F32),
            pltpu.VMEM((rows, width), BF),
            pltpu.VMEM((rows, width), BF),
            *[pltpu.VMEM((2, 4) + block, BF)] * 4,
            *[pltpu.VMEM((4, 4) + block, BF)] * 2,
            *[pltpu.VMEM((2, 4) + block, BF)] * 2,
            pltpu.SemaphoreType.DMA((2, 2)),
            pltpu.SemaphoreType.DMA((2, 4)),
            pltpu.SemaphoreType.DMA((2,)),
            pltpu.SemaphoreType.DMA((2,)),
            pltpu.SemaphoreType.DMA((2, 4)),
            pltpu.SemaphoreType.DMA((2, 4)),
        ],
        compiler_params=params(collective_id=1, has_side_effects=True),
        name="feed",
    )(length, context, tokens, marks, vectors, a_full, b_full, c_full, cotangent)


def mix_grad_kernel(normed, dq, dk, dv, grad_out):
    j = pl.program_id(0)
    for index, source in enumerate((dq, dk, dv)):

        @pl.when(j == index)
        def _():
            grad_out[...] = tn(normed[...], source[...])


def run_mix_grad(normed, dq, dk, dv):
    rows, width = normed.shape
    return pl.pallas_call(
        mix_grad_kernel,
        grid=(3,),
        in_specs=[fixed(rows, width)] * 4,
        out_specs=pl.BlockSpec((width, width), lambda j: (0, j)),
        out_shape=jax.ShapeDtypeStruct((width, 3 * width), F32),
        compiler_params=params(),
        name="mix_grad",
    )(normed, dq, dk, dv)


def input_part(tokens, marks, vectors, weights, sources, middle_back):
    start = tokens.astype(F32) + tn(marks, vectors.astype(BF))
    normal, inverse = normalise(start)
    grad = nt(sources[0], weights[0])
    for source, weight in zip(sources[1:], weights[1:]):
        grad += nt(source, weight)
    gain = jnp.sum(grad * normal, axis=0, keepdims=True)
    shift = jnp.sum(grad, axis=0, keepdims=True)
    result = middle_back + norm_back(grad, normal, inverse, vectors[0:1, :])
    spread = tn(marks, jnp.ones(vectors.shape, BF))
    mark = jnp.sum(spread * result, axis=0, keepdims=True)
    return result, gain, shift, mark


def input_kernel(tokens, marks, vectors, weight, dq, dk, dv, middle_back, input_grad, sums):
    i = pl.program_id(0)
    width = tokens.shape[1]
    weights = [weight[:, k * width : (k + 1) * width] for k in range(3)]
    result, gain, shift, mark = input_part(
        tokens[...], marks[...], vectors[...], weights, (dq[...], dk[...], dv[...]), middle_back[...]
    )
    input_grad[...] = result
    both = jnp.concatenate([gain, shift, mark, jnp.zeros((5, width), F32)], axis=0)

    @pl.when(i == 0)
    def _():
        sums[...] = both

    @pl.when(i > 0)
    def _():
        sums[...] += both


def run_input(tokens, marks, vectors, weight, dq, dk, dv, middle_back, tile=256):
    rows, width = tokens.shape
    spec = pl.BlockSpec((tile, width), lambda i: (i, 0))
    return pl.pallas_call(
        input_kernel,
        grid=(rows // tile,),
        in_specs=[
            spec,
            pl.BlockSpec((16, tile), lambda i: (0, i)),
            fixed(16, width),
            fixed(width, 3 * width),
            spec,
            spec,
            spec,
            spec,
        ],
        out_specs=[spec, fixed(8, width)],
        out_shape=shapes(((rows, width), F32), ((8, width), F32)),
        compiler_params=params(),
        name="input_grad",
    )(tokens, marks, vectors, weight, dq, dk, dv, middle_back)


BETA = 1.0 - STEP ** (-0.8)


def last_kernel(
    row_flag, normed, dq, dk, dv, proj_keep, proj_send, fin_e, fin_s, marks, vectors, gain2,
    old_rows, moment, plain, tokens_in, mix_in, back_in, w_mix_in, w_proj_in, w_expand_in, w_shrink_in,
    input_grad, grads, rows_new, sums_a, sums_b, vector_sum,
    tokens, mix, back, w_mix, w_proj, w_expand, w_shrink,
    keep, send, pair, out1, in1, out2, in2, out3, in3, out4, in4, hold,
    full_a, full_b, vec_out, vec_in, slots_a, slots_b,
    loads, pair_sent, pair_got, sent1, got1, sent, got, full_sent, full_got, vec_sent, vec_got,
    slot_sent, slot_got,
):
    spot = Spot()
    c, dp, fs = spot.c, spot.dp, spot.fs
    local = [
        pltpu.make_async_copy(src, dst, loads.at[k])
        for k, (src, dst) in enumerate(
            (
                (tokens_in, tokens), (mix_in.at[pl.ds(0, 3)], mix), (back_in, back),
                (w_mix_in, w_mix), (w_proj_in, w_proj), (w_expand_in, w_expand), (w_shrink_in, w_shrink),
            )
        )
    ]
    for copy in local:
        copy.start()
    greet([spot.row(k) for k in range(1, 8)] + [spot.first, spot.second, spot.diag])
    trio = (spot.first, spot.second, spot.diag)

    def share_b(g, k):
        place = full_b.at[g, dp]
        return link(place, place, full_sent.at[g, k], full_got.at[g, dp], trio[k])

    def share_a(h, k):
        place = full_a.at[dp, h]
        return link(place, place, full_sent.at[2 + h, k], full_got.at[2 + h, dp], trio[k])

    def shared_b(g):
        for q in spot.qs[1:]:
            place = full_b.at[g, q]
            link(place, place, full_sent.at[g, 0], full_got.at[g, q], spot.first).wait_recv()

    def shared_a(h):
        for q in spot.qs[1:]:
            place = full_a.at[q, h]
            link(place, place, full_sent.at[2 + h, 0], full_got.at[2 + h, q], spot.first).wait_recv()

    full_b[0, dp] = fin_e[...]
    full_b[1, dp] = fin_s[...]
    for g in range(2):
        for k in range(3):
            share_b(g, k).start()

    def pair_copy(h, q):
        return link(
            send.at[h, q], pair.at[h, q], pair_sent.at[h, q], pair_got.at[h, q], spot.core
        )

    def first_copy(h, p2):
        return link(
            out1.at[h, p2], in1.at[h, p2], sent1.at[h, p2], got1.at[h, p2], spot.first
        )

    def copy(stage, h):
        src, dst, target = (
            (out2, in2, spot.second), (out3, in3, spot.near), (out4, in4, spot.far),
        )[stage]
        return link(src.at[h], dst.at[h], sent.at[stage, h], got.at[stage, h], target)

    def half_grad(h, q):
        columns = slice(h * 384, (h + 1) * 384)
        if q == 3:

            @pl.when(c >= 0)
            def _():
                for r in range(4):
                    keep[h, 3, r] = proj_keep[r, :, columns]
                    send[h, 3, r] = proj_send[r, :, columns]
        else:
            grad = tn(normed[...], (dq, dk, dv)[q][:, columns])
            for z in range(4):
                r = spot.rel_z(z)
                for cc in range(2):
                    piece = grad[(2 * z + cc) * 96 : (2 * z + cc + 1) * 96, :].astype(BF)

                    @pl.when(c == cc)
                    def _():
                        keep[h, q, r] = piece

                    @pl.when(c != cc)
                    def _():
                        send[h, q, r] = piece

        pair_copy(h, q).start()

    def stage1(h):
        for p2, q in enumerate((spot.qs[1], spot.qs[3])):
            pair_copy(h, q).wait_recv()
            for r in range(4):
                out1[h, p2, r] = total_of(keep[h, q, r], pair[h, q, r]).astype(BF)
            first_copy(h, p2).start()

    def stage2(h):
        q = spot.qs[2]
        pair_copy(h, q).wait_recv()
        first_copy(h, 1).wait_recv()
        for r in range(4):
            out2[h, r] = total_of(keep[h, q, r], pair[h, q, r], in1[h, 1, r]).astype(BF)
        copy(0, h).start()

    def stage3(h):
        pair_copy(h, dp).wait_recv()
        first_copy(h, 0).wait_recv()
        copy(0, h).wait_recv()
        for r in (2, 3, 0, 1):
            value = total_of(keep[h, dp, r], pair[h, dp, r], in1[h, 0, r], in2[h, r])
            if r >= 2:
                out3[h, r - 2] = value.astype(BF)
            else:
                hold[h, r] = value
            if r == 3:
                copy(1, h).start()

    def stage4(h):
        copy(1, h).wait_recv()
        out4[h] = total_of(hold[h, 1], in3[h, 1]).astype(BF)
        copy(2, h).start()
        hold[h, 0] = total_of(hold[h, 0], in3[h, 0])

    def stage5(h):
        copy(2, h).wait_recv()
        full_a[dp, h] = total_of(hold[h, 0], in4[h]).astype(BF)
        for k in range(3):
            share_a(h, k).start()

    sums = []

    def input_rows(t):
        part = pl.ds(t * 256, 256)
        weights = [rows_of(mix.at[k]) for k in range(3)]
        result, gain, shift, mark = input_part(
            tokens[part, :], marks[:, part], vectors[...], weights,
            (dq[part, :], dk[part, :], dv[part, :]), back[part, :],
        )
        input_grad[part, :] = result
        sums.append((gain, shift, mark))

    hops = (spot.core, spot.first, spot.second, spot.near, spot.far)

    def vec_copy(k):
        return link(vec_out.at[k], vec_in.at[k], vec_sent.at[k], vec_got.at[k], hops[k])

    def vec_first():
        gain, shift, mark = (
            sums[0][k] + sums[1][k] + sums[2][k] + sums[3][k] for k in range(3)
        )
        flag = (row_flag[0] == 1).astype(F32)
        value = jnp.concatenate(
            [
                gain, shift, gain2[0:2, :], mark * (1.0 - flag), mark * flag,
                jnp.zeros((2, 768), F32),
            ],
            axis=0,
        )
        vec_out[0] = value
        vec_copy(0).start()

    def vec_next(k):
        vec_copy(k).wait_recv()
        value = vec_out[k] + vec_in[k]
        if k < 4:
            vec_out[k + 1] = value
            vec_copy(k + 1).start()
        else:
            vector_sum[...] = value
        return value

    def wide_stats(blocks, index):
        squares = [b * b for b in blocks]
        total = jnp.sum(squares[0] + 1e-30, axis=1, keepdims=True)
        for square in squares[1:]:
            total = total + jnp.sum(square + 1e-30, axis=1, keepdims=True)
        row = BETA * old_rows[index] + (1.0 - BETA) * (total / (768.0 * len(blocks)))
        rows_new[index] = jnp.broadcast_to(row, (96, 128))
        inverse = 1.0 / row
        cols = [jnp.sum(square + 1e-30, axis=0, keepdims=True) for square in squares]
        scaled = [jnp.sum(square * inverse, axis=0, keepdims=True) for square in squares]
        return jnp.sum(row, axis=0, keepdims=True), cols, scaled

    def lanes(value):
        return jnp.broadcast_to(value, (1, 768))

    def square_sum(ref):
        value = ref[...]
        return lanes(jnp.sum(jnp.sum(value * value, axis=0, keepdims=True), axis=1, keepdims=True))

    def slot_copy(kind, k):
        place = (slots_a, slots_b)[kind].at[fs]
        return link(place, place, slot_sent.at[kind, k], slot_got.at[kind, fs], spot.row(k))

    def slot_sum(kind, out):
        for k in range(1, 8):
            other = (fs + k) % 8
            place = (slots_a, slots_b)[kind].at[other]
            link(place, place, slot_sent.at[kind, k], slot_got.at[kind, other], spot.row(k)).wait_recv()
        slots = (slots_a, slots_b)[kind]
        value = slots[0]
        for f in range(1, 8):
            value = value + slots[f]
        out[...] = value

    def stats_b():
        shared_b(0)
        shared_b(1)
        for g in range(2):
            for q in range(4):
                grads[1 + g, q] = full_b[g, q]
        blocks = [full_b[0, q].astype(F32) for q in range(4)]
        total, cols, scaled = wide_stats(blocks, 2)
        total_s, cols_s, scaled_s = None, None, None
        for q in range(4):
            t, col, sc = wide_stats([full_b[1, q].astype(F32)], 3 + q)
            total_s = t if q == 0 else total_s + t
            cols_s = col[0] if q == 0 else cols_s + col[0]
            scaled_s = sc[0] if q == 0 else scaled_s + sc[0]
        for k in range(5, 7):
            local[k].wait()
        plains = plain[...]
        slots_b[fs] = jnp.concatenate(
            cols + scaled + [cols_s, scaled_s, lanes(total), lanes(total_s)]
            + [square_sum(w_expand), square_sum(w_shrink), jnp.zeros((2, 768), F32)]
            + [jnp.broadcast_to(jnp.sum(plains * plains, axis=1, keepdims=True), (8, 768))],
            axis=0,
        )
        for k in range(1, 8):
            slot_copy(1, k).start()

    def stats_a(vector):
        blocks = [
            jnp.concatenate([full_a[q, 0], full_a[q, 1]], axis=1) for q in range(4)
        ]
        for q in range(4):
            grads[0, q] = blocks[q]
        blocks = [b.astype(F32) for b in blocks]
        total, cols, scaled = wide_stats(blocks[:3], 0)
        total_p, cols_p, scaled_p = wide_stats(blocks[3:], 1)
        for k in range(3, 5):
            local[k].wait()
        lane = lax.broadcasted_iota(jnp.int32, (8, 768), 1) - 96 * fs
        moment_new = BETA * moment[...] + (1.0 - BETA) * (vector * vector + 1e-30)
        step = vector * lax.rsqrt(moment_new)
        step = jnp.where((lane >= 0) & (lane < 96), step * step, 0.0)
        slots_a[fs] = jnp.concatenate(
            cols + cols_p + scaled + scaled_p + [lanes(total), lanes(total_p)]
            + [square_sum(w_mix), square_sum(w_proj), jnp.zeros((4, 768), F32)]
            + [jnp.broadcast_to(jnp.sum(step, axis=1, keepdims=True), (8, 768))],
            axis=0,
        )
        for k in range(1, 8):
            slot_copy(0, k).start()

    for q in (3, 0, 1, 2):
        half_grad(0, q)
    half_grad(1, 3)
    half_grad(1, 0)
    stage1(0)
    half_grad(1, 1)
    half_grad(1, 2)
    for k in range(3):
        local[k].wait()
    input_rows(0)
    stage1(1)
    stage2(0)
    input_rows(1)
    input_rows(2)
    stage2(1)
    stage3(0)
    input_rows(3)
    vec_first()
    stats_b()
    vec_next(0)
    stage4(0)
    stage3(1)
    vec_next(1)
    stage5(0)
    stage4(1)
    vec_next(2)
    vec_next(3)
    stage5(1)
    vector = vec_next(4)
    slot_sum(1, sums_b)
    shared_a(0)
    shared_a(1)
    stats_a(vector)
    for g in range(2):
        for k in range(3):
            share_b(g, k).wait_send()
            share_a(g, k).wait_send()
        for q in range(4):
            pair_copy(g, q).wait_send()
        for p2 in range(2):
            first_copy(g, p2).wait_send()
        for stage in range(3):
            copy(stage, g).wait_send()
    for k in range(5):
        vec_copy(k).wait_send()
    slot_sum(0, sums_a)
    for kind in range(2):
        for k in range(1, 8):
            slot_copy(kind, k).wait_send()


def run_last(row_flag, normed, dq, dk, dv, proj_keep, proj_send, fin_e, fin_s, marks, vectors, gain2,
             old_rows, moment, plain, tokens, a_full, middle_back, w_mix, w_proj, w_expand, w_shrink):
    rows, width = normed.shape
    half = (96, 384)
    block = (96, 768)
    sem = pltpu.SemaphoreType.DMA
    return pl.pallas_call(
        last_kernel,
        in_specs=[
            SCALARS, *[pl.BlockSpec(memory_space=pltpu.VMEM)] * 14, *[ANYWHERE] * 7,
        ],
        out_specs=[pl.BlockSpec(memory_space=pltpu.VMEM)] * 6,
        out_shape=shapes(
            ((rows, width), F32), ((3, 4) + block, BF), ((7, 96, 128), F32),
            ((24, 768), F32), ((24, 768), F32), ((8, 768), F32),
        ),
        scratch_shapes=[
            pltpu.VMEM((rows, width), BF),
            pltpu.VMEM((3, 4, 2) + block, BF),
            pltpu.VMEM((rows, width), F32),
            pltpu.VMEM(w_mix.shape, F32),
            pltpu.VMEM(w_proj.shape, F32),
            pltpu.VMEM(w_expand.shape, F32),
            pltpu.VMEM(w_shrink.shape, F32),
            *[pltpu.VMEM((2, 4, 4) + half, BF)] * 3,
            *[pltpu.VMEM((2, 2, 4) + half, BF)] * 2,
            *[pltpu.VMEM((2, 4) + half, BF)] * 2,
            *[pltpu.VMEM((2, 2) + half, BF)] * 2,
            *[pltpu.VMEM((2,) + half, BF)] * 2,
            pltpu.VMEM((2, 2) + half, F32),
            pltpu.VMEM((4, 2) + half, BF),
            pltpu.VMEM((2, 4) + block, BF),
            pltpu.VMEM((5, 8, 768), F32),
            pltpu.VMEM((5, 8, 768), F32),
            pltpu.VMEM((8, 24, 768), F32),
            pltpu.VMEM((8, 24, 768), F32),
            sem((7,)),
            sem((2, 4)), sem((2, 4)), sem((2, 2)), sem((2, 2)), sem((3, 2)), sem((3, 2)),
            sem((4, 3)), sem((4, 4)), sem((5,)), sem((5,)), sem((2, 8)), sem((2, 8)),
        ],
        compiler_params=params(collective_id=3, has_side_effects=True),
        name="last",
    )(row_flag, normed, dq, dk, dv, proj_keep, proj_send, fin_e, fin_s, marks, vectors, gain2,
      old_rows, moment, plain, tokens, a_full, middle_back, w_mix, w_proj, w_expand, w_shrink)


def step_kernel(
    grad_a, grad_e, grad_s, w_mix, w_proj, w_expand, w_shrink, rows, old_cols, sums_a, sums_b,
    vector_grad, vectors, moment,
    mix_grad, proj_grad, expand_grad, shrink_grad, mix_new, proj_new, expand_new, shrink_new,
    cols_new, vector_new, moment_new, *, owners
):
    q = pl.program_id(0)
    height = 96.0 * owners

    @pl.when(q == 0)
    def _():
        parts = [sums_a[0:4, :], sums_b[0:4, :]]
        cols_new[0:8, :] = BETA * old_cols[0:8, :] + (1.0 - BETA) * (
            jnp.concatenate(parts, axis=0) / height
        )
        tall = BETA * old_cols[8:9, :] + (1.0 - BETA) * (sums_b[8:9, :] / (4.0 * height))
        cols_new[8:16, :] = jnp.broadcast_to(tall, (8, 768))
        old = moment[...]
        grad = vector_grad[...]
        new = BETA * old + (1.0 - BETA) * (grad * grad + 1e-30)
        moment_new[...] = new
        width = 96.0 * owners
        clip = jnp.maximum(1.0, jnp.sqrt(sums_a[16:22, 0:1] / width) / CLIP)
        rate = RATE * jnp.maximum(0.001, jnp.sqrt(sums_b[16:22, 0:1] / width))
        vector_new[...] = vectors[...] - rate * ((grad * lax.rsqrt(new)) / clip)

    def update(grad, weight, row, col, scaled, all_cols, row_total, square, count, wide):
        row_mean = row_total / count
        entries = count * wide
        update_square = row_mean * jnp.sum(
            jnp.sum(scaled / all_cols, axis=1, keepdims=True), axis=0, keepdims=True
        )
        clip = jnp.maximum(1.0, jnp.sqrt(update_square / entries) / CLIP)
        rate = RATE * jnp.maximum(0.001, jnp.sqrt(square / entries))
        factor = rate / clip
        return weight - factor * (grad * lax.rsqrt(row * (col / row_mean)))

    def one(ref, k):
        return ref[k : k + 1, 0:1]

    a = grad_a[0, 0].astype(F32)
    col = cols_new[pl.ds(q, 1), :]

    @pl.when(q < 3)
    def _():
        mix_grad[...] = a
        mix_new[...] = update(
            a, w_mix[...], rows[0][:, 0:1], col, sums_a[4:7, :], cols_new[0:3, :],
            one(sums_a, 8), one(sums_a, 10), height, 2304.0,
        )

    @pl.when(q == 3)
    def _():
        proj_grad[...] = a
        proj_new[...] = update(
            a, w_proj[...], rows[1][:, 0:1], col, sums_a[7:8, :], cols_new[3:4, :],
            one(sums_a, 9), one(sums_a, 11), height, 768.0,
        )

    e = grad_e[0, 0].astype(F32)
    expand_grad[...] = e
    expand_new[...] = update(
        e, w_expand[...], rows[2][:, 0:1], cols_new[pl.ds(4 + q, 1), :], sums_b[4:8, :], cols_new[4:8, :],
        one(sums_b, 10), one(sums_b, 12), height, 3072.0,
    )
    t = grad_s[0, 0].astype(F32)
    shrink_grad[...] = t
    shrink_new[...] = update(
        t, w_shrink[...], rows[3 + q][:, 0:1], cols_new[8:9, :], sums_b[9:10, :], cols_new[8:9, :],
        one(sums_b, 11), one(sums_b, 13), 4.0 * height, 768.0,
    )


def run_step(grads, w_mix, w_proj, w_expand, w_shrink, rows, old_cols, sums_a, sums_b,
             vector_grad, vectors, moment, owners):
    block = (96, 768)
    wide = pl.BlockSpec(block, lambda q: (0, q))
    three = pl.BlockSpec(block, lambda q: (0, jnp.minimum(q, 2)))
    tall = pl.BlockSpec(block, lambda q: (q, 0))
    return pl.pallas_call(
        functools.partial(step_kernel, owners=owners),
        grid=(4,),
        in_specs=[
            pl.BlockSpec((1, 1) + block, lambda q: (0, q, 0, 0)),
            pl.BlockSpec((1, 1) + block, lambda q: (1, q, 0, 0)),
            pl.BlockSpec((1, 1) + block, lambda q: (2, q, 0, 0)),
            three, fixed(*block), wide, tall,
            fixed(7, 96, 128), fixed(16, 768), fixed(24, 768), fixed(24, 768),
            fixed(6, 96), fixed(6, 96), fixed(6, 96),
        ],
        out_specs=[
            three, fixed(*block), wide, tall, three, fixed(*block), wide, tall,
            fixed(16, 768), fixed(6, 96), fixed(6, 96),
        ],
        out_shape=shapes(
            *[(w.shape, F32) for w in (w_mix, w_proj, w_expand, w_shrink)] * 2,
            ((16, 768), F32), ((6, 96), F32), ((6, 96), F32),
        ),
        compiler_params=params(),
        name="step",
    )(grads, grads, grads, w_mix, w_proj, w_expand, w_shrink, rows, old_cols, sums_a, sums_b,
      vector_grad, vectors, moment)


def masks(row_flag, sentence_mask, token_mask, lengths):
    length = sentence_mask.shape[1]
    valid = (lax.broadcasted_iota(jnp.int32, (1, length), 1) < lengths[:, None]).astype(jnp.int32)
    is_token = (row_flag == 1).astype(jnp.int32)[:, None]
    return jnp.concatenate(
        [
            jnp.zeros((4, length), jnp.int32),
            sentence_mask * valid * (1 - is_token),
            token_mask * valid * is_token,
            jnp.zeros((10, length), jnp.int32),
        ]
    ).astype(BF)


def staged_body(
    tokens, cotangent, row_flag, sentence_mask, token_mask, lengths,
    mix_weight, proj_weight, expand_weight, shrink_weight, norm_vectors,
    mix_rows, proj_rows, expand_rows, shrink_rows,
    mix_cols, proj_cols, expand_cols, shrink_cols, vector_moment,
):
    length, width = tokens.shape[1:]
    tokens = tokens.reshape(length, width)
    cotangent = cotangent.reshape(length, width)
    fs = lax.axis_index("fsdp")
    owners = lax.axis_size("fsdp")
    share = norm_vectors.shape[1]
    marks = masks(row_flag, sentence_mask, token_mask, lengths)
    packed = jnp.pad(norm_vectors, ((0, 10), (0, 128 - share))).astype(BF)
    old_rows = jnp.concatenate([mix_rows, proj_rows, expand_rows, shrink_rows]).reshape(7, 96, 1)
    old_cols = jnp.concatenate([mix_cols, proj_cols, expand_cols, shrink_cols]).reshape(9, 768)
    old_cols = jnp.pad(old_cols, ((0, 7), (0, 0)))
    moment = lax.dynamic_update_slice(jnp.ones((8, width), F32), vector_moment, (0, fs * share))
    plain = lax.dynamic_update_slice(jnp.zeros((8, width), F32), norm_vectors, (0, fs * share))
    a_full, b_full, c_full, vectors, normed, mixed, context, kept = run_front(
        lengths, tokens, marks, packed, mix_weight, proj_weight, expand_weight, shrink_weight
    )
    (block_output, middle_back, ctx_back, gain2, proj_keep, proj_send,
     near_e, near_s, got_e, got_s) = run_feed_send(
        lengths, context, tokens, marks, vectors, a_full, b_full, c_full, cotangent
    )
    dq, dk, dv, fin_e, fin_s = run_attend_back_send(
        lengths, kept, mixed, ctx_back, near_e, got_e, near_s, got_s
    )
    input_grad, grads, rows, sums_a, sums_b, vector_sum = run_last(
        row_flag, normed, dq, dk, dv, proj_keep, proj_send, fin_e, fin_s, marks, vectors, gain2,
        old_rows, moment, plain, tokens, a_full, middle_back,
        mix_weight, proj_weight, expand_weight, shrink_weight,
    )
    vector_grad = lax.dynamic_slice(vector_sum, (0, fs * share), (6, share))
    (mix_grad, proj_grad, expand_grad, shrink_grad, mix_new, proj_new, expand_new, shrink_new,
     cols, vector_new, moment_new) = run_step(
        grads, mix_weight, proj_weight, expand_weight, shrink_weight, rows, old_cols, sums_a, sums_b,
        vector_grad, norm_vectors, vector_moment, owners,
    )
    flat = rows[:, :, 0].reshape(-1)
    return (
        block_output.reshape(1, length, width),
        input_grad.reshape(1, length, width),
        mix_grad, proj_grad, expand_grad, shrink_grad, vector_grad,
        mix_new, proj_new, expand_new, shrink_new, vector_new,
        flat[0:96], flat[96:192], flat[192:288], flat[288:672],
        cols[0:3].reshape(-1), cols[3], cols[4:8].reshape(-1), cols[8],
        moment_new,
    )


def plain_body(
    tokens, cotangent, row_flag, sentence_mask, token_mask, lengths,
    mix_weight, proj_weight, expand_weight, shrink_weight, norm_vectors,
    mix_rows, proj_rows, expand_rows, shrink_rows,
    mix_cols, proj_cols, expand_cols, shrink_cols, vector_moment,
):
    length, width = tokens.shape[1:]
    tokens = tokens.reshape(length, width)
    cotangent = cotangent.reshape(length, width)
    owners = lax.axis_size("fsdp")
    marks = masks(row_flag, sentence_mask, token_mask, lengths)
    is_token = (row_flag == 1).astype(F32)[:, None]
    mix_full = lax.all_gather(mix_weight.astype(BF), "fsdp", axis=0, tiled=True)
    proj_full = lax.all_gather(proj_weight.astype(BF), "fsdp", axis=0, tiled=True)
    expand_full = lax.all_gather(expand_weight.astype(BF), "fsdp", axis=0, tiled=True)
    shrink_full = lax.all_gather(shrink_weight.astype(BF), "fsdp", axis=0, tiled=True)
    vectors = lax.all_gather(norm_vectors.astype(BF), "fsdp", axis=1, tiled=True).astype(F32)
    vectors = jnp.concatenate([vectors, jnp.zeros((10, width), F32)])
    normed, mixed = run_mixed(tokens, marks, vectors, mix_full)
    context, kept = run_attend(lengths, mixed)
    block_output, middle_back, ctx_back, gain2, proj_local, expand_local, shrink_local = run_feed(
        lengths, context, tokens, marks, vectors, proj_full, expand_full, shrink_full, cotangent
    )
    dq, dk, dv = run_attend_back(lengths, kept, mixed, ctx_back)
    mix_local = run_mix_grad(normed, dq, dk, dv)
    input_grad, gain1 = run_input(tokens, marks, vectors, mix_full, dq, dk, dv, middle_back)
    vector_local = jnp.concatenate(
        [gain1[0:2], gain2[0:2], gain1[2:3] * (1.0 - is_token), gain1[2:3] * is_token]
    )
    local = (mix_local, proj_local, expand_local, shrink_local)
    shards = [lax.psum_scatter(g, "fsdp", scatter_dimension=0, tiled=True) for g in local]
    shards.append(lax.psum_scatter(vector_local, "fsdp", scatter_dimension=1, tiled=True))
    mix_grad, proj_grad, expand_grad, shrink_grad, vector_grad = lax.psum(tuple(shards), "dp")

    grads = (mix_grad, proj_grad, expand_grad, shrink_grad)
    weights = (mix_weight, proj_weight, expand_weight, shrink_weight)
    old_rows = (mix_rows, proj_rows, expand_rows, shrink_rows)
    old_cols = (mix_cols, proj_cols, expand_cols, shrink_cols)
    rows_new, col_parts, scaled_parts = [], [], []
    for g, r in zip(grads, old_rows):
        square = g * g + 1e-30
        row = BETA * r + (1.0 - BETA) * jnp.mean(square, axis=1)
        rows_new.append(row)
        col_parts.append(jnp.sum(square, axis=0))
        scaled_parts.append(jnp.sum(g * g * (1.0 / row)[:, None], axis=0))
    moment_new = BETA * vector_moment + (1.0 - BETA) * (vector_grad * vector_grad + 1e-30)
    vector_step = vector_grad * lax.rsqrt(moment_new)
    small = jnp.concatenate(
        [
            jnp.stack([jnp.sum(r) for r in rows_new]),
            jnp.stack([jnp.sum(w * w) for w in weights]),
            jnp.sum(vector_step * vector_step, axis=1),
            jnp.sum(norm_vectors * norm_vectors, axis=1),
        ]
    )
    packed = lax.psum(jnp.concatenate(col_parts + scaled_parts + [small]), "fsdp")
    offset = 0
    total_cols = sum(col.shape[0] for col in old_cols)
    small = packed[2 * total_cols :]
    cols_new, new_weights = [], []
    for index in range(4):
        count = grads[index].shape[0] * owners
        wide = old_cols[index].shape[0]
        entries = count * wide
        col = BETA * old_cols[index] + (1.0 - BETA) * packed[offset : offset + wide] / count
        scaled = packed[total_cols + offset : total_cols + offset + wide]
        offset += wide
        cols_new.append(col)
        row_mean = small[index] / count
        update_square = row_mean * jnp.sum(scaled / col)
        clip_factor = jnp.maximum(1.0, jnp.sqrt(update_square / entries) / CLIP)
        rate = RATE * jnp.maximum(0.001, jnp.sqrt(small[4 + index] / entries))
        approx = rows_new[index][:, None] * col[None, :] / row_mean
        step = grads[index] * lax.rsqrt(approx)
        new_weights.append(weights[index] - (rate / clip_factor) * step)
    vector_clip = jnp.maximum(1.0, jnp.sqrt(small[8:14] / width) / CLIP)
    vector_rate = RATE * jnp.maximum(0.001, jnp.sqrt(small[14:20] / width))
    vector_new = norm_vectors - vector_rate[:, None] * (vector_step / vector_clip[:, None])
    return (
        block_output.reshape(1, length, width),
        input_grad.reshape(1, length, width),
        mix_grad, proj_grad, expand_grad, shrink_grad, vector_grad,
        *new_weights, vector_new, *rows_new, *cols_new, moment_new,
    )


def solution(mesh):
    sequence = P(AXES, None, None)
    ins = (
        sequence, sequence, P(AXES), P(AXES, None), P(AXES, None), P(AXES),
        P("fsdp", None), P("fsdp", None), P("fsdp", None), P("fsdp", None), P(None, "fsdp"),
        P("fsdp"), P("fsdp"), P("fsdp"), P("fsdp"), P(), P(), P(), P(), P(None, "fsdp"),
    )
    outs = (
        sequence, sequence,
        P("fsdp", None), P("fsdp", None), P("fsdp", None), P("fsdp", None), P(None, "fsdp"),
        P("fsdp", None), P("fsdp", None), P("fsdp", None), P("fsdp", None), P(None, "fsdp"),
        P("fsdp"), P("fsdp"), P("fsdp"), P("fsdp"), P(), P(), P(), P(), P(None, "fsdp"),
    )
    staged = (mesh.shape["dp"], mesh.shape["fsdp"]) == (4, 8)
    body = staged_body if staged else plain_body
    return jax.shard_map(body, mesh=mesh, in_specs=ins, out_specs=outs, check_vma=False)
```

```python
import functools

import jax
import jax.numpy as jnp
from jax import lax
from jax.experimental import pallas as pl
from jax.experimental.pallas import tpu as pltpu
from jax.sharding import PartitionSpec as P

HEADS = 12
STEP = 10
RATE = 0.5
CLIP = 1.0
F32 = jnp.float32
BF = jnp.bfloat16
VMEM_LIMIT = 60 * 1024 * 1024
AXES = ("dp", "fsdp")


def nn(a, b):
    return lax.dot_general(a, b, (((1,), (0,)), ((), ())), preferred_element_type=F32)


def nt(a, b):
    return lax.dot_general(a, b, (((1,), (1,)), ((), ())), preferred_element_type=F32)


def tn(a, b):
    return lax.dot_general(a, b, (((0,), (0,)), ((), ())), preferred_element_type=F32)


def normalise(h):
    mean = jnp.mean(h, axis=-1, keepdims=True)
    centered = h - mean
    inverse = lax.rsqrt(jnp.mean(centered * centered, axis=-1, keepdims=True) + 1e-06)
    return centered * inverse, inverse


def norm_back(grad, normal, inverse, gain):
    scaled = grad * gain
    first = jnp.mean(scaled, axis=-1, keepdims=True)
    second = jnp.mean(scaled * normal, axis=-1, keepdims=True)
    return inverse * (scaled - first - normal * second)


def params(**kw):
    return pltpu.CompilerParams(vmem_limit_bytes=VMEM_LIMIT, **kw)


def fixed(*shape):
    return pl.BlockSpec(shape, lambda *_: (0,) * len(shape), pipeline_mode=pl.Buffered(1))


ANYWHERE = pl.BlockSpec(memory_space=pl.ANY)
SCALARS = pl.BlockSpec(memory_space=pltpu.SMEM)


def shapes(*items):
    return [jax.ShapeDtypeStruct(shape, kind) for shape, kind in items]


def rows_of(ref):
    value = ref[...]
    return value.reshape(-1, value.shape[-1])


def mixed_kernel(tokens, marks, vectors, weight, normed, mixed):
    start = tokens[...].astype(F32) + tn(marks[...], vectors[...].astype(BF))
    normal, _ = normalise(start)
    low = (normal * vectors[0:1, :] + vectors[1:2, :]).astype(BF)
    normed[...] = low
    result = nn(low, weight[...]).astype(BF)
    for k in range(mixed.shape[0]):
        mixed[k] = result[:, k * 128 : (k + 1) * 128]


def run_mixed(tokens, marks, vectors, weight):
    rows, width = tokens.shape
    cols = weight.shape[1]
    tile = 256
    return pl.pallas_call(
        mixed_kernel,
        grid=(rows // tile,),
        in_specs=[
            pl.BlockSpec((tile, width), lambda i: (i, 0)),
            pl.BlockSpec((16, tile), lambda i: (0, i)),
            pl.BlockSpec((16, width), lambda i: (0, 0)),
            pl.BlockSpec((width, cols), lambda i: (0, 0)),
        ],
        out_specs=[
            pl.BlockSpec((tile, width), lambda i: (i, 0)),
            pl.BlockSpec((cols // 128, tile, 128), lambda i: (0, i, 0)),
        ],
        out_shape=[
            jax.ShapeDtypeStruct((rows, width), BF),
            jax.ShapeDtypeStruct((cols // 128, rows, 128), BF),
        ],
        compiler_params=params(),
        name="mixed",
    )(tokens, marks, vectors, weight)


def lane_iota(rows):
    return lax.broadcasted_iota(jnp.int32, (rows, 128), 1)


def key_extra(rows, length, base):
    lane = lane_iota(rows)
    row = lax.broadcasted_iota(jnp.int32, (rows, 128), 0)
    mask = jnp.where(row < length, 0.0, -1e30)
    ones = jnp.where((lane > base) & (lane < base + 4), 1.0, 0.0)
    return jnp.where(lane == base, mask, ones).astype(BF)


def attend_pair(length, query, key, value, context, kept, tile):
    rows = query.shape[0]
    lane = lane_iota(tile)
    lane_all = lane_iota(rows)
    count = rows // tile
    keys = [
        jnp.where(lane_all < 64, key[...], key_extra(rows, length, 64)),
        jnp.where(lane_all >= 64, key[...], key_extra(rows, length, 0)),
    ]
    values = value[...]

    def first(head, t):
        base = 64 - 64 * head
        mine = (lane < 64) if head == 0 else (lane >= 64)
        one = jnp.where(lane == base, 1.0, 0.0).astype(BF)
        q = jnp.where(mine, query[pl.ds(t * tile, tile), :] * BF(0.125), one)
        return q, nt(q, keys[head])

    def second(head, t, q, score):
        base = 64 - 64 * head
        mine = (lane < 64) if head == 0 else (lane >= 64)
        top = jnp.max(score, axis=-1, keepdims=True)
        expo = jnp.exp(score - top)
        total = jnp.sum(expo, axis=-1, keepdims=True)
        probs = (expo * (1.0 / total)).astype(BF)
        lse = top + jnp.log(total)
        high = lse.astype(BF).astype(F32)
        rest = lse - high
        mid = rest.astype(BF).astype(F32)
        extra = jnp.where(lane == base, 1.0, 0.0)
        extra = jnp.where(lane == base + 1, -high, extra)
        extra = jnp.where(lane == base + 2, -mid, extra)
        extra = jnp.where(lane == base + 3, mid - rest, extra)
        kept[head, pl.ds(t * tile, tile), :] = jnp.where(mine, q, extra.astype(BF))
        return probs

    order = [(head, t) for head in range(2) for t in range(count)]
    outs = {}
    ahead = first(*order[0])
    waiting = None
    for n, spot in enumerate(order):
        now = ahead
        if n + 1 < len(order):
            ahead = first(*order[n + 1])
        if waiting is not None:
            outs[waiting[0]] = nn(waiting[1], values)
        waiting = (spot, second(*spot, *now))
    outs[waiting[0]] = nn(waiting[1], values)
    for t in range(count):
        context[pl.ds(t * tile, tile), :] = jnp.where(lane < 64, outs[0, t], outs[1, t]).astype(BF)


def attend_kernel(length, query, key, value, context, kept, *, tile):
    attend_pair(length[0], query.at[0], key.at[0], value.at[0], context, kept, tile)


def run_attend(length, mixed, tile=256):
    groups, rows, _ = mixed.shape
    pairs = groups // 3
    return pl.pallas_call(
        functools.partial(attend_kernel, tile=tile),
        grid=(pairs,),
        in_specs=[
            pl.BlockSpec(memory_space=pltpu.SMEM),
            pl.BlockSpec((1, rows, 128), lambda p: (p, 0, 0)),
            pl.BlockSpec((1, rows, 128), lambda p: (pairs + p, 0, 0)),
            pl.BlockSpec((1, rows, 128), lambda p: (2 * pairs + p, 0, 0)),
        ],
        out_specs=[
            pl.BlockSpec((rows, 128), lambda p: (0, p)),
            pl.BlockSpec((2, rows, 128), lambda p: (p, 0, 0)),
        ],
        out_shape=[
            jax.ShapeDtypeStruct((rows, pairs * 128), BF),
            jax.ShapeDtypeStruct((2 * pairs, rows, 128), BF),
        ],
        compiler_params=params(),
        name="attend",
    )(length, mixed, mixed, mixed)


class Spot:
    def __init__(self):
        fs = lax.axis_index("fsdp")
        dp = lax.axis_index("dp")
        self.fs, self.dp = fs, dp
        self.c, self.z = fs % 2, fs // 2
        z0, z1 = self.z % 2, self.z // 2
        near, far = z1 * 2 + (1 - z0), (1 - z1) * 2 + z0
        self.zs = (self.z, near, far, (1 - z1) * 2 + (1 - z0))
        x, y = dp % 2, dp // 2
        turn_x, turn_y = 1 - 2 * x, 1 - 2 * y
        first = (y + turn_y * self.c) * 2 + x + turn_x * (1 - self.c)
        second = (y + turn_y * (1 - self.c)) * 2 + x + turn_x * self.c
        self.qs = (dp, first, second, (1 - y) * 2 + 1 - x)
        self.near = (dp, near * 2 + self.c)
        self.far = (dp, far * 2 + self.c)
        self.first = (first, fs)
        self.second = (second, fs)
        self.core = (dp, self.z * 2 + 1 - self.c)

        self.diag = (self.qs[3], fs)
        self.bits = (x, y, z0, z1)
        along_x, along_y = y * 2 + 1 - x, (1 - y) * 2 + x
        self.order = (self.qs[3], along_x, along_y, dp)
        self.first_order = tuple(
            a + (b - a) * self.c
            for a, b in (
                (along_y, along_x), (dp, self.qs[3]), (self.qs[3], dp), (along_x, along_y)
            )
        )

    def row(self, k):
        return (self.dp, (self.fs + k) % 8)

    def other(self, cc):
        return self.c if cc == 0 else 1 - self.c

    def rel_z(self, z):
        low, high = z % 2, z // 2
        near = low + self.bits[2] - 2 * low * self.bits[2]
        far = high + self.bits[3] - 2 * high * self.bits[3]
        return near * 2 + far


def greet(peers):
    barrier = pltpu.get_barrier_semaphore()
    for peer in peers:
        pl.semaphore_signal(barrier, inc=1, device_id=peer, device_id_type=MESH)
    pl.semaphore_wait(barrier, len(peers))


def link(src, dst, send_sem, recv_sem, target):
    return pltpu.make_async_remote_copy(
        src_ref=src, dst_ref=dst, send_sem=send_sem, recv_sem=recv_sem,
        device_id=target, device_id_type=MESH,
    )


def total_of(*parts):
    value = parts[0].astype(F32)
    for part in parts[1:]:
        value = value + part.astype(F32)
    return value


MESH = pl.DeviceIdType.MESH
SPLIT = (80, 80, 80)


def front_kernel(
    length, row_flag, tokens, sentence, token, share, mix_w, proj_w, expand_w, shrink_w,
    a_out, b_out, c_out, vectors_out, marks, normed_out, mixed_out, context, kept,
    stage, stage_z, own, own_z, w_a, share_pad, vec_in, vectors, normed, mixed,
    send, recv, send_z, recv_z, vec_send, vec_recv, local, local_z, *, tile
):
    step = pl.program_id(0)
    spot = Spot()
    c, dp = spot.c, spot.dp
    rows = tokens.shape[0]

    uppers = [pl.ds(0, n) for n in SPLIT]
    lowers = [pl.ds(n, 96 - n) for n in SPLIT]

    def block(g, z, cc, q):
        if g == 0:
            return w_a.at[q, z, cc, uppers[0]]
        if g == 1:
            return b_out.at[q, z, cc, uppers[1]]
        return c_out.at[z, cc, q, uppers[2]]

    def slab(g, z, cc):
        if g == 0:
            return w_a.at[:, z, cc, lowers[0]]
        if g == 1:
            return b_out.at[:, z, cc, lowers[1]]
        return c_out.at[z, cc, :, lowers[2]]

    def remote_z(g, z, cc, kind, target, mine=False):
        dst = slab(g, z, cc)
        return link(
            own_z.at[g - 1, :, pl.ds(0, 96 - SPLIT[g])] if mine and g > 0 else dst, dst,
            send_z.at[g, kind], recv_z.at[g, z * 2 + cc], target,
        )

    def push_z(g, k, kind, target, mine=False):
        remote_z(g, spot.zs[k], c, kind, target, mine).start()

    def arrive_z(g, k):
        remote_z(g, spot.zs[k], c, 0, spot.core).wait_recv()

    def remote(g, z, cc, q, kind, target, mine=False):
        dst = block(g, z, cc, q)
        return pltpu.make_async_remote_copy(
            src_ref=own.at[g - 1, uppers[g]] if mine and g > 0 else dst,
            dst_ref=dst,
            send_sem=send.at[g, kind],
            recv_sem=recv.at[g, (z * 2 + cc) * 4 + q],
            device_id=target,
            device_id_type=MESH,
        )

    def push(g, z, q, kind, target, mine=False):
        remote(g, z, c, q, kind, target, mine).start()

    def arrive(g, z, cc, q):
        remote(g, z, cc, q, 0, spot.core).wait_recv()

    def phase0(g):
        push(g, spot.z, dp, 0, spot.far, True)
        push(g, spot.z, dp, 1, spot.near, True)
        push(g, spot.z, dp, 7, spot.second, True)
        push(g, spot.z, dp, 3, spot.first, True)
        push(g, spot.z, dp, 15, spot.core, True)

    def phase0z(g):
        push_z(g, 0, 0, spot.far, True)
        push_z(g, 0, 1, spot.near, True)
        push_z(g, 0, 3, spot.core, True)

    def spread(g, k):
        push(g, spot.zs[k], dp, 7 + k, spot.second)
        push(g, spot.zs[k], dp, 3 + k, spot.first)
        push(g, spot.zs[k], dp, 15 + k, spot.core)

    def phase1(g):
        arrive(g, spot.zs[2], c, dp)
        push(g, spot.zs[2], dp, 2, spot.near)
        spread(g, 2)

    def phase1z(g):
        arrive_z(g, 2)
        push_z(g, 2, 2, spot.near)
        push_z(g, 2, 5, spot.core)

    def phase2(g):
        arrive(g, spot.zs[1], c, dp)
        spread(g, 1)
        arrive(g, spot.zs[3], c, dp)
        spread(g, 3)

    def phase2z(g):
        arrive_z(g, 1)
        push_z(g, 1, 4, spot.core)
        arrive_z(g, 3)
        push_z(g, 3, 6, spot.core)

    def phase3(g):
        for k in range(4):
            arrive(g, spot.zs[k], c, spot.qs[1])
            push(g, spot.zs[k], spot.qs[1], 11 + k, spot.second)
            push(g, spot.zs[k], spot.qs[1], 19 + k, spot.core)

    def phase4(g):
        for m in (2, 3):
            for k in range(4):
                arrive(g, spot.zs[k], c, spot.qs[m])
                push(g, spot.zs[k], spot.qs[m], 15 + 4 * m + k, spot.core)

    def phase5(g):
        @pl.loop(0, 4)
        def _(z):
            for q in range(4):
                arrive(g, z, 1 - c, q)
            remote_z(g, z, 1 - c, 0, spot.core).wait_recv()

    def phase6(g):
        @pl.loop(0, 31)
        def _(kind):
            remote(g, spot.z, c, dp, kind, spot.core, True).wait_send()

        @pl.loop(0, 7)
        def _(kind):
            remote_z(g, spot.z, c, kind, spot.core, True).wait_send()

    def vec_copy(k):
        return pltpu.make_async_remote_copy(
            src_ref=vec_in.at[spot.fs],
            dst_ref=vec_in.at[spot.fs],
            send_sem=vec_send.at[k],
            recv_sem=vec_recv.at[spot.fs],
            device_id=spot.row(k),
            device_id_type=MESH,
        )

    def vec_arrive(k):
        other = (spot.fs + k) % 8
        pltpu.make_async_remote_copy(
            src_ref=vec_in.at[other],
            dst_ref=vec_in.at[other],
            send_sem=vec_send.at[k],
            recv_sem=vec_recv.at[other],
            device_id=spot.row(k),
            device_id_type=MESH,
        ).wait_recv()

    def keep_copies():
        return (
            pltpu.make_async_copy(w_a, a_out, local.at[3]),
            pltpu.make_async_copy(own.at[0, uppers[1]], block(1, spot.z, c, dp), local.at[4]),
            pltpu.make_async_copy(own.at[1, uppers[2]], block(2, spot.z, c, dp), local.at[5]),
            pltpu.make_async_copy(own_z.at[0, :, pl.ds(0, 96 - SPLIT[1])], slab(1, spot.z, c), local.at[8]),
            pltpu.make_async_copy(own_z.at[1, :, pl.ds(0, 96 - SPLIT[2])], slab(2, spot.z, c), local.at[9]),
            pltpu.make_async_copy(normed, normed_out, local.at[6]),
            pltpu.make_async_copy(mixed, mixed_out, local.at[7]),
        )

    @pl.when(step == 0)
    def _():
        barrier = pltpu.get_barrier_semaphore()
        peers = [spot.row(k) for k in range(1, 8)] + [spot.first, spot.second]
        for peer in peers:
            pl.semaphore_signal(barrier, inc=1, device_id=peer, device_id_type=MESH)

        columns = pl.ds(pl.multiple_of(dp * 768, 128), 768)

        @pl.when(dp < 3)
        def _():
            pltpu.make_async_copy(mix_w.at[:, columns], stage.at[0], local.at[0]).start()

        @pl.when(dp == 3)
        def _():
            pltpu.make_async_copy(proj_w, stage.at[0], local.at[0]).start()

        second = pltpu.make_async_copy(expand_w.at[:, columns], stage.at[1], local.at[1])
        second.start()
        third = pltpu.make_async_copy(
            shrink_w.at[pl.ds(pl.multiple_of(dp * 96, 32), 96), :], stage.at[2], local.at[2]
        )
        third.start()

        def slab_copy(g, q):
            if g == 0:
                src = proj_w.at[lowers[0], :] if q == 3 else mix_w.at[lowers[0], pl.ds(q * 768, 768)]
            elif g == 1:
                src = expand_w.at[lowers[1], pl.ds(q * 768, 768)]
            else:
                src = shrink_w.at[pl.ds(q * 96 + SPLIT[2], 96 - SPLIT[2]), :]
            return pltpu.make_async_copy(
                src, stage_z.at[g, q, pl.ds(0, 96 - SPLIT[g])], local_z.at[g, q]
            )

        for g in range(3):
            for q in range(4):
                slab_copy(g, q).start()
        share_pad[...] = jnp.zeros((16, 128), F32)
        share_pad[0:6, 0:96] = share[...]
        vec_in[spot.fs] = share_pad[...].astype(BF)
        position = lax.broadcasted_iota(jnp.int32, (1, rows), 1)
        flag = (row_flag[0] == 1).astype(F32)
        line = lax.broadcasted_iota(jnp.int32, (16, rows), 0)
        of_sentence = jnp.where(position < length[0], sentence[...].astype(F32), 0.0) * (1.0 - flag)
        of_token = jnp.where(position < length[0], token[...].astype(F32), 0.0) * flag
        marked = jnp.where(line == 4, of_sentence, jnp.where(line == 5, of_token, 0.0))
        marks[...] = marked.astype(BF)
        pltpu.make_async_copy(proj_w, stage.at[0], local.at[0]).wait()
        w_a[dp, spot.z, c, 0 : SPLIT[0]] = stage[0, 0 : SPLIT[0]].astype(BF)
        pl.semaphore_wait(barrier, len(peers))
        phase0(0)
        for k in range(1, 8):
            vec_copy(k).start()
        for q in range(4):
            slab_copy(0, q).wait()
            w_a[q, spot.z, c, SPLIT[0] : 96] = stage_z[0, q, 0 : 96 - SPLIT[0]].astype(BF)
        phase0z(0)
        second.wait()
        own[0] = stage[1].astype(BF)
        third.wait()
        own[1] = stage[2].astype(BF)
        for g in (1, 2):
            for q in range(4):
                slab_copy(g, q).wait()
                own_z[g - 1, q] = stage_z[g, q].astype(BF)
        copies = keep_copies()
        for copy in copies[1:5]:
            copy.start()
        for k in range(1, 8):
            vec_arrive(k)
        total = jnp.zeros((16, 768), F32)
        for f in range(8):
            row = lax.broadcasted_iota(jnp.int32, (128, 768), 0)
            lane = lax.broadcasted_iota(jnp.int32, (128, 768), 1)
            pick = jnp.where((lane - 96 * f == row) & (row < 96), 1.0, 0.0).astype(BF)
            total += nn(vec_in[f], pick)
        vectors[...] = total
        vectors_out[...] = total

        def norm(t):
            part = pl.ds(t * 256, 256)
            start = tokens[part, :].astype(F32) + tn(marks[:, part], total.astype(BF))
            normal, _ = normalise(start)
            normed[part, :] = (normal * total[0:1, :] + total[1:2, :]).astype(BF)

        norm(0)
        phase1(0)
        norm(1)
        phase2(0)
        norm(2)
        phase1z(0)
        norm(3)
        phase3(0)
        phase2z(0)
        phase0(1)
        phase0(2)
        phase0z(1)
        phase0z(2)
        phase4(0)
        phase5(0)
        copies[0].start()
        copies[5].start()
        for q in range(3):
            weight = rows_of(w_a.at[q])
            for t in range(4):
                part = pl.ds(t * 256, 256)
                result = nn(normed[part, :], weight).astype(BF)
                for k in range(6):
                    mixed[q * 6 + k, part, :] = result[:, k * 128 : (k + 1) * 128]
            if q == 0:
                phase1(1)
                phase1(2)
            if q == 2:
                phase2(1)
                phase2(2)
        copies[6].start()

    @pl.when(step > 0)
    def _():
        p = step - 1
        attend_pair(length[0], mixed.at[p], mixed.at[6 + p], mixed.at[12 + p], context, kept, tile)

    for at, phase, g in (
        (1, phase3, 1), (2, phase3, 2), (2, phase1z, 1), (3, phase1z, 2), (4, phase2z, 1),
        (5, phase2z, 2), (5, phase4, 1), (6, phase4, 2),
    ):

        @pl.when(step == at)
        def _():
            phase(g)

    @pl.when(step == 6)
    def _():
        phase5(1)
        phase5(2)
        for g in range(3):
            phase6(g)
        for k in range(1, 8):
            vec_copy(k).wait_send()
        for copy in keep_copies():
            copy.wait()


def run_front(length, row_flag, tokens, sentence, token, share, mix_w, proj_w, expand_w, shrink_w, tile=256):
    rows, width = tokens.shape
    anywhere = pl.BlockSpec(memory_space=pl.ANY)
    once = pl.Buffered(1)

    def whole(*shape):
        return pl.BlockSpec(shape, lambda i: (0,) * len(shape), pipeline_mode=once)

    return pl.pallas_call(
        functools.partial(front_kernel, tile=tile),
        grid=(7,),
        in_specs=[
            SCALARS,
            SCALARS,
            whole(rows, width),
            whole(1, rows),
            whole(1, rows),
            whole(*share.shape),
            anywhere,
            anywhere,
            anywhere,
            anywhere,
        ],
        out_specs=[
            anywhere,
            anywhere,
            anywhere,
            whole(16, width),
            whole(16, rows),
            anywhere,
            anywhere,
            pl.BlockSpec((rows, 128), lambda i: (0, jnp.maximum(i - 1, 0))),
            pl.BlockSpec((2, rows, 128), lambda i: (jnp.maximum(i - 1, 0), 0, 0)),
        ],
        out_shape=[
            jax.ShapeDtypeStruct((4, 4, 2, 96, 768), BF),
            jax.ShapeDtypeStruct((4, 4, 2, 96, 768), BF),
            jax.ShapeDtypeStruct((4, 2, 4, 96, 768), BF),
            jax.ShapeDtypeStruct((16, width), F32),
            jax.ShapeDtypeStruct((16, rows), BF),
            jax.ShapeDtypeStruct((rows, width), BF),
            jax.ShapeDtypeStruct((18, rows, 128), BF),
            jax.ShapeDtypeStruct((rows, width), BF),
            jax.ShapeDtypeStruct((12, rows, 128), BF),
        ],
        scratch_shapes=[
            pltpu.VMEM((3, 96, 768), F32),
            pltpu.VMEM((3, 4, 32, 768), F32),
            pltpu.VMEM((2, 96, 768), BF),
            pltpu.VMEM((2, 4, 32, 768), BF),
            pltpu.VMEM((4, 4, 2, 96, 768), BF),
            pltpu.VMEM((16, 128), F32),
            pltpu.VMEM((8, 16, 128), BF),
            pltpu.VMEM((16, width), F32),
            pltpu.VMEM((rows, width), BF),
            pltpu.VMEM((18, rows, 128), BF),
            pltpu.SemaphoreType.DMA((3, 31)),
            pltpu.SemaphoreType.DMA((3, 32)),
            pltpu.SemaphoreType.DMA((3, 7)),
            pltpu.SemaphoreType.DMA((3, 8)),
            pltpu.SemaphoreType.DMA((8,)),
            pltpu.SemaphoreType.DMA((8,)),
            pltpu.SemaphoreType.DMA((10,)),
            pltpu.SemaphoreType.DMA((3, 4)),
        ],
        compiler_params=params(collective_id=0, has_side_effects=True),
        name="front",
    )(length, row_flag, tokens, sentence, token, share, mix_w, proj_w, expand_w, shrink_w)


def attend_back_pair(length, kept, key, value, ctx_grad, dq, dk, dv, tile):
    rows = key.shape[0]
    lane = lane_iota(tile)
    lane_all = lane_iota(rows)
    count = rows // tile
    plain, plain_values = key[...], value[...]
    keys = [
        jnp.where(lane_all < 64, plain, key_extra(rows, length, 64)),
        jnp.where(lane_all >= 64, plain, key_extra(rows, length, 0)),
    ]
    zero = jnp.zeros_like(plain_values)
    values = [
        jnp.where(lane_all < 64, plain_values, zero),
        jnp.where(lane_all >= 64, plain_values, zero),
    ]

    def first(head, t):
        q = kept[head, pl.ds(t * tile, tile), :]
        grad = ctx_grad[pl.ds(t * tile, tile), :]
        return q, grad, nt(keys[head], q), nt(values[head], grad)

    sums = {}

    def second(head, t, q, grad, score, prob_back):
        probs = jnp.exp(score)
        product = probs * prob_back
        delta = jnp.sum(product, axis=0, keepdims=True)
        score_back = (product - probs * delta).astype(BF)
        dv_part = nn(probs.astype(BF), grad)
        dk_part = nn(score_back, q)
        sums[head, "v"] = dv_part if t == 0 else sums[head, "v"] + dv_part
        sums[head, "k"] = dk_part if t == 0 else sums[head, "k"] + dk_part
        sums[head, t] = tn(score_back, plain)

    order = [(head, t) for head in range(2) for t in range(count)]
    ahead = first(*order[0])
    for n, spot in enumerate(order):
        now = ahead
        if n + 1 < len(order):
            ahead = first(*order[n + 1])
        second(*spot, *now)
    dk[...] = jnp.where(lane_all < 64, sums[0, "k"], sums[1, "k"]).astype(BF)
    dv[...] = jnp.where(lane_all < 64, sums[0, "v"], sums[1, "v"]).astype(BF)
    for t in range(count):
        both = jnp.where(lane < 64, sums[0, t], sums[1, t]) * 0.125
        dq[pl.ds(t * tile, tile), :] = both.astype(BF)


def attend_back_head(length, head, kept, key, value, ctx_grad, dq, dk, dv, tile):
    rows = key.shape[0]
    lane = lane_iota(tile) - 64 * head
    lane_all = lane_iota(rows) - 64 * head
    mine = (lane >= 0) & (lane < 64)
    mine_all = (lane_all >= 0) & (lane_all < 64)
    count = rows // tile
    plain = key[...]
    keys = jnp.where(mine_all, plain, key_extra(rows, length, 64 - 64 * head))
    values = jnp.where(mine_all, value[...], jnp.zeros_like(plain))

    def first(t):
        q = kept[pl.ds(t * tile, tile), :]
        grad = ctx_grad[pl.ds(t * tile, tile), :]
        return q, grad, nt(keys, q), nt(values, grad)

    dv_sum = dk_sum = None
    ahead = first(0)
    for t in range(count):
        q, grad, score, prob_back = ahead
        if t + 1 < count:
            ahead = first(t + 1)
        probs = jnp.exp(score)
        product = probs * prob_back
        delta = jnp.sum(product, axis=0, keepdims=True)
        score_back = (product - probs * delta).astype(BF)
        dv_part = nn(probs.astype(BF), grad)
        dk_part = nn(score_back, q)
        dv_sum = dv_part if t == 0 else dv_sum + dv_part
        dk_sum = dk_part if t == 0 else dk_sum + dk_part
        part = pl.ds(t * tile, tile)
        dq[part, :] = jnp.where(mine, (tn(score_back, plain) * 0.125).astype(BF), dq[part, :])
    dk[...] = jnp.where(mine_all, dk_sum.astype(BF), dk[...])
    dv[...] = jnp.where(mine_all, dv_sum.astype(BF), dv[...])


def attend_back_kernel(length, kept, key, value, ctx_grad, dq, dk, dv, *, tile):
    attend_back_pair(length[0], kept, key.at[0], value.at[0], ctx_grad, dq, dk, dv, tile)


def run_attend_back(length, kept, mixed, ctx_grad, tile=128):
    groups, rows, _ = mixed.shape
    pairs = groups // 3
    width = pairs * 128
    spec = pl.BlockSpec((rows, 128), lambda p: (0, p))
    return pl.pallas_call(
        functools.partial(attend_back_kernel, tile=tile),
        grid=(pairs,),
        in_specs=[
            pl.BlockSpec(memory_space=pltpu.SMEM),
            pl.BlockSpec((2, rows, 128), lambda p: (p, 0, 0)),
            pl.BlockSpec((1, rows, 128), lambda p: (pairs + p, 0, 0)),
            pl.BlockSpec((1, rows, 128), lambda p: (2 * pairs + p, 0, 0)),
            spec,
        ],
        out_specs=[spec, spec, spec],
        out_shape=[jax.ShapeDtypeStruct((rows, width), BF)] * 3,
        compiler_params=params(),
        name="attend_back",
    )(length, kept, mixed, mixed, ctx_grad)


def gelu_pair(v):
    cdf = 0.5 * (1.0 + lax.erf(v * 0.7071067811865476))
    return v * cdf, cdf + v * jnp.exp(-0.5 * v * v) * 0.3989422804014327


def feed_start(
    length, context, tokens, marks, vectors, proj, cotangent, middle, normed, bound, out_sum, back_sum, tile
):
    @pl.loop(0, tokens.shape[0] // tile)
    def _(t):
        part = pl.ds(pl.multiple_of(t * tile, tile), tile)
        start = tokens[part, :].astype(F32) + tn(marks[:, part], vectors[...].astype(BF))
        mid = start + nn(context[part, :], proj)
        middle[part, :] = mid
        out_sum[part, :] = jnp.zeros_like(mid)
        back_sum[part, :] = jnp.zeros_like(mid)
        normal, _ = normalise(mid)
        normed[part, :] = (normal * vectors[2:3, :] + vectors[3:4, :]).astype(BF)
        row = t * tile + lax.broadcasted_iota(jnp.int32, (tile, 1), 0)
        kept = jnp.where(row < length, cotangent[part, :].astype(F32), 0.0)
        bound[part, :] = kept.astype(BF)


def feed_chunk(expand, shrink, normed, bound, active, inner_back, out_sum, back_sum, tile):
    @pl.loop(0, normed.shape[0] // tile, unroll=2)
    def _(t):
        part = pl.ds(pl.multiple_of(t * tile, tile), tile)
        inner = nn(normed[part, :], expand)
        act_back = nt(bound[part, :], shrink)
        act, slope = gelu_pair(inner)
        act = act.astype(BF)
        active[part, :] = act
        back = (act_back * slope).astype(BF)
        inner_back[part, :] = back
        out_sum[part, :] += nn(act, shrink)
        back_sum[part, :] += nt(back, expand)


def feed_finish(
    vectors, proj, middle, normed, bound, out_sum, back_sum, output, middle_back, ctx_back, gain_grads, tile
):
    gain_grads[...] = jnp.zeros_like(gain_grads)

    @pl.loop(0, middle.shape[0] // tile)
    def _(t):
        part = pl.ds(pl.multiple_of(t * tile, tile), tile)
        mid = middle[part, :]
        output[part, :] = (mid + out_sum[part, :]).astype(BF)
        normal, inverse = normalise(mid)
        grad = back_sum[part, :]
        gain_grads[0:1, :] += jnp.sum(grad * normal, axis=0, keepdims=True)
        gain_grads[1:2, :] += jnp.sum(grad, axis=0, keepdims=True)
        back = bound[part, :].astype(F32) + norm_back(grad, normal, inverse, vectors[2:3, :])
        middle_back[part, :] = back
        low = back.astype(BF)
        normed[part, :] = low
        ctx_back[part, :] = nt(low, proj).astype(BF)


def feed_kernel(
    length, context, tokens, marks, vectors, proj, expand, shrink, cotangent,
    output, middle_back, ctx_back, gain_grads, proj_grad, expand_grad, shrink_grad,
    middle, normed, bound, out_sum, active, inner_back, *, tile
):
    j = pl.program_id(0)

    @pl.when(j == 0)
    def _():
        feed_start(
            length[0], context, tokens, marks, vectors, proj[...], cotangent, middle, normed, bound,
            out_sum, middle_back, tile,
        )

    feed_chunk(
        expand[...], shrink[...], normed, bound, active, inner_back, out_sum, middle_back, tile
    )
    expand_grad[...] = tn(normed[...], inner_back[...])
    shrink_grad[...] = tn(active[...], bound[...])

    @pl.when(j == pl.num_programs(0) - 1)
    def _():
        feed_finish(
            vectors, proj[...], middle, normed, bound, out_sum, middle_back,
            output, middle_back, ctx_back, gain_grads, tile,
        )
        proj_grad[...] = tn(context[...], normed[...])


def run_feed(length, context, tokens, marks, vectors, proj, expand, shrink, cotangent, tile=256):
    rows, width = tokens.shape
    inner = expand.shape[1]
    chunk = width
    wide = pl.BlockSpec((width, chunk), lambda j: (0, j))
    tall = pl.BlockSpec((chunk, width), lambda j: (j, 0))
    return pl.pallas_call(
        functools.partial(feed_kernel, tile=tile),
        grid=(inner // chunk,),
        in_specs=[
            SCALARS, fixed(rows, width), fixed(rows, width), fixed(16, rows), fixed(16, width),
            fixed(width, width), wide, tall, fixed(rows, width),
        ],
        out_specs=[
            fixed(rows, width), fixed(rows, width), fixed(rows, width), fixed(8, width),
            fixed(width, width), wide, tall,
        ],
        out_shape=shapes(
            ((rows, width), BF), ((rows, width), F32), ((rows, width), BF), ((8, width), F32),
            ((width, width), F32), ((width, inner), F32), ((inner, width), F32),
        ),
        scratch_shapes=[
            pltpu.VMEM((rows, width), F32),
            pltpu.VMEM((rows, width), BF),
            pltpu.VMEM((rows, width), BF),
            pltpu.VMEM((rows, width), F32),
            pltpu.VMEM((rows, chunk), BF),
            pltpu.VMEM((rows, chunk), BF),
        ],
        compiler_params=params(),
        name="feed",
    )(length, context, tokens, marks, vectors, proj, expand, shrink, cotangent)


def feed_send_kernel(
    length, context, tokens, marks, vectors, proj, expand, shrink, cotangent,
    output, middle_back, ctx_back, gain_grads, proj_box, near_e, near_s, rest_s, got_e, got_s,
    middle, normed, bound, out_sum, active, inner_back,
    box_e, box_s, pair_e, pair_s, out_e, out_s,
    pair_sem, pair_got, first_e_sem, first_e_got, first_s_sem, first_s_got, *, tile
):
    j = pl.program_id(0)
    spot = Spot()
    c = spot.c

    def pair_copy(step, g):
        slot = step % 2
        src, dst = (box_e, pair_e) if g == 0 else (box_s, pair_s)
        return link(
            src.at[1, slot], dst.at[step], pair_sem.at[g, slot], pair_got.at[g, step], spot.core
        )

    def first_e(p2):
        return link(
            out_e.at[p2], got_e.at[p2], first_e_sem.at[p2], first_e_got.at[p2], spot.first
        )

    def first_s(p2, r):
        return link(
            out_s.at[p2, r], got_s.at[p2, r], first_s_sem.at[p2, r], first_s_got.at[p2, r], spot.first
        )

    def keep_e(step, p2):
        @pl.loop(0, 4)
        def _(r):
            near_e[p2, r] = total_of(box_e[0, step % 2, r], pair_e[step, r]).astype(BF)

    def push_e(step, p2):
        @pl.loop(0, 4)
        def _(r):
            out_e[p2, r] = total_of(box_e[0, step % 2, r], pair_e[step, r]).astype(BF)

        first_e(p2).start()

    def to_first(step):
        slot = step % 2
        pair_copy(step, 0).wait_recv()
        if step == 0:
            push_e(0, 1)
        elif step == 3:
            keep_e(3, 0)
        else:

            @pl.when(c == step - 1)
            def _():
                push_e(step, 0)

            @pl.when(c != step - 1)
            def _():
                keep_e(step, 1)

        pair_copy(step, 1).wait_recv()
        r = spot.rel_z(spot.order[step])
        for p2, q in enumerate((spot.qs[1], spot.qs[3])):
            value = total_of(box_s[0, slot, q], pair_s[step, q]).astype(BF)
            if step < 3:
                out_s[p2, r] = value
                first_s(p2, r).start()
            else:
                rest_s[p2] = value
        for p2, q in enumerate((spot.qs[0], spot.qs[2])):
            near_s[p2, r] = total_of(box_s[0, slot, q], pair_s[step, q]).astype(BF)

    @pl.when(j == 0)
    def _():
        greet([spot.core, spot.first])
        feed_start(
            length[0], context, tokens, marks, vectors, rows_of(proj), cotangent,
            middle, normed, bound, out_sum, middle_back, tile,
        )

    feed_chunk(
        rows_of(expand), rows_of(shrink), normed, bound, active, inner_back,
        out_sum, middle_back, tile,
    )
    for step in range(3):

        @pl.when(j == step + 1)
        def _():
            to_first(step)

    slot = j % 2

    @pl.when(j >= 2)
    def _():
        pair_copy(j - 2, 0).wait_send()
        pair_copy(j - 2, 1).wait_send()

    grad_e = tn(normed[...], inner_back[...])
    for z in range(4):
        r = spot.rel_z(z)
        for cc in range(2):
            piece = grad_e[(2 * z + cc) * 96 : (2 * z + cc + 1) * 96, :]
            box_e[spot.other(cc), slot, r] = piece.astype(BF)
    pair_copy(j, 0).start()
    grad_s = tn(active[...], bound[...])
    for cc in range(2):
        for q in range(4):
            piece = grad_s[(cc * 4 + q) * 96 : (cc * 4 + q + 1) * 96, :]
            box_s[spot.other(cc), slot, q] = piece.astype(BF)
    pair_copy(j, 1).start()

    @pl.when(j == 3)
    def _():
        feed_finish(
            vectors, rows_of(proj), middle, normed, bound, out_sum, middle_back,
            output, middle_back, ctx_back, gain_grads, tile,
        )
        grad_p = tn(context[...], normed[...])
        for z in range(4):
            r = spot.rel_z(z)
            for cc in range(2):
                piece = grad_p[(2 * z + cc) * 96 : (2 * z + cc + 1) * 96, :]
                proj_box[spot.other(cc), r] = piece.astype(BF)
        to_first(3)
        for step in (2, 3):
            for g in range(2):
                pair_copy(step, g).wait_send()
        first_e(0).wait_send()
        first_e(1).wait_send()
        first_e(0).wait_recv()
        first_e(1).wait_recv()
        for step in range(3):
            r = spot.rel_z(spot.order[step])
            for p2 in range(2):
                first_s(p2, r).wait_send()
        for p2 in range(2):
            for z in spot.first_order[:3]:
                first_s(p2, spot.rel_z(z)).wait_recv()


def run_feed_send(length, context, tokens, marks, vectors, a_full, b_full, c_full, cotangent, tile=256):
    rows, width = tokens.shape
    block = (96, 768)

    def chunk_at(j):
        dp = lax.axis_index("dp")
        x, y = dp % 2, dp // 2
        turn_x = jnp.where(j < 2, 1, 0)
        turn_y = jnp.where(j % 2 == 0, 1, 0) * jnp.where(j < 3, 1, 0)
        return (y + turn_y - 2 * y * turn_y) * 2 + x + turn_x - 2 * x * turn_x

    return pl.pallas_call(
        functools.partial(feed_send_kernel, tile=tile),
        grid=(4,),
        in_specs=[
            SCALARS, fixed(rows, width), fixed(rows, width), fixed(16, rows), fixed(16, width),
            pl.BlockSpec((1, 4, 2) + block, lambda j: (3, 0, 0, 0, 0), pipeline_mode=pl.Buffered(1)),
            pl.BlockSpec((1, 4, 2) + block, lambda j: (chunk_at(j), 0, 0, 0, 0)),
            pl.BlockSpec((1, 2, 4) + block, lambda j: (chunk_at(j), 0, 0, 0, 0)),
            fixed(rows, width),
        ],
        out_specs=[
            fixed(rows, width), fixed(rows, width), fixed(rows, width), fixed(8, width),
            fixed(2, 4, *block), fixed(2, 4, *block), fixed(2, 4, *block),
            fixed(2, *block), ANYWHERE, ANYWHERE,
        ],
        out_shape=shapes(
            ((rows, width), BF), ((rows, width), F32), ((rows, width), BF), ((8, width), F32),
            *[((2, 4) + block, BF)] * 3,
            ((2,) + block, BF), *[((2, 4) + block, BF)] * 2,
        ),
        scratch_shapes=[
            pltpu.VMEM((rows, width), F32),
            pltpu.VMEM((rows, width), BF),
            pltpu.VMEM((rows, width), BF),
            pltpu.VMEM((rows, width), F32),
            pltpu.VMEM((rows, width), BF),
            pltpu.VMEM((rows, width), BF),
            *[pltpu.VMEM((2, 2, 4) + block, BF)] * 2,
            *[pltpu.VMEM((4, 4) + block, BF)] * 2,
            *[pltpu.VMEM((2, 4) + block, BF)] * 2,
            pltpu.SemaphoreType.DMA((2, 2)),
            pltpu.SemaphoreType.DMA((2, 4)),
            pltpu.SemaphoreType.DMA((2,)),
            pltpu.SemaphoreType.DMA((2,)),
            pltpu.SemaphoreType.DMA((2, 4)),
            pltpu.SemaphoreType.DMA((2, 4)),
        ],
        compiler_params=params(collective_id=1, has_side_effects=True),
        name="feed",
    )(length, context, tokens, marks, vectors, a_full, b_full, c_full, cotangent)


def mix_grad_kernel(normed, dq, dk, dv, grad_out):
    j = pl.program_id(0)
    for index, source in enumerate((dq, dk, dv)):

        @pl.when(j == index)
        def _():
            grad_out[...] = tn(normed[...], source[...])


def run_mix_grad(normed, dq, dk, dv):
    rows, width = normed.shape
    return pl.pallas_call(
        mix_grad_kernel,
        grid=(3,),
        in_specs=[fixed(rows, width)] * 4,
        out_specs=pl.BlockSpec((width, width), lambda j: (0, j)),
        out_shape=jax.ShapeDtypeStruct((width, 3 * width), F32),
        compiler_params=params(),
        name="mix_grad",
    )(normed, dq, dk, dv)


def input_part(tokens, marks, vectors, weights, sources, middle_back):
    start = tokens.astype(F32) + tn(marks, vectors.astype(BF))
    normal, inverse = normalise(start)
    grad = nt(sources[0], weights[0])
    for source, weight in zip(sources[1:], weights[1:]):
        grad += nt(source, weight)
    gain = jnp.sum(grad * normal, axis=0, keepdims=True)
    shift = jnp.sum(grad, axis=0, keepdims=True)
    result = middle_back + norm_back(grad, normal, inverse, vectors[0:1, :])
    spread = tn(marks, jnp.ones(vectors.shape, BF))
    mark = jnp.sum(spread * result, axis=0, keepdims=True)
    return result, gain, shift, mark


def input_kernel(tokens, marks, vectors, weight, dq, dk, dv, middle_back, input_grad, sums):
    i = pl.program_id(0)
    width = tokens.shape[1]
    weights = [weight[:, k * width : (k + 1) * width] for k in range(3)]
    result, gain, shift, mark = input_part(
        tokens[...], marks[...], vectors[...], weights, (dq[...], dk[...], dv[...]), middle_back[...]
    )
    input_grad[...] = result
    both = jnp.concatenate([gain, shift, mark, jnp.zeros((5, width), F32)], axis=0)

    @pl.when(i == 0)
    def _():
        sums[...] = both

    @pl.when(i > 0)
    def _():
        sums[...] += both


def run_input(tokens, marks, vectors, weight, dq, dk, dv, middle_back, tile=256):
    rows, width = tokens.shape
    spec = pl.BlockSpec((tile, width), lambda i: (i, 0))
    return pl.pallas_call(
        input_kernel,
        grid=(rows // tile,),
        in_specs=[
            spec,
            pl.BlockSpec((16, tile), lambda i: (0, i)),
            fixed(16, width),
            fixed(width, 3 * width),
            spec,
            spec,
            spec,
            spec,
        ],
        out_specs=[spec, fixed(8, width)],
        out_shape=shapes(((rows, width), F32), ((8, width), F32)),
        compiler_params=params(),
        name="input_grad",
    )(tokens, marks, vectors, weight, dq, dk, dv, middle_back)


BETA = 1.0 - STEP ** (-0.8)


def back_kernel(
    length, row_flag, kept, key, value, ctx_grad, near_e, near_s, rest_s,
    normed, proj_box, marks, vectors, gain2, mix_rows, proj_rows, expand_rows, shrink_rows, moment, plain,
    got_e_in, got_s_in, tokens_in, mix_in, back_in, w_mix_in, w_proj_in, w_expand_in, w_shrink_in,
    input_grad, grads, rows_new, sums_a, sums_b, vector_sum,
    tokens, mix, back, w_mix, w_proj, w_expand, w_shrink, grads_qkv,
    got, out2b, in2b, out3b, in3b, out4b, in4b, holdb,
    box, pair, out1, in1, out2, in2, out3, in3, out4, in4, hold,
    full_a, full_b, vec_q, vec_f, slots_a, slots_b, gains,
    loads, got_sem, late_sent, late_got, sentb, gotb,
    pair_sent, pair_got, sent1, got1, sent, landed, full_sent, full_got,
    vecq_sent, vecq_got, vecf_sent, vecf_got, slot_sent, slot_got, *, tile
):
    step = pl.program_id(0)
    spot = Spot()
    c, dp, fs = spot.c, spot.dp, spot.fs
    trio = (spot.first, spot.second, spot.diag)
    local = [
        pltpu.make_async_copy(src, dst, loads.at[k])
        for k, (src, dst) in enumerate(
            (
                (tokens_in, tokens), (mix_in.at[pl.ds(0, 3)], mix), (back_in, back),
                (w_mix_in, w_mix), (w_proj_in, w_proj), (w_expand_in, w_expand), (w_shrink_in, w_shrink),
            )
        )
    ]

    near = (near_e, near_s)
    load_e = pltpu.make_async_copy(got_e_in, got.at[0], got_sem.at[0])

    def late_s(p2):
        r = spot.rel_z(dp)
        return link(
            rest_s.at[p2], got.at[1, p2, r], late_sent.at[p2], late_got.at[p2], spot.first
        )

    def late_s_came(p2):
        r = spot.rel_z(spot.first_order[3])
        link(
            rest_s.at[p2], got.at[1, p2, r], late_sent.at[p2], late_got.at[p2], spot.first
        ).wait_recv()

    def load_s(k):
        r = spot.rel_z(spot.first_order[k])
        return pltpu.make_async_copy(got_s_in.at[:, r], got.at[1, :, r], got_sem.at[2 + k])

    def begin():
        load_e.start()
        for k in range(3):
            load_s(k).start()
        greet([spot.core, spot.near, spot.far, column[2], spot.first, spot.second, spot.diag])
        for p2 in range(2):
            late_s(p2).start()
        load_e.wait()
        stage2b(0)
        for copy in local:
            copy.start()

    def late():
        for k in range(3):
            load_s(k).wait()
        for p2 in range(2):
            late_s_came(p2)

    def copyb(stage, g):
        src, dst, target = (
            (out2b, in2b, spot.second), (out3b, in3b, spot.near), (out4b, in4b, spot.far),
        )[stage]
        return link(src.at[g], dst.at[g], sentb.at[stage, g], gotb.at[stage, g], target)

    def stage2b(g):
        @pl.loop(0, 4)
        def _(r):
            out2b[g, r] = total_of(near[g][1, r], got[g, 1, r]).astype(BF)

        copyb(0, g).start()

    def stage3b(g):
        copyb(0, g).wait_recv()

        @pl.loop(0, 2)
        def _(r):
            out3b[g, r] = total_of(near[g][0, 2 + r], got[g, 0, 2 + r], in2b[g, 2 + r]).astype(BF)

        copyb(1, g).start()

        @pl.loop(0, 2)
        def _(r):
            holdb[g, r] = total_of(near[g][0, r], got[g, 0, r], in2b[g, r])


    def stage4b(g):
        copyb(1, g).wait_recv()
        out4b[g] = total_of(holdb[g, 1], in3b[g, 1]).astype(BF)
        copyb(2, g).start()
        holdb[g, 0] = total_of(holdb[g, 0], in3b[g, 0])

    def stage5b(g):
        copyb(2, g).wait_recv()
        full_b[g, dp] = total_of(holdb[g, 0], in4b[g]).astype(BF)
        for k in range(3):
            share_b(g, k).start()

    def share_b(g, k):
        place = full_b.at[g, dp]
        return link(place, place, full_sent.at[g, k], full_got.at[g, dp], trio[k])

    def share_a(h, k):
        place = full_a.at[dp, h]
        return link(place, place, full_sent.at[2 + h, k], full_got.at[2 + h, dp], trio[k])

    def shared_b(g):
        for q in spot.qs[1:]:
            place = full_b.at[g, q]
            link(place, place, full_sent.at[g, 0], full_got.at[g, q], spot.first).wait_recv()

    def shared_a(h):
        for q in spot.qs[1:]:
            place = full_a.at[q, h]
            link(place, place, full_sent.at[2 + h, 0], full_got.at[2 + h, q], spot.first).wait_recv()

    def pair_copy(h, q):
        return link(
            box.at[1, h, q], pair.at[h, q], pair_sent.at[h, q], pair_got.at[h, q], spot.core
        )

    def first_copy(h, p2):
        return link(
            out1.at[h, p2], in1.at[h, p2], sent1.at[h, p2], got1.at[h, p2], spot.first
        )

    def copy(stage, h):
        src, dst, target = (
            (out2, in2, spot.second), (out3, in3, spot.near), (out4, in4, spot.far),
        )[stage]
        return link(src.at[h], dst.at[h], sent.at[stage, h], landed.at[stage, h], target)

    def third_grad(h):
        @pl.loop(0, 4)
        def _(r):
            for side in range(2):
                for k in range(3):

                    @pl.when(h == k)
                    def _():
                        box[side, h, 3, r] = proj_box[side, r, :, k * 256 : (k + 1) * 256]

        pair_copy(h, 3).start()

        @pl.loop(0, 3)
        def _(q):
            columns = pl.ds(pl.multiple_of(h * 256, 256), 256)
            grad = tn(normed[...], grads_qkv[q, :, columns])
            for z in range(4):
                r = spot.rel_z(z)
                for cc in range(2):
                    piece = grad[(2 * z + cc) * 96 : (2 * z + cc + 1) * 96, :]
                    box[spot.other(cc), h, q, r] = piece.astype(BF)
            pair_copy(h, q).start()

    def stage1(h):
        for p2, q in enumerate((spot.qs[1], spot.qs[3])):
            pair_copy(h, q).wait_recv()

            @pl.loop(0, 4)
            def _(r):
                out1[h, p2, r] = total_of(box[0, h, q, r], pair[h, q, r]).astype(BF)

            first_copy(h, p2).start()

    def stage2(h):
        q = spot.qs[2]
        pair_copy(h, q).wait_recv()
        first_copy(h, 1).wait_recv()

        @pl.loop(0, 4)
        def _(r):
            out2[h, r] = total_of(box[0, h, q, r], pair[h, q, r], in1[h, 1, r]).astype(BF)

        copy(0, h).start()

    def stage3(h):
        pair_copy(h, dp).wait_recv()
        first_copy(h, 0).wait_recv()
        copy(0, h).wait_recv()

        @pl.loop(0, 2)
        def _(r):
            value = total_of(box[0, h, dp, 2 + r], pair[h, dp, 2 + r], in1[h, 0, 2 + r], in2[h, 2 + r])
            out3[h, r] = value.astype(BF)

        copy(1, h).start()

        @pl.loop(0, 2)
        def _(r):
            hold[h, r] = total_of(box[0, h, dp, r], pair[h, dp, r], in1[h, 0, r], in2[h, r])


    def stage4(h):
        copy(1, h).wait_recv()
        out4[h] = total_of(hold[h, 1], in3[h, 1]).astype(BF)
        copy(2, h).start()
        hold[h, 0] = total_of(hold[h, 0], in3[h, 0])

    def stage5(h):
        copy(2, h).wait_recv()
        full_a[dp, h] = total_of(hold[h, 0], in4[h]).astype(BF)
        for k in range(3):
            share_a(h, k).start()

    def input_rows(first, count):
        weights = [rows_of(mix.at[k]) for k in range(3)]

        @pl.loop(first, first + count)
        def _(t):
            part = pl.ds(pl.multiple_of(t * 256, 256), 256)
            result, gain, shift, mark = input_part(
                tokens[part, :], marks[:, part], vectors[...], weights,
                [grads_qkv[k, part, :] for k in range(3)], back[part, :],
            )
            input_grad[part, :] = result
            gains[0:1, :] += gain
            gains[1:2, :] += shift
            gains[2:3, :] += mark

    column = (spot.near, spot.far, (dp, spot.zs[3] * 2 + c))

    def vecq_copy(k):
        place = vec_q.at[dp]
        return link(place, place, vecq_sent.at[k], vecq_got.at[dp], trio[k])

    def vec_pair():
        place = vec_f.at[4 + c]
        return link(place, place, vecf_sent.at[3], vecf_got.at[4 + c], spot.core)

    def vecf_copy(k):
        place = vec_f.at[spot.z]
        return link(place, place, vecf_sent.at[k], vecf_got.at[spot.z], column[k])

    def vec_first():
        gain, shift, mark = (gains[k : k + 1, :] for k in range(3))
        flag = (row_flag[0] == 1).astype(F32)
        vec_q[dp] = jnp.concatenate(
            [
                gain, shift, gain2[0:2, :], mark * (1.0 - flag), mark * flag,
                jnp.zeros((2, 768), F32),
            ],
            axis=0,
        )
        for k in range(3):
            vecq_copy(k).start()

    def vec_second():
        for q in spot.qs[1:]:
            place = vec_q.at[q]
            link(place, place, vecq_sent.at[0], vecq_got.at[q], spot.first).wait_recv()
        vec_f[4 + c] = vec_q[0] + vec_q[1] + vec_q[2] + vec_q[3]
        vec_pair().start()

    def vec_spread():
        place = vec_f.at[5 - c]
        link(place, place, vecf_sent.at[3], vecf_got.at[5 - c], spot.core).wait_recv()
        vec_f[spot.z] = vec_f[4] + vec_f[5]
        for k in range(3):
            vecf_copy(k).start()

    def vec_third():
        for k in range(1, 4):
            other = spot.zs[k]
            place = vec_f.at[other]
            link(place, place, vecf_sent.at[0], vecf_got.at[other], spot.near).wait_recv()
        value = vec_f[0] + vec_f[1] + vec_f[2] + vec_f[3]
        return value

    def old_row(index):
        if index < 3:
            line = (mix_rows, proj_rows, expand_rows)[index][...].reshape(1, 96)
        else:
            at = 96 * (index - 3)
            line = shrink_rows[...].reshape(1, 384)[:, at : at + 96]
        return jnp.broadcast_to(line, (8, 96)).T[:, 0:1]

    def wide_stats(blocks, index):
        squares = [b * b for b in blocks]
        total = jnp.sum(squares[0] + 1e-30, axis=1, keepdims=True)
        for square in squares[1:]:
            total = total + jnp.sum(square + 1e-30, axis=1, keepdims=True)
        row = BETA * old_row(index) + (1.0 - BETA) * (total / (768.0 * len(blocks)))
        rows_new[index] = jnp.broadcast_to(row, (96, 128))
        inverse = 1.0 / row
        cols = [jnp.sum(square + 1e-30, axis=0, keepdims=True) for square in squares]
        scaled = [jnp.sum(square * inverse, axis=0, keepdims=True) for square in squares]
        return jnp.sum(row, axis=0, keepdims=True), cols, scaled

    def square_sum(ref):
        value = ref[...]
        return jnp.sum(jnp.sum(value * value, axis=0, keepdims=True), axis=1, keepdims=True)

    def tiles(value):
        return [value[:, 128 * k : 128 * (k + 1)] for k in range(6)]

    def eight(value):
        return jnp.concatenate([value, jnp.zeros((2, 1), F32)], axis=0)

    def scalar_tile(left, right):
        lane = lax.broadcasted_iota(jnp.int32, (8, 128), 1)
        column = jnp.concatenate(left + [jnp.zeros((8 - len(left), 1), F32)], axis=0)
        return jnp.where(
            lane < 64, jnp.broadcast_to(column, (8, 128)), jnp.broadcast_to(right, (8, 128))
        )

    def slot_pair(kind):
        slots = (slots_a, slots_b)[kind]
        return link(
            slots.at[4 + c], slots.at[4 + c], slot_sent.at[kind, 3], slot_got.at[kind, 4 + c], spot.core
        )

    def slot_copy(kind, k):
        place = (slots_a, slots_b)[kind].at[spot.z]
        return link(place, place, slot_sent.at[kind, k], slot_got.at[kind, spot.z], column[k])

    def slot_spread(kind):
        slots = (slots_a, slots_b)[kind]
        link(
            slots.at[5 - c], slots.at[5 - c], slot_sent.at[kind, 3], slot_got.at[kind, 5 - c], spot.core
        ).wait_recv()
        slots[spot.z] = slots[4] + slots[5]
        for k in range(3):
            slot_copy(kind, k).start()

    def slot_sum(kind, out):
        slots = (slots_a, slots_b)[kind]
        for k in range(1, 4):
            other = spot.zs[k]
            place = slots.at[other]
            link(place, place, slot_sent.at[kind, 0], slot_got.at[kind, other], spot.near).wait_recv()
        out[...] = slots[0] + slots[1] + slots[2] + slots[3]

    def stats_b():
        shared_b(0)
        shared_b(1)
        for g in range(2):
            for q in range(4):
                grads[1 + g, q] = full_b[g, q]
        blocks = [full_b[0, q].astype(F32) for q in range(4)]
        total, cols, scaled = wide_stats(blocks, 2)
        total_s, cols_s, scaled_s = None, None, None
        for q in range(4):
            t, col, sc = wide_stats([full_b[1, q].astype(F32)], 3 + q)
            total_s = t if q == 0 else total_s + t
            cols_s = col[0] if q == 0 else cols_s + col[0]
            scaled_s = sc[0] if q == 0 else scaled_s + sc[0]
        for k in range(5, 7):
            local[k].wait()
        plains = plain[...]
        slots_b[4 + c] = jnp.concatenate(
            tiles(jnp.concatenate(cols + scaled, axis=0))
            + tiles(jnp.concatenate([cols_s, scaled_s], axis=0))
            + [jnp.zeros((4, 128), F32)]
            + [
                scalar_tile(
                    [total, total_s, square_sum(w_expand), square_sum(w_shrink)],
                    eight(jnp.sum(plains * plains, axis=1, keepdims=True)),
                )
            ],
            axis=0,
        )
        slot_pair(1).start()

    def stats_a(vector):
        blocks = [
            jnp.concatenate([full_a[q, h] for h in range(3)], axis=1) for q in range(4)
        ]
        for q in range(4):
            grads[0, q] = blocks[q]
        blocks = [b.astype(F32) for b in blocks]
        total, cols, scaled = wide_stats(blocks[:3], 0)
        total_p, cols_p, scaled_p = wide_stats(blocks[3:], 1)
        for k in range(3, 5):
            local[k].wait()
        mine = pltpu.roll(vector, (768 - 96 * fs) % 768, 1)
        vector_sum[...] = mine[:, 0:128]
        mine = mine[0:6, 0:96]
        moment_new = BETA * moment[...] + (1.0 - BETA) * (mine * mine + 1e-30)
        change = mine * lax.rsqrt(moment_new)
        slots_a[4 + c] = jnp.concatenate(
            tiles(jnp.concatenate(cols + cols_p + scaled + scaled_p, axis=0))
            + [
                scalar_tile(
                    [total, total_p, square_sum(w_mix), square_sum(w_proj)],
                    eight(jnp.sum(change * change, axis=1, keepdims=True)),
                )
            ],
            axis=0,
        )
        slot_pair(0).start()

    @pl.when(step == 0)
    def _():
        begin()

    @pl.when(step < 12)
    def _():
        columns = pl.ds(pl.multiple_of(step // 2 * 128, 128), 128)
        attend_back_head(
            length[0], step % 2, kept.at[0], key.at[0], value.at[0], ctx_grad,
            grads_qkv.at[0, :, columns], grads_qkv.at[1, :, columns], grads_qkv.at[2, :, columns], tile,
        )

    @pl.when((step == 3) | (step == 7) | (step == 11))
    def _():
        third_grad(step // 4)

    for at, stage, g in (
        (2, stage3b, 0), (4, stage3b, 1), (5, stage4b, 0), (7, stage4b, 1), (7, stage5b, 0), (9, stage5b, 1),
    ):

        @pl.when(step == at)
        def _():
            stage(g)

    @pl.when(step == 0)
    def _():
        late()
        stage2b(1)
        gains[...] = jnp.zeros((8, 768), F32)

    @pl.when((step == 4) | (step == 8))
    def _():
        stage1(step // 4 - 1)

    @pl.when((step == 6) | (step == 10))
    def _():
        stage2((step - 6) // 4)

    @pl.when((step == 8) | (step == 12))
    def _():
        stage3((step - 8) // 4)

    @pl.when(step == 10)
    def _():
        stage4(0)

    @pl.when(step == 12)
    def _():
        for k in range(3):
            local[k].wait()
        stage1(2)
        input_rows(0, 2)
        stage5(0)
        stage2(2)
        stage4(1)
        input_rows(2, 2)
        vec_first()
        stage3(2)
        stage5(1)
        stats_b()
        vec_second()
        slot_spread(1)
        stage4(2)
        vec_spread()
        vector = vec_third()
        stage5(2)
        slot_sum(1, sums_b)
        for h in range(3):
            shared_a(h)
        stats_a(vector)
        slot_spread(0)
        for p2 in range(2):
            late_s(p2).wait_send()
        for g in range(2):
            for k in range(3):
                share_b(g, k).wait_send()
            for stage in range(3):
                copyb(stage, g).wait_send()

        @pl.loop(0, 3)
        def _(h):
            for k in range(3):
                share_a(h, k).wait_send()
            for q in range(4):
                pair_copy(h, q).wait_send()
            for p2 in range(2):
                first_copy(h, p2).wait_send()
            for stage in range(3):
                copy(stage, h).wait_send()

        for k in range(3):
            vecq_copy(k).wait_send()
        vec_pair().wait_send()
        for k in range(3):
            vecf_copy(k).wait_send()
        slot_sum(0, sums_a)
        for kind in range(2):
            slot_pair(kind).wait_send()
            for k in range(3):
                slot_copy(kind, k).wait_send()


def run_back(length, row_flag, kept, mixed, ctx_grad, near_e, near_s, rest_s, normed, proj_box,
             marks, vectors, gain2, mix_rows, proj_rows, expand_rows, shrink_rows, moment, plain, got_e, got_s, tokens, a_full, middle_back,
             w_mix, w_proj, w_expand, w_shrink, tile=128):
    rows, width = normed.shape
    third = (96, 256)
    block = (96, 768)
    sem = pltpu.SemaphoreType.DMA

    def at(p):
        return jnp.minimum(p, 11)

    return pl.pallas_call(
        functools.partial(back_kernel, tile=tile),
        grid=(13,),
        in_specs=[
            SCALARS,
            SCALARS,
            pl.BlockSpec((1, rows, 128), lambda p: (at(p), 0, 0)),
            pl.BlockSpec((1, rows, 128), lambda p: (6 + at(p) // 2, 0, 0)),
            pl.BlockSpec((1, rows, 128), lambda p: (12 + at(p) // 2, 0, 0)),
            pl.BlockSpec((rows, 128), lambda p: (0, at(p) // 2)),
            fixed(2, 4, *block), fixed(2, 4, *block), fixed(2, *block),
            fixed(rows, width), fixed(2, 4, *block), fixed(16, rows), fixed(16, width), fixed(8, width),
            fixed(96), fixed(96), fixed(96), fixed(384), fixed(6, 96), fixed(6, 96),
            *[ANYWHERE] * 9,
        ],
        out_specs=[
            fixed(rows, width), fixed(3, 4, *block), fixed(7, 96, 128), fixed(56, 128), fixed(72, 128),
            fixed(8, 128),
        ],
        out_shape=shapes(
            ((rows, width), F32), ((3, 4) + block, BF), ((7, 96, 128), F32),
            ((56, 128), F32), ((72, 128), F32), ((8, 128), F32),
        ),
        scratch_shapes=[
            pltpu.VMEM((rows, width), BF),
            pltpu.VMEM((3, 4, 2) + block, BF),
            pltpu.VMEM((rows, width), F32),
            pltpu.VMEM(w_mix.shape, F32),
            pltpu.VMEM(w_proj.shape, F32),
            pltpu.VMEM(w_expand.shape, F32),
            pltpu.VMEM(w_shrink.shape, F32),
            pltpu.VMEM((3, rows, width), BF),
            pltpu.VMEM((2, 2, 4) + block, BF),
            *[pltpu.VMEM((2, 4) + block, BF)] * 2,
            *[pltpu.VMEM((2, 2) + block, BF)] * 2,
            *[pltpu.VMEM((2,) + block, BF)] * 2,
            pltpu.VMEM((2, 2) + block, F32),
            pltpu.VMEM((2, 3, 4, 4) + third, BF),
            pltpu.VMEM((3, 4, 4) + third, BF),
            *[pltpu.VMEM((3, 2, 4) + third, BF)] * 2,
            *[pltpu.VMEM((3, 4) + third, BF)] * 2,
            *[pltpu.VMEM((3, 2) + third, BF)] * 2,
            *[pltpu.VMEM((3,) + third, BF)] * 2,
            pltpu.VMEM((3, 2) + third, F32),
            pltpu.VMEM((4, 3) + third, BF),
            pltpu.VMEM((2, 4) + block, BF),
            pltpu.VMEM((4, 8, 768), F32),
            pltpu.VMEM((6, 8, 768), F32),
            pltpu.VMEM((6, 56, 128), F32),
            pltpu.VMEM((6, 72, 128), F32),
            pltpu.VMEM((8, 768), F32),
            sem((7,)), sem((5,)), sem((2,)), sem((2,)), sem((3, 2)), sem((3, 2)),
            sem((3, 4)), sem((3, 4)), sem((3, 2)), sem((3, 2)), sem((3, 3)), sem((3, 3)),
            sem((5, 3)), sem((5, 4)),
            sem((3,)), sem((4,)), sem((4,)), sem((6,)), sem((2, 4)), sem((2, 6)),
        ],
        compiler_params=params(collective_id=2, has_side_effects=True),
        name="back",
    )(length, row_flag, kept, mixed, mixed, ctx_grad, near_e, near_s, rest_s, normed, proj_box,
      marks, vectors, gain2, mix_rows, proj_rows, expand_rows, shrink_rows, moment, plain, got_e, got_s, tokens, a_full, middle_back,
      w_mix, w_proj, w_expand, w_shrink)


def step_kernel(
    grad_a, grad_e, grad_s, w_mix, w_proj, w_expand, w_shrink, rows,
    mix_cols, proj_cols, expand_cols, shrink_cols, sums_a, sums_b, vector_sum, vectors, moment,
    output_in, input_grad_in,
    mix_grad, proj_grad, expand_grad, shrink_grad, mix_new, proj_new, expand_new, shrink_new,
    mix_rows_new, proj_rows_new, expand_rows_new, shrink_rows_new,
    mix_cols_new, proj_cols_new, expand_cols_new, shrink_cols_new,
    vector_grad, vector_new, moment_new, output, input_grad, cols_new, *, owners
):
    q = pl.program_id(0)
    height = 96.0 * owners
    output[...] = output_in[...]
    input_grad[...] = input_grad_in[...]

    def wide(ref, at, row, count, of):
        return jnp.concatenate(
            [ref[at + of * k + row : at + of * k + row + count, :] for k in range(6)], axis=1
        )

    def one(ref, at, k):
        return ref[at + k : at + k + 1, 0:1]

    @pl.when(q == 0)
    def _():
        def lines(ref, count):
            value = ref[...].reshape(1, 768 * count)
            return [value[:, 768 * k : 768 * (k + 1)] for k in range(count)]

        def flat(first, count):
            value = jnp.concatenate([cols_new[k : k + 1, :] for k in range(first, first + count)], axis=1)
            return value.reshape(768 * count)

        parts = [wide(sums_a, 0, 0, 4, 8), wide(sums_b, 0, 0, 4, 8)]
        old = lines(mix_cols, 3) + lines(proj_cols, 1) + lines(expand_cols, 4)
        cols_new[0:8, :] = BETA * jnp.concatenate(old, axis=0) + (1.0 - BETA) * (
            jnp.concatenate(parts, axis=0) / height
        )
        tall = BETA * lines(shrink_cols, 1)[0] + (1.0 - BETA) * (
            wide(sums_b, 48, 0, 1, 2) / (4.0 * height)
        )
        cols_new[8:16, :] = jnp.broadcast_to(tall, (8, 768))
        mix_cols_new[...] = flat(0, 3)
        proj_cols_new[...] = flat(3, 1)
        expand_cols_new[...] = flat(4, 4)
        shrink_cols_new[...] = flat(8, 1)
        turned = [rows[k].T[0:1, :] for k in range(7)]
        mix_rows_new[...] = turned[0].reshape(96)
        proj_rows_new[...] = turned[1].reshape(96)
        expand_rows_new[...] = turned[2].reshape(96)
        shrink_rows_new[...] = jnp.concatenate(turned[3:], axis=1).reshape(384)
        grad = vector_sum[0:6, 0:96]
        vector_grad[...] = grad
        new = BETA * moment[...] + (1.0 - BETA) * (grad * grad + 1e-30)
        moment_new[...] = new
        width = 96.0 * owners
        clip = jnp.maximum(1.0, jnp.sqrt(sums_a[48:54, 64:65] / width) / CLIP)
        rate = RATE * jnp.maximum(0.001, jnp.sqrt(sums_b[64:70, 64:65] / width))
        vector_new[...] = vectors[...] - rate * ((grad * lax.rsqrt(new)) / clip)

    def update(grad, weight, row, col, scaled, all_cols, row_total, square, count, across):
        row_mean = row_total / count
        entries = count * across
        update_square = row_mean * jnp.sum(
            jnp.sum(scaled / all_cols, axis=1, keepdims=True), axis=0, keepdims=True
        )
        clip = jnp.maximum(1.0, jnp.sqrt(update_square / entries) / CLIP)
        rate = RATE * jnp.maximum(0.001, jnp.sqrt(square / entries))
        factor = rate / clip
        return weight - factor * (grad * lax.rsqrt(row * (col / row_mean)))

    a = grad_a[0, 0].astype(F32)
    col = cols_new[pl.ds(q, 1), :]

    @pl.when(q < 3)
    def _():
        mix_grad[...] = a
        mix_new[...] = update(
            a, w_mix[...], rows[0][:, 0:1], col, wide(sums_a, 0, 4, 3, 8), cols_new[0:3, :],
            one(sums_a, 48, 0), one(sums_a, 48, 2), height, 2304.0,
        )

    @pl.when(q == 3)
    def _():
        proj_grad[...] = a
        proj_new[...] = update(
            a, w_proj[...], rows[1][:, 0:1], col, wide(sums_a, 0, 7, 1, 8), cols_new[3:4, :],
            one(sums_a, 48, 1), one(sums_a, 48, 3), height, 768.0,
        )

    e = grad_e[0, 0].astype(F32)
    expand_grad[...] = e
    expand_new[...] = update(
        e, w_expand[...], rows[2][:, 0:1], cols_new[pl.ds(4 + q, 1), :], wide(sums_b, 0, 4, 4, 8), cols_new[4:8, :],
        one(sums_b, 64, 0), one(sums_b, 64, 2), height, 3072.0,
    )
    t = grad_s[0, 0].astype(F32)
    shrink_grad[...] = t
    shrink_new[...] = update(
        t, w_shrink[...], rows[3 + q][:, 0:1], cols_new[8:9, :], wide(sums_b, 48, 1, 1, 2), cols_new[8:9, :],
        one(sums_b, 64, 1), one(sums_b, 64, 3), 4.0 * height, 768.0,
    )

def run_step(grads, w_mix, w_proj, w_expand, w_shrink, rows, mix_cols, proj_cols, expand_cols, shrink_cols,
             sums_a, sums_b, vector_sum, vectors, moment, output, input_grad, owners):
    block = (96, 768)
    wide = pl.BlockSpec(block, lambda q: (0, q))
    three = pl.BlockSpec(block, lambda q: (0, jnp.minimum(q, 2)))
    tall = pl.BlockSpec(block, lambda q: (q, 0))
    part = pl.BlockSpec((output.shape[0] // 4, 768), lambda q: (q, 0))
    return pl.pallas_call(
        functools.partial(step_kernel, owners=owners),
        grid=(4,),
        in_specs=[
            pl.BlockSpec((1, 1) + block, lambda q: (0, q, 0, 0)),
            pl.BlockSpec((1, 1) + block, lambda q: (1, q, 0, 0)),
            pl.BlockSpec((1, 1) + block, lambda q: (2, q, 0, 0)),
            three, fixed(*block), wide, tall,
            fixed(7, 96, 128), fixed(2304), fixed(768), fixed(3072), fixed(768),
            fixed(56, 128), fixed(72, 128), fixed(8, 128), fixed(6, 96), fixed(6, 96),
            part, part,
        ],
        out_specs=[
            three, fixed(*block), wide, tall, three, fixed(*block), wide, tall,
            fixed(96), fixed(96), fixed(96), fixed(384), fixed(2304), fixed(768), fixed(3072), fixed(768),
            fixed(6, 96), fixed(6, 96), fixed(6, 96), part, part,
        ],
        out_shape=shapes(
            *[(w.shape, F32) for w in (w_mix, w_proj, w_expand, w_shrink)] * 2,
            *[((n,), F32) for n in (96, 96, 96, 384, 2304, 768, 3072, 768)],
            *[((6, 96), F32)] * 3, (output.shape, BF), (input_grad.shape, F32),
        ),
        scratch_shapes=[pltpu.VMEM((16, 768), F32)],
        compiler_params=params(),
        name="step",
    )(grads, grads, grads, w_mix, w_proj, w_expand, w_shrink, rows, mix_cols, proj_cols, expand_cols,
      shrink_cols, sums_a, sums_b, vector_sum, vectors, moment, output, input_grad)


def masks(row_flag, sentence_mask, token_mask, lengths):
    length = sentence_mask.shape[1]
    valid = (lax.broadcasted_iota(jnp.int32, (1, length), 1) < lengths[:, None]).astype(jnp.int32)
    is_token = (row_flag == 1).astype(jnp.int32)[:, None]
    return jnp.concatenate(
        [
            jnp.zeros((4, length), jnp.int32),
            sentence_mask * valid * (1 - is_token),
            token_mask * valid * is_token,
            jnp.zeros((10, length), jnp.int32),
        ]
    ).astype(BF)


def staged_body(
    tokens, cotangent, row_flag, sentence_mask, token_mask, lengths,
    mix_weight, proj_weight, expand_weight, shrink_weight, norm_vectors,
    mix_rows, proj_rows, expand_rows, shrink_rows,
    mix_cols, proj_cols, expand_cols, shrink_cols, vector_moment,
):
    length, width = tokens.shape[1:]
    tokens = tokens.reshape(length, width)
    cotangent = cotangent.reshape(length, width)
    owners = lax.axis_size("fsdp")
    a_full, b_full, c_full, vectors, marks, normed, mixed, context, kept = run_front(
        lengths, row_flag, tokens, sentence_mask, token_mask, norm_vectors,
        mix_weight, proj_weight, expand_weight, shrink_weight,
    )
    (block_output, middle_back, ctx_back, gain2, proj_box,
     near_e, near_s, rest_s, got_e, got_s) = run_feed_send(
        lengths, context, tokens, marks, vectors, a_full, b_full, c_full, cotangent
    )
    input_grad, grads, rows, sums_a, sums_b, vector_sum = run_back(
        lengths, row_flag, kept, mixed, ctx_back, near_e, near_s, rest_s, normed, proj_box,
        marks, vectors, gain2, mix_rows, proj_rows, expand_rows, shrink_rows, vector_moment, norm_vectors,
        got_e, got_s, tokens, a_full, middle_back, mix_weight, proj_weight, expand_weight, shrink_weight,
    )
    (mix_grad, proj_grad, expand_grad, shrink_grad, mix_new, proj_new, expand_new, shrink_new,
     *statistics, vector_grad, vector_new, moment_new, block_output, input_grad) = run_step(
        grads, mix_weight, proj_weight, expand_weight, shrink_weight, rows,
        mix_cols, proj_cols, expand_cols, shrink_cols, sums_a, sums_b, vector_sum,
        norm_vectors, vector_moment, block_output, input_grad, owners,
    )
    return (
        block_output.reshape(1, length, width),
        input_grad.reshape(1, length, width),
        mix_grad, proj_grad, expand_grad, shrink_grad, vector_grad,
        mix_new, proj_new, expand_new, shrink_new, vector_new, *statistics, moment_new,
    )


def plain_body(
    tokens, cotangent, row_flag, sentence_mask, token_mask, lengths,
    mix_weight, proj_weight, expand_weight, shrink_weight, norm_vectors,
    mix_rows, proj_rows, expand_rows, shrink_rows,
    mix_cols, proj_cols, expand_cols, shrink_cols, vector_moment,
):
    length, width = tokens.shape[1:]
    tokens = tokens.reshape(length, width)
    cotangent = cotangent.reshape(length, width)
    owners = lax.axis_size("fsdp")
    marks = masks(row_flag, sentence_mask, token_mask, lengths)
    is_token = (row_flag == 1).astype(F32)[:, None]
    mix_full = lax.all_gather(mix_weight.astype(BF), "fsdp", axis=0, tiled=True)
    proj_full = lax.all_gather(proj_weight.astype(BF), "fsdp", axis=0, tiled=True)
    expand_full = lax.all_gather(expand_weight.astype(BF), "fsdp", axis=0, tiled=True)
    shrink_full = lax.all_gather(shrink_weight.astype(BF), "fsdp", axis=0, tiled=True)
    vectors = lax.all_gather(norm_vectors.astype(BF), "fsdp", axis=1, tiled=True).astype(F32)
    vectors = jnp.concatenate([vectors, jnp.zeros((10, width), F32)])
    normed, mixed = run_mixed(tokens, marks, vectors, mix_full)
    context, kept = run_attend(lengths, mixed)
    block_output, middle_back, ctx_back, gain2, proj_local, expand_local, shrink_local = run_feed(
        lengths, context, tokens, marks, vectors, proj_full, expand_full, shrink_full, cotangent
    )
    dq, dk, dv = run_attend_back(lengths, kept, mixed, ctx_back)
    mix_local = run_mix_grad(normed, dq, dk, dv)
    input_grad, gain1 = run_input(tokens, marks, vectors, mix_full, dq, dk, dv, middle_back)
    vector_local = jnp.concatenate(
        [gain1[0:2], gain2[0:2], gain1[2:3] * (1.0 - is_token), gain1[2:3] * is_token]
    )
    local = (mix_local, proj_local, expand_local, shrink_local)
    shards = [lax.psum_scatter(g, "fsdp", scatter_dimension=0, tiled=True) for g in local]
    shards.append(lax.psum_scatter(vector_local, "fsdp", scatter_dimension=1, tiled=True))
    mix_grad, proj_grad, expand_grad, shrink_grad, vector_grad = lax.psum(tuple(shards), "dp")

    grads = (mix_grad, proj_grad, expand_grad, shrink_grad)
    weights = (mix_weight, proj_weight, expand_weight, shrink_weight)
    old_rows = (mix_rows, proj_rows, expand_rows, shrink_rows)
    old_cols = (mix_cols, proj_cols, expand_cols, shrink_cols)
    rows_new, col_parts, scaled_parts = [], [], []
    for g, r in zip(grads, old_rows):
        square = g * g + 1e-30
        row = BETA * r + (1.0 - BETA) * jnp.mean(square, axis=1)
        rows_new.append(row)
        col_parts.append(jnp.sum(square, axis=0))
        scaled_parts.append(jnp.sum(g * g * (1.0 / row)[:, None], axis=0))
    moment_new = BETA * vector_moment + (1.0 - BETA) * (vector_grad * vector_grad + 1e-30)
    vector_step = vector_grad * lax.rsqrt(moment_new)
    small = jnp.concatenate(
        [
            jnp.stack([jnp.sum(r) for r in rows_new]),
            jnp.stack([jnp.sum(w * w) for w in weights]),
            jnp.sum(vector_step * vector_step, axis=1),
            jnp.sum(norm_vectors * norm_vectors, axis=1),
        ]
    )
    packed = lax.psum(jnp.concatenate(col_parts + scaled_parts + [small]), "fsdp")
    offset = 0
    total_cols = sum(col.shape[0] for col in old_cols)
    small = packed[2 * total_cols :]
    cols_new, new_weights = [], []
    for index in range(4):
        count = grads[index].shape[0] * owners
        wide = old_cols[index].shape[0]
        entries = count * wide
        col = BETA * old_cols[index] + (1.0 - BETA) * packed[offset : offset + wide] / count
        scaled = packed[total_cols + offset : total_cols + offset + wide]
        offset += wide
        cols_new.append(col)
        row_mean = small[index] / count
        update_square = row_mean * jnp.sum(scaled / col)
        clip_factor = jnp.maximum(1.0, jnp.sqrt(update_square / entries) / CLIP)
        rate = RATE * jnp.maximum(0.001, jnp.sqrt(small[4 + index] / entries))
        approx = rows_new[index][:, None] * col[None, :] / row_mean
        step = grads[index] * lax.rsqrt(approx)
        new_weights.append(weights[index] - (rate / clip_factor) * step)
    vector_clip = jnp.maximum(1.0, jnp.sqrt(small[8:14] / width) / CLIP)
    vector_rate = RATE * jnp.maximum(0.001, jnp.sqrt(small[14:20] / width))
    vector_new = norm_vectors - vector_rate[:, None] * (vector_step / vector_clip[:, None])
    return (
        block_output.reshape(1, length, width),
        input_grad.reshape(1, length, width),
        mix_grad, proj_grad, expand_grad, shrink_grad, vector_grad,
        *new_weights, vector_new, *rows_new, *cols_new, moment_new,
    )


def solution(mesh):
    sequence = P(AXES, None, None)
    ins = (
        sequence, sequence, P(AXES), P(AXES, None), P(AXES, None), P(AXES),
        P("fsdp", None), P("fsdp", None), P("fsdp", None), P("fsdp", None), P(None, "fsdp"),
        P("fsdp"), P("fsdp"), P("fsdp"), P("fsdp"), P(), P(), P(), P(), P(None, "fsdp"),
    )
    outs = (
        sequence, sequence,
        P("fsdp", None), P("fsdp", None), P("fsdp", None), P("fsdp", None), P(None, "fsdp"),
        P("fsdp", None), P("fsdp", None), P("fsdp", None), P("fsdp", None), P(None, "fsdp"),
        P("fsdp"), P("fsdp"), P("fsdp"), P("fsdp"), P(), P(), P(), P(), P(None, "fsdp"),
    )
    staged = (mesh.shape["dp"], mesh.shape["fsdp"]) == (4, 8)
    body = staged_body if staged else plain_body
    return jax.shard_map(body, mesh=mesh, in_specs=ins, out_specs=outs, check_vma=False)
```

```python
import functools

import jax
import jax.numpy as jnp
from jax import lax
from jax.experimental import pallas as pl
from jax.experimental.pallas import tpu as pltpu
from jax.sharding import PartitionSpec as P

HEADS = 12
STEP = 10
RATE = 0.5
CLIP = 1.0
F32 = jnp.float32
BF = jnp.bfloat16
VMEM_LIMIT = 60 * 1024 * 1024
AXES = ("dp", "fsdp")


def nn(a, b):
    return lax.dot_general(a, b, (((1,), (0,)), ((), ())), preferred_element_type=F32)


def nt(a, b):
    return lax.dot_general(a, b, (((1,), (1,)), ((), ())), preferred_element_type=F32)


def tn(a, b):
    return lax.dot_general(a, b, (((0,), (0,)), ((), ())), preferred_element_type=F32)


def normalise(h):
    mean = jnp.mean(h, axis=-1, keepdims=True)
    centered = h - mean
    inverse = lax.rsqrt(jnp.mean(centered * centered, axis=-1, keepdims=True) + 1e-06)
    return centered * inverse, inverse


def norm_back(grad, normal, inverse, gain):
    scaled = grad * gain
    first = jnp.mean(scaled, axis=-1, keepdims=True)
    second = jnp.mean(scaled * normal, axis=-1, keepdims=True)
    return inverse * (scaled - first - normal * second)


def params(**kw):
    return pltpu.CompilerParams(vmem_limit_bytes=VMEM_LIMIT, **kw)


def fixed(*shape):
    return pl.BlockSpec(shape, lambda *_: (0,) * len(shape), pipeline_mode=pl.Buffered(1))


ANYWHERE = pl.BlockSpec(memory_space=pl.ANY)
SCALARS = pl.BlockSpec(memory_space=pltpu.SMEM)


def shapes(*items):
    return [jax.ShapeDtypeStruct(shape, kind) for shape, kind in items]


def rows_of(ref):
    value = ref[...]
    return value.reshape(-1, value.shape[-1])


def mixed_kernel(tokens, marks, vectors, weight, normed, mixed):
    start = tokens[...].astype(F32) + tn(marks[...], vectors[...].astype(BF))
    normal, _ = normalise(start)
    low = (normal * vectors[0:1, :] + vectors[1:2, :]).astype(BF)
    normed[...] = low
    result = nn(low, weight[...]).astype(BF)
    for k in range(mixed.shape[0]):
        mixed[k] = result[:, k * 128 : (k + 1) * 128]


def run_mixed(tokens, marks, vectors, weight):
    rows, width = tokens.shape
    cols = weight.shape[1]
    tile = 256
    return pl.pallas_call(
        mixed_kernel,
        grid=(rows // tile,),
        in_specs=[
            pl.BlockSpec((tile, width), lambda i: (i, 0)),
            pl.BlockSpec((16, tile), lambda i: (0, i)),
            pl.BlockSpec((16, width), lambda i: (0, 0)),
            pl.BlockSpec((width, cols), lambda i: (0, 0)),
        ],
        out_specs=[
            pl.BlockSpec((tile, width), lambda i: (i, 0)),
            pl.BlockSpec((cols // 128, tile, 128), lambda i: (0, i, 0)),
        ],
        out_shape=[
            jax.ShapeDtypeStruct((rows, width), BF),
            jax.ShapeDtypeStruct((cols // 128, rows, 128), BF),
        ],
        compiler_params=params(),
        name="mixed",
    )(tokens, marks, vectors, weight)


def lane_iota(rows):
    return lax.broadcasted_iota(jnp.int32, (rows, 128), 1)


def key_extra(rows, length, base):
    lane = lane_iota(rows)
    row = lax.broadcasted_iota(jnp.int32, (rows, 128), 0)
    mask = jnp.where(row < length, 0.0, -1e30)
    ones = jnp.where((lane > base) & (lane < base + 4), 1.0, 0.0)
    return jnp.where(lane == base, mask, ones).astype(BF)


def attend_pair(length, query, key, value, context, kept, tile):
    rows = query.shape[0]
    lane = lane_iota(tile)
    lane_all = lane_iota(rows)
    count = rows // tile
    keys = [
        jnp.where(lane_all < 64, key[...], key_extra(rows, length, 64)),
        jnp.where(lane_all >= 64, key[...], key_extra(rows, length, 0)),
    ]
    values = value[...]

    def first(head, t):
        base = 64 - 64 * head
        mine = (lane < 64) if head == 0 else (lane >= 64)
        one = jnp.where(lane == base, 1.0, 0.0).astype(BF)
        q = jnp.where(mine, query[pl.ds(t * tile, tile), :] * BF(0.125), one)
        return q, nt(q, keys[head])

    def second(head, t, q, score):
        base = 64 - 64 * head
        mine = (lane < 64) if head == 0 else (lane >= 64)
        top = jnp.max(score, axis=-1, keepdims=True)
        expo = jnp.exp(score - top)
        total = jnp.sum(expo, axis=-1, keepdims=True)
        probs = (expo * (1.0 / total)).astype(BF)
        lse = top + jnp.log(total)
        high = lse.astype(BF).astype(F32)
        rest = lse - high
        mid = rest.astype(BF).astype(F32)
        extra = jnp.where(lane == base, 1.0, 0.0)
        extra = jnp.where(lane == base + 1, -high, extra)
        extra = jnp.where(lane == base + 2, -mid, extra)
        extra = jnp.where(lane == base + 3, mid - rest, extra)
        kept[head, pl.ds(t * tile, tile), :] = jnp.where(mine, q, extra.astype(BF))
        return probs

    order = [(head, t) for head in range(2) for t in range(count)]
    outs = {}
    ahead = first(*order[0])
    waiting = None
    for n, spot in enumerate(order):
        now = ahead
        if n + 1 < len(order):
            ahead = first(*order[n + 1])
        if waiting is not None:
            outs[waiting[0]] = nn(waiting[1], values)
        waiting = (spot, second(*spot, *now))
    outs[waiting[0]] = nn(waiting[1], values)
    for t in range(count):
        context[pl.ds(t * tile, tile), :] = jnp.where(lane < 64, outs[0, t], outs[1, t]).astype(BF)


def attend_kernel(length, query, key, value, context, kept, *, tile):
    attend_pair(length[0], query.at[0], key.at[0], value.at[0], context, kept, tile)


def run_attend(length, mixed, tile=256):
    groups, rows, _ = mixed.shape
    pairs = groups // 3
    return pl.pallas_call(
        functools.partial(attend_kernel, tile=tile),
        grid=(pairs,),
        in_specs=[
            pl.BlockSpec(memory_space=pltpu.SMEM),
            pl.BlockSpec((1, rows, 128), lambda p: (p, 0, 0)),
            pl.BlockSpec((1, rows, 128), lambda p: (pairs + p, 0, 0)),
            pl.BlockSpec((1, rows, 128), lambda p: (2 * pairs + p, 0, 0)),
        ],
        out_specs=[
            pl.BlockSpec((rows, 128), lambda p: (0, p)),
            pl.BlockSpec((2, rows, 128), lambda p: (p, 0, 0)),
        ],
        out_shape=[
            jax.ShapeDtypeStruct((rows, pairs * 128), BF),
            jax.ShapeDtypeStruct((2 * pairs, rows, 128), BF),
        ],
        compiler_params=params(),
        name="attend",
    )(length, mixed, mixed, mixed)


class Spot:
    def __init__(self):
        fs = lax.axis_index("fsdp")
        dp = lax.axis_index("dp")
        self.fs, self.dp = fs, dp
        self.c, self.z = fs % 2, fs // 2
        z0, z1 = self.z % 2, self.z // 2
        near, far = z1 * 2 + (1 - z0), (1 - z1) * 2 + z0
        self.zs = (self.z, near, far, (1 - z1) * 2 + (1 - z0))
        x, y = dp % 2, dp // 2
        turn_x, turn_y = 1 - 2 * x, 1 - 2 * y
        first = (y + turn_y * self.c) * 2 + x + turn_x * (1 - self.c)
        second = (y + turn_y * (1 - self.c)) * 2 + x + turn_x * self.c
        self.qs = (dp, first, second, (1 - y) * 2 + 1 - x)
        self.near = (dp, near * 2 + self.c)
        self.far = (dp, far * 2 + self.c)
        self.first = (first, fs)
        self.second = (second, fs)
        self.core = (dp, self.z * 2 + 1 - self.c)

        self.diag = (self.qs[3], fs)
        self.bits = (x, y, z0, z1)
        along_x, along_y = y * 2 + 1 - x, (1 - y) * 2 + x
        self.order = (self.qs[3], along_x, along_y, dp)
        self.first_order = tuple(
            a + (b - a) * self.c
            for a, b in (
                (along_y, along_x), (dp, self.qs[3]), (self.qs[3], dp), (along_x, along_y)
            )
        )

    def row(self, k):
        return (self.dp, (self.fs + k) % 8)

    def other(self, cc):
        return self.c if cc == 0 else 1 - self.c

    def rel_z(self, z):
        low, high = z % 2, z // 2
        near = low + self.bits[2] - 2 * low * self.bits[2]
        far = high + self.bits[3] - 2 * high * self.bits[3]
        return near * 2 + far


def greet(peers):
    barrier = pltpu.get_barrier_semaphore()
    for peer in peers:
        pl.semaphore_signal(barrier, inc=1, device_id=peer, device_id_type=MESH)


def greeted(peers):
    pl.semaphore_wait(pltpu.get_barrier_semaphore(), len(peers))


def link(src, dst, send_sem, recv_sem, target):
    return pltpu.make_async_remote_copy(
        src_ref=src, dst_ref=dst, send_sem=send_sem, recv_sem=recv_sem,
        device_id=target, device_id_type=MESH,
    )


def total_of(*parts):
    value = parts[0].astype(F32)
    for part in parts[1:]:
        value = value + part.astype(F32)
    return value


MESH = pl.DeviceIdType.MESH
SPLIT = (80, 80, 80)


def front_kernel(
    length, row_flag, tokens, sentence, token, share, moment, mix_w, proj_w, expand_w, shrink_w,
    a_out, b_out, c_out, vectors_out, old_out, marks, normed_out, mixed_out, context, kept,
    stage, stage_z, own, own_z, w_a, share_pad, vec_in, old_in, vectors, normed, mixed,
    send, recv, send_z, recv_z, vec_send, vec_recv, old_send, old_recv, local, local_z, *, tile
):
    step = pl.program_id(0)
    spot = Spot()
    c, dp = spot.c, spot.dp
    rows = tokens.shape[0]

    uppers = [pl.ds(0, n) for n in SPLIT]
    lowers = [pl.ds(n, 96 - n) for n in SPLIT]

    def block(g, z, cc, q):
        if g == 0:
            return w_a.at[q, z, cc, uppers[0]]
        if g == 1:
            return b_out.at[q, z, cc, uppers[1]]
        return c_out.at[z, cc, q, uppers[2]]

    def slab(g, z, cc):
        if g == 0:
            return w_a.at[:, z, cc, lowers[0]]
        if g == 1:
            return b_out.at[:, z, cc, lowers[1]]
        return c_out.at[z, cc, :, lowers[2]]

    def remote_z(g, z, cc, kind, target, mine=False):
        dst = slab(g, z, cc)
        return link(
            own_z.at[g - 1, :, pl.ds(0, 96 - SPLIT[g])] if mine and g > 0 else dst, dst,
            send_z.at[g, kind], recv_z.at[g, z * 2 + cc], target,
        )

    def push_z(g, k, kind, target, mine=False):
        remote_z(g, spot.zs[k], c, kind, target, mine).start()

    def arrive_z(g, k):
        remote_z(g, spot.zs[k], c, 0, spot.core).wait_recv()

    def remote(g, z, cc, q, kind, target, mine=False):
        dst = block(g, z, cc, q)
        return pltpu.make_async_remote_copy(
            src_ref=own.at[g - 1, uppers[g]] if mine and g > 0 else dst,
            dst_ref=dst,
            send_sem=send.at[g, kind],
            recv_sem=recv.at[g, (z * 2 + cc) * 4 + q],
            device_id=target,
            device_id_type=MESH,
        )

    def push(g, z, q, kind, target, mine=False):
        remote(g, z, c, q, kind, target, mine).start()

    def arrive(g, z, cc, q):
        remote(g, z, cc, q, 0, spot.core).wait_recv()

    def phase0(g):
        push(g, spot.z, dp, 0, spot.far, True)
        push(g, spot.z, dp, 1, spot.near, True)

    def phase0b(g):
        push(g, spot.z, dp, 7, spot.second, True)
        push(g, spot.z, dp, 3, spot.first, True)
        push(g, spot.z, dp, 15, spot.core, True)

    def phase0z(g):
        push_z(g, 0, 0, spot.far, True)
        push_z(g, 0, 1, spot.near, True)
        push_z(g, 0, 3, spot.core, True)

    def spread(g, k):
        push(g, spot.zs[k], dp, 7 + k, spot.second)
        push(g, spot.zs[k], dp, 3 + k, spot.first)
        push(g, spot.zs[k], dp, 15 + k, spot.core)

    def phase1(g):
        arrive(g, spot.zs[2], c, dp)
        push(g, spot.zs[2], dp, 2, spot.near)
        spread(g, 2)

    def phase1z(g):
        arrive_z(g, 2)
        push_z(g, 2, 2, spot.near)
        push_z(g, 2, 5, spot.core)

    def phase2(g):
        arrive(g, spot.zs[1], c, dp)
        spread(g, 1)
        arrive(g, spot.zs[3], c, dp)
        spread(g, 3)

    def phase2z(g):
        arrive_z(g, 1)
        push_z(g, 1, 4, spot.core)
        arrive_z(g, 3)
        push_z(g, 3, 6, spot.core)

    def phase3(g):
        for k in range(4):
            arrive(g, spot.zs[k], c, spot.qs[1])
            push(g, spot.zs[k], spot.qs[1], 11 + k, spot.second)
            push(g, spot.zs[k], spot.qs[1], 19 + k, spot.core)

    def phase4(g):
        for m in (2, 3):
            for k in range(4):
                arrive(g, spot.zs[k], c, spot.qs[m])
                push(g, spot.zs[k], spot.qs[m], 15 + 4 * m + k, spot.core)

    def phase5(g):
        @pl.loop(0, 4)
        def _(z):
            for q in range(4):
                arrive(g, z, 1 - c, q)
            remote_z(g, z, 1 - c, 0, spot.core).wait_recv()

    def phase6(g):
        @pl.loop(0, 31)
        def _(kind):
            remote(g, spot.z, c, dp, kind, spot.core, True).wait_send()

        @pl.loop(0, 7)
        def _(kind):
            remote_z(g, spot.z, c, kind, spot.core, True).wait_send()

    def vec_copy(k):
        return pltpu.make_async_remote_copy(
            src_ref=vec_in.at[spot.fs],
            dst_ref=vec_in.at[spot.fs],
            send_sem=vec_send.at[k],
            recv_sem=vec_recv.at[spot.fs],
            device_id=spot.row(k),
            device_id_type=MESH,
        )

    def vec_arrive(k):
        other = (spot.fs + k) % 8
        pltpu.make_async_remote_copy(
            src_ref=vec_in.at[other],
            dst_ref=vec_in.at[other],
            send_sem=vec_send.at[k],
            recv_sem=vec_recv.at[other],
            device_id=spot.row(k),
            device_id_type=MESH,
        ).wait_recv()

    def old_copy(k, at):
        place = old_in.at[at]
        return link(place, place, old_send.at[k], old_recv.at[at], spot.row(k))

    def keep_copies():
        return (
            pltpu.make_async_copy(w_a, a_out, local.at[3]),
            pltpu.make_async_copy(own.at[0, uppers[1]], block(1, spot.z, c, dp), local.at[4]),
            pltpu.make_async_copy(own.at[1, uppers[2]], block(2, spot.z, c, dp), local.at[5]),
            pltpu.make_async_copy(own_z.at[0, :, pl.ds(0, 96 - SPLIT[1])], slab(1, spot.z, c), local.at[8]),
            pltpu.make_async_copy(own_z.at[1, :, pl.ds(0, 96 - SPLIT[2])], slab(2, spot.z, c), local.at[9]),
            pltpu.make_async_copy(normed, normed_out, local.at[6]),
            pltpu.make_async_copy(mixed, mixed_out, local.at[7]),
        )

    @pl.when(step == 0)
    def _():
        barrier = pltpu.get_barrier_semaphore()
        peers = [spot.row(k) for k in range(1, 8)] + [spot.first, spot.second]
        for peer in peers:
            pl.semaphore_signal(barrier, inc=1, device_id=peer, device_id_type=MESH)

        columns = pl.ds(pl.multiple_of(dp * 768, 128), 768)

        @pl.when(dp < 3)
        def _():
            pltpu.make_async_copy(mix_w.at[:, columns], stage.at[0], local.at[0]).start()

        @pl.when(dp == 3)
        def _():
            pltpu.make_async_copy(proj_w, stage.at[0], local.at[0]).start()

        second = pltpu.make_async_copy(expand_w.at[:, columns], stage.at[1], local.at[1])
        second.start()
        third = pltpu.make_async_copy(
            shrink_w.at[pl.ds(pl.multiple_of(dp * 96, 32), 96), :], stage.at[2], local.at[2]
        )
        third.start()

        def slab_copy(g, q):
            if g == 0:
                src = proj_w.at[lowers[0], :] if q == 3 else mix_w.at[lowers[0], pl.ds(q * 768, 768)]
            elif g == 1:
                src = expand_w.at[lowers[1], pl.ds(q * 768, 768)]
            else:
                src = shrink_w.at[pl.ds(q * 96 + SPLIT[2], 96 - SPLIT[2]), :]
            return pltpu.make_async_copy(
                src, stage_z.at[g, q, pl.ds(0, 96 - SPLIT[g])], local_z.at[g, q]
            )

        for g in range(3):
            for q in range(4):
                slab_copy(g, q).start()
        share_pad[...] = jnp.zeros((16, 128), F32)
        share_pad[0:6, 0:96] = share[...]
        share_pad[8:14, 0:96] = moment[...]
        old_in[spot.fs] = share_pad[...]
        vec_in[spot.fs] = share_pad[...].astype(BF)
        position = lax.broadcasted_iota(jnp.int32, (1, rows), 1)
        flag = (row_flag[0] == 1).astype(F32)
        line = lax.broadcasted_iota(jnp.int32, (16, rows), 0)
        of_sentence = jnp.where(position < length[0], sentence[...].astype(F32), 0.0) * (1.0 - flag)
        of_token = jnp.where(position < length[0], token[...].astype(F32), 0.0) * flag
        marked = jnp.where(line == 4, of_sentence, jnp.where(line == 5, of_token, 0.0))
        marks[...] = marked.astype(BF)
        pltpu.make_async_copy(proj_w, stage.at[0], local.at[0]).wait()
        w_a[dp, spot.z, c, 0 : SPLIT[0]] = stage[0, 0 : SPLIT[0]].astype(BF)
        pl.semaphore_wait(barrier, len(peers))
        phase0(0)
        phase0b(0)
        for k in range(1, 8):
            vec_copy(k).start()
            old_copy(k, spot.fs).start()
        for q in range(4):
            slab_copy(0, q).wait()
            w_a[q, spot.z, c, SPLIT[0] : 96] = stage_z[0, q, 0 : 96 - SPLIT[0]].astype(BF)
        phase0z(0)
        second.wait()
        own[0] = stage[1].astype(BF)
        third.wait()
        own[1] = stage[2].astype(BF)
        for g in (1, 2):
            for q in range(4):
                slab_copy(g, q).wait()
                own_z[g - 1, q] = stage_z[g, q].astype(BF)
        copies = keep_copies()
        for copy in copies[1:5]:
            copy.start()
        for k in range(1, 8):
            vec_arrive(k)
        total = jnp.zeros((16, 768), F32)
        for f in range(8):
            row = lax.broadcasted_iota(jnp.int32, (128, 768), 0)
            lane = lax.broadcasted_iota(jnp.int32, (128, 768), 1)
            pick = jnp.where((lane - 96 * f == row) & (row < 96), 1.0, 0.0).astype(BF)
            total += nn(vec_in[f], pick)
        vectors[...] = total
        vectors_out[...] = total

        def norm(t):
            part = pl.ds(t * 256, 256)
            start = tokens[part, :].astype(F32) + tn(marks[:, part], total.astype(BF))
            normal, _ = normalise(start)
            normed[part, :] = (normal * total[0:1, :] + total[1:2, :]).astype(BF)

        norm(0)
        norm(1)
        phase1(0)
        phase0(1)
        phase0(2)
        norm(2)
        phase2(0)
        norm(3)
        phase1z(0)
        phase3(0)
        phase0b(1)
        phase1(1)
        phase2z(0)

        @pl.loop(0, 4)
        def _(z):
            remote_z(0, z, 1 - c, 0, spot.core).wait_recv()

        @pl.loop(0, 4)
        def _(k):
            q = jnp.where(
                k < 2, jnp.where(k == 0, spot.qs[0], spot.qs[1]), jnp.where(k == 2, spot.qs[2], spot.qs[3])
            )

            @pl.loop(0, 4)
            def _(z):
                arrive(0, z, 1 - c, q)

            @pl.when(q < 3)
            def _():
                weight = rows_of(w_a.at[q])

                @pl.loop(0, 4, unroll=2)
                def _(t):
                    part = pl.ds(pl.multiple_of(t * 256, 256), 256)
                    result = nn(normed[part, :], weight).astype(BF)
                    for n in range(6):
                        mixed[q * 6 + n, part, :] = result[:, n * 128 : (n + 1) * 128]

            @pl.when(k == 0)
            def _():
                phase4(0)
                phase0b(2)

            @pl.when(k == 1)
            def _():
                phase1(2)
                phase0z(1)
                phase0z(2)

            @pl.when(k == 2)
            def _():
                phase2(1)

            @pl.when(k == 3)
            def _():
                phase2(2)

        copies[0].start()
        copies[5].start()
        copies[6].start()

    @pl.when(step > 0)
    def _():
        p = step - 1
        attend_pair(length[0], mixed.at[p], mixed.at[6 + p], mixed.at[12 + p], context, kept, tile)

    for at, phase, g in (
        (1, phase3, 1), (2, phase3, 2), (2, phase1z, 1), (3, phase1z, 2), (3, phase2z, 1),
        (4, phase4, 1), (4, phase2z, 2), (5, phase4, 2),
    ):

        @pl.when(step == at)
        def _():
            phase(g)

    @pl.when(step == 6)
    def _():
        phase5(1)
        phase5(2)
        for g in range(3):
            phase6(g)
        for k in range(1, 8):
            old_copy(k, spot.fs).wait_send()
            old_copy(k, (spot.fs + k) % 8).wait_recv()
        old_out[...] = old_in[...]
        for k in range(1, 8):
            vec_copy(k).wait_send()
        for copy in keep_copies():
            copy.wait()


def run_front(length, row_flag, tokens, sentence, token, share, moment, mix_w, proj_w, expand_w, shrink_w, tile=256):
    rows, width = tokens.shape
    anywhere = pl.BlockSpec(memory_space=pl.ANY)
    once = pl.Buffered(1)

    def whole(*shape):
        return pl.BlockSpec(shape, lambda i: (0,) * len(shape), pipeline_mode=once)

    return pl.pallas_call(
        functools.partial(front_kernel, tile=tile),
        grid=(7,),
        in_specs=[
            SCALARS,
            SCALARS,
            whole(rows, width),
            whole(1, rows),
            whole(1, rows),
            whole(*share.shape),
            whole(*moment.shape),
            anywhere,
            anywhere,
            anywhere,
            anywhere,
        ],
        out_specs=[
            anywhere,
            anywhere,
            anywhere,
            whole(16, width),
            whole(8, 16, 128),
            whole(16, rows),
            anywhere,
            anywhere,
            pl.BlockSpec((rows, 128), lambda i: (0, jnp.maximum(i - 1, 0))),
            pl.BlockSpec((2, rows, 128), lambda i: (jnp.maximum(i - 1, 0), 0, 0)),
        ],
        out_shape=[
            jax.ShapeDtypeStruct((4, 4, 2, 96, 768), BF),
            jax.ShapeDtypeStruct((4, 4, 2, 96, 768), BF),
            jax.ShapeDtypeStruct((4, 2, 4, 96, 768), BF),
            jax.ShapeDtypeStruct((16, width), F32),
            jax.ShapeDtypeStruct((8, 16, 128), F32),
            jax.ShapeDtypeStruct((16, rows), BF),
            jax.ShapeDtypeStruct((rows, width), BF),
            jax.ShapeDtypeStruct((18, rows, 128), BF),
            jax.ShapeDtypeStruct((rows, width), BF),
            jax.ShapeDtypeStruct((12, rows, 128), BF),
        ],
        scratch_shapes=[
            pltpu.VMEM((3, 96, 768), F32),
            pltpu.VMEM((3, 4, 32, 768), F32),
            pltpu.VMEM((2, 96, 768), BF),
            pltpu.VMEM((2, 4, 32, 768), BF),
            pltpu.VMEM((4, 4, 2, 96, 768), BF),
            pltpu.VMEM((16, 128), F32),
            pltpu.VMEM((8, 16, 128), BF),
            pltpu.VMEM((8, 16, 128), F32),
            pltpu.VMEM((16, width), F32),
            pltpu.VMEM((rows, width), BF),
            pltpu.VMEM((18, rows, 128), BF),
            pltpu.SemaphoreType.DMA((3, 31)),
            pltpu.SemaphoreType.DMA((3, 32)),
            pltpu.SemaphoreType.DMA((3, 7)),
            pltpu.SemaphoreType.DMA((3, 8)),
            *[pltpu.SemaphoreType.DMA((8,))] * 4,
            pltpu.SemaphoreType.DMA((10,)),
            pltpu.SemaphoreType.DMA((3, 4)),
        ],
        compiler_params=params(collective_id=0, has_side_effects=True),
        name="front",
    )(length, row_flag, tokens, sentence, token, share, moment, mix_w, proj_w, expand_w, shrink_w)


def attend_back_pair(length, kept, key, value, ctx_grad, dq, dk, dv, tile):
    rows = key.shape[0]
    lane = lane_iota(tile)
    lane_all = lane_iota(rows)
    count = rows // tile
    plain, plain_values = key[...], value[...]
    keys = [
        jnp.where(lane_all < 64, plain, key_extra(rows, length, 64)),
        jnp.where(lane_all >= 64, plain, key_extra(rows, length, 0)),
    ]
    zero = jnp.zeros_like(plain_values)
    values = [
        jnp.where(lane_all < 64, plain_values, zero),
        jnp.where(lane_all >= 64, plain_values, zero),
    ]

    def first(head, t):
        q = kept[head, pl.ds(t * tile, tile), :]
        grad = ctx_grad[pl.ds(t * tile, tile), :]
        return q, grad, nt(keys[head], q), nt(values[head], grad)

    sums = {}

    def second(head, t, q, grad, score, prob_back):
        probs = jnp.exp(score)
        product = probs * prob_back
        delta = jnp.sum(product, axis=0, keepdims=True)
        score_back = (product - probs * delta).astype(BF)
        dv_part = nn(probs.astype(BF), grad)
        dk_part = nn(score_back, q)
        sums[head, "v"] = dv_part if t == 0 else sums[head, "v"] + dv_part
        sums[head, "k"] = dk_part if t == 0 else sums[head, "k"] + dk_part
        sums[head, t] = tn(score_back, plain)

    order = [(head, t) for head in range(2) for t in range(count)]
    ahead = first(*order[0])
    for n, spot in enumerate(order):
        now = ahead
        if n + 1 < len(order):
            ahead = first(*order[n + 1])
        second(*spot, *now)
    dk[...] = jnp.where(lane_all < 64, sums[0, "k"], sums[1, "k"]).astype(BF)
    dv[...] = jnp.where(lane_all < 64, sums[0, "v"], sums[1, "v"]).astype(BF)
    for t in range(count):
        both = jnp.where(lane < 64, sums[0, t], sums[1, t]) * 0.125
        dq[pl.ds(t * tile, tile), :] = both.astype(BF)


def attend_back_head(length, head, kept, key, value, ctx_grad, dq, dk, dv, tile):
    rows = key.shape[0]
    lane = lane_iota(tile) - 64 * head
    lane_all = lane_iota(rows) - 64 * head
    mine = (lane >= 0) & (lane < 64)
    mine_all = (lane_all >= 0) & (lane_all < 64)
    count = rows // tile
    plain = key[...]
    keys = jnp.where(mine_all, plain, key_extra(rows, length, 64 - 64 * head))
    values = jnp.where(mine_all, value[...], jnp.zeros_like(plain))

    def first(t):
        q = kept[pl.ds(t * tile, tile), :]
        grad = ctx_grad[pl.ds(t * tile, tile), :]
        return q, grad, nt(keys, q), nt(values, grad)

    dv_sum = dk_sum = None
    ahead = first(0)
    for t in range(count):
        q, grad, score, prob_back = ahead
        if t + 1 < count:
            ahead = first(t + 1)
        probs = jnp.exp(score)
        product = probs * prob_back
        delta = jnp.sum(product, axis=0, keepdims=True)
        score_back = (product - probs * delta).astype(BF)
        dv_part = nn(probs.astype(BF), grad)
        dk_part = nn(score_back, q)
        dv_sum = dv_part if t == 0 else dv_sum + dv_part
        dk_sum = dk_part if t == 0 else dk_sum + dk_part
        part = pl.ds(t * tile, tile)
        dq[part, :] = jnp.where(mine, (tn(score_back, plain) * 0.125).astype(BF), dq[part, :])
    dk[...] = jnp.where(mine_all, dk_sum.astype(BF), dk[...])
    dv[...] = jnp.where(mine_all, dv_sum.astype(BF), dv[...])


def attend_back_kernel(length, kept, key, value, ctx_grad, dq, dk, dv, *, tile):
    attend_back_pair(length[0], kept, key.at[0], value.at[0], ctx_grad, dq, dk, dv, tile)


def run_attend_back(length, kept, mixed, ctx_grad, tile=128):
    groups, rows, _ = mixed.shape
    pairs = groups // 3
    width = pairs * 128
    spec = pl.BlockSpec((rows, 128), lambda p: (0, p))
    return pl.pallas_call(
        functools.partial(attend_back_kernel, tile=tile),
        grid=(pairs,),
        in_specs=[
            pl.BlockSpec(memory_space=pltpu.SMEM),
            pl.BlockSpec((2, rows, 128), lambda p: (p, 0, 0)),
            pl.BlockSpec((1, rows, 128), lambda p: (pairs + p, 0, 0)),
            pl.BlockSpec((1, rows, 128), lambda p: (2 * pairs + p, 0, 0)),
            spec,
        ],
        out_specs=[spec, spec, spec],
        out_shape=[jax.ShapeDtypeStruct((rows, width), BF)] * 3,
        compiler_params=params(),
        name="attend_back",
    )(length, kept, mixed, mixed, ctx_grad)


def gelu_pair(v):
    cdf = 0.5 * (1.0 + lax.erf(v * 0.7071067811865476))
    return v * cdf, cdf + v * jnp.exp(-0.5 * v * v) * 0.3989422804014327


def feed_start(
    length, context, tokens, marks, vectors, proj, cotangent, middle, normed, bound, out_sum, back_sum, tile
):
    @pl.loop(0, tokens.shape[0] // tile)
    def _(t):
        part = pl.ds(pl.multiple_of(t * tile, tile), tile)
        start = tokens[part, :].astype(F32) + tn(marks[:, part], vectors[...].astype(BF))
        mid = start + nn(context[part, :], proj)
        middle[part, :] = mid
        out_sum[part, :] = jnp.zeros_like(mid)
        back_sum[part, :] = jnp.zeros_like(mid)
        normal, _ = normalise(mid)
        normed[part, :] = (normal * vectors[2:3, :] + vectors[3:4, :]).astype(BF)
        row = t * tile + lax.broadcasted_iota(jnp.int32, (tile, 1), 0)
        kept = jnp.where(row < length, cotangent[part, :].astype(F32), 0.0)
        bound[part, :] = kept.astype(BF)


def feed_chunk(expand, shrink, normed, bound, active, inner_back, out_sum, back_sum, tile):
    @pl.loop(0, normed.shape[0] // tile, unroll=2)
    def _(t):
        part = pl.ds(pl.multiple_of(t * tile, tile), tile)
        inner = nn(normed[part, :], expand)
        act_back = nt(bound[part, :], shrink)
        act, slope = gelu_pair(inner)
        act = act.astype(BF)
        active[part, :] = act
        back = (act_back * slope).astype(BF)
        inner_back[part, :] = back
        out_sum[part, :] += nn(act, shrink)
        back_sum[part, :] += nt(back, expand)


def feed_finish(
    vectors, proj, middle, normed, bound, out_sum, back_sum, output, middle_back, ctx_back, gain_grads, tile
):
    gain_grads[...] = jnp.zeros_like(gain_grads)

    @pl.loop(0, middle.shape[0] // tile)
    def _(t):
        part = pl.ds(pl.multiple_of(t * tile, tile), tile)
        mid = middle[part, :]
        output[part, :] = (mid + out_sum[part, :]).astype(BF)
        normal, inverse = normalise(mid)
        grad = back_sum[part, :]
        gain_grads[0:1, :] += jnp.sum(grad * normal, axis=0, keepdims=True)
        gain_grads[1:2, :] += jnp.sum(grad, axis=0, keepdims=True)
        back = bound[part, :].astype(F32) + norm_back(grad, normal, inverse, vectors[2:3, :])
        middle_back[part, :] = back
        low = back.astype(BF)
        normed[part, :] = low
        ctx_back[part, :] = nt(low, proj).astype(BF)


def feed_kernel(
    length, context, tokens, marks, vectors, proj, expand, shrink, cotangent,
    output, middle_back, ctx_back, gain_grads, proj_grad, expand_grad, shrink_grad,
    middle, normed, bound, out_sum, active, inner_back, *, tile
):
    j = pl.program_id(0)

    @pl.when(j == 0)
    def _():
        feed_start(
            length[0], context, tokens, marks, vectors, proj[...], cotangent, middle, normed, bound,
            out_sum, middle_back, tile,
        )

    feed_chunk(
        expand[...], shrink[...], normed, bound, active, inner_back, out_sum, middle_back, tile
    )
    expand_grad[...] = tn(normed[...], inner_back[...])
    shrink_grad[...] = tn(active[...], bound[...])

    @pl.when(j == pl.num_programs(0) - 1)
    def _():
        feed_finish(
            vectors, proj[...], middle, normed, bound, out_sum, middle_back,
            output, middle_back, ctx_back, gain_grads, tile,
        )
        proj_grad[...] = tn(context[...], normed[...])


def run_feed(length, context, tokens, marks, vectors, proj, expand, shrink, cotangent, tile=256):
    rows, width = tokens.shape
    inner = expand.shape[1]
    chunk = width
    wide = pl.BlockSpec((width, chunk), lambda j: (0, j))
    tall = pl.BlockSpec((chunk, width), lambda j: (j, 0))
    return pl.pallas_call(
        functools.partial(feed_kernel, tile=tile),
        grid=(inner // chunk,),
        in_specs=[
            SCALARS, fixed(rows, width), fixed(rows, width), fixed(16, rows), fixed(16, width),
            fixed(width, width), wide, tall, fixed(rows, width),
        ],
        out_specs=[
            fixed(rows, width), fixed(rows, width), fixed(rows, width), fixed(8, width),
            fixed(width, width), wide, tall,
        ],
        out_shape=shapes(
            ((rows, width), BF), ((rows, width), F32), ((rows, width), BF), ((8, width), F32),
            ((width, width), F32), ((width, inner), F32), ((inner, width), F32),
        ),
        scratch_shapes=[
            pltpu.VMEM((rows, width), F32),
            pltpu.VMEM((rows, width), BF),
            pltpu.VMEM((rows, width), BF),
            pltpu.VMEM((rows, width), F32),
            pltpu.VMEM((rows, chunk), BF),
            pltpu.VMEM((rows, chunk), BF),
        ],
        compiler_params=params(),
        name="feed",
    )(length, context, tokens, marks, vectors, proj, expand, shrink, cotangent)


def feed_send_kernel(
    length, context, tokens, marks, vectors, proj, expand, shrink, cotangent,
    output, middle_back, ctx_back, gain_grads, proj_box, near_e, near_s, rest_s, got_e, got_s,
    middle, normed, bound, out_sum, active, inner_back,
    box_e, box_s, pair_e, pair_s, out_e, out_s,
    pair_sem, pair_got, first_e_sem, first_e_got, first_s_sem, first_s_got, *, tile
):
    j = pl.program_id(0)
    spot = Spot()
    c = spot.c

    peers = [spot.core, spot.first]

    def pair_copy(step, g):
        slot = step % 2
        src, dst = (box_e, pair_e) if g == 0 else (box_s, pair_s)
        return link(
            src.at[1, slot], dst.at[step], pair_sem.at[g, slot], pair_got.at[g, step], spot.core
        )

    def first_e(p2):
        return link(
            out_e.at[p2], got_e.at[p2], first_e_sem.at[p2], first_e_got.at[p2], spot.first
        )

    def first_s(p2, r):
        return link(
            out_s.at[p2, r], got_s.at[p2, r], first_s_sem.at[p2, r], first_s_got.at[p2, r], spot.first
        )

    def keep_e(step, p2):
        @pl.loop(0, 4)
        def _(r):
            near_e[p2, r] = total_of(box_e[0, step % 2, r], pair_e[step, r]).astype(BF)

    def push_e(step, p2):
        @pl.loop(0, 4)
        def _(r):
            out_e[p2, r] = total_of(box_e[0, step % 2, r], pair_e[step, r]).astype(BF)

        first_e(p2).start()

    def to_first(step):
        slot = step % 2
        pair_copy(step, 0).wait_recv()
        if step == 0:
            push_e(0, 1)
        elif step == 3:
            keep_e(3, 0)
        else:

            @pl.when(c == step - 1)
            def _():
                push_e(step, 0)

            @pl.when(c != step - 1)
            def _():
                keep_e(step, 1)

        pair_copy(step, 1).wait_recv()
        r = spot.rel_z(spot.order[step])
        for p2, q in enumerate((spot.qs[1], spot.qs[3])):
            value = total_of(box_s[0, slot, q], pair_s[step, q]).astype(BF)
            if step < 3:
                out_s[p2, r] = value
                first_s(p2, r).start()
            else:
                rest_s[p2] = value
        for p2, q in enumerate((spot.qs[0], spot.qs[2])):
            near_s[p2, r] = total_of(box_s[0, slot, q], pair_s[step, q]).astype(BF)

    @pl.when(j == 0)
    def _():
        greet(peers)
        feed_start(
            length[0], context, tokens, marks, vectors, rows_of(proj), cotangent,
            middle, normed, bound, out_sum, middle_back, tile,
        )

    feed_chunk(
        rows_of(expand), rows_of(shrink), normed, bound, active, inner_back,
        out_sum, middle_back, tile,
    )

    @pl.when(j == 0)
    def _():
        greeted(peers)

    for step in range(3):

        @pl.when(j == step + 1)
        def _():
            to_first(step)

    slot = j % 2

    @pl.when(j >= 2)
    def _():
        pair_copy(j - 2, 0).wait_send()
        pair_copy(j - 2, 1).wait_send()

    grad_e = tn(normed[...], inner_back[...])
    for z in range(4):
        r = spot.rel_z(z)
        for cc in range(2):
            piece = grad_e[(2 * z + cc) * 96 : (2 * z + cc + 1) * 96, :]
            box_e[spot.other(cc), slot, r] = piece.astype(BF)
    pair_copy(j, 0).start()
    grad_s = tn(active[...], bound[...])
    for cc in range(2):
        for q in range(4):
            piece = grad_s[(cc * 4 + q) * 96 : (cc * 4 + q + 1) * 96, :]
            box_s[spot.other(cc), slot, q] = piece.astype(BF)
    pair_copy(j, 1).start()

    @pl.when(j == 3)
    def _():
        feed_finish(
            vectors, rows_of(proj), middle, normed, bound, out_sum, middle_back,
            output, middle_back, ctx_back, gain_grads, tile,
        )
        grad_p = tn(context[...], normed[...])
        for z in range(4):
            r = spot.rel_z(z)
            for cc in range(2):
                piece = grad_p[(2 * z + cc) * 96 : (2 * z + cc + 1) * 96, :]
                proj_box[spot.other(cc), r] = piece.astype(BF)
        to_first(3)
        for step in (2, 3):
            for g in range(2):
                pair_copy(step, g).wait_send()
        first_e(0).wait_send()
        first_e(1).wait_send()
        first_e(0).wait_recv()
        first_e(1).wait_recv()
        for step in range(3):
            r = spot.rel_z(spot.order[step])
            for p2 in range(2):
                first_s(p2, r).wait_send()
        for p2 in range(2):
            for z in spot.first_order[:3]:
                first_s(p2, spot.rel_z(z)).wait_recv()


def run_feed_send(length, context, tokens, marks, vectors, a_full, b_full, c_full, cotangent, tile=256):
    rows, width = tokens.shape
    block = (96, 768)

    def chunk_at(j):
        dp = lax.axis_index("dp")
        x, y = dp % 2, dp // 2
        turn_x = jnp.where(j < 2, 1, 0)
        turn_y = jnp.where(j % 2 == 0, 1, 0) * jnp.where(j < 3, 1, 0)
        return (y + turn_y - 2 * y * turn_y) * 2 + x + turn_x - 2 * x * turn_x

    return pl.pallas_call(
        functools.partial(feed_send_kernel, tile=tile),
        grid=(4,),
        in_specs=[
            SCALARS, fixed(rows, width), fixed(rows, width), fixed(16, rows), fixed(16, width),
            pl.BlockSpec((1, 4, 2) + block, lambda j: (3, 0, 0, 0, 0), pipeline_mode=pl.Buffered(1)),
            pl.BlockSpec((1, 4, 2) + block, lambda j: (chunk_at(j), 0, 0, 0, 0)),
            pl.BlockSpec((1, 2, 4) + block, lambda j: (chunk_at(j), 0, 0, 0, 0)),
            fixed(rows, width),
        ],
        out_specs=[
            fixed(rows, width), fixed(rows, width), fixed(rows, width), fixed(8, width),
            fixed(2, 4, *block), fixed(2, 4, *block), fixed(2, 4, *block),
            fixed(2, *block), ANYWHERE, ANYWHERE,
        ],
        out_shape=shapes(
            ((rows, width), BF), ((rows, width), F32), ((rows, width), BF), ((8, width), F32),
            *[((2, 4) + block, BF)] * 3,
            ((2,) + block, BF), *[((2, 4) + block, BF)] * 2,
        ),
        scratch_shapes=[
            pltpu.VMEM((rows, width), F32),
            pltpu.VMEM((rows, width), BF),
            pltpu.VMEM((rows, width), BF),
            pltpu.VMEM((rows, width), F32),
            pltpu.VMEM((rows, width), BF),
            pltpu.VMEM((rows, width), BF),
            *[pltpu.VMEM((2, 2, 4) + block, BF)] * 2,
            *[pltpu.VMEM((4, 4) + block, BF)] * 2,
            *[pltpu.VMEM((2, 4) + block, BF)] * 2,
            pltpu.SemaphoreType.DMA((2, 2)),
            pltpu.SemaphoreType.DMA((2, 4)),
            pltpu.SemaphoreType.DMA((2,)),
            pltpu.SemaphoreType.DMA((2,)),
            pltpu.SemaphoreType.DMA((2, 4)),
            pltpu.SemaphoreType.DMA((2, 4)),
        ],
        compiler_params=params(collective_id=1, has_side_effects=True),
        name="feed",
    )(length, context, tokens, marks, vectors, a_full, b_full, c_full, cotangent)


def mix_grad_kernel(normed, dq, dk, dv, grad_out):
    j = pl.program_id(0)
    for index, source in enumerate((dq, dk, dv)):

        @pl.when(j == index)
        def _():
            grad_out[...] = tn(normed[...], source[...])


def run_mix_grad(normed, dq, dk, dv):
    rows, width = normed.shape
    return pl.pallas_call(
        mix_grad_kernel,
        grid=(3,),
        in_specs=[fixed(rows, width)] * 4,
        out_specs=pl.BlockSpec((width, width), lambda j: (0, j)),
        out_shape=jax.ShapeDtypeStruct((width, 3 * width), F32),
        compiler_params=params(),
        name="mix_grad",
    )(normed, dq, dk, dv)


def input_part(tokens, marks, vectors, weights, sources, middle_back):
    start = tokens.astype(F32) + tn(marks, vectors.astype(BF))
    normal, inverse = normalise(start)
    grad = nt(sources[0], weights[0])
    for source, weight in zip(sources[1:], weights[1:]):
        grad += nt(source, weight)
    gain = jnp.sum(grad * normal, axis=0, keepdims=True)
    shift = jnp.sum(grad, axis=0, keepdims=True)
    result = middle_back + norm_back(grad, normal, inverse, vectors[0:1, :])
    spread = tn(marks, jnp.ones(vectors.shape, BF))
    mark = jnp.sum(spread * result, axis=0, keepdims=True)
    return result, gain, shift, mark


def input_kernel(tokens, marks, vectors, weight, dq, dk, dv, middle_back, input_grad, sums):
    i = pl.program_id(0)
    width = tokens.shape[1]
    weights = [weight[:, k * width : (k + 1) * width] for k in range(3)]
    result, gain, shift, mark = input_part(
        tokens[...], marks[...], vectors[...], weights, (dq[...], dk[...], dv[...]), middle_back[...]
    )
    input_grad[...] = result
    both = jnp.concatenate([gain, shift, mark, jnp.zeros((5, width), F32)], axis=0)

    @pl.when(i == 0)
    def _():
        sums[...] = both

    @pl.when(i > 0)
    def _():
        sums[...] += both


def run_input(tokens, marks, vectors, weight, dq, dk, dv, middle_back, tile=256):
    rows, width = tokens.shape
    spec = pl.BlockSpec((tile, width), lambda i: (i, 0))
    return pl.pallas_call(
        input_kernel,
        grid=(rows // tile,),
        in_specs=[
            spec,
            pl.BlockSpec((16, tile), lambda i: (0, i)),
            fixed(16, width),
            fixed(width, 3 * width),
            spec,
            spec,
            spec,
            spec,
        ],
        out_specs=[spec, fixed(8, width)],
        out_shape=shapes(((rows, width), F32), ((8, width), F32)),
        compiler_params=params(),
        name="input_grad",
    )(tokens, marks, vectors, weight, dq, dk, dv, middle_back)


BETA = 1.0 - STEP ** (-0.8)


def back_kernel(
    length, row_flag, kept, key, value, ctx_grad, near_e, near_s, rest_s,
    normed, proj_box, marks, vectors, gain2, mix_rows, proj_rows, expand_rows, shrink_rows,
    got_e_in, got_s_in, tokens_in, mix_in, back_in, w_mix_in, w_proj_in, w_expand_in, w_shrink_in,
    input_grad, grads, rows_new, sums_a, sums_b, vector_sum,
    tokens, mix, back, w_mix, w_proj, w_expand, w_shrink, grads_qkv,
    got, out2b, in2b, out3b, in3b, out4b, in4b, holdb,
    box, pair, out1, in1, out2, in2, out3, in3, out4, in4, hold,
    full_a, full_b, vec_q, vec_f, slots_a, slots_b, gains, columns_old,
    loads, got_sem, late_sent, late_got, sentb, gotb,
    pair_sent, pair_got, sent1, got1, sent, landed, full_sent, full_got,
    vecq_sent, vecq_got, vecf_sent, vecf_got, slot_sent, slot_got, *, tile
):
    step = pl.program_id(0)
    spot = Spot()
    c, dp, fs = spot.c, spot.dp, spot.fs
    trio = (spot.first, spot.second, spot.diag)
    local = [
        pltpu.make_async_copy(src, dst, loads.at[k])
        for k, (src, dst) in enumerate(
            (
                (tokens_in, tokens), (mix_in.at[pl.ds(0, 3)], mix), (back_in, back),
                (w_mix_in, w_mix), (w_proj_in, w_proj), (w_expand_in, w_expand), (w_shrink_in, w_shrink),
            )
        )
    ]

    near = (near_e, near_s)
    load_e = pltpu.make_async_copy(got_e_in, got.at[0], got_sem.at[0])

    def late_s(p2):
        r = spot.rel_z(dp)
        return link(
            rest_s.at[p2], got.at[1, p2, r], late_sent.at[p2], late_got.at[p2], spot.first
        )

    def late_s_came(p2):
        r = spot.rel_z(spot.first_order[3])
        link(
            rest_s.at[p2], got.at[1, p2, r], late_sent.at[p2], late_got.at[p2], spot.first
        ).wait_recv()

    def load_s(k):
        r = spot.rel_z(spot.first_order[k])
        return pltpu.make_async_copy(got_s_in.at[:, r], got.at[1, :, r], got_sem.at[2 + k])

    peers = [spot.core, spot.near, spot.far, (dp, spot.zs[3] * 2 + c), spot.first, spot.second, spot.diag]

    def begin():
        load_e.start()
        for k in range(3):
            load_s(k).start()
        greet(peers)
        for copy in local:
            copy.start()

    def begin_copies():
        greeted(peers)
        for p2 in range(2):
            late_s(p2).start()
        load_e.wait()
        stage2b(0)

    def late():
        for k in range(3):
            load_s(k).wait()
        for p2 in range(2):
            late_s_came(p2)

    def copyb(stage, g):
        src, dst, target = (
            (out2b, in2b, spot.second), (out3b, in3b, spot.near), (out4b, in4b, spot.far),
        )[stage]
        return link(src.at[g], dst.at[g], sentb.at[stage, g], gotb.at[stage, g], target)

    def stage2b(g):
        @pl.loop(0, 4)
        def _(r):
            out2b[g, r] = total_of(near[g][1, r], got[g, 1, r]).astype(BF)

        copyb(0, g).start()

    def stage3b(g):
        copyb(0, g).wait_recv()

        @pl.loop(0, 2)
        def _(r):
            out3b[g, r] = total_of(near[g][0, 2 + r], got[g, 0, 2 + r], in2b[g, 2 + r]).astype(BF)

        copyb(1, g).start()

        @pl.loop(0, 2)
        def _(r):
            holdb[g, r] = total_of(near[g][0, r], got[g, 0, r], in2b[g, r])


    def stage4b(g):
        copyb(1, g).wait_recv()
        out4b[g] = total_of(holdb[g, 1], in3b[g, 1]).astype(BF)
        copyb(2, g).start()
        holdb[g, 0] = total_of(holdb[g, 0], in3b[g, 0])

    def stage5b(g):
        copyb(2, g).wait_recv()
        full_b[g, dp] = total_of(holdb[g, 0], in4b[g]).astype(BF)
        for k in range(3):
            share_b(g, k).start()

    def share_b(g, k):
        place = full_b.at[g, dp]
        return link(place, place, full_sent.at[g, k], full_got.at[g, dp], trio[k])

    def share_a(h, k):
        place = full_a.at[dp, h]
        return link(place, place, full_sent.at[2 + h, k], full_got.at[2 + h, dp], trio[k])

    def shared_b(g):
        for q in spot.qs[1:]:
            place = full_b.at[g, q]
            link(place, place, full_sent.at[g, 0], full_got.at[g, q], spot.first).wait_recv()

    def shared_a(h):
        for q in spot.qs[1:]:
            place = full_a.at[q, h]
            link(place, place, full_sent.at[2 + h, 0], full_got.at[2 + h, q], spot.first).wait_recv()

    def pair_copy(h, q):
        return link(
            box.at[1, h, q], pair.at[h, q], pair_sent.at[h, q], pair_got.at[h, q], spot.core
        )

    def first_copy(h, p2):
        return link(
            out1.at[h, p2], in1.at[h, p2], sent1.at[h, p2], got1.at[h, p2], spot.first
        )

    def copy(stage, h):
        src, dst, target = (
            (out2, in2, spot.second), (out3, in3, spot.near), (out4, in4, spot.far),
        )[stage]
        return link(src.at[h], dst.at[h], sent.at[stage, h], landed.at[stage, h], target)

    def third_grad(h):
        @pl.loop(0, 4)
        def _(r):
            for side in range(2):
                for k in range(3):

                    @pl.when(h == k)
                    def _():
                        box[side, h, 3, r] = proj_box[side, r, :, k * 256 : (k + 1) * 256]

        pair_copy(h, 3).start()

        columns = pl.ds(pl.multiple_of(h * 256, 256), 256)
        sources = jnp.concatenate([grads_qkv[q, :, columns] for q in range(3)], axis=1)
        grad = tn(normed[...], sources)
        for q in range(3):
            for z in range(4):
                r = spot.rel_z(z)
                for cc in range(2):
                    piece = grad[(2 * z + cc) * 96 : (2 * z + cc + 1) * 96, q * 256 : (q + 1) * 256]
                    box[spot.other(cc), h, q, r] = piece.astype(BF)
            pair_copy(h, q).start()

    def stage1(h):
        for p2, q in enumerate((spot.qs[1], spot.qs[3])):
            pair_copy(h, q).wait_recv()

            @pl.loop(0, 4)
            def _(r):
                out1[h, p2, r] = total_of(box[0, h, q, r], pair[h, q, r]).astype(BF)

            first_copy(h, p2).start()

    def stage2(h):
        q = spot.qs[2]
        pair_copy(h, q).wait_recv()
        first_copy(h, 1).wait_recv()

        @pl.loop(0, 4)
        def _(r):
            out2[h, r] = total_of(box[0, h, q, r], pair[h, q, r], in1[h, 1, r]).astype(BF)

        copy(0, h).start()

    def stage3(h):
        pair_copy(h, dp).wait_recv()
        first_copy(h, 0).wait_recv()
        copy(0, h).wait_recv()

        @pl.loop(0, 2)
        def _(r):
            value = total_of(box[0, h, dp, 2 + r], pair[h, dp, 2 + r], in1[h, 0, 2 + r], in2[h, 2 + r])
            out3[h, r] = value.astype(BF)

        copy(1, h).start()

        @pl.loop(0, 2)
        def _(r):
            hold[h, r] = total_of(box[0, h, dp, r], pair[h, dp, r], in1[h, 0, r], in2[h, r])


    def stage4(h):
        copy(1, h).wait_recv()
        out4[h] = total_of(hold[h, 1], in3[h, 1]).astype(BF)
        copy(2, h).start()
        hold[h, 0] = total_of(hold[h, 0], in3[h, 0])

    def stage5(h):
        copy(2, h).wait_recv()
        full_a[dp, h] = total_of(hold[h, 0], in4[h]).astype(BF)
        for k in range(3):
            share_a(h, k).start()

    def input_rows(t):
        weights = [rows_of(mix.at[k]) for k in range(3)]
        part = pl.ds(pl.multiple_of(t * 256, 256), 256)
        result, gain, shift, mark = input_part(
            tokens[part, :], marks[:, part], vectors[...], weights,
            [grads_qkv[k, part, :] for k in range(3)], back[part, :],
        )
        back[part, :] = result
        gains[0:1, :] += gain
        gains[1:2, :] += shift
        gains[2:3, :] += mark

    column = (spot.near, spot.far, (dp, spot.zs[3] * 2 + c))
    result_copy = pltpu.make_async_copy(back, input_grad, loads.at[7])

    def vecq_copy(k):
        place = vec_q.at[dp]
        return link(place, place, vecq_sent.at[k], vecq_got.at[dp], trio[k])

    def vec_pair():
        place = vec_f.at[4 + c]
        return link(place, place, vecf_sent.at[3], vecf_got.at[4 + c], spot.core)

    def vecf_copy(k):
        place = vec_f.at[spot.z]
        return link(place, place, vecf_sent.at[k], vecf_got.at[spot.z], column[k])

    def vec_first():
        gain, shift, mark = (gains[k : k + 1, :] for k in range(3))
        flag = (row_flag[0] == 1).astype(F32)
        vec_q[dp] = jnp.concatenate(
            [
                gain, shift, gain2[0:2, :], mark * (1.0 - flag), mark * flag,
                jnp.zeros((2, 768), F32),
            ],
            axis=0,
        )
        for k in range(3):
            vecq_copy(k).start()

    def vec_second():
        for q in spot.qs[1:]:
            place = vec_q.at[q]
            link(place, place, vecq_sent.at[0], vecq_got.at[q], spot.first).wait_recv()
        vec_f[4 + c] = vec_q[0] + vec_q[1] + vec_q[2] + vec_q[3]
        vec_pair().start()

    def vec_spread():
        place = vec_f.at[5 - c]
        link(place, place, vecf_sent.at[3], vecf_got.at[5 - c], spot.core).wait_recv()
        vec_f[spot.z] = vec_f[4] + vec_f[5]
        for k in range(3):
            vecf_copy(k).start()

    def vec_third():
        for k in range(1, 4):
            other = spot.zs[k]
            place = vec_f.at[other]
            link(place, place, vecf_sent.at[0], vecf_got.at[other], spot.near).wait_recv()
        vector_sum[...] = vec_f[0] + vec_f[1] + vec_f[2] + vec_f[3]

    def turn_rows():
        lines = [ref[...].reshape(1, 96) for ref in (mix_rows, proj_rows, expand_rows)]
        tall = shrink_rows[...].reshape(1, 384)
        lines += [tall[:, 96 * k : 96 * (k + 1)] for k in range(4)]
        columns_old[0:96, 0:8] = jnp.concatenate(lines + lines[:1], axis=0).T
        for k in range(3, 7):
            local[k].wait()
        squares = [square_sum(w) for w in (w_mix, w_proj, w_expand, w_shrink)]
        columns_old[96:104, 0:1] = jnp.concatenate(squares + squares, axis=0)

    def old_row(index):
        return columns_old[0:96, index : index + 1]

    def wide_stats(blocks, index):
        squares = [b * b for b in blocks]
        total = jnp.sum(squares[0] + 1e-30, axis=1, keepdims=True)
        for square in squares[1:]:
            total = total + jnp.sum(square + 1e-30, axis=1, keepdims=True)
        row = BETA * old_row(index) + (1.0 - BETA) * (total / (768.0 * len(blocks)))
        rows_new[index] = jnp.broadcast_to(row, (96, 128))
        inverse = 1.0 / row
        cols = [jnp.sum(square + 1e-30, axis=0, keepdims=True) for square in squares]
        scaled = [jnp.sum(square * inverse, axis=0, keepdims=True) for square in squares]
        return jnp.sum(row, axis=0, keepdims=True), cols, scaled

    def square_sum(ref):
        value = ref[...]
        return jnp.sum(jnp.sum(value * value, axis=0, keepdims=True), axis=1, keepdims=True)

    def tiles(value):
        return [value[:, 128 * k : 128 * (k + 1)] for k in range(6)]

    def scalar_tile(values):
        column = jnp.concatenate(values + [jnp.zeros((8 - len(values), 1), F32)], axis=0)
        return jnp.broadcast_to(column, (8, 128))

    def slot_pair(kind):
        slots = (slots_a, slots_b)[kind]
        return link(
            slots.at[4 + c], slots.at[4 + c], slot_sent.at[kind, 3], slot_got.at[kind, 4 + c], spot.core
        )

    def slot_copy(kind, k):
        place = (slots_a, slots_b)[kind].at[spot.z]
        return link(place, place, slot_sent.at[kind, k], slot_got.at[kind, spot.z], column[k])

    def slot_spread(kind):
        slots = (slots_a, slots_b)[kind]
        link(
            slots.at[5 - c], slots.at[5 - c], slot_sent.at[kind, 3], slot_got.at[kind, 5 - c], spot.core
        ).wait_recv()
        slots[spot.z] = slots[4] + slots[5]
        for k in range(3):
            slot_copy(kind, k).start()

    def slot_sum(kind, out):
        slots = (slots_a, slots_b)[kind]
        for k in range(1, 4):
            other = spot.zs[k]
            place = slots.at[other]
            link(place, place, slot_sent.at[kind, 0], slot_got.at[kind, other], spot.near).wait_recv()
        out[...] = slots[0] + slots[1] + slots[2] + slots[3]

    def stats_b():
        shared_b(0)
        shared_b(1)
        for g in range(2):
            for q in range(4):
                grads[1 + g, q] = full_b[g, q]
        blocks = [full_b[0, q].astype(F32) for q in range(4)]
        total, cols, scaled = wide_stats(blocks, 2)
        total_s, cols_s, scaled_s = None, None, None
        for q in range(4):
            t, col, sc = wide_stats([full_b[1, q].astype(F32)], 3 + q)
            total_s = t if q == 0 else total_s + t
            cols_s = col[0] if q == 0 else cols_s + col[0]
            scaled_s = sc[0] if q == 0 else scaled_s + sc[0]
        slots_b[4 + c] = jnp.concatenate(
            tiles(jnp.concatenate(cols + scaled, axis=0))
            + tiles(jnp.concatenate([cols_s, scaled_s], axis=0))
            + [jnp.zeros((4, 128), F32)]
            + [
                scalar_tile([total, total_s, columns_old[98:99, 0:1], columns_old[99:100, 0:1]])
            ],
            axis=0,
        )
        slot_pair(1).start()

    def stats_a():
        blocks = [
            jnp.concatenate([full_a[q, h] for h in range(3)], axis=1) for q in range(4)
        ]
        for q in range(4):
            grads[0, q] = blocks[q]
        blocks = [b.astype(F32) for b in blocks]
        total, cols, scaled = wide_stats(blocks[:3], 0)
        total_p, cols_p, scaled_p = wide_stats(blocks[3:], 1)
        slots_a[4 + c] = jnp.concatenate(
            tiles(jnp.concatenate(cols + cols_p + scaled + scaled_p, axis=0))
            + [
                scalar_tile([total, total_p, columns_old[96:97, 0:1], columns_old[97:98, 0:1]])
            ],
            axis=0,
        )
        slot_pair(0).start()

    @pl.when(step == 0)
    def _():
        begin()

    @pl.when(step < 12)
    def _():
        columns = pl.ds(pl.multiple_of(step // 2 * 128, 128), 128)
        attend_back_head(
            length[0], step % 2, kept.at[0], key.at[0], value.at[0], ctx_grad,
            grads_qkv.at[0, :, columns], grads_qkv.at[1, :, columns], grads_qkv.at[2, :, columns], tile,
        )

    @pl.when(step == 0)
    def _():
        begin_copies()
        gains[...] = jnp.zeros((8, 768), F32)

    @pl.when(step == 1)
    def _():
        late()
        stage2b(1)

    @pl.when((step == 3) | (step == 7) | (step == 11))
    def _():
        third_grad(step // 4)

    for at, stage, g in (
        (2, stage3b, 0), (4, stage3b, 1), (5, stage4b, 0), (7, stage4b, 1), (7, stage5b, 0), (9, stage5b, 1),
    ):

        @pl.when(step == at)
        def _():
            stage(g)

    @pl.when((step == 4) | (step == 8))
    def _():
        stage1(step // 4 - 1)

    @pl.when((step == 6) | (step == 11))
    def _():
        stage2(step // 8)

    @pl.when(step == 8)
    def _():
        stage3(0)

    @pl.when(step == 10)
    def _():
        stage4(0)

    @pl.when(step == 9)
    def _():
        turn_rows()

    @pl.when(step == 12)
    def _():
        stage1(2)
        for k in range(3):
            local[k].wait()
        stage5(0)

        @pl.loop(0, 4)
        def _(t):
            input_rows(t)

            @pl.when(t == 0)
            def _():
                stage3(1)

            @pl.when(t == 1)
            def _():
                stage2(2)

            @pl.when(t == 2)
            def _():
                stage4(1)
                stage3(2)

        result_copy.start()
        vec_first()
        stage4(2)
        stage5(1)
        stats_b()
        stage5(2)
        vec_second()
        slot_spread(1)
        for h in range(3):
            shared_a(h)
        stats_a()
        vec_spread()
        slot_sum(1, sums_b)
        slot_spread(0)
        for p2 in range(2):
            late_s(p2).wait_send()
        for g in range(2):
            for k in range(3):
                share_b(g, k).wait_send()
            for stage in range(3):
                copyb(stage, g).wait_send()

        @pl.loop(0, 3)
        def _(h):
            for k in range(3):
                share_a(h, k).wait_send()
            for q in range(4):
                pair_copy(h, q).wait_send()
            for p2 in range(2):
                first_copy(h, p2).wait_send()
            for stage in range(3):
                copy(stage, h).wait_send()

        for k in range(3):
            vecq_copy(k).wait_send()
        vec_pair().wait_send()
        for k in range(3):
            vecf_copy(k).wait_send()
        result_copy.wait()
        vec_third()
        slot_sum(0, sums_a)
        for kind in range(2):
            slot_pair(kind).wait_send()
            for k in range(3):
                slot_copy(kind, k).wait_send()


def run_back(length, row_flag, kept, mixed, ctx_grad, near_e, near_s, rest_s, normed, proj_box,
             marks, vectors, gain2, mix_rows, proj_rows, expand_rows, shrink_rows, got_e, got_s, tokens, a_full, middle_back,
             w_mix, w_proj, w_expand, w_shrink, tile=128):
    rows, width = normed.shape
    third = (96, 256)
    block = (96, 768)
    sem = pltpu.SemaphoreType.DMA

    def at(p):
        return jnp.minimum(p, 11)

    return pl.pallas_call(
        functools.partial(back_kernel, tile=tile),
        grid=(13,),
        in_specs=[
            SCALARS,
            SCALARS,
            pl.BlockSpec((1, rows, 128), lambda p: (at(p), 0, 0)),
            pl.BlockSpec((1, rows, 128), lambda p: (6 + at(p) // 2, 0, 0)),
            pl.BlockSpec((1, rows, 128), lambda p: (12 + at(p) // 2, 0, 0)),
            pl.BlockSpec((rows, 128), lambda p: (0, at(p) // 2)),
            fixed(2, 4, *block), fixed(2, 4, *block), fixed(2, *block),
            fixed(rows, width), fixed(2, 4, *block), fixed(16, rows), fixed(16, width), fixed(8, width),
            fixed(96), fixed(96), fixed(96), fixed(384),
            *[ANYWHERE] * 9,
        ],
        out_specs=[
            ANYWHERE, fixed(3, 4, *block), fixed(7, 96, 128), fixed(56, 128), fixed(72, 128),
            fixed(8, width),
        ],
        out_shape=shapes(
            ((rows, width), F32), ((3, 4) + block, BF), ((7, 96, 128), F32),
            ((56, 128), F32), ((72, 128), F32), ((8, width), F32),
        ),
        scratch_shapes=[
            pltpu.VMEM((rows, width), BF),
            pltpu.VMEM((3, 4, 2) + block, BF),
            pltpu.VMEM((rows, width), F32),
            pltpu.VMEM(w_mix.shape, F32),
            pltpu.VMEM(w_proj.shape, F32),
            pltpu.VMEM(w_expand.shape, F32),
            pltpu.VMEM(w_shrink.shape, F32),
            pltpu.VMEM((3, rows, width), BF),
            pltpu.VMEM((2, 2, 4) + block, BF),
            *[pltpu.VMEM((2, 4) + block, BF)] * 2,
            *[pltpu.VMEM((2, 2) + block, BF)] * 2,
            *[pltpu.VMEM((2,) + block, BF)] * 2,
            pltpu.VMEM((2, 2) + block, F32),
            pltpu.VMEM((2, 3, 4, 4) + third, BF),
            pltpu.VMEM((3, 4, 4) + third, BF),
            *[pltpu.VMEM((3, 2, 4) + third, BF)] * 2,
            *[pltpu.VMEM((3, 4) + third, BF)] * 2,
            *[pltpu.VMEM((3, 2) + third, BF)] * 2,
            *[pltpu.VMEM((3,) + third, BF)] * 2,
            pltpu.VMEM((3, 2) + third, F32),
            pltpu.VMEM((4, 3) + third, BF),
            pltpu.VMEM((2, 4) + block, BF),
            pltpu.VMEM((4, 8, 768), F32),
            pltpu.VMEM((6, 8, 768), F32),
            pltpu.VMEM((6, 56, 128), F32),
            pltpu.VMEM((6, 72, 128), F32),
            pltpu.VMEM((8, 768), F32),
            pltpu.VMEM((104, 128), F32),
            sem((8,)), sem((5,)), sem((2,)), sem((2,)), sem((3, 2)), sem((3, 2)),
            sem((3, 4)), sem((3, 4)), sem((3, 2)), sem((3, 2)), sem((3, 3)), sem((3, 3)),
            sem((5, 3)), sem((5, 4)),
            sem((3,)), sem((4,)), sem((4,)), sem((6,)), sem((2, 4)), sem((2, 6)),
        ],
        compiler_params=params(collective_id=2, has_side_effects=True),
        name="back",
    )(length, row_flag, kept, mixed, mixed, ctx_grad, near_e, near_s, rest_s, normed, proj_box,
      marks, vectors, gain2, mix_rows, proj_rows, expand_rows, shrink_rows, got_e, got_s, tokens, a_full, middle_back,
      w_mix, w_proj, w_expand, w_shrink)


def step_kernel(
    grad_a, grad_e, grad_s, w_mix, w_proj, w_expand, w_shrink, rows,
    mix_cols, proj_cols, expand_cols, shrink_cols, sums_a, sums_b, vector_sum, old, vectors, moment,
    output_in, input_grad_in,
    mix_grad, proj_grad, expand_grad, shrink_grad, mix_new, proj_new, expand_new, shrink_new,
    mix_rows_new, proj_rows_new, expand_rows_new, shrink_rows_new,
    mix_cols_new, proj_cols_new, expand_cols_new, shrink_cols_new,
    vector_grad, vector_new, moment_new, output, input_grad, cols_new, *, owners
):
    q = pl.program_id(0)
    height = 96.0 * owners
    output[...] = output_in[...]
    input_grad[...] = input_grad_in[...]

    def wide(ref, at, row, count, of):
        return jnp.concatenate(
            [ref[at + of * k + row : at + of * k + row + count, :] for k in range(6)], axis=1
        )

    def one(ref, at, k):
        return ref[at + k : at + k + 1, 0:1]

    @pl.when(q == 0)
    def _():
        def lines(ref, count):
            value = ref[...].reshape(1, 768 * count)
            return [value[:, 768 * k : 768 * (k + 1)] for k in range(count)]

        def flat(first, count):
            value = jnp.concatenate([cols_new[k : k + 1, :] for k in range(first, first + count)], axis=1)
            return value.reshape(768 * count)

        parts = [wide(sums_a, 0, 0, 4, 8), wide(sums_b, 0, 0, 4, 8)]
        before = lines(mix_cols, 3) + lines(proj_cols, 1) + lines(expand_cols, 4)
        cols_new[0:8, :] = BETA * jnp.concatenate(before, axis=0) + (1.0 - BETA) * (
            jnp.concatenate(parts, axis=0) / height
        )
        tall = BETA * lines(shrink_cols, 1)[0] + (1.0 - BETA) * (
            wide(sums_b, 48, 0, 1, 2) / (4.0 * height)
        )
        cols_new[8:16, :] = jnp.broadcast_to(tall, (8, 768))
        mix_cols_new[...] = flat(0, 3)
        proj_cols_new[...] = flat(3, 1)
        expand_cols_new[...] = flat(4, 4)
        shrink_cols_new[...] = flat(8, 1)
        turned = [rows[k].T[0:1, :] for k in range(7)]
        mix_rows_new[...] = turned[0].reshape(96)
        proj_rows_new[...] = turned[1].reshape(96)
        expand_rows_new[...] = turned[2].reshape(96)
        shrink_rows_new[...] = jnp.concatenate(turned[3:], axis=1).reshape(384)
        fs = lax.axis_index("fsdp")
        grads = vector_sum[...]
        steps, squares = 0.0, 0.0
        for owner in range(8):
            part = pltpu.roll(grads, (768 - 96 * owner) % 768, 1)[0:6, 0:96]
            change = part * lax.rsqrt(
                BETA * old[owner, 8:14, 0:96] + (1.0 - BETA) * (part * part + 1e-30)
            )
            steps += jnp.sum(change * change, axis=1, keepdims=True)
            plain = old[owner, 0:6, 0:96]
            squares += jnp.sum(plain * plain, axis=1, keepdims=True)
        grad = pltpu.roll(grads, (768 - 96 * fs) % 768, 1)[0:6, 0:96]
        vector_grad[...] = grad
        new = BETA * moment[...] + (1.0 - BETA) * (grad * grad + 1e-30)
        moment_new[...] = new
        clip = jnp.maximum(1.0, jnp.sqrt(steps / 768.0) / CLIP)
        rate = RATE * jnp.maximum(0.001, jnp.sqrt(squares / 768.0))
        vector_new[...] = vectors[...] - rate * ((grad * lax.rsqrt(new)) / clip)

    def update(grad, weight, row, col, scaled, all_cols, row_total, square, count, across):
        row_mean = row_total / count
        entries = count * across
        update_square = row_mean * jnp.sum(
            jnp.sum(scaled / all_cols, axis=1, keepdims=True), axis=0, keepdims=True
        )
        clip = jnp.maximum(1.0, jnp.sqrt(update_square / entries) / CLIP)
        rate = RATE * jnp.maximum(0.001, jnp.sqrt(square / entries))
        factor = rate / clip
        return weight - factor * (grad * lax.rsqrt(row * (col / row_mean)))

    a = grad_a[0, 0].astype(F32)
    col = cols_new[pl.ds(q, 1), :]

    @pl.when(q < 3)
    def _():
        mix_grad[...] = a
        mix_new[...] = update(
            a, w_mix[...], rows[0][:, 0:1], col, wide(sums_a, 0, 4, 3, 8), cols_new[0:3, :],
            one(sums_a, 48, 0), one(sums_a, 48, 2), height, 2304.0,
        )

    @pl.when(q == 3)
    def _():
        proj_grad[...] = a
        proj_new[...] = update(
            a, w_proj[...], rows[1][:, 0:1], col, wide(sums_a, 0, 7, 1, 8), cols_new[3:4, :],
            one(sums_a, 48, 1), one(sums_a, 48, 3), height, 768.0,
        )

    e = grad_e[0, 0].astype(F32)
    expand_grad[...] = e
    expand_new[...] = update(
        e, w_expand[...], rows[2][:, 0:1], cols_new[pl.ds(4 + q, 1), :], wide(sums_b, 0, 4, 4, 8), cols_new[4:8, :],
        one(sums_b, 64, 0), one(sums_b, 64, 2), height, 3072.0,
    )
    t = grad_s[0, 0].astype(F32)
    shrink_grad[...] = t
    shrink_new[...] = update(
        t, w_shrink[...], rows[3 + q][:, 0:1], cols_new[8:9, :], wide(sums_b, 48, 1, 1, 2), cols_new[8:9, :],
        one(sums_b, 64, 1), one(sums_b, 64, 3), 4.0 * height, 768.0,
    )

def run_step(grads, w_mix, w_proj, w_expand, w_shrink, rows, mix_cols, proj_cols, expand_cols, shrink_cols,
             sums_a, sums_b, vector_sum, old, vectors, moment, output, input_grad, owners):
    block = (96, 768)
    wide = pl.BlockSpec(block, lambda q: (0, q))
    three = pl.BlockSpec(block, lambda q: (0, jnp.minimum(q, 2)))
    tall = pl.BlockSpec(block, lambda q: (q, 0))
    part = pl.BlockSpec((output.shape[0] // 4, 768), lambda q: (q, 0))
    return pl.pallas_call(
        functools.partial(step_kernel, owners=owners),
        grid=(4,),
        in_specs=[
            pl.BlockSpec((1, 1) + block, lambda q: (0, q, 0, 0)),
            pl.BlockSpec((1, 1) + block, lambda q: (1, q, 0, 0)),
            pl.BlockSpec((1, 1) + block, lambda q: (2, q, 0, 0)),
            three, fixed(*block), wide, tall,
            fixed(7, 96, 128), fixed(2304), fixed(768), fixed(3072), fixed(768),
            fixed(56, 128), fixed(72, 128), fixed(8, 768), fixed(8, 16, 128), fixed(6, 96), fixed(6, 96),
            part, part,
        ],
        out_specs=[
            three, fixed(*block), wide, tall, three, fixed(*block), wide, tall,
            fixed(96), fixed(96), fixed(96), fixed(384), fixed(2304), fixed(768), fixed(3072), fixed(768),
            fixed(6, 96), fixed(6, 96), fixed(6, 96), part, part,
        ],
        out_shape=shapes(
            *[(w.shape, F32) for w in (w_mix, w_proj, w_expand, w_shrink)] * 2,
            *[((n,), F32) for n in (96, 96, 96, 384, 2304, 768, 3072, 768)],
            *[((6, 96), F32)] * 3, (output.shape, BF), (input_grad.shape, F32),
        ),
        scratch_shapes=[pltpu.VMEM((16, 768), F32)],
        compiler_params=params(),
        name="step",
    )(grads, grads, grads, w_mix, w_proj, w_expand, w_shrink, rows, mix_cols, proj_cols, expand_cols,
      shrink_cols, sums_a, sums_b, vector_sum, old, vectors, moment, output, input_grad)


def masks(row_flag, sentence_mask, token_mask, lengths):
    length = sentence_mask.shape[1]
    valid = (lax.broadcasted_iota(jnp.int32, (1, length), 1) < lengths[:, None]).astype(jnp.int32)
    is_token = (row_flag == 1).astype(jnp.int32)[:, None]
    return jnp.concatenate(
        [
            jnp.zeros((4, length), jnp.int32),
            sentence_mask * valid * (1 - is_token),
            token_mask * valid * is_token,
            jnp.zeros((10, length), jnp.int32),
        ]
    ).astype(BF)


def staged_body(
    tokens, cotangent, row_flag, sentence_mask, token_mask, lengths,
    mix_weight, proj_weight, expand_weight, shrink_weight, norm_vectors,
    mix_rows, proj_rows, expand_rows, shrink_rows,
    mix_cols, proj_cols, expand_cols, shrink_cols, vector_moment,
):
    length, width = tokens.shape[1:]
    tokens = tokens.reshape(length, width)
    cotangent = cotangent.reshape(length, width)
    owners = lax.axis_size("fsdp")
    a_full, b_full, c_full, vectors, old, marks, normed, mixed, context, kept = run_front(
        lengths, row_flag, tokens, sentence_mask, token_mask, norm_vectors, vector_moment,
        mix_weight, proj_weight, expand_weight, shrink_weight,
    )
    (block_output, middle_back, ctx_back, gain2, proj_box,
     near_e, near_s, rest_s, got_e, got_s) = run_feed_send(
        lengths, context, tokens, marks, vectors, a_full, b_full, c_full, cotangent
    )
    input_grad, grads, rows, sums_a, sums_b, vector_sum = run_back(
        lengths, row_flag, kept, mixed, ctx_back, near_e, near_s, rest_s, normed, proj_box,
        marks, vectors, gain2, mix_rows, proj_rows, expand_rows, shrink_rows,
        got_e, got_s, tokens, a_full, middle_back, mix_weight, proj_weight, expand_weight, shrink_weight,
    )
    (mix_grad, proj_grad, expand_grad, shrink_grad, mix_new, proj_new, expand_new, shrink_new,
     *statistics, vector_grad, vector_new, moment_new, block_output, input_grad) = run_step(
        grads, mix_weight, proj_weight, expand_weight, shrink_weight, rows,
        mix_cols, proj_cols, expand_cols, shrink_cols, sums_a, sums_b, vector_sum, old,
        norm_vectors, vector_moment, block_output, input_grad, owners,
    )
    return (
        block_output.reshape(1, length, width),
        input_grad.reshape(1, length, width),
        mix_grad, proj_grad, expand_grad, shrink_grad, vector_grad,
        mix_new, proj_new, expand_new, shrink_new, vector_new, *statistics, moment_new,
    )


def plain_body(
    tokens, cotangent, row_flag, sentence_mask, token_mask, lengths,
    mix_weight, proj_weight, expand_weight, shrink_weight, norm_vectors,
    mix_rows, proj_rows, expand_rows, shrink_rows,
    mix_cols, proj_cols, expand_cols, shrink_cols, vector_moment,
):
    length, width = tokens.shape[1:]
    tokens = tokens.reshape(length, width)
    cotangent = cotangent.reshape(length, width)
    owners = lax.axis_size("fsdp")
    marks = masks(row_flag, sentence_mask, token_mask, lengths)
    is_token = (row_flag == 1).astype(F32)[:, None]
    mix_full = lax.all_gather(mix_weight.astype(BF), "fsdp", axis=0, tiled=True)
    proj_full = lax.all_gather(proj_weight.astype(BF), "fsdp", axis=0, tiled=True)
    expand_full = lax.all_gather(expand_weight.astype(BF), "fsdp", axis=0, tiled=True)
    shrink_full = lax.all_gather(shrink_weight.astype(BF), "fsdp", axis=0, tiled=True)
    vectors = lax.all_gather(norm_vectors.astype(BF), "fsdp", axis=1, tiled=True).astype(F32)
    vectors = jnp.concatenate([vectors, jnp.zeros((10, width), F32)])
    normed, mixed = run_mixed(tokens, marks, vectors, mix_full)
    context, kept = run_attend(lengths, mixed)
    block_output, middle_back, ctx_back, gain2, proj_local, expand_local, shrink_local = run_feed(
        lengths, context, tokens, marks, vectors, proj_full, expand_full, shrink_full, cotangent
    )
    dq, dk, dv = run_attend_back(lengths, kept, mixed, ctx_back)
    mix_local = run_mix_grad(normed, dq, dk, dv)
    input_grad, gain1 = run_input(tokens, marks, vectors, mix_full, dq, dk, dv, middle_back)
    vector_local = jnp.concatenate(
        [gain1[0:2], gain2[0:2], gain1[2:3] * (1.0 - is_token), gain1[2:3] * is_token]
    )
    local = (mix_local, proj_local, expand_local, shrink_local)
    shards = [lax.psum_scatter(g, "fsdp", scatter_dimension=0, tiled=True) for g in local]
    shards.append(lax.psum_scatter(vector_local, "fsdp", scatter_dimension=1, tiled=True))
    mix_grad, proj_grad, expand_grad, shrink_grad, vector_grad = lax.psum(tuple(shards), "dp")

    grads = (mix_grad, proj_grad, expand_grad, shrink_grad)
    weights = (mix_weight, proj_weight, expand_weight, shrink_weight)
    old_rows = (mix_rows, proj_rows, expand_rows, shrink_rows)
    old_cols = (mix_cols, proj_cols, expand_cols, shrink_cols)
    rows_new, col_parts, scaled_parts = [], [], []
    for g, r in zip(grads, old_rows):
        square = g * g + 1e-30
        row = BETA * r + (1.0 - BETA) * jnp.mean(square, axis=1)
        rows_new.append(row)
        col_parts.append(jnp.sum(square, axis=0))
        scaled_parts.append(jnp.sum(g * g * (1.0 / row)[:, None], axis=0))
    moment_new = BETA * vector_moment + (1.0 - BETA) * (vector_grad * vector_grad + 1e-30)
    vector_step = vector_grad * lax.rsqrt(moment_new)
    small = jnp.concatenate(
        [
            jnp.stack([jnp.sum(r) for r in rows_new]),
            jnp.stack([jnp.sum(w * w) for w in weights]),
            jnp.sum(vector_step * vector_step, axis=1),
            jnp.sum(norm_vectors * norm_vectors, axis=1),
        ]
    )
    packed = lax.psum(jnp.concatenate(col_parts + scaled_parts + [small]), "fsdp")
    offset = 0
    total_cols = sum(col.shape[0] for col in old_cols)
    small = packed[2 * total_cols :]
    cols_new, new_weights = [], []
    for index in range(4):
        count = grads[index].shape[0] * owners
        wide = old_cols[index].shape[0]
        entries = count * wide
        col = BETA * old_cols[index] + (1.0 - BETA) * packed[offset : offset + wide] / count
        scaled = packed[total_cols + offset : total_cols + offset + wide]
        offset += wide
        cols_new.append(col)
        row_mean = small[index] / count
        update_square = row_mean * jnp.sum(scaled / col)
        clip_factor = jnp.maximum(1.0, jnp.sqrt(update_square / entries) / CLIP)
        rate = RATE * jnp.maximum(0.001, jnp.sqrt(small[4 + index] / entries))
        approx = rows_new[index][:, None] * col[None, :] / row_mean
        step = grads[index] * lax.rsqrt(approx)
        new_weights.append(weights[index] - (rate / clip_factor) * step)
    vector_clip = jnp.maximum(1.0, jnp.sqrt(small[8:14] / width) / CLIP)
    vector_rate = RATE * jnp.maximum(0.001, jnp.sqrt(small[14:20] / width))
    vector_new = norm_vectors - vector_rate[:, None] * (vector_step / vector_clip[:, None])
    return (
        block_output.reshape(1, length, width),
        input_grad.reshape(1, length, width),
        mix_grad, proj_grad, expand_grad, shrink_grad, vector_grad,
        *new_weights, vector_new, *rows_new, *cols_new, moment_new,
    )


def solution(mesh):
    sequence = P(AXES, None, None)
    ins = (
        sequence, sequence, P(AXES), P(AXES, None), P(AXES, None), P(AXES),
        P("fsdp", None), P("fsdp", None), P("fsdp", None), P("fsdp", None), P(None, "fsdp"),
        P("fsdp"), P("fsdp"), P("fsdp"), P("fsdp"), P(), P(), P(), P(), P(None, "fsdp"),
    )
    outs = (
        sequence, sequence,
        P("fsdp", None), P("fsdp", None), P("fsdp", None), P("fsdp", None), P(None, "fsdp"),
        P("fsdp", None), P("fsdp", None), P("fsdp", None), P("fsdp", None), P(None, "fsdp"),
        P("fsdp"), P("fsdp"), P("fsdp"), P("fsdp"), P(), P(), P(), P(), P(None, "fsdp"),
    )
    staged = (mesh.shape["dp"], mesh.shape["fsdp"]) == (4, 8)
    body = staged_body if staged else plain_body
    return jax.shard_map(body, mesh=mesh, in_specs=ins, out_specs=outs, check_vma=False)
```

```python
import functools

import jax
import jax.numpy as jnp
from jax import lax
from jax.experimental import pallas as pl
from jax.experimental.pallas import tpu as pltpu
from jax.sharding import PartitionSpec as P

HEADS = 12
STEP = 10
RATE = 0.5
CLIP = 1.0
F32 = jnp.float32
BF = jnp.bfloat16
VMEM_LIMIT = 60 * 1024 * 1024
AXES = ("dp", "fsdp")


def nn(a, b):
    return lax.dot_general(a, b, (((1,), (0,)), ((), ())), preferred_element_type=F32)


def nt(a, b):
    return lax.dot_general(a, b, (((1,), (1,)), ((), ())), preferred_element_type=F32)


def tn(a, b):
    return lax.dot_general(a, b, (((0,), (0,)), ((), ())), preferred_element_type=F32)


def normalise(h):
    mean = jnp.mean(h, axis=-1, keepdims=True)
    centered = h - mean
    inverse = lax.rsqrt(jnp.mean(centered * centered, axis=-1, keepdims=True) + 1e-06)
    return centered * inverse, inverse


def norm_back(grad, normal, inverse, gain):
    scaled = grad * gain
    first = jnp.mean(scaled, axis=-1, keepdims=True)
    second = jnp.mean(scaled * normal, axis=-1, keepdims=True)
    return inverse * (scaled - first - normal * second)


def params(**kw):
    return pltpu.CompilerParams(vmem_limit_bytes=VMEM_LIMIT, **kw)


def fixed(*shape):
    return pl.BlockSpec(shape, lambda *_: (0,) * len(shape), pipeline_mode=pl.Buffered(1))


ANYWHERE = pl.BlockSpec(memory_space=pl.ANY)
SCALARS = pl.BlockSpec(memory_space=pltpu.SMEM)


def shapes(*items):
    return [jax.ShapeDtypeStruct(shape, kind) for shape, kind in items]


def rows_of(ref):
    value = ref[...]
    return value.reshape(-1, value.shape[-1])


def mixed_kernel(tokens, marks, vectors, weight, normed, mixed):
    start = tokens[...].astype(F32) + tn(marks[...], vectors[...].astype(BF))
    normal, _ = normalise(start)
    low = (normal * vectors[0:1, :] + vectors[1:2, :]).astype(BF)
    normed[...] = low
    result = nn(low, weight[...]).astype(BF)
    for k in range(mixed.shape[0]):
        mixed[k] = result[:, k * 128 : (k + 1) * 128]


def run_mixed(tokens, marks, vectors, weight):
    rows, width = tokens.shape
    cols = weight.shape[1]
    tile = 256
    return pl.pallas_call(
        mixed_kernel,
        grid=(rows // tile,),
        in_specs=[
            pl.BlockSpec((tile, width), lambda i: (i, 0)),
            pl.BlockSpec((16, tile), lambda i: (0, i)),
            pl.BlockSpec((16, width), lambda i: (0, 0)),
            pl.BlockSpec((width, cols), lambda i: (0, 0)),
        ],
        out_specs=[
            pl.BlockSpec((tile, width), lambda i: (i, 0)),
            pl.BlockSpec((cols // 128, tile, 128), lambda i: (0, i, 0)),
        ],
        out_shape=[
            jax.ShapeDtypeStruct((rows, width), BF),
            jax.ShapeDtypeStruct((cols // 128, rows, 128), BF),
        ],
        compiler_params=params(),
        name="mixed",
    )(tokens, marks, vectors, weight)


def lane_iota(rows):
    return lax.broadcasted_iota(jnp.int32, (rows, 128), 1)


def key_extra(rows, length, base):
    lane = lane_iota(rows)
    row = lax.broadcasted_iota(jnp.int32, (rows, 128), 0)
    mask = jnp.where(row < length, 0.0, -1e30)
    ones = jnp.where((lane > base) & (lane < base + 4), 1.0, 0.0)
    return jnp.where(lane == base, mask, ones).astype(BF)


def attend_pair(length, query, key, value, context, kept, tile):
    rows = query.shape[0]
    lane = lane_iota(tile)
    lane_all = lane_iota(rows)
    count = rows // tile
    keys = [
        jnp.where(lane_all < 64, key[...], key_extra(rows, length, 64)),
        jnp.where(lane_all >= 64, key[...], key_extra(rows, length, 0)),
    ]
    values = value[...]

    def first(head, t):
        base = 64 - 64 * head
        mine = (lane < 64) if head == 0 else (lane >= 64)
        one = jnp.where(lane == base, 1.0, 0.0).astype(BF)
        q = jnp.where(mine, query[pl.ds(t * tile, tile), :] * BF(0.125), one)
        return q, nt(q, keys[head])

    def second(head, t, q, score):
        base = 64 - 64 * head
        mine = (lane < 64) if head == 0 else (lane >= 64)
        top = jnp.max(score, axis=-1, keepdims=True)
        expo = jnp.exp(score - top)
        total = jnp.sum(expo, axis=-1, keepdims=True)
        probs = (expo * (1.0 / total)).astype(BF)
        lse = top + jnp.log(total)
        high = lse.astype(BF).astype(F32)
        rest = lse - high
        mid = rest.astype(BF).astype(F32)
        extra = jnp.where(lane == base, 1.0, 0.0)
        extra = jnp.where(lane == base + 1, -high, extra)
        extra = jnp.where(lane == base + 2, -mid, extra)
        extra = jnp.where(lane == base + 3, mid - rest, extra)
        kept[head, pl.ds(t * tile, tile), :] = jnp.where(mine, q, extra.astype(BF))
        return probs

    order = [(head, t) for head in range(2) for t in range(count)]
    outs = {}
    ahead = first(*order[0])
    waiting = None
    for n, spot in enumerate(order):
        now = ahead
        if n + 1 < len(order):
            ahead = first(*order[n + 1])
        if waiting is not None:
            outs[waiting[0]] = nn(waiting[1], values)
        waiting = (spot, second(*spot, *now))
    outs[waiting[0]] = nn(waiting[1], values)
    for t in range(count):
        context[pl.ds(t * tile, tile), :] = jnp.where(lane < 64, outs[0, t], outs[1, t]).astype(BF)


def attend_kernel(length, query, key, value, context, kept, *, tile):
    attend_pair(length[0], query.at[0], key.at[0], value.at[0], context, kept, tile)


def run_attend(length, mixed, tile=256):
    groups, rows, _ = mixed.shape
    pairs = groups // 3
    return pl.pallas_call(
        functools.partial(attend_kernel, tile=tile),
        grid=(pairs,),
        in_specs=[
            pl.BlockSpec(memory_space=pltpu.SMEM),
            pl.BlockSpec((1, rows, 128), lambda p: (p, 0, 0)),
            pl.BlockSpec((1, rows, 128), lambda p: (pairs + p, 0, 0)),
            pl.BlockSpec((1, rows, 128), lambda p: (2 * pairs + p, 0, 0)),
        ],
        out_specs=[
            pl.BlockSpec((rows, 128), lambda p: (0, p)),
            pl.BlockSpec((2, rows, 128), lambda p: (p, 0, 0)),
        ],
        out_shape=[
            jax.ShapeDtypeStruct((rows, pairs * 128), BF),
            jax.ShapeDtypeStruct((2 * pairs, rows, 128), BF),
        ],
        compiler_params=params(),
        name="attend",
    )(length, mixed, mixed, mixed)


class Spot:
    def __init__(self):
        fs = lax.axis_index("fsdp")
        dp = lax.axis_index("dp")
        self.fs, self.dp = fs, dp
        self.c, self.z = fs % 2, fs // 2
        z0, z1 = self.z % 2, self.z // 2
        near, far = z1 * 2 + (1 - z0), (1 - z1) * 2 + z0
        self.zs = (self.z, near, far, (1 - z1) * 2 + (1 - z0))
        x, y = dp % 2, dp // 2
        turn_x, turn_y = 1 - 2 * x, 1 - 2 * y
        first = (y + turn_y * self.c) * 2 + x + turn_x * (1 - self.c)
        second = (y + turn_y * (1 - self.c)) * 2 + x + turn_x * self.c
        self.qs = (dp, first, second, (1 - y) * 2 + 1 - x)
        self.near = (dp, near * 2 + self.c)
        self.far = (dp, far * 2 + self.c)
        self.first = (first, fs)
        self.second = (second, fs)
        self.core = (dp, self.z * 2 + 1 - self.c)

        self.diag = (self.qs[3], fs)
        self.bits = (x, y, z0, z1)
        along_x, along_y = y * 2 + 1 - x, (1 - y) * 2 + x
        self.order = (self.qs[3], along_x, along_y, dp)
        self.first_order = tuple(
            a + (b - a) * self.c
            for a, b in (
                (along_y, along_x), (dp, self.qs[3]), (self.qs[3], dp), (along_x, along_y)
            )
        )

    def row(self, k):
        return (self.dp, (self.fs + k) % 8)

    def other(self, cc):
        return self.c if cc == 0 else 1 - self.c

    def rel_z(self, z):
        low, high = z % 2, z // 2
        near = low + self.bits[2] - 2 * low * self.bits[2]
        far = high + self.bits[3] - 2 * high * self.bits[3]
        return near * 2 + far


def greet(peers):
    barrier = pltpu.get_barrier_semaphore()
    for peer in peers:
        pl.semaphore_signal(barrier, inc=1, device_id=peer, device_id_type=MESH)


def greeted(peers):
    pl.semaphore_wait(pltpu.get_barrier_semaphore(), len(peers))


def link(src, dst, send_sem, recv_sem, target):
    return pltpu.make_async_remote_copy(
        src_ref=src, dst_ref=dst, send_sem=send_sem, recv_sem=recv_sem,
        device_id=target, device_id_type=MESH,
    )


def total_of(*parts):
    value = parts[0].astype(F32)
    for part in parts[1:]:
        value = value + part.astype(F32)
    return value


MESH = pl.DeviceIdType.MESH
SPLIT = (80, 80, 80)


def front_kernel(
    length, row_flag, tokens, sentence, token, share, moment, mix_w, proj_w, expand_w, shrink_w,
    a_out, b_out, c_out, vectors_out, old_out, marks, normed_out, mixed_out, context, kept,
    stage, stage_z, own, own_z, w_a, share_pad, vec_in, old_in, vectors, normed, mixed,
    send, recv, send_z, recv_z, vec_send, vec_recv, old_send, old_recv, local, local_z, *, tile
):
    step = pl.program_id(0)
    spot = Spot()
    c, dp = spot.c, spot.dp
    rows = tokens.shape[0]

    uppers = [pl.ds(0, n) for n in SPLIT]
    lowers = [pl.ds(n, 96 - n) for n in SPLIT]

    def block(g, z, cc, q):
        if g == 0:
            return w_a.at[q, z, cc, uppers[0]]
        if g == 1:
            return b_out.at[q, z, cc, uppers[1]]
        return c_out.at[z, cc, q, uppers[2]]

    def slab(g, z, cc):
        if g == 0:
            return w_a.at[:, z, cc, lowers[0]]
        if g == 1:
            return b_out.at[:, z, cc, lowers[1]]
        return c_out.at[z, cc, :, lowers[2]]

    def remote_z(g, z, cc, kind, target, mine=False):
        dst = slab(g, z, cc)
        return link(
            own_z.at[g - 1, :, pl.ds(0, 96 - SPLIT[g])] if mine and g > 0 else dst, dst,
            send_z.at[g, kind], recv_z.at[g, z * 2 + cc], target,
        )

    def push_z(g, k, kind, target, mine=False):
        remote_z(g, spot.zs[k], c, kind, target, mine).start()

    def arrive_z(g, k):
        remote_z(g, spot.zs[k], c, 0, spot.core).wait_recv()

    def remote(g, z, cc, q, kind, target, mine=False):
        dst = block(g, z, cc, q)
        return pltpu.make_async_remote_copy(
            src_ref=own.at[g - 1, uppers[g]] if mine and g > 0 else dst,
            dst_ref=dst,
            send_sem=send.at[g, kind],
            recv_sem=recv.at[g, (z * 2 + cc) * 4 + q],
            device_id=target,
            device_id_type=MESH,
        )

    def push(g, z, q, kind, target, mine=False):
        remote(g, z, c, q, kind, target, mine).start()

    def arrive(g, z, cc, q):
        remote(g, z, cc, q, 0, spot.core).wait_recv()

    def phase0(g):
        push(g, spot.z, dp, 0, spot.far, True)
        push(g, spot.z, dp, 1, spot.near, True)

    def phase0b(g):
        push(g, spot.z, dp, 7, spot.second, True)
        push(g, spot.z, dp, 3, spot.first, True)
        push(g, spot.z, dp, 15, spot.core, True)

    def phase0z(g):
        push_z(g, 0, 0, spot.far, True)
        push_z(g, 0, 1, spot.near, True)
        push_z(g, 0, 3, spot.core, True)

    def spread(g, k):
        push(g, spot.zs[k], dp, 7 + k, spot.second)
        push(g, spot.zs[k], dp, 3 + k, spot.first)
        push(g, spot.zs[k], dp, 15 + k, spot.core)

    def phase1(g):
        arrive(g, spot.zs[2], c, dp)
        push(g, spot.zs[2], dp, 2, spot.near)
        spread(g, 2)

    def phase1z(g):
        arrive_z(g, 2)
        push_z(g, 2, 2, spot.near)
        push_z(g, 2, 5, spot.core)

    def phase2(g):
        arrive(g, spot.zs[1], c, dp)
        spread(g, 1)
        arrive(g, spot.zs[3], c, dp)
        spread(g, 3)

    def phase2z(g):
        arrive_z(g, 1)
        push_z(g, 1, 4, spot.core)
        arrive_z(g, 3)
        push_z(g, 3, 6, spot.core)

    def phase3(g):
        for k in range(4):
            arrive(g, spot.zs[k], c, spot.qs[1])
            push(g, spot.zs[k], spot.qs[1], 11 + k, spot.second)
            push(g, spot.zs[k], spot.qs[1], 19 + k, spot.core)

    def phase4(g):
        for m in (2, 3):
            for k in range(4):
                arrive(g, spot.zs[k], c, spot.qs[m])
                push(g, spot.zs[k], spot.qs[m], 15 + 4 * m + k, spot.core)

    def phase5(g):
        @pl.loop(0, 4)
        def _(z):
            for q in range(4):
                arrive(g, z, 1 - c, q)
            remote_z(g, z, 1 - c, 0, spot.core).wait_recv()

    def phase6(g):
        @pl.loop(0, 31)
        def _(kind):
            remote(g, spot.z, c, dp, kind, spot.core, True).wait_send()

        @pl.loop(0, 7)
        def _(kind):
            remote_z(g, spot.z, c, kind, spot.core, True).wait_send()

    def vec_copy(k):
        return pltpu.make_async_remote_copy(
            src_ref=vec_in.at[spot.fs],
            dst_ref=vec_in.at[spot.fs],
            send_sem=vec_send.at[k],
            recv_sem=vec_recv.at[spot.fs],
            device_id=spot.row(k),
            device_id_type=MESH,
        )

    def vec_arrive(k):
        other = (spot.fs + k) % 8
        pltpu.make_async_remote_copy(
            src_ref=vec_in.at[other],
            dst_ref=vec_in.at[other],
            send_sem=vec_send.at[k],
            recv_sem=vec_recv.at[other],
            device_id=spot.row(k),
            device_id_type=MESH,
        ).wait_recv()

    def old_copy(k, at):
        place = old_in.at[at]
        return link(place, place, old_send.at[k], old_recv.at[at], spot.row(k))

    def keep_copies():
        return (
            pltpu.make_async_copy(w_a, a_out, local.at[3]),
            pltpu.make_async_copy(own.at[0, uppers[1]], block(1, spot.z, c, dp), local.at[4]),
            pltpu.make_async_copy(own.at[1, uppers[2]], block(2, spot.z, c, dp), local.at[5]),
            pltpu.make_async_copy(own_z.at[0, :, pl.ds(0, 96 - SPLIT[1])], slab(1, spot.z, c), local.at[8]),
            pltpu.make_async_copy(own_z.at[1, :, pl.ds(0, 96 - SPLIT[2])], slab(2, spot.z, c), local.at[9]),
            pltpu.make_async_copy(normed, normed_out, local.at[6]),
            pltpu.make_async_copy(mixed, mixed_out, local.at[7]),
        )

    @pl.when(step == 0)
    def _():
        barrier = pltpu.get_barrier_semaphore()
        peers = [spot.row(k) for k in range(1, 8)] + [spot.first, spot.second]
        for peer in peers:
            pl.semaphore_signal(barrier, inc=1, device_id=peer, device_id_type=MESH)

        columns = pl.ds(pl.multiple_of(dp * 768, 128), 768)

        @pl.when(dp < 3)
        def _():
            pltpu.make_async_copy(mix_w.at[:, columns], stage.at[0], local.at[0]).start()

        @pl.when(dp == 3)
        def _():
            pltpu.make_async_copy(proj_w, stage.at[0], local.at[0]).start()

        second = pltpu.make_async_copy(expand_w.at[:, columns], stage.at[1], local.at[1])
        second.start()
        third = pltpu.make_async_copy(
            shrink_w.at[pl.ds(pl.multiple_of(dp * 96, 32), 96), :], stage.at[2], local.at[2]
        )
        third.start()

        def slab_copy(g, q):
            if g == 0:
                src = proj_w.at[lowers[0], :] if q == 3 else mix_w.at[lowers[0], pl.ds(q * 768, 768)]
            elif g == 1:
                src = expand_w.at[lowers[1], pl.ds(q * 768, 768)]
            else:
                src = shrink_w.at[pl.ds(q * 96 + SPLIT[2], 96 - SPLIT[2]), :]
            return pltpu.make_async_copy(
                src, stage_z.at[g, q, pl.ds(0, 96 - SPLIT[g])], local_z.at[g, q]
            )

        for g in range(3):
            for q in range(4):
                slab_copy(g, q).start()
        share_pad[...] = jnp.zeros((16, 128), F32)
        share_pad[0:6, 0:96] = share[...]
        share_pad[8:14, 0:96] = moment[...]
        old_in[spot.fs] = share_pad[...]
        vec_in[spot.fs] = share_pad[...].astype(BF)
        position = lax.broadcasted_iota(jnp.int32, (1, rows), 1)
        flag = (row_flag[0] == 1).astype(F32)
        line = lax.broadcasted_iota(jnp.int32, (16, rows), 0)
        of_sentence = jnp.where(position < length[0], sentence[...].astype(F32), 0.0) * (1.0 - flag)
        of_token = jnp.where(position < length[0], token[...].astype(F32), 0.0) * flag
        marked = jnp.where(line == 4, of_sentence, jnp.where(line == 5, of_token, 0.0))
        marks[...] = marked.astype(BF)
        pltpu.make_async_copy(proj_w, stage.at[0], local.at[0]).wait()
        w_a[dp, spot.z, c, 0 : SPLIT[0]] = stage[0, 0 : SPLIT[0]].astype(BF)
        pl.semaphore_wait(barrier, len(peers))
        phase0(0)
        phase0b(0)
        for k in range(1, 8):
            vec_copy(k).start()
            old_copy(k, spot.fs).start()
        for q in range(4):
            slab_copy(0, q).wait()
            w_a[q, spot.z, c, SPLIT[0] : 96] = stage_z[0, q, 0 : 96 - SPLIT[0]].astype(BF)
        phase0z(0)
        second.wait()
        own[0] = stage[1].astype(BF)
        third.wait()
        own[1] = stage[2].astype(BF)
        for g in (1, 2):
            for q in range(4):
                slab_copy(g, q).wait()
                own_z[g - 1, q] = stage_z[g, q].astype(BF)
        copies = keep_copies()
        for copy in copies[1:5]:
            copy.start()
        for k in range(1, 8):
            vec_arrive(k)
        total = jnp.zeros((16, 768), F32)
        for f in range(8):
            row = lax.broadcasted_iota(jnp.int32, (128, 768), 0)
            lane = lax.broadcasted_iota(jnp.int32, (128, 768), 1)
            pick = jnp.where((lane - 96 * f == row) & (row < 96), 1.0, 0.0).astype(BF)
            total += nn(vec_in[f], pick)
        vectors[...] = total
        vectors_out[...] = total

        def norm(t):
            part = pl.ds(t * 256, 256)
            start = tokens[part, :].astype(F32) + tn(marks[:, part], total.astype(BF))
            normal, _ = normalise(start)
            normed[part, :] = (normal * total[0:1, :] + total[1:2, :]).astype(BF)

        norm(0)
        norm(1)
        phase1(0)
        norm(2)
        phase2(0)
        norm(3)
        phase1z(0)
        phase0(1)
        phase0(2)
        phase3(0)
        phase0b(1)
        phase1(1)
        phase2z(0)

        @pl.loop(0, 4)
        def _(z):
            remote_z(0, z, 1 - c, 0, spot.core).wait_recv()

        @pl.loop(0, 4)
        def _(k):
            q = jnp.where(
                k < 2, jnp.where(k == 0, spot.qs[0], spot.qs[1]), jnp.where(k == 2, spot.qs[2], spot.qs[3])
            )

            @pl.loop(0, 4)
            def _(z):
                arrive(0, z, 1 - c, q)

            @pl.when(q < 3)
            def _():
                weight = rows_of(w_a.at[q])

                @pl.loop(0, 4, unroll=2)
                def _(t):
                    part = pl.ds(pl.multiple_of(t * 256, 256), 256)
                    result = nn(normed[part, :], weight).astype(BF)
                    for n in range(6):
                        mixed[q * 6 + n, part, :] = result[:, n * 128 : (n + 1) * 128]

            @pl.when(k == 0)
            def _():
                phase4(0)
                phase0b(2)

            @pl.when(k == 1)
            def _():
                phase1(2)
                phase0z(1)
                phase0z(2)

            @pl.when(k == 2)
            def _():
                phase2(1)

            @pl.when(k == 3)
            def _():
                phase2(2)

        copies[0].start()
        copies[5].start()
        copies[6].start()

    @pl.when(step > 0)
    def _():
        p = step - 1
        attend_pair(length[0], mixed.at[p], mixed.at[6 + p], mixed.at[12 + p], context, kept, tile)

    for at, phase, g in (
        (1, phase3, 1), (2, phase3, 2), (2, phase1z, 1), (3, phase1z, 2), (3, phase2z, 1),
        (4, phase4, 1), (4, phase2z, 2), (5, phase4, 2),
    ):

        @pl.when(step == at)
        def _():
            phase(g)

    @pl.when(step == 6)
    def _():
        phase5(1)
        phase5(2)
        for g in range(3):
            phase6(g)
        for k in range(1, 8):
            old_copy(k, spot.fs).wait_send()
            old_copy(k, (spot.fs + k) % 8).wait_recv()
        old_out[...] = old_in[...]
        for k in range(1, 8):
            vec_copy(k).wait_send()
        for copy in keep_copies():
            copy.wait()


def run_front(length, row_flag, tokens, sentence, token, share, moment, mix_w, proj_w, expand_w, shrink_w, tile=256):
    rows, width = tokens.shape
    anywhere = pl.BlockSpec(memory_space=pl.ANY)
    once = pl.Buffered(1)

    def whole(*shape):
        return pl.BlockSpec(shape, lambda i: (0,) * len(shape), pipeline_mode=once)

    return pl.pallas_call(
        functools.partial(front_kernel, tile=tile),
        grid=(7,),
        in_specs=[
            SCALARS,
            SCALARS,
            whole(rows, width),
            whole(1, rows),
            whole(1, rows),
            whole(*share.shape),
            whole(*moment.shape),
            anywhere,
            anywhere,
            anywhere,
            anywhere,
        ],
        out_specs=[
            anywhere,
            anywhere,
            anywhere,
            whole(16, width),
            whole(8, 16, 128),
            whole(16, rows),
            anywhere,
            anywhere,
            pl.BlockSpec((rows, 128), lambda i: (0, jnp.maximum(i - 1, 0))),
            pl.BlockSpec((2, rows, 128), lambda i: (jnp.maximum(i - 1, 0), 0, 0)),
        ],
        out_shape=[
            jax.ShapeDtypeStruct((4, 4, 2, 96, 768), BF),
            jax.ShapeDtypeStruct((4, 4, 2, 96, 768), BF),
            jax.ShapeDtypeStruct((4, 2, 4, 96, 768), BF),
            jax.ShapeDtypeStruct((16, width), F32),
            jax.ShapeDtypeStruct((8, 16, 128), F32),
            jax.ShapeDtypeStruct((16, rows), BF),
            jax.ShapeDtypeStruct((rows, width), BF),
            jax.ShapeDtypeStruct((18, rows, 128), BF),
            jax.ShapeDtypeStruct((rows, width), BF),
            jax.ShapeDtypeStruct((12, rows, 128), BF),
        ],
        scratch_shapes=[
            pltpu.VMEM((3, 96, 768), F32),
            pltpu.VMEM((3, 4, 32, 768), F32),
            pltpu.VMEM((2, 96, 768), BF),
            pltpu.VMEM((2, 4, 32, 768), BF),
            pltpu.VMEM((4, 4, 2, 96, 768), BF),
            pltpu.VMEM((16, 128), F32),
            pltpu.VMEM((8, 16, 128), BF),
            pltpu.VMEM((8, 16, 128), F32),
            pltpu.VMEM((16, width), F32),
            pltpu.VMEM((rows, width), BF),
            pltpu.VMEM((18, rows, 128), BF),
            pltpu.SemaphoreType.DMA((3, 31)),
            pltpu.SemaphoreType.DMA((3, 32)),
            pltpu.SemaphoreType.DMA((3, 7)),
            pltpu.SemaphoreType.DMA((3, 8)),
            *[pltpu.SemaphoreType.DMA((8,))] * 4,
            pltpu.SemaphoreType.DMA((10,)),
            pltpu.SemaphoreType.DMA((3, 4)),
        ],
        compiler_params=params(collective_id=0, has_side_effects=True),
        name="front",
    )(length, row_flag, tokens, sentence, token, share, moment, mix_w, proj_w, expand_w, shrink_w)


def attend_back_pair(length, kept, key, value, ctx_grad, dq, dk, dv, tile):
    rows = key.shape[0]
    lane = lane_iota(tile)
    lane_all = lane_iota(rows)
    count = rows // tile
    plain, plain_values = key[...], value[...]
    keys = [
        jnp.where(lane_all < 64, plain, key_extra(rows, length, 64)),
        jnp.where(lane_all >= 64, plain, key_extra(rows, length, 0)),
    ]
    zero = jnp.zeros_like(plain_values)
    values = [
        jnp.where(lane_all < 64, plain_values, zero),
        jnp.where(lane_all >= 64, plain_values, zero),
    ]

    def first(head, t):
        q = kept[head, pl.ds(t * tile, tile), :]
        grad = ctx_grad[pl.ds(t * tile, tile), :]
        return q, grad, nt(keys[head], q), nt(values[head], grad)

    sums = {}

    def second(head, t, q, grad, score, prob_back):
        probs = jnp.exp(score)
        product = probs * prob_back
        delta = jnp.sum(product, axis=0, keepdims=True)
        score_back = (product - probs * delta).astype(BF)
        dv_part = nn(probs.astype(BF), grad)
        dk_part = nn(score_back, q)
        sums[head, "v"] = dv_part if t == 0 else sums[head, "v"] + dv_part
        sums[head, "k"] = dk_part if t == 0 else sums[head, "k"] + dk_part
        sums[head, t] = tn(score_back, plain)

    order = [(head, t) for head in range(2) for t in range(count)]
    ahead = first(*order[0])
    for n, spot in enumerate(order):
        now = ahead
        if n + 1 < len(order):
            ahead = first(*order[n + 1])
        second(*spot, *now)
    dk[...] = jnp.where(lane_all < 64, sums[0, "k"], sums[1, "k"]).astype(BF)
    dv[...] = jnp.where(lane_all < 64, sums[0, "v"], sums[1, "v"]).astype(BF)
    for t in range(count):
        both = jnp.where(lane < 64, sums[0, t], sums[1, t]) * 0.125
        dq[pl.ds(t * tile, tile), :] = both.astype(BF)


def attend_back_head(length, head, kept, key, value, ctx_grad, dq, dk, dv, tile):
    rows = key.shape[0]
    lane = lane_iota(tile) - 64 * head
    lane_all = lane_iota(rows) - 64 * head
    mine = (lane >= 0) & (lane < 64)
    mine_all = (lane_all >= 0) & (lane_all < 64)
    count = rows // tile
    plain = key[...]
    keys = jnp.where(mine_all, plain, key_extra(rows, length, 64 - 64 * head))
    values = jnp.where(mine_all, value[...], jnp.zeros_like(plain))

    def first(t):
        q = kept[pl.ds(t * tile, tile), :]
        grad = ctx_grad[pl.ds(t * tile, tile), :]
        return q, grad, nt(keys, q), nt(values, grad)

    dv_sum = dk_sum = None
    ahead = first(0)
    for t in range(count):
        q, grad, score, prob_back = ahead
        if t + 1 < count:
            ahead = first(t + 1)
        probs = jnp.exp(score)
        product = probs * prob_back
        delta = jnp.sum(product, axis=0, keepdims=True)
        score_back = (product - probs * delta).astype(BF)
        dv_part = nn(probs.astype(BF), grad)
        dk_part = nn(score_back, q)
        dv_sum = dv_part if t == 0 else dv_sum + dv_part
        dk_sum = dk_part if t == 0 else dk_sum + dk_part
        part = pl.ds(t * tile, tile)
        dq[part, :] = jnp.where(mine, (tn(score_back, plain) * 0.125).astype(BF), dq[part, :])
    dk[...] = jnp.where(mine_all, dk_sum.astype(BF), dk[...])
    dv[...] = jnp.where(mine_all, dv_sum.astype(BF), dv[...])


def attend_back_kernel(length, kept, key, value, ctx_grad, dq, dk, dv, *, tile):
    attend_back_pair(length[0], kept, key.at[0], value.at[0], ctx_grad, dq, dk, dv, tile)


def run_attend_back(length, kept, mixed, ctx_grad, tile=128):
    groups, rows, _ = mixed.shape
    pairs = groups // 3
    width = pairs * 128
    spec = pl.BlockSpec((rows, 128), lambda p: (0, p))
    return pl.pallas_call(
        functools.partial(attend_back_kernel, tile=tile),
        grid=(pairs,),
        in_specs=[
            pl.BlockSpec(memory_space=pltpu.SMEM),
            pl.BlockSpec((2, rows, 128), lambda p: (p, 0, 0)),
            pl.BlockSpec((1, rows, 128), lambda p: (pairs + p, 0, 0)),
            pl.BlockSpec((1, rows, 128), lambda p: (2 * pairs + p, 0, 0)),
            spec,
        ],
        out_specs=[spec, spec, spec],
        out_shape=[jax.ShapeDtypeStruct((rows, width), BF)] * 3,
        compiler_params=params(),
        name="attend_back",
    )(length, kept, mixed, mixed, ctx_grad)


def gelu_pair(v):
    cdf = 0.5 * (1.0 + lax.erf(v * 0.7071067811865476))
    return v * cdf, cdf + v * jnp.exp(-0.5 * v * v) * 0.3989422804014327


def feed_start(
    length, context, tokens, marks, vectors, proj, cotangent, middle, normed, bound, out_sum, back_sum, tile
):
    @pl.loop(0, tokens.shape[0] // tile)
    def _(t):
        part = pl.ds(pl.multiple_of(t * tile, tile), tile)
        start = tokens[part, :].astype(F32) + tn(marks[:, part], vectors[...].astype(BF))
        mid = start + nn(context[part, :], proj)
        middle[part, :] = mid
        out_sum[part, :] = jnp.zeros_like(mid)
        back_sum[part, :] = jnp.zeros_like(mid)
        normal, _ = normalise(mid)
        normed[part, :] = (normal * vectors[2:3, :] + vectors[3:4, :]).astype(BF)
        row = t * tile + lax.broadcasted_iota(jnp.int32, (tile, 1), 0)
        kept = jnp.where(row < length, cotangent[part, :].astype(F32), 0.0)
        bound[part, :] = kept.astype(BF)


def feed_chunk(expand, shrink, normed, bound, active, inner_back, out_sum, back_sum, tile):
    @pl.loop(0, normed.shape[0] // tile, unroll=2)
    def _(t):
        part = pl.ds(pl.multiple_of(t * tile, tile), tile)
        inner = nn(normed[part, :], expand)
        act_back = nt(bound[part, :], shrink)
        act, slope = gelu_pair(inner)
        act = act.astype(BF)
        active[part, :] = act
        back = (act_back * slope).astype(BF)
        inner_back[part, :] = back
        out_sum[part, :] += nn(act, shrink)
        back_sum[part, :] += nt(back, expand)


def feed_finish(
    vectors, proj, middle, normed, bound, out_sum, back_sum, output, middle_back, ctx_back, gain_grads, tile
):
    gain_grads[...] = jnp.zeros_like(gain_grads)

    @pl.loop(0, middle.shape[0] // tile)
    def _(t):
        part = pl.ds(pl.multiple_of(t * tile, tile), tile)
        mid = middle[part, :]
        output[part, :] = (mid + out_sum[part, :]).astype(BF)
        normal, inverse = normalise(mid)
        grad = back_sum[part, :]
        gain_grads[0:1, :] += jnp.sum(grad * normal, axis=0, keepdims=True)
        gain_grads[1:2, :] += jnp.sum(grad, axis=0, keepdims=True)
        back = bound[part, :].astype(F32) + norm_back(grad, normal, inverse, vectors[2:3, :])
        middle_back[part, :] = back
        low = back.astype(BF)
        normed[part, :] = low
        ctx_back[part, :] = nt(low, proj).astype(BF)


def feed_kernel(
    length, context, tokens, marks, vectors, proj, expand, shrink, cotangent,
    output, middle_back, ctx_back, gain_grads, proj_grad, expand_grad, shrink_grad,
    middle, normed, bound, out_sum, active, inner_back, *, tile
):
    j = pl.program_id(0)

    @pl.when(j == 0)
    def _():
        feed_start(
            length[0], context, tokens, marks, vectors, proj[...], cotangent, middle, normed, bound,
            out_sum, middle_back, tile,
        )

    feed_chunk(
        expand[...], shrink[...], normed, bound, active, inner_back, out_sum, middle_back, tile
    )
    expand_grad[...] = tn(normed[...], inner_back[...])
    shrink_grad[...] = tn(active[...], bound[...])

    @pl.when(j == pl.num_programs(0) - 1)
    def _():
        feed_finish(
            vectors, proj[...], middle, normed, bound, out_sum, middle_back,
            output, middle_back, ctx_back, gain_grads, tile,
        )
        proj_grad[...] = tn(context[...], normed[...])


def run_feed(length, context, tokens, marks, vectors, proj, expand, shrink, cotangent, tile=256):
    rows, width = tokens.shape
    inner = expand.shape[1]
    chunk = width
    wide = pl.BlockSpec((width, chunk), lambda j: (0, j))
    tall = pl.BlockSpec((chunk, width), lambda j: (j, 0))
    return pl.pallas_call(
        functools.partial(feed_kernel, tile=tile),
        grid=(inner // chunk,),
        in_specs=[
            SCALARS, fixed(rows, width), fixed(rows, width), fixed(16, rows), fixed(16, width),
            fixed(width, width), wide, tall, fixed(rows, width),
        ],
        out_specs=[
            fixed(rows, width), fixed(rows, width), fixed(rows, width), fixed(8, width),
            fixed(width, width), wide, tall,
        ],
        out_shape=shapes(
            ((rows, width), BF), ((rows, width), F32), ((rows, width), BF), ((8, width), F32),
            ((width, width), F32), ((width, inner), F32), ((inner, width), F32),
        ),
        scratch_shapes=[
            pltpu.VMEM((rows, width), F32),
            pltpu.VMEM((rows, width), BF),
            pltpu.VMEM((rows, width), BF),
            pltpu.VMEM((rows, width), F32),
            pltpu.VMEM((rows, chunk), BF),
            pltpu.VMEM((rows, chunk), BF),
        ],
        compiler_params=params(),
        name="feed",
    )(length, context, tokens, marks, vectors, proj, expand, shrink, cotangent)


def feed_send_kernel(
    length, context, tokens, marks, vectors, proj, expand, shrink, cotangent,
    output_out, middle_out, ctx_out, gain_grads, proj_box, near_e, near_s, rest_s, got_e, got_s,
    output, middle_back, ctx_back, middle, normed, bound, out_sum, active, inner_back,
    results, box_e, box_s, pair_e, pair_s, out_e, out_s,
    pair_sem, pair_got, first_e_sem, first_e_got, first_s_sem, first_s_got, *, tile
):
    j = pl.program_id(0)
    spot = Spot()
    c = spot.c

    peers = [spot.core, spot.first]
    leaving = [
        pltpu.make_async_copy(src, dst, results.at[k])
        for k, (src, dst) in enumerate(
            ((output, output_out), (middle_back, middle_out), (ctx_back, ctx_out))
        )
    ]

    def pair_copy(step, g):
        slot = step % 2
        src, dst = (box_e, pair_e) if g == 0 else (box_s, pair_s)
        return link(
            src.at[1, slot], dst.at[step], pair_sem.at[g, slot], pair_got.at[g, step], spot.core
        )

    def first_e(p2):
        return link(
            out_e.at[p2], got_e.at[p2], first_e_sem.at[p2], first_e_got.at[p2], spot.first
        )

    def first_s(p2, r):
        return link(
            out_s.at[p2, r], got_s.at[p2, r], first_s_sem.at[p2, r], first_s_got.at[p2, r], spot.first
        )

    def keep_e(step, p2):
        @pl.loop(0, 4)
        def _(r):
            near_e[p2, r] = total_of(box_e[0, step % 2, r], pair_e[step, r]).astype(BF)

    def push_e(step, p2):
        @pl.loop(0, 4)
        def _(r):
            out_e[p2, r] = total_of(box_e[0, step % 2, r], pair_e[step, r]).astype(BF)

        first_e(p2).start()

    def to_first(step):
        slot = step % 2
        pair_copy(step, 0).wait_recv()
        if step == 0:
            push_e(0, 1)
        elif step == 3:
            keep_e(3, 0)
        else:

            @pl.when(c == step - 1)
            def _():
                push_e(step, 0)

            @pl.when(c != step - 1)
            def _():
                keep_e(step, 1)

        pair_copy(step, 1).wait_recv()
        r = spot.rel_z(spot.order[step])
        for p2, q in enumerate((spot.qs[1], spot.qs[3])):
            value = total_of(box_s[0, slot, q], pair_s[step, q]).astype(BF)
            if step < 3:
                out_s[p2, r] = value
                first_s(p2, r).start()
            else:
                rest_s[p2] = value
        for p2, q in enumerate((spot.qs[0], spot.qs[2])):
            near_s[p2, r] = total_of(box_s[0, slot, q], pair_s[step, q]).astype(BF)

    @pl.when(j == 0)
    def _():
        greet(peers)
        feed_start(
            length[0], context, tokens, marks, vectors, rows_of(proj), cotangent,
            middle, normed, bound, out_sum, middle_back, tile,
        )

    feed_chunk(
        rows_of(expand), rows_of(shrink), normed, bound, active, inner_back,
        out_sum, middle_back, tile,
    )

    @pl.when(j == 0)
    def _():
        greeted(peers)

    for step in range(3):

        @pl.when(j == step + 1)
        def _():
            to_first(step)

    slot = j % 2

    @pl.when(j >= 2)
    def _():
        pair_copy(j - 2, 0).wait_send()
        pair_copy(j - 2, 1).wait_send()

    grad_e = tn(normed[...], inner_back[...])
    for z in range(4):
        r = spot.rel_z(z)
        for cc in range(2):
            piece = grad_e[(2 * z + cc) * 96 : (2 * z + cc + 1) * 96, :]
            box_e[spot.other(cc), slot, r] = piece.astype(BF)
    pair_copy(j, 0).start()
    grad_s = tn(active[...], bound[...])
    for cc in range(2):
        for q in range(4):
            piece = grad_s[(cc * 4 + q) * 96 : (cc * 4 + q + 1) * 96, :]
            box_s[spot.other(cc), slot, q] = piece.astype(BF)
    pair_copy(j, 1).start()

    @pl.when(j == 3)
    def _():
        feed_finish(
            vectors, rows_of(proj), middle, normed, bound, out_sum, middle_back,
            output, middle_back, ctx_back, gain_grads, tile,
        )
        for copy in leaving:
            copy.start()
        grad_p = tn(context[...], normed[...])
        for z in range(4):
            r = spot.rel_z(z)
            for cc in range(2):
                piece = grad_p[(2 * z + cc) * 96 : (2 * z + cc + 1) * 96, :]
                proj_box[spot.other(cc), r] = piece.astype(BF)
        to_first(3)
        for copy in leaving:
            copy.wait()
        for step in (2, 3):
            for g in range(2):
                pair_copy(step, g).wait_send()
        first_e(0).wait_send()
        first_e(1).wait_send()
        first_e(0).wait_recv()
        first_e(1).wait_recv()
        for step in range(3):
            r = spot.rel_z(spot.order[step])
            for p2 in range(2):
                first_s(p2, r).wait_send()
        for p2 in range(2):
            for z in spot.first_order[:3]:
                first_s(p2, spot.rel_z(z)).wait_recv()


def run_feed_send(length, context, tokens, marks, vectors, a_full, b_full, c_full, cotangent, tile=256):
    rows, width = tokens.shape
    block = (96, 768)

    def chunk_at(j):
        dp = lax.axis_index("dp")
        x, y = dp % 2, dp // 2
        turn_x = jnp.where(j < 2, 1, 0)
        turn_y = jnp.where(j % 2 == 0, 1, 0) * jnp.where(j < 3, 1, 0)
        return (y + turn_y - 2 * y * turn_y) * 2 + x + turn_x - 2 * x * turn_x

    return pl.pallas_call(
        functools.partial(feed_send_kernel, tile=tile),
        grid=(4,),
        in_specs=[
            SCALARS, fixed(rows, width), fixed(rows, width), fixed(16, rows), fixed(16, width),
            pl.BlockSpec((1, 4, 2) + block, lambda j: (3, 0, 0, 0, 0), pipeline_mode=pl.Buffered(1)),
            pl.BlockSpec((1, 4, 2) + block, lambda j: (chunk_at(j), 0, 0, 0, 0)),
            pl.BlockSpec((1, 2, 4) + block, lambda j: (chunk_at(j), 0, 0, 0, 0)),
            fixed(rows, width),
        ],
        out_specs=[
            ANYWHERE, ANYWHERE, ANYWHERE, fixed(8, width),
            fixed(2, 4, *block), fixed(2, 4, *block), fixed(2, 4, *block),
            fixed(2, *block), ANYWHERE, ANYWHERE,
        ],
        out_shape=shapes(
            ((rows, width), BF), ((rows, width), F32), ((rows, width), BF), ((8, width), F32),
            *[((2, 4) + block, BF)] * 3,
            ((2,) + block, BF), *[((2, 4) + block, BF)] * 2,
        ),
        scratch_shapes=[
            pltpu.VMEM((rows, width), BF),
            pltpu.VMEM((rows, width), F32),
            pltpu.VMEM((rows, width), BF),
            pltpu.VMEM((rows, width), F32),
            pltpu.VMEM((rows, width), BF),
            pltpu.VMEM((rows, width), BF),
            pltpu.VMEM((rows, width), F32),
            pltpu.VMEM((rows, width), BF),
            pltpu.VMEM((rows, width), BF),
            pltpu.SemaphoreType.DMA((3,)),
            *[pltpu.VMEM((2, 2, 4) + block, BF)] * 2,
            *[pltpu.VMEM((4, 4) + block, BF)] * 2,
            *[pltpu.VMEM((2, 4) + block, BF)] * 2,
            pltpu.SemaphoreType.DMA((2, 2)),
            pltpu.SemaphoreType.DMA((2, 4)),
            pltpu.SemaphoreType.DMA((2,)),
            pltpu.SemaphoreType.DMA((2,)),
            pltpu.SemaphoreType.DMA((2, 4)),
            pltpu.SemaphoreType.DMA((2, 4)),
        ],
        compiler_params=params(collective_id=1, has_side_effects=True),
        name="feed",
    )(length, context, tokens, marks, vectors, a_full, b_full, c_full, cotangent)


def mix_grad_kernel(normed, dq, dk, dv, grad_out):
    j = pl.program_id(0)
    for index, source in enumerate((dq, dk, dv)):

        @pl.when(j == index)
        def _():
            grad_out[...] = tn(normed[...], source[...])


def run_mix_grad(normed, dq, dk, dv):
    rows, width = normed.shape
    return pl.pallas_call(
        mix_grad_kernel,
        grid=(3,),
        in_specs=[fixed(rows, width)] * 4,
        out_specs=pl.BlockSpec((width, width), lambda j: (0, j)),
        out_shape=jax.ShapeDtypeStruct((width, 3 * width), F32),
        compiler_params=params(),
        name="mix_grad",
    )(normed, dq, dk, dv)


def input_part(tokens, marks, vectors, weights, sources, middle_back):
    start = tokens.astype(F32) + tn(marks, vectors.astype(BF))
    normal, inverse = normalise(start)
    grad = nt(sources[0], weights[0])
    for source, weight in zip(sources[1:], weights[1:]):
        grad += nt(source, weight)
    gain = jnp.sum(grad * normal, axis=0, keepdims=True)
    shift = jnp.sum(grad, axis=0, keepdims=True)
    result = middle_back + norm_back(grad, normal, inverse, vectors[0:1, :])
    spread = tn(marks, jnp.ones(vectors.shape, BF))
    mark = jnp.sum(spread * result, axis=0, keepdims=True)
    return result, gain, shift, mark


def input_kernel(tokens, marks, vectors, weight, dq, dk, dv, middle_back, input_grad, sums):
    i = pl.program_id(0)
    width = tokens.shape[1]
    weights = [weight[:, k * width : (k + 1) * width] for k in range(3)]
    result, gain, shift, mark = input_part(
        tokens[...], marks[...], vectors[...], weights, (dq[...], dk[...], dv[...]), middle_back[...]
    )
    input_grad[...] = result
    both = jnp.concatenate([gain, shift, mark, jnp.zeros((5, width), F32)], axis=0)

    @pl.when(i == 0)
    def _():
        sums[...] = both

    @pl.when(i > 0)
    def _():
        sums[...] += both


def run_input(tokens, marks, vectors, weight, dq, dk, dv, middle_back, tile=256):
    rows, width = tokens.shape
    spec = pl.BlockSpec((tile, width), lambda i: (i, 0))
    return pl.pallas_call(
        input_kernel,
        grid=(rows // tile,),
        in_specs=[
            spec,
            pl.BlockSpec((16, tile), lambda i: (0, i)),
            fixed(16, width),
            fixed(width, 3 * width),
            spec,
            spec,
            spec,
            spec,
        ],
        out_specs=[spec, fixed(8, width)],
        out_shape=shapes(((rows, width), F32), ((8, width), F32)),
        compiler_params=params(),
        name="input_grad",
    )(tokens, marks, vectors, weight, dq, dk, dv, middle_back)


BETA = 1.0 - STEP ** (-0.8)


def back_kernel(
    length, row_flag, kept, key, value, ctx_grad, rest_s, marks, vectors, gain2, mix_rows, proj_rows, expand_rows, shrink_rows,
    near_e_in, near_s_in, normed_in, proj_box_in, got_e_in, got_s_in, tokens_in, mix_in, back_in, w_mix_in, w_proj_in, w_expand_in, w_shrink_in,
    input_grad, grads, rows_new, sums_a, sums_b, vector_sum,
    tokens, mix, back, w_mix, w_proj, w_expand, w_shrink, near_e, near_s, normed, proj_box, grads_qkv,
    got, out2b, in2b, out3b, in3b, out4b, in4b, holdb,
    box, pair, out1, in1, out2, in2, out3, in3, out4, in4, hold,
    full_a, full_b, vec_q, vec_f, slots_a, slots_b, gains, columns_old,
    loads, got_sem, late_sent, late_got, sentb, gotb,
    pair_sent, pair_got, sent1, got1, sent, landed, full_sent, full_got,
    vecq_sent, vecq_got, vecf_sent, vecf_got, slot_sent, slot_got, *, tile
):
    step = pl.program_id(0)
    spot = Spot()
    c, dp, fs = spot.c, spot.dp, spot.fs
    trio = (spot.first, spot.second, spot.diag)
    local = [
        pltpu.make_async_copy(src, dst, loads.at[k])
        for k, (src, dst) in enumerate(
            (
                (tokens_in, tokens), (mix_in.at[pl.ds(0, 3)], mix), (back_in, back),
                (w_mix_in, w_mix), (w_proj_in, w_proj), (w_expand_in, w_expand), (w_shrink_in, w_shrink),
            )
        )
    ]

    early = [
        pltpu.make_async_copy(src, dst, loads.at[8 + k])
        for k, (src, dst) in enumerate(
            ((near_e_in, near_e), (near_s_in, near_s), (normed_in, normed), (proj_box_in, proj_box))
        )
    ]

    near = (near_e, near_s)
    load_e = pltpu.make_async_copy(got_e_in, got.at[0], got_sem.at[0])

    def late_s(p2):
        r = spot.rel_z(dp)
        return link(
            rest_s.at[p2], got.at[1, p2, r], late_sent.at[p2], late_got.at[p2], spot.first
        )

    def late_s_came(p2):
        r = spot.rel_z(spot.first_order[3])
        link(
            rest_s.at[p2], got.at[1, p2, r], late_sent.at[p2], late_got.at[p2], spot.first
        ).wait_recv()

    def load_s(k):
        r = spot.rel_z(spot.first_order[k])
        return pltpu.make_async_copy(got_s_in.at[:, r], got.at[1, :, r], got_sem.at[2 + k])

    peers = [spot.core, spot.near, spot.far, (dp, spot.zs[3] * 2 + c), spot.first, spot.second, spot.diag]

    def begin():
        load_e.start()
        early[0].start()
        for k in range(3):
            load_s(k).start()
        greet(peers)
        for copy in early[1:]:
            copy.start()
        for copy in local:
            copy.start()

    def begin_copies():
        greeted(peers)
        for p2 in range(2):
            late_s(p2).start()
        load_e.wait()
        early[0].wait()
        stage2b(0)

    def late():
        for k in range(3):
            load_s(k).wait()
        for p2 in range(2):
            late_s_came(p2)

    def copyb(stage, g):
        src, dst, target = (
            (out2b, in2b, spot.second), (out3b, in3b, spot.near), (out4b, in4b, spot.far),
        )[stage]
        return link(src.at[g], dst.at[g], sentb.at[stage, g], gotb.at[stage, g], target)

    def stage2b(g):
        @pl.loop(0, 4)
        def _(r):
            out2b[g, r] = total_of(near[g][1, r], got[g, 1, r]).astype(BF)

        copyb(0, g).start()

    def stage3b(g):
        copyb(0, g).wait_recv()

        @pl.loop(0, 2)
        def _(r):
            out3b[g, r] = total_of(near[g][0, 2 + r], got[g, 0, 2 + r], in2b[g, 2 + r]).astype(BF)

        copyb(1, g).start()

        @pl.loop(0, 2)
        def _(r):
            holdb[g, r] = total_of(near[g][0, r], got[g, 0, r], in2b[g, r])


    def stage4b(g):
        copyb(1, g).wait_recv()
        out4b[g] = total_of(holdb[g, 1], in3b[g, 1]).astype(BF)
        copyb(2, g).start()
        holdb[g, 0] = total_of(holdb[g, 0], in3b[g, 0])

    def stage5b(g):
        copyb(2, g).wait_recv()
        full_b[g, dp] = total_of(holdb[g, 0], in4b[g]).astype(BF)
        for k in range(3):
            share_b(g, k).start()

    def share_b(g, k):
        place = full_b.at[g, dp]
        return link(place, place, full_sent.at[g, k], full_got.at[g, dp], trio[k])

    def share_a(h, k):
        place = full_a.at[dp, h]
        return link(place, place, full_sent.at[2 + h, k], full_got.at[2 + h, dp], trio[k])

    def shared_b(g):
        for q in spot.qs[1:]:
            place = full_b.at[g, q]
            link(place, place, full_sent.at[g, 0], full_got.at[g, q], spot.first).wait_recv()

    def shared_a(h):
        for q in spot.qs[1:]:
            place = full_a.at[q, h]
            link(place, place, full_sent.at[2 + h, 0], full_got.at[2 + h, q], spot.first).wait_recv()

    def pair_copy(h, q):
        return link(
            box.at[1, h, q], pair.at[h, q], pair_sent.at[h, q], pair_got.at[h, q], spot.core
        )

    def first_copy(h, p2):
        return link(
            out1.at[h, p2], in1.at[h, p2], sent1.at[h, p2], got1.at[h, p2], spot.first
        )

    def copy(stage, h):
        src, dst, target = (
            (out2, in2, spot.second), (out3, in3, spot.near), (out4, in4, spot.far),
        )[stage]
        return link(src.at[h], dst.at[h], sent.at[stage, h], landed.at[stage, h], target)

    def third_grad(h):
        @pl.loop(0, 4)
        def _(r):
            for side in range(2):
                for k in range(3):

                    @pl.when(h == k)
                    def _():
                        box[side, h, 3, r] = proj_box[side, r, :, k * 256 : (k + 1) * 256]

        pair_copy(h, 3).start()

        columns = pl.ds(pl.multiple_of(h * 256, 256), 256)
        sources = jnp.concatenate([grads_qkv[q, :, columns] for q in range(3)], axis=1)
        grad = tn(normed[...], sources)
        for q in range(3):
            for z in range(4):
                r = spot.rel_z(z)
                for cc in range(2):
                    piece = grad[(2 * z + cc) * 96 : (2 * z + cc + 1) * 96, q * 256 : (q + 1) * 256]
                    box[spot.other(cc), h, q, r] = piece.astype(BF)
            pair_copy(h, q).start()

    def stage1(h):
        for p2, q in enumerate((spot.qs[1], spot.qs[3])):
            pair_copy(h, q).wait_recv()

            @pl.loop(0, 4)
            def _(r):
                out1[h, p2, r] = total_of(box[0, h, q, r], pair[h, q, r]).astype(BF)

            first_copy(h, p2).start()

    def stage2(h):
        q = spot.qs[2]
        pair_copy(h, q).wait_recv()
        first_copy(h, 1).wait_recv()

        @pl.loop(0, 4)
        def _(r):
            out2[h, r] = total_of(box[0, h, q, r], pair[h, q, r], in1[h, 1, r]).astype(BF)

        copy(0, h).start()

    def stage3(h):
        pair_copy(h, dp).wait_recv()
        first_copy(h, 0).wait_recv()
        copy(0, h).wait_recv()

        @pl.loop(0, 2)
        def _(r):
            value = total_of(box[0, h, dp, 2 + r], pair[h, dp, 2 + r], in1[h, 0, 2 + r], in2[h, 2 + r])
            out3[h, r] = value.astype(BF)

        copy(1, h).start()

        @pl.loop(0, 2)
        def _(r):
            hold[h, r] = total_of(box[0, h, dp, r], pair[h, dp, r], in1[h, 0, r], in2[h, r])


    def stage4(h):
        copy(1, h).wait_recv()
        out4[h] = total_of(hold[h, 1], in3[h, 1]).astype(BF)
        copy(2, h).start()
        hold[h, 0] = total_of(hold[h, 0], in3[h, 0])

    def stage5(h):
        copy(2, h).wait_recv()
        full_a[dp, h] = total_of(hold[h, 0], in4[h]).astype(BF)
        for k in range(3):
            share_a(h, k).start()

    def input_rows(t):
        weights = [rows_of(mix.at[k]) for k in range(3)]
        part = pl.ds(pl.multiple_of(t * 256, 256), 256)
        result, gain, shift, mark = input_part(
            tokens[part, :], marks[:, part], vectors[...], weights,
            [grads_qkv[k, part, :] for k in range(3)], back[part, :],
        )
        back[part, :] = result
        gains[0:1, :] += gain
        gains[1:2, :] += shift
        gains[2:3, :] += mark

    column = (spot.near, spot.far, (dp, spot.zs[3] * 2 + c))
    result_copy = pltpu.make_async_copy(back, input_grad, loads.at[7])

    def vecq_copy(k):
        place = vec_q.at[dp]
        return link(place, place, vecq_sent.at[k], vecq_got.at[dp], trio[k])

    def vec_pair():
        place = vec_f.at[4 + c]
        return link(place, place, vecf_sent.at[3], vecf_got.at[4 + c], spot.core)

    def vecf_copy(k):
        place = vec_f.at[spot.z]
        return link(place, place, vecf_sent.at[k], vecf_got.at[spot.z], column[k])

    def vec_first():
        gain, shift, mark = (gains[k : k + 1, :] for k in range(3))
        flag = (row_flag[0] == 1).astype(F32)
        vec_q[dp] = jnp.concatenate(
            [
                gain, shift, gain2[0:2, :], mark * (1.0 - flag), mark * flag,
                jnp.zeros((2, 768), F32),
            ],
            axis=0,
        )
        for k in range(3):
            vecq_copy(k).start()

    def vec_second():
        for q in spot.qs[1:]:
            place = vec_q.at[q]
            link(place, place, vecq_sent.at[0], vecq_got.at[q], spot.first).wait_recv()
        vec_f[4 + c] = vec_q[0] + vec_q[1] + vec_q[2] + vec_q[3]
        vec_pair().start()

    def vec_spread():
        place = vec_f.at[5 - c]
        link(place, place, vecf_sent.at[3], vecf_got.at[5 - c], spot.core).wait_recv()
        vec_f[spot.z] = vec_f[4] + vec_f[5]
        for k in range(3):
            vecf_copy(k).start()

    def vec_third():
        for k in range(1, 4):
            other = spot.zs[k]
            place = vec_f.at[other]
            link(place, place, vecf_sent.at[0], vecf_got.at[other], spot.near).wait_recv()
        vector_sum[...] = vec_f[0] + vec_f[1] + vec_f[2] + vec_f[3]

    def turn_rows():
        lines = [ref[...].reshape(1, 96) for ref in (mix_rows, proj_rows, expand_rows)]
        tall = shrink_rows[...].reshape(1, 384)
        lines += [tall[:, 96 * k : 96 * (k + 1)] for k in range(4)]
        columns_old[0:96, 0:8] = jnp.concatenate(lines + lines[:1], axis=0).T
        for k in range(3, 7):
            local[k].wait()
        squares = [square_sum(w) for w in (w_mix, w_proj, w_expand, w_shrink)]
        columns_old[96:104, 0:1] = jnp.concatenate(squares + squares, axis=0)

    def old_row(index):
        return columns_old[0:96, index : index + 1]

    def wide_stats(blocks, index):
        squares = [b * b for b in blocks]
        total = jnp.sum(squares[0] + 1e-30, axis=1, keepdims=True)
        for square in squares[1:]:
            total = total + jnp.sum(square + 1e-30, axis=1, keepdims=True)
        row = BETA * old_row(index) + (1.0 - BETA) * (total / (768.0 * len(blocks)))
        rows_new[index] = jnp.broadcast_to(row, (96, 128))
        inverse = 1.0 / row
        cols = [jnp.sum(square + 1e-30, axis=0, keepdims=True) for square in squares]
        scaled = [jnp.sum(square * inverse, axis=0, keepdims=True) for square in squares]
        return jnp.sum(row, axis=0, keepdims=True), cols, scaled

    def square_sum(ref):
        value = ref[...]
        return jnp.sum(jnp.sum(value * value, axis=0, keepdims=True), axis=1, keepdims=True)

    def tiles(value):
        return [value[:, 128 * k : 128 * (k + 1)] for k in range(6)]

    def scalar_tile(values):
        column = jnp.concatenate(values + [jnp.zeros((8 - len(values), 1), F32)], axis=0)
        return jnp.broadcast_to(column, (8, 128))

    def slot_pair(kind):
        slots = (slots_a, slots_b)[kind]
        return link(
            slots.at[4 + c], slots.at[4 + c], slot_sent.at[kind, 3], slot_got.at[kind, 4 + c], spot.core
        )

    def slot_copy(kind, k):
        place = (slots_a, slots_b)[kind].at[spot.z]
        return link(place, place, slot_sent.at[kind, k], slot_got.at[kind, spot.z], column[k])

    def slot_spread(kind):
        slots = (slots_a, slots_b)[kind]
        link(
            slots.at[5 - c], slots.at[5 - c], slot_sent.at[kind, 3], slot_got.at[kind, 5 - c], spot.core
        ).wait_recv()
        slots[spot.z] = slots[4] + slots[5]
        for k in range(3):
            slot_copy(kind, k).start()

    def slot_sum(kind, out):
        slots = (slots_a, slots_b)[kind]
        for k in range(1, 4):
            other = spot.zs[k]
            place = slots.at[other]
            link(place, place, slot_sent.at[kind, 0], slot_got.at[kind, other], spot.near).wait_recv()
        out[...] = slots[0] + slots[1] + slots[2] + slots[3]

    def stats_b():
        shared_b(0)
        shared_b(1)
        for g in range(2):
            for q in range(4):
                grads[1 + g, q] = full_b[g, q]
        blocks = [full_b[0, q].astype(F32) for q in range(4)]
        total, cols, scaled = wide_stats(blocks, 2)
        total_s, cols_s, scaled_s = None, None, None
        for q in range(4):
            t, col, sc = wide_stats([full_b[1, q].astype(F32)], 3 + q)
            total_s = t if q == 0 else total_s + t
            cols_s = col[0] if q == 0 else cols_s + col[0]
            scaled_s = sc[0] if q == 0 else scaled_s + sc[0]
        slots_b[4 + c] = jnp.concatenate(
            tiles(jnp.concatenate(cols + scaled, axis=0))
            + tiles(jnp.concatenate([cols_s, scaled_s], axis=0))
            + [jnp.zeros((4, 128), F32)]
            + [
                scalar_tile([total, total_s, columns_old[98:99, 0:1], columns_old[99:100, 0:1]])
            ],
            axis=0,
        )
        slot_pair(1).start()

    def stats_a():
        blocks = [
            jnp.concatenate([full_a[q, h] for h in range(3)], axis=1) for q in range(4)
        ]
        for q in range(4):
            grads[0, q] = blocks[q]
        blocks = [b.astype(F32) for b in blocks]
        total, cols, scaled = wide_stats(blocks[:3], 0)
        total_p, cols_p, scaled_p = wide_stats(blocks[3:], 1)
        slots_a[4 + c] = jnp.concatenate(
            tiles(jnp.concatenate(cols + cols_p + scaled + scaled_p, axis=0))
            + [
                scalar_tile([total, total_p, columns_old[96:97, 0:1], columns_old[97:98, 0:1]])
            ],
            axis=0,
        )
        slot_pair(0).start()

    @pl.when(step == 0)
    def _():
        begin()

    @pl.when(step < 12)
    def _():
        columns = pl.ds(pl.multiple_of(step // 2 * 128, 128), 128)
        attend_back_head(
            length[0], step % 2, kept.at[0], key.at[0], value.at[0], ctx_grad,
            grads_qkv.at[0, :, columns], grads_qkv.at[1, :, columns], grads_qkv.at[2, :, columns], tile,
        )

    @pl.when(step == 0)
    def _():
        begin_copies()
        gains[...] = jnp.zeros((8, 768), F32)

    @pl.when(step == 1)
    def _():
        late()
        for copy in early[1:]:
            copy.wait()
        stage2b(1)

    @pl.when((step == 3) | (step == 7) | (step == 11))
    def _():
        third_grad(step // 4)

    for at, stage, g in (
        (2, stage3b, 0), (4, stage3b, 1), (5, stage4b, 0), (7, stage4b, 1), (7, stage5b, 0), (9, stage5b, 1),
    ):

        @pl.when(step == at)
        def _():
            stage(g)

    @pl.when((step == 4) | (step == 8))
    def _():
        stage1(step // 4 - 1)

    @pl.when((step == 6) | (step == 11))
    def _():
        stage2(step // 8)

    @pl.when(step == 8)
    def _():
        stage3(0)

    @pl.when(step == 10)
    def _():
        stage4(0)

    @pl.when(step == 9)
    def _():
        turn_rows()

    @pl.when(step == 12)
    def _():
        stage1(2)
        for k in range(3):
            local[k].wait()
        stage5(0)

        @pl.loop(0, 4)
        def _(t):
            input_rows(t)

            @pl.when(t == 0)
            def _():
                stage3(1)

            @pl.when(t == 1)
            def _():
                stage2(2)

            @pl.when(t == 2)
            def _():
                stage4(1)
                stage3(2)

        result_copy.start()
        vec_first()
        stage4(2)
        stage5(1)
        stats_b()
        stage5(2)
        vec_second()
        slot_spread(1)
        for h in range(3):
            shared_a(h)
        stats_a()
        vec_spread()
        slot_sum(1, sums_b)
        slot_spread(0)
        for p2 in range(2):
            late_s(p2).wait_send()
        for g in range(2):
            for k in range(3):
                share_b(g, k).wait_send()
            for stage in range(3):
                copyb(stage, g).wait_send()

        @pl.loop(0, 3)
        def _(h):
            for k in range(3):
                share_a(h, k).wait_send()
            for q in range(4):
                pair_copy(h, q).wait_send()
            for p2 in range(2):
                first_copy(h, p2).wait_send()
            for stage in range(3):
                copy(stage, h).wait_send()

        for k in range(3):
            vecq_copy(k).wait_send()
        vec_pair().wait_send()
        for k in range(3):
            vecf_copy(k).wait_send()
        result_copy.wait()
        vec_third()
        slot_sum(0, sums_a)
        for kind in range(2):
            slot_pair(kind).wait_send()
            for k in range(3):
                slot_copy(kind, k).wait_send()


def run_back(length, row_flag, kept, mixed, ctx_grad, rest_s, near_e, near_s, normed, proj_box,
             marks, vectors, gain2, mix_rows, proj_rows, expand_rows, shrink_rows, got_e, got_s, tokens, a_full, middle_back,
             w_mix, w_proj, w_expand, w_shrink, tile=128):
    rows, width = normed.shape
    third = (96, 256)
    block = (96, 768)
    sem = pltpu.SemaphoreType.DMA

    def at(p):
        return jnp.minimum(p, 11)

    return pl.pallas_call(
        functools.partial(back_kernel, tile=tile),
        grid=(13,),
        in_specs=[
            SCALARS,
            SCALARS,
            pl.BlockSpec((1, rows, 128), lambda p: (at(p), 0, 0)),
            pl.BlockSpec((1, rows, 128), lambda p: (6 + at(p) // 2, 0, 0)),
            pl.BlockSpec((1, rows, 128), lambda p: (12 + at(p) // 2, 0, 0)),
            pl.BlockSpec((rows, 128), lambda p: (0, at(p) // 2)),
            fixed(2, *block), fixed(16, rows), fixed(16, width), fixed(8, width),
            fixed(96), fixed(96), fixed(96), fixed(384),
            *[ANYWHERE] * 13,
        ],
        out_specs=[
            ANYWHERE, fixed(3, 4, *block), fixed(7, 96, 128), fixed(56, 128), fixed(72, 128),
            fixed(8, width),
        ],
        out_shape=shapes(
            ((rows, width), F32), ((3, 4) + block, BF), ((7, 96, 128), F32),
            ((56, 128), F32), ((72, 128), F32), ((8, width), F32),
        ),
        scratch_shapes=[
            pltpu.VMEM((rows, width), BF),
            pltpu.VMEM((3, 4, 2) + block, BF),
            pltpu.VMEM((rows, width), F32),
            pltpu.VMEM(w_mix.shape, F32),
            pltpu.VMEM(w_proj.shape, F32),
            pltpu.VMEM(w_expand.shape, F32),
            pltpu.VMEM(w_shrink.shape, F32),
            *[pltpu.VMEM((2, 4) + block, BF)] * 2,
            pltpu.VMEM((rows, width), BF),
            pltpu.VMEM((2, 4) + block, BF),
            pltpu.VMEM((3, rows, width), BF),
            pltpu.VMEM((2, 2, 4) + block, BF),
            *[pltpu.VMEM((2, 4) + block, BF)] * 2,
            *[pltpu.VMEM((2, 2) + block, BF)] * 2,
            *[pltpu.VMEM((2,) + block, BF)] * 2,
            pltpu.VMEM((2, 2) + block, F32),
            pltpu.VMEM((2, 3, 4, 4) + third, BF),
            pltpu.VMEM((3, 4, 4) + third, BF),
            *[pltpu.VMEM((3, 2, 4) + third, BF)] * 2,
            *[pltpu.VMEM((3, 4) + third, BF)] * 2,
            *[pltpu.VMEM((3, 2) + third, BF)] * 2,
            *[pltpu.VMEM((3,) + third, BF)] * 2,
            pltpu.VMEM((3, 2) + third, F32),
            pltpu.VMEM((4, 3) + third, BF),
            pltpu.VMEM((2, 4) + block, BF),
            pltpu.VMEM((4, 8, 768), F32),
            pltpu.VMEM((6, 8, 768), F32),
            pltpu.VMEM((6, 56, 128), F32),
            pltpu.VMEM((6, 72, 128), F32),
            pltpu.VMEM((8, 768), F32),
            pltpu.VMEM((104, 128), F32),
            sem((12,)), sem((5,)), sem((2,)), sem((2,)), sem((3, 2)), sem((3, 2)),
            sem((3, 4)), sem((3, 4)), sem((3, 2)), sem((3, 2)), sem((3, 3)), sem((3, 3)),
            sem((5, 3)), sem((5, 4)),
            sem((3,)), sem((4,)), sem((4,)), sem((6,)), sem((2, 4)), sem((2, 6)),
        ],
        compiler_params=params(collective_id=2, has_side_effects=True),
        name="back",
    )(length, row_flag, kept, mixed, mixed, ctx_grad, rest_s, marks, vectors, gain2, mix_rows, proj_rows, expand_rows, shrink_rows, near_e, near_s, normed, proj_box,
      got_e, got_s, tokens, a_full, middle_back, w_mix, w_proj, w_expand, w_shrink)


def step_kernel(
    grad_a, grad_e, grad_s, w_mix, w_proj, w_expand, w_shrink, rows,
    mix_cols, proj_cols, expand_cols, shrink_cols, sums_a, sums_b, vector_sum, old, vectors, moment,
    output_in, input_grad_in,
    mix_grad, proj_grad, expand_grad, shrink_grad, mix_new, proj_new, expand_new, shrink_new,
    mix_rows_new, proj_rows_new, expand_rows_new, shrink_rows_new,
    mix_cols_new, proj_cols_new, expand_cols_new, shrink_cols_new,
    vector_grad, vector_new, moment_new, output, input_grad, cols_new, *, owners
):
    q = pl.program_id(0)
    height = 96.0 * owners
    output[...] = output_in[...]
    input_grad[...] = input_grad_in[...]

    def wide(ref, at, row, count, of):
        return jnp.concatenate(
            [ref[at + of * k + row : at + of * k + row + count, :] for k in range(6)], axis=1
        )

    def one(ref, at, k):
        return ref[at + k : at + k + 1, 0:1]

    @pl.when(q == 0)
    def _():
        def lines(ref, count):
            value = ref[...].reshape(1, 768 * count)
            return [value[:, 768 * k : 768 * (k + 1)] for k in range(count)]

        def flat(first, count):
            value = jnp.concatenate([cols_new[k : k + 1, :] for k in range(first, first + count)], axis=1)
            return value.reshape(768 * count)

        parts = [wide(sums_a, 0, 0, 4, 8), wide(sums_b, 0, 0, 4, 8)]
        before = lines(mix_cols, 3) + lines(proj_cols, 1) + lines(expand_cols, 4)
        cols_new[0:8, :] = BETA * jnp.concatenate(before, axis=0) + (1.0 - BETA) * (
            jnp.concatenate(parts, axis=0) / height
        )
        tall = BETA * lines(shrink_cols, 1)[0] + (1.0 - BETA) * (
            wide(sums_b, 48, 0, 1, 2) / (4.0 * height)
        )
        cols_new[8:16, :] = jnp.broadcast_to(tall, (8, 768))
        mix_cols_new[...] = flat(0, 3)
        proj_cols_new[...] = flat(3, 1)
        expand_cols_new[...] = flat(4, 4)
        shrink_cols_new[...] = flat(8, 1)
        turned = [rows[k].T[0:1, :] for k in range(7)]
        mix_rows_new[...] = turned[0].reshape(96)
        proj_rows_new[...] = turned[1].reshape(96)
        expand_rows_new[...] = turned[2].reshape(96)
        shrink_rows_new[...] = jnp.concatenate(turned[3:], axis=1).reshape(384)
        fs = lax.axis_index("fsdp")
        grads = vector_sum[...]
        steps, squares = 0.0, 0.0
        for owner in range(8):
            part = pltpu.roll(grads, (768 - 96 * owner) % 768, 1)[0:6, 0:96]
            change = part * lax.rsqrt(
                BETA * old[owner, 8:14, 0:96] + (1.0 - BETA) * (part * part + 1e-30)
            )
            steps += jnp.sum(change * change, axis=1, keepdims=True)
            plain = old[owner, 0:6, 0:96]
            squares += jnp.sum(plain * plain, axis=1, keepdims=True)
        grad = pltpu.roll(grads, (768 - 96 * fs) % 768, 1)[0:6, 0:96]
        vector_grad[...] = grad
        new = BETA * moment[...] + (1.0 - BETA) * (grad * grad + 1e-30)
        moment_new[...] = new
        clip = jnp.maximum(1.0, jnp.sqrt(steps / 768.0) / CLIP)
        rate = RATE * jnp.maximum(0.001, jnp.sqrt(squares / 768.0))
        vector_new[...] = vectors[...] - rate * ((grad * lax.rsqrt(new)) / clip)

    def update(grad, weight, row, col, scaled, all_cols, row_total, square, count, across):
        row_mean = row_total / count
        entries = count * across
        update_square = row_mean * jnp.sum(
            jnp.sum(scaled / all_cols, axis=1, keepdims=True), axis=0, keepdims=True
        )
        clip = jnp.maximum(1.0, jnp.sqrt(update_square / entries) / CLIP)
        rate = RATE * jnp.maximum(0.001, jnp.sqrt(square / entries))
        factor = rate / clip
        return weight - factor * (grad * lax.rsqrt(row * (col / row_mean)))

    a = grad_a[0, 0].astype(F32)
    col = cols_new[pl.ds(q, 1), :]

    @pl.when(q < 3)
    def _():
        mix_grad[...] = a
        mix_new[...] = update(
            a, w_mix[...], rows[0][:, 0:1], col, wide(sums_a, 0, 4, 3, 8), cols_new[0:3, :],
            one(sums_a, 48, 0), one(sums_a, 48, 2), height, 2304.0,
        )

    @pl.when(q == 3)
    def _():
        proj_grad[...] = a
        proj_new[...] = update(
            a, w_proj[...], rows[1][:, 0:1], col, wide(sums_a, 0, 7, 1, 8), cols_new[3:4, :],
            one(sums_a, 48, 1), one(sums_a, 48, 3), height, 768.0,
        )

    e = grad_e[0, 0].astype(F32)
    expand_grad[...] = e
    expand_new[...] = update(
        e, w_expand[...], rows[2][:, 0:1], cols_new[pl.ds(4 + q, 1), :], wide(sums_b, 0, 4, 4, 8), cols_new[4:8, :],
        one(sums_b, 64, 0), one(sums_b, 64, 2), height, 3072.0,
    )
    t = grad_s[0, 0].astype(F32)
    shrink_grad[...] = t
    shrink_new[...] = update(
        t, w_shrink[...], rows[3 + q][:, 0:1], cols_new[8:9, :], wide(sums_b, 48, 1, 1, 2), cols_new[8:9, :],
        one(sums_b, 64, 1), one(sums_b, 64, 3), 4.0 * height, 768.0,
    )

def run_step(grads, w_mix, w_proj, w_expand, w_shrink, rows, mix_cols, proj_cols, expand_cols, shrink_cols,
             sums_a, sums_b, vector_sum, old, vectors, moment, output, input_grad, owners):
    block = (96, 768)
    wide = pl.BlockSpec(block, lambda q: (0, q))
    three = pl.BlockSpec(block, lambda q: (0, jnp.minimum(q, 2)))
    tall = pl.BlockSpec(block, lambda q: (q, 0))
    part = pl.BlockSpec((output.shape[0] // 4, 768), lambda q: (q, 0))
    return pl.pallas_call(
        functools.partial(step_kernel, owners=owners),
        grid=(4,),
        in_specs=[
            pl.BlockSpec((1, 1) + block, lambda q: (0, q, 0, 0)),
            pl.BlockSpec((1, 1) + block, lambda q: (1, q, 0, 0)),
            pl.BlockSpec((1, 1) + block, lambda q: (2, q, 0, 0)),
            three, fixed(*block), wide, tall,
            fixed(7, 96, 128), fixed(2304), fixed(768), fixed(3072), fixed(768),
            fixed(56, 128), fixed(72, 128), fixed(8, 768), fixed(8, 16, 128), fixed(6, 96), fixed(6, 96),
            part, part,
        ],
        out_specs=[
            three, fixed(*block), wide, tall, three, fixed(*block), wide, tall,
            fixed(96), fixed(96), fixed(96), fixed(384), fixed(2304), fixed(768), fixed(3072), fixed(768),
            fixed(6, 96), fixed(6, 96), fixed(6, 96), part, part,
        ],
        out_shape=shapes(
            *[(w.shape, F32) for w in (w_mix, w_proj, w_expand, w_shrink)] * 2,
            *[((n,), F32) for n in (96, 96, 96, 384, 2304, 768, 3072, 768)],
            *[((6, 96), F32)] * 3, (output.shape, BF), (input_grad.shape, F32),
        ),
        scratch_shapes=[pltpu.VMEM((16, 768), F32)],
        compiler_params=params(),
        name="step",
    )(grads, grads, grads, w_mix, w_proj, w_expand, w_shrink, rows, mix_cols, proj_cols, expand_cols,
      shrink_cols, sums_a, sums_b, vector_sum, old, vectors, moment, output, input_grad)


def masks(row_flag, sentence_mask, token_mask, lengths):
    length = sentence_mask.shape[1]
    valid = (lax.broadcasted_iota(jnp.int32, (1, length), 1) < lengths[:, None]).astype(jnp.int32)
    is_token = (row_flag == 1).astype(jnp.int32)[:, None]
    return jnp.concatenate(
        [
            jnp.zeros((4, length), jnp.int32),
            sentence_mask * valid * (1 - is_token),
            token_mask * valid * is_token,
            jnp.zeros((10, length), jnp.int32),
        ]
    ).astype(BF)


def staged_body(
    tokens, cotangent, row_flag, sentence_mask, token_mask, lengths,
    mix_weight, proj_weight, expand_weight, shrink_weight, norm_vectors,
    mix_rows, proj_rows, expand_rows, shrink_rows,
    mix_cols, proj_cols, expand_cols, shrink_cols, vector_moment,
):
    length, width = tokens.shape[1:]
    tokens = tokens.reshape(length, width)
    cotangent = cotangent.reshape(length, width)
    owners = lax.axis_size("fsdp")
    a_full, b_full, c_full, vectors, old, marks, normed, mixed, context, kept = run_front(
        lengths, row_flag, tokens, sentence_mask, token_mask, norm_vectors, vector_moment,
        mix_weight, proj_weight, expand_weight, shrink_weight,
    )
    (block_output, middle_back, ctx_back, gain2, proj_box,
     near_e, near_s, rest_s, got_e, got_s) = run_feed_send(
        lengths, context, tokens, marks, vectors, a_full, b_full, c_full, cotangent
    )
    input_grad, grads, rows, sums_a, sums_b, vector_sum = run_back(
        lengths, row_flag, kept, mixed, ctx_back, rest_s, near_e, near_s, normed, proj_box,
        marks, vectors, gain2, mix_rows, proj_rows, expand_rows, shrink_rows,
        got_e, got_s, tokens, a_full, middle_back, mix_weight, proj_weight, expand_weight, shrink_weight,
    )
    (mix_grad, proj_grad, expand_grad, shrink_grad, mix_new, proj_new, expand_new, shrink_new,
     *statistics, vector_grad, vector_new, moment_new, block_output, input_grad) = run_step(
        grads, mix_weight, proj_weight, expand_weight, shrink_weight, rows,
        mix_cols, proj_cols, expand_cols, shrink_cols, sums_a, sums_b, vector_sum, old,
        norm_vectors, vector_moment, block_output, input_grad, owners,
    )
    return (
        block_output.reshape(1, length, width),
        input_grad.reshape(1, length, width),
        mix_grad, proj_grad, expand_grad, shrink_grad, vector_grad,
        mix_new, proj_new, expand_new, shrink_new, vector_new, *statistics, moment_new,
    )


def plain_body(
    tokens, cotangent, row_flag, sentence_mask, token_mask, lengths,
    mix_weight, proj_weight, expand_weight, shrink_weight, norm_vectors,
    mix_rows, proj_rows, expand_rows, shrink_rows,
    mix_cols, proj_cols, expand_cols, shrink_cols, vector_moment,
):
    length, width = tokens.shape[1:]
    tokens = tokens.reshape(length, width)
    cotangent = cotangent.reshape(length, width)
    owners = lax.axis_size("fsdp")
    marks = masks(row_flag, sentence_mask, token_mask, lengths)
    is_token = (row_flag == 1).astype(F32)[:, None]
    mix_full = lax.all_gather(mix_weight.astype(BF), "fsdp", axis=0, tiled=True)
    proj_full = lax.all_gather(proj_weight.astype(BF), "fsdp", axis=0, tiled=True)
    expand_full = lax.all_gather(expand_weight.astype(BF), "fsdp", axis=0, tiled=True)
    shrink_full = lax.all_gather(shrink_weight.astype(BF), "fsdp", axis=0, tiled=True)
    vectors = lax.all_gather(norm_vectors.astype(BF), "fsdp", axis=1, tiled=True).astype(F32)
    vectors = jnp.concatenate([vectors, jnp.zeros((10, width), F32)])
    normed, mixed = run_mixed(tokens, marks, vectors, mix_full)
    context, kept = run_attend(lengths, mixed)
    block_output, middle_back, ctx_back, gain2, proj_local, expand_local, shrink_local = run_feed(
        lengths, context, tokens, marks, vectors, proj_full, expand_full, shrink_full, cotangent
    )
    dq, dk, dv = run_attend_back(lengths, kept, mixed, ctx_back)
    mix_local = run_mix_grad(normed, dq, dk, dv)
    input_grad, gain1 = run_input(tokens, marks, vectors, mix_full, dq, dk, dv, middle_back)
    vector_local = jnp.concatenate(
        [gain1[0:2], gain2[0:2], gain1[2:3] * (1.0 - is_token), gain1[2:3] * is_token]
    )
    local = (mix_local, proj_local, expand_local, shrink_local)
    shards = [lax.psum_scatter(g, "fsdp", scatter_dimension=0, tiled=True) for g in local]
    shards.append(lax.psum_scatter(vector_local, "fsdp", scatter_dimension=1, tiled=True))
    mix_grad, proj_grad, expand_grad, shrink_grad, vector_grad = lax.psum(tuple(shards), "dp")

    grads = (mix_grad, proj_grad, expand_grad, shrink_grad)
    weights = (mix_weight, proj_weight, expand_weight, shrink_weight)
    old_rows = (mix_rows, proj_rows, expand_rows, shrink_rows)
    old_cols = (mix_cols, proj_cols, expand_cols, shrink_cols)
    rows_new, col_parts, scaled_parts = [], [], []
    for g, r in zip(grads, old_rows):
        square = g * g + 1e-30
        row = BETA * r + (1.0 - BETA) * jnp.mean(square, axis=1)
        rows_new.append(row)
        col_parts.append(jnp.sum(square, axis=0))
        scaled_parts.append(jnp.sum(g * g * (1.0 / row)[:, None], axis=0))
    moment_new = BETA * vector_moment + (1.0 - BETA) * (vector_grad * vector_grad + 1e-30)
    vector_step = vector_grad * lax.rsqrt(moment_new)
    small = jnp.concatenate(
        [
            jnp.stack([jnp.sum(r) for r in rows_new]),
            jnp.stack([jnp.sum(w * w) for w in weights]),
            jnp.sum(vector_step * vector_step, axis=1),
            jnp.sum(norm_vectors * norm_vectors, axis=1),
        ]
    )
    packed = lax.psum(jnp.concatenate(col_parts + scaled_parts + [small]), "fsdp")
    offset = 0
    total_cols = sum(col.shape[0] for col in old_cols)
    small = packed[2 * total_cols :]
    cols_new, new_weights = [], []
    for index in range(4):
        count = grads[index].shape[0] * owners
        wide = old_cols[index].shape[0]
        entries = count * wide
        col = BETA * old_cols[index] + (1.0 - BETA) * packed[offset : offset + wide] / count
        scaled = packed[total_cols + offset : total_cols + offset + wide]
        offset += wide
        cols_new.append(col)
        row_mean = small[index] / count
        update_square = row_mean * jnp.sum(scaled / col)
        clip_factor = jnp.maximum(1.0, jnp.sqrt(update_square / entries) / CLIP)
        rate = RATE * jnp.maximum(0.001, jnp.sqrt(small[4 + index] / entries))
        approx = rows_new[index][:, None] * col[None, :] / row_mean
        step = grads[index] * lax.rsqrt(approx)
        new_weights.append(weights[index] - (rate / clip_factor) * step)
    vector_clip = jnp.maximum(1.0, jnp.sqrt(small[8:14] / width) / CLIP)
    vector_rate = RATE * jnp.maximum(0.001, jnp.sqrt(small[14:20] / width))
    vector_new = norm_vectors - vector_rate[:, None] * (vector_step / vector_clip[:, None])
    return (
        block_output.reshape(1, length, width),
        input_grad.reshape(1, length, width),
        mix_grad, proj_grad, expand_grad, shrink_grad, vector_grad,
        *new_weights, vector_new, *rows_new, *cols_new, moment_new,
    )


def solution(mesh):
    sequence = P(AXES, None, None)
    ins = (
        sequence, sequence, P(AXES), P(AXES, None), P(AXES, None), P(AXES),
        P("fsdp", None), P("fsdp", None), P("fsdp", None), P("fsdp", None), P(None, "fsdp"),
        P("fsdp"), P("fsdp"), P("fsdp"), P("fsdp"), P(), P(), P(), P(), P(None, "fsdp"),
    )
    outs = (
        sequence, sequence,
        P("fsdp", None), P("fsdp", None), P("fsdp", None), P("fsdp", None), P(None, "fsdp"),
        P("fsdp", None), P("fsdp", None), P("fsdp", None), P("fsdp", None), P(None, "fsdp"),
        P("fsdp"), P("fsdp"), P("fsdp"), P("fsdp"), P(), P(), P(), P(), P(None, "fsdp"),
    )
    staged = (mesh.shape["dp"], mesh.shape["fsdp"]) == (4, 8)
    body = staged_body if staged else plain_body
    return jax.shard_map(body, mesh=mesh, in_specs=ins, out_specs=outs, check_vma=False)
```

```python
import functools

import jax
import jax.numpy as jnp
from jax import lax
from jax.experimental import pallas as pl
from jax.experimental.pallas import tpu as pltpu
from jax.sharding import PartitionSpec as P

HEADS = 12
STEP = 10
RATE = 0.5
CLIP = 1.0
F32 = jnp.float32
BF = jnp.bfloat16
VMEM_LIMIT = 60 * 1024 * 1024
AXES = ("dp", "fsdp")


def nn(a, b):
    return lax.dot_general(a, b, (((1,), (0,)), ((), ())), preferred_element_type=F32)


def nt(a, b):
    return lax.dot_general(a, b, (((1,), (1,)), ((), ())), preferred_element_type=F32)


def tn(a, b):
    return lax.dot_general(a, b, (((0,), (0,)), ((), ())), preferred_element_type=F32)


def normalise(h):
    mean = jnp.mean(h, axis=-1, keepdims=True)
    centered = h - mean
    inverse = lax.rsqrt(jnp.mean(centered * centered, axis=-1, keepdims=True) + 1e-06)
    return centered * inverse, inverse


def norm_back(grad, normal, inverse, gain):
    scaled = grad * gain
    first = jnp.mean(scaled, axis=-1, keepdims=True)
    second = jnp.mean(scaled * normal, axis=-1, keepdims=True)
    return inverse * (scaled - first - normal * second)


def params(**kw):
    return pltpu.CompilerParams(vmem_limit_bytes=VMEM_LIMIT, **kw)


def fixed(*shape):
    return pl.BlockSpec(shape, lambda *_: (0,) * len(shape), pipeline_mode=pl.Buffered(1))


ANYWHERE = pl.BlockSpec(memory_space=pl.ANY)
SCALARS = pl.BlockSpec(memory_space=pltpu.SMEM)


def shapes(*items):
    return [jax.ShapeDtypeStruct(shape, kind) for shape, kind in items]


def rows_of(ref):
    value = ref[...]
    return value.reshape(-1, value.shape[-1])


def mixed_kernel(tokens, marks, vectors, weight, normed, mixed):
    start = tokens[...].astype(F32) + tn(marks[...], vectors[...].astype(BF))
    normal, _ = normalise(start)
    low = (normal * vectors[0:1, :] + vectors[1:2, :]).astype(BF)
    normed[...] = low
    result = nn(low, weight[...]).astype(BF)
    for k in range(mixed.shape[0]):
        mixed[k] = result[:, k * 128 : (k + 1) * 128]


def run_mixed(tokens, marks, vectors, weight):
    rows, width = tokens.shape
    cols = weight.shape[1]
    tile = 256
    return pl.pallas_call(
        mixed_kernel,
        grid=(rows // tile,),
        in_specs=[
            pl.BlockSpec((tile, width), lambda i: (i, 0)),
            pl.BlockSpec((16, tile), lambda i: (0, i)),
            pl.BlockSpec((16, width), lambda i: (0, 0)),
            pl.BlockSpec((width, cols), lambda i: (0, 0)),
        ],
        out_specs=[
            pl.BlockSpec((tile, width), lambda i: (i, 0)),
            pl.BlockSpec((cols // 128, tile, 128), lambda i: (0, i, 0)),
        ],
        out_shape=[
            jax.ShapeDtypeStruct((rows, width), BF),
            jax.ShapeDtypeStruct((cols // 128, rows, 128), BF),
        ],
        compiler_params=params(),
        name="mixed",
    )(tokens, marks, vectors, weight)


def lane_iota(rows):
    return lax.broadcasted_iota(jnp.int32, (rows, 128), 1)


def key_extra(rows, length, base):
    lane = lane_iota(rows)
    row = lax.broadcasted_iota(jnp.int32, (rows, 128), 0)
    mask = jnp.where(row < length, 0.0, -1e30)
    ones = jnp.where((lane > base) & (lane < base + 4), 1.0, 0.0)
    return jnp.where(lane == base, mask, ones).astype(BF)


def attend_pair(length, query, key, value, context, kept, tile):
    rows = query.shape[0]
    lane = lane_iota(tile)
    lane_all = lane_iota(rows)
    count = rows // tile
    keys = [
        jnp.where(lane_all < 64, key[...], key_extra(rows, length, 64)),
        jnp.where(lane_all >= 64, key[...], key_extra(rows, length, 0)),
    ]
    values = value[...]

    def first(head, t):
        base = 64 - 64 * head
        mine = (lane < 64) if head == 0 else (lane >= 64)
        one = jnp.where(lane == base, 1.0, 0.0).astype(BF)
        q = jnp.where(mine, query[pl.ds(t * tile, tile), :] * BF(0.125), one)
        return q, nt(q, keys[head])

    def second(head, t, q, score):
        base = 64 - 64 * head
        mine = (lane < 64) if head == 0 else (lane >= 64)
        top = jnp.max(score, axis=-1, keepdims=True)
        expo = jnp.exp(score - top)
        total = jnp.sum(expo, axis=-1, keepdims=True)
        probs = (expo * (1.0 / total)).astype(BF)
        lse = top + jnp.log(total)
        high = lse.astype(BF).astype(F32)
        rest = lse - high
        mid = rest.astype(BF).astype(F32)
        extra = jnp.where(lane == base, 1.0, 0.0)
        extra = jnp.where(lane == base + 1, -high, extra)
        extra = jnp.where(lane == base + 2, -mid, extra)
        extra = jnp.where(lane == base + 3, mid - rest, extra)
        kept[head, pl.ds(t * tile, tile), :] = jnp.where(mine, q, extra.astype(BF))
        return probs

    order = [(head, t) for head in range(2) for t in range(count)]
    outs = {}
    ahead = first(*order[0])
    waiting = None
    for n, spot in enumerate(order):
        now = ahead
        if n + 1 < len(order):
            ahead = first(*order[n + 1])
        if waiting is not None:
            outs[waiting[0]] = nn(waiting[1], values)
        waiting = (spot, second(*spot, *now))
    outs[waiting[0]] = nn(waiting[1], values)
    for t in range(count):
        context[pl.ds(t * tile, tile), :] = jnp.where(lane < 64, outs[0, t], outs[1, t]).astype(BF)


def attend_kernel(length, query, key, value, context, kept, *, tile):
    attend_pair(length[0], query.at[0], key.at[0], value.at[0], context, kept, tile)


def run_attend(length, mixed, tile=256):
    groups, rows, _ = mixed.shape
    pairs = groups // 3
    return pl.pallas_call(
        functools.partial(attend_kernel, tile=tile),
        grid=(pairs,),
        in_specs=[
            pl.BlockSpec(memory_space=pltpu.SMEM),
            pl.BlockSpec((1, rows, 128), lambda p: (p, 0, 0)),
            pl.BlockSpec((1, rows, 128), lambda p: (pairs + p, 0, 0)),
            pl.BlockSpec((1, rows, 128), lambda p: (2 * pairs + p, 0, 0)),
        ],
        out_specs=[
            pl.BlockSpec((rows, 128), lambda p: (0, p)),
            pl.BlockSpec((2, rows, 128), lambda p: (p, 0, 0)),
        ],
        out_shape=[
            jax.ShapeDtypeStruct((rows, pairs * 128), BF),
            jax.ShapeDtypeStruct((2 * pairs, rows, 128), BF),
        ],
        compiler_params=params(),
        name="attend",
    )(length, mixed, mixed, mixed)


class Spot:
    def __init__(self):
        fs = lax.axis_index("fsdp")
        dp = lax.axis_index("dp")
        self.fs, self.dp = fs, dp
        self.c, self.z = fs % 2, fs // 2
        z0, z1 = self.z % 2, self.z // 2
        near, far = z1 * 2 + (1 - z0), (1 - z1) * 2 + z0
        self.zs = (self.z, near, far, (1 - z1) * 2 + (1 - z0))
        x, y = dp % 2, dp // 2
        turn_x, turn_y = 1 - 2 * x, 1 - 2 * y
        first = (y + turn_y * self.c) * 2 + x + turn_x * (1 - self.c)
        second = (y + turn_y * (1 - self.c)) * 2 + x + turn_x * self.c
        self.qs = (dp, first, second, (1 - y) * 2 + 1 - x)
        self.near = (dp, near * 2 + self.c)
        self.far = (dp, far * 2 + self.c)
        self.first = (first, fs)
        self.second = (second, fs)
        self.core = (dp, self.z * 2 + 1 - self.c)

        self.diag = (self.qs[3], fs)
        self.bits = (x, y, z0, z1)
        along_x, along_y = y * 2 + 1 - x, (1 - y) * 2 + x
        self.order = (self.qs[3], along_x, along_y, dp)
        self.first_order = tuple(
            a + (b - a) * self.c
            for a, b in (
                (along_y, along_x), (dp, self.qs[3]), (self.qs[3], dp), (along_x, along_y)
            )
        )

    def row(self, k):
        return (self.dp, (self.fs + k) % 8)

    def other(self, cc):
        return self.c if cc == 0 else 1 - self.c

    def rel_z(self, z):
        low, high = z % 2, z // 2
        near = low + self.bits[2] - 2 * low * self.bits[2]
        far = high + self.bits[3] - 2 * high * self.bits[3]
        return near * 2 + far


def greet(peers):
    barrier = pltpu.get_barrier_semaphore()
    for peer in peers:
        pl.semaphore_signal(barrier, inc=1, device_id=peer, device_id_type=MESH)


def greeted(peers):
    pl.semaphore_wait(pltpu.get_barrier_semaphore(), len(peers))


def link(src, dst, send_sem, recv_sem, target):
    return pltpu.make_async_remote_copy(
        src_ref=src, dst_ref=dst, send_sem=send_sem, recv_sem=recv_sem,
        device_id=target, device_id_type=MESH,
    )


def total_of(*parts):
    value = parts[0].astype(F32)
    for part in parts[1:]:
        value = value + part.astype(F32)
    return value


MESH = pl.DeviceIdType.MESH
SPLIT = (80, 80, 80)


def front_kernel(
    length, row_flag, tokens, sentence, token, share, moment, mix_w, proj_w, expand_w, shrink_w,
    a_out, b_out, c_out, vectors_out, old_out, marks, normed_out, mixed_out, context, kept,
    stage, stage_z, own, own_z, w_a, share_pad, vec_in, old_in, vectors, normed, mixed,
    send, recv, send_z, recv_z, vec_send, vec_recv, old_send, old_recv, local, local_z, *, tile
):
    step = pl.program_id(0)
    spot = Spot()
    c, dp = spot.c, spot.dp
    rows = tokens.shape[0]

    uppers = [pl.ds(0, n) for n in SPLIT]
    lowers = [pl.ds(n, 96 - n) for n in SPLIT]

    def block(g, z, cc, q):
        if g == 0:
            return w_a.at[q, z, cc, uppers[0]]
        if g == 1:
            return b_out.at[q, z, cc, uppers[1]]
        return c_out.at[z, cc, q, uppers[2]]

    def slab(g, z, cc):
        if g == 0:
            return w_a.at[:, z, cc, lowers[0]]
        if g == 1:
            return b_out.at[:, z, cc, lowers[1]]
        return c_out.at[z, cc, :, lowers[2]]

    def remote_z(g, z, cc, kind, target, mine=False):
        dst = slab(g, z, cc)
        return link(
            own_z.at[g - 1, :, pl.ds(0, 96 - SPLIT[g])] if mine and g > 0 else dst, dst,
            send_z.at[g, kind], recv_z.at[g, z * 2 + cc], target,
        )

    def push_z(g, k, kind, target, mine=False):
        remote_z(g, spot.zs[k], c, kind, target, mine).start()

    def arrive_z(g, k):
        remote_z(g, spot.zs[k], c, 0, spot.core).wait_recv()

    def remote(g, z, cc, q, kind, target, mine=False):
        dst = block(g, z, cc, q)
        return pltpu.make_async_remote_copy(
            src_ref=own.at[g - 1, uppers[g]] if mine and g > 0 else dst,
            dst_ref=dst,
            send_sem=send.at[g, kind],
            recv_sem=recv.at[g, (z * 2 + cc) * 4 + q],
            device_id=target,
            device_id_type=MESH,
        )

    def push(g, z, q, kind, target, mine=False):
        remote(g, z, c, q, kind, target, mine).start()

    def arrive(g, z, cc, q):
        remote(g, z, cc, q, 0, spot.core).wait_recv()

    def phase0(g):
        push(g, spot.z, dp, 0, spot.far, True)
        push(g, spot.z, dp, 1, spot.near, True)

    def phase0b(g):
        push(g, spot.z, dp, 7, spot.second, True)
        push(g, spot.z, dp, 3, spot.first, True)
        push(g, spot.z, dp, 15, spot.core, True)

    def phase0z(g):
        push_z(g, 0, 0, spot.far, True)
        push_z(g, 0, 1, spot.near, True)
        push_z(g, 0, 3, spot.core, True)

    def spread(g, k):
        push(g, spot.zs[k], dp, 7 + k, spot.second)
        push(g, spot.zs[k], dp, 3 + k, spot.first)
        push(g, spot.zs[k], dp, 15 + k, spot.core)

    def phase1(g):
        arrive(g, spot.zs[2], c, dp)
        push(g, spot.zs[2], dp, 2, spot.near)
        spread(g, 2)

    def phase1z(g):
        arrive_z(g, 2)
        push_z(g, 2, 2, spot.near)
        push_z(g, 2, 5, spot.core)

    def phase2(g):
        arrive(g, spot.zs[1], c, dp)
        spread(g, 1)
        arrive(g, spot.zs[3], c, dp)
        spread(g, 3)

    def phase2z(g):
        arrive_z(g, 1)
        push_z(g, 1, 4, spot.core)
        arrive_z(g, 3)
        push_z(g, 3, 6, spot.core)

    def phase3(g):
        for k in range(4):
            arrive(g, spot.zs[k], c, spot.qs[1])
            push(g, spot.zs[k], spot.qs[1], 11 + k, spot.second)
            push(g, spot.zs[k], spot.qs[1], 19 + k, spot.core)

    def phase4(g):
        for m in (2, 3):
            for k in range(4):
                arrive(g, spot.zs[k], c, spot.qs[m])
                push(g, spot.zs[k], spot.qs[m], 15 + 4 * m + k, spot.core)

    def phase5(g):
        @pl.loop(0, 4)
        def _(z):
            for q in range(4):
                arrive(g, z, 1 - c, q)
            remote_z(g, z, 1 - c, 0, spot.core).wait_recv()

    def phase6(g):
        @pl.loop(0, 31)
        def _(kind):
            remote(g, spot.z, c, dp, kind, spot.core, True).wait_send()

        @pl.loop(0, 7)
        def _(kind):
            remote_z(g, spot.z, c, kind, spot.core, True).wait_send()

    def vec_copy(k):
        return pltpu.make_async_remote_copy(
            src_ref=vec_in.at[spot.fs],
            dst_ref=vec_in.at[spot.fs],
            send_sem=vec_send.at[k],
            recv_sem=vec_recv.at[spot.fs],
            device_id=spot.row(k),
            device_id_type=MESH,
        )

    def vec_arrive(k):
        other = (spot.fs + k) % 8
        pltpu.make_async_remote_copy(
            src_ref=vec_in.at[other],
            dst_ref=vec_in.at[other],
            send_sem=vec_send.at[k],
            recv_sem=vec_recv.at[other],
            device_id=spot.row(k),
            device_id_type=MESH,
        ).wait_recv()

    def old_copy(k, at):
        place = old_in.at[at]
        return link(place, place, old_send.at[k], old_recv.at[at], spot.row(k))

    def keep_copies():
        return (
            pltpu.make_async_copy(w_a, a_out, local.at[3]),
            pltpu.make_async_copy(own.at[0, uppers[1]], block(1, spot.z, c, dp), local.at[4]),
            pltpu.make_async_copy(own.at[1, uppers[2]], block(2, spot.z, c, dp), local.at[5]),
            pltpu.make_async_copy(own_z.at[0, :, pl.ds(0, 96 - SPLIT[1])], slab(1, spot.z, c), local.at[8]),
            pltpu.make_async_copy(own_z.at[1, :, pl.ds(0, 96 - SPLIT[2])], slab(2, spot.z, c), local.at[9]),
            pltpu.make_async_copy(normed, normed_out, local.at[6]),
            pltpu.make_async_copy(mixed, mixed_out, local.at[7]),
        )

    @pl.when(step == 0)
    def _():
        barrier = pltpu.get_barrier_semaphore()
        peers = [spot.row(k) for k in range(1, 8)] + [spot.first, spot.second]
        for peer in peers:
            pl.semaphore_signal(barrier, inc=1, device_id=peer, device_id_type=MESH)

        columns = pl.ds(pl.multiple_of(dp * 768, 128), 768)

        @pl.when(dp < 3)
        def _():
            pltpu.make_async_copy(mix_w.at[:, columns], stage.at[0], local.at[0]).start()

        @pl.when(dp == 3)
        def _():
            pltpu.make_async_copy(proj_w, stage.at[0], local.at[0]).start()

        second = pltpu.make_async_copy(expand_w.at[:, columns], stage.at[1], local.at[1])
        second.start()
        third = pltpu.make_async_copy(
            shrink_w.at[pl.ds(pl.multiple_of(dp * 96, 32), 96), :], stage.at[2], local.at[2]
        )
        third.start()

        def slab_copy(g, q):
            if g == 0:
                src = proj_w.at[lowers[0], :] if q == 3 else mix_w.at[lowers[0], pl.ds(q * 768, 768)]
            elif g == 1:
                src = expand_w.at[lowers[1], pl.ds(q * 768, 768)]
            else:
                src = shrink_w.at[pl.ds(q * 96 + SPLIT[2], 96 - SPLIT[2]), :]
            return pltpu.make_async_copy(
                src, stage_z.at[g, q, pl.ds(0, 96 - SPLIT[g])], local_z.at[g, q]
            )

        for g in range(3):
            for q in range(4):
                slab_copy(g, q).start()
        share_pad[...] = jnp.zeros((16, 128), F32)
        share_pad[0:6, 0:96] = share[...]
        share_pad[8:14, 0:96] = moment[...]
        old_in[spot.fs] = share_pad[...]
        vec_in[spot.fs] = share_pad[...].astype(BF)
        position = lax.broadcasted_iota(jnp.int32, (1, rows), 1)
        flag = (row_flag[0] == 1).astype(F32)
        line = lax.broadcasted_iota(jnp.int32, (16, rows), 0)
        of_sentence = jnp.where(position < length[0], sentence[...].astype(F32), 0.0) * (1.0 - flag)
        of_token = jnp.where(position < length[0], token[...].astype(F32), 0.0) * flag
        marked = jnp.where(line == 4, of_sentence, jnp.where(line == 5, of_token, 0.0))
        marks[...] = marked.astype(BF)
        pltpu.make_async_copy(proj_w, stage.at[0], local.at[0]).wait()
        w_a[dp, spot.z, c, 0 : SPLIT[0]] = stage[0, 0 : SPLIT[0]].astype(BF)
        pl.semaphore_wait(barrier, len(peers))
        phase0(0)
        phase0b(0)
        for k in range(1, 8):
            vec_copy(k).start()
            old_copy(k, spot.fs).start()
        for q in range(4):
            slab_copy(0, q).wait()
            w_a[q, spot.z, c, SPLIT[0] : 96] = stage_z[0, q, 0 : 96 - SPLIT[0]].astype(BF)
        phase0z(0)
        second.wait()
        own[0] = stage[1].astype(BF)
        third.wait()
        own[1] = stage[2].astype(BF)
        for g in (1, 2):
            for q in range(4):
                slab_copy(g, q).wait()
                own_z[g - 1, q] = stage_z[g, q].astype(BF)
        copies = keep_copies()
        for copy in copies[1:5]:
            copy.start()
        for k in range(1, 8):
            vec_arrive(k)
        total = jnp.zeros((16, 768), F32)
        for f in range(8):
            row = lax.broadcasted_iota(jnp.int32, (128, 768), 0)
            lane = lax.broadcasted_iota(jnp.int32, (128, 768), 1)
            pick = jnp.where((lane - 96 * f == row) & (row < 96), 1.0, 0.0).astype(BF)
            total += nn(vec_in[f], pick)
        vectors[...] = total
        vectors_out[...] = total

        def norm(t):
            part = pl.ds(t * 256, 256)
            start = tokens[part, :].astype(F32) + tn(marks[:, part], total.astype(BF))
            normal, _ = normalise(start)
            normed[part, :] = (normal * total[0:1, :] + total[1:2, :]).astype(BF)

        norm(0)
        norm(1)
        phase1(0)
        norm(2)
        phase2(0)
        norm(3)
        phase1z(0)
        phase0(1)
        phase0(2)
        phase3(0)
        phase0b(1)
        phase1(1)
        phase2z(0)

        @pl.loop(0, 4)
        def _(z):
            remote_z(0, z, 1 - c, 0, spot.core).wait_recv()

        @pl.loop(0, 4)
        def _(k):
            q = jnp.where(
                k < 2, jnp.where(k == 0, spot.qs[0], spot.qs[1]), jnp.where(k == 2, spot.qs[2], spot.qs[3])
            )

            @pl.loop(0, 4)
            def _(z):
                arrive(0, z, 1 - c, q)

            @pl.when(q < 3)
            def _():
                weight = rows_of(w_a.at[q])

                @pl.loop(0, 4, unroll=2)
                def _(t):
                    part = pl.ds(pl.multiple_of(t * 256, 256), 256)
                    result = nn(normed[part, :], weight).astype(BF)
                    for n in range(6):
                        mixed[q * 6 + n, part, :] = result[:, n * 128 : (n + 1) * 128]

            @pl.when(k == 0)
            def _():
                phase4(0)
                phase0b(2)

            @pl.when(k == 1)
            def _():
                phase1(2)
                phase0z(1)
                phase0z(2)

            @pl.when(k == 2)
            def _():
                phase2(1)

            @pl.when(k == 3)
            def _():
                phase2(2)

        copies[0].start()
        copies[5].start()
        copies[6].start()

    @pl.when(step > 0)
    def _():
        p = step - 1
        attend_pair(length[0], mixed.at[p], mixed.at[6 + p], mixed.at[12 + p], context, kept, tile)

    for at, phase, g in (
        (1, phase3, 1), (2, phase3, 2), (2, phase1z, 1), (3, phase1z, 2), (3, phase2z, 1),
        (4, phase4, 1), (4, phase2z, 2), (5, phase4, 2),
    ):

        @pl.when(step == at)
        def _():
            phase(g)

    @pl.when(step == 6)
    def _():
        phase5(1)
        phase5(2)
        for g in range(3):
            phase6(g)
        for k in range(1, 8):
            old_copy(k, spot.fs).wait_send()
            old_copy(k, (spot.fs + k) % 8).wait_recv()
        old_out[...] = old_in[...]
        for k in range(1, 8):
            vec_copy(k).wait_send()
        for copy in keep_copies():
            copy.wait()


def run_front(length, row_flag, tokens, sentence, token, share, moment, mix_w, proj_w, expand_w, shrink_w, tile=256):
    rows, width = tokens.shape
    anywhere = pl.BlockSpec(memory_space=pl.ANY)
    once = pl.Buffered(1)

    def whole(*shape):
        return pl.BlockSpec(shape, lambda i: (0,) * len(shape), pipeline_mode=once)

    return pl.pallas_call(
        functools.partial(front_kernel, tile=tile),
        grid=(7,),
        in_specs=[
            SCALARS,
            SCALARS,
            whole(rows, width),
            whole(1, rows),
            whole(1, rows),
            whole(*share.shape),
            whole(*moment.shape),
            anywhere,
            anywhere,
            anywhere,
            anywhere,
        ],
        out_specs=[
            anywhere,
            anywhere,
            anywhere,
            whole(16, width),
            whole(8, 16, 128),
            whole(16, rows),
            anywhere,
            anywhere,
            pl.BlockSpec((rows, 128), lambda i: (0, jnp.maximum(i - 1, 0))),
            pl.BlockSpec((2, rows, 128), lambda i: (jnp.maximum(i - 1, 0), 0, 0)),
        ],
        out_shape=[
            jax.ShapeDtypeStruct((4, 4, 2, 96, 768), BF),
            jax.ShapeDtypeStruct((4, 4, 2, 96, 768), BF),
            jax.ShapeDtypeStruct((4, 2, 4, 96, 768), BF),
            jax.ShapeDtypeStruct((16, width), F32),
            jax.ShapeDtypeStruct((8, 16, 128), F32),
            jax.ShapeDtypeStruct((16, rows), BF),
            jax.ShapeDtypeStruct((rows, width), BF),
            jax.ShapeDtypeStruct((18, rows, 128), BF),
            jax.ShapeDtypeStruct((rows, width), BF),
            jax.ShapeDtypeStruct((12, rows, 128), BF),
        ],
        scratch_shapes=[
            pltpu.VMEM((3, 96, 768), F32),
            pltpu.VMEM((3, 4, 32, 768), F32),
            pltpu.VMEM((2, 96, 768), BF),
            pltpu.VMEM((2, 4, 32, 768), BF),
            pltpu.VMEM((4, 4, 2, 96, 768), BF),
            pltpu.VMEM((16, 128), F32),
            pltpu.VMEM((8, 16, 128), BF),
            pltpu.VMEM((8, 16, 128), F32),
            pltpu.VMEM((16, width), F32),
            pltpu.VMEM((rows, width), BF),
            pltpu.VMEM((18, rows, 128), BF),
            pltpu.SemaphoreType.DMA((3, 31)),
            pltpu.SemaphoreType.DMA((3, 32)),
            pltpu.SemaphoreType.DMA((3, 7)),
            pltpu.SemaphoreType.DMA((3, 8)),
            *[pltpu.SemaphoreType.DMA((8,))] * 4,
            pltpu.SemaphoreType.DMA((10,)),
            pltpu.SemaphoreType.DMA((3, 4)),
        ],
        compiler_params=params(collective_id=0, has_side_effects=True),
        name="front",
    )(length, row_flag, tokens, sentence, token, share, moment, mix_w, proj_w, expand_w, shrink_w)


def attend_back_pair(length, kept, key, value, ctx_grad, dq, dk, dv, tile):
    rows = key.shape[0]
    lane = lane_iota(tile)
    lane_all = lane_iota(rows)
    count = rows // tile
    plain, plain_values = key[...], value[...]
    keys = [
        jnp.where(lane_all < 64, plain, key_extra(rows, length, 64)),
        jnp.where(lane_all >= 64, plain, key_extra(rows, length, 0)),
    ]
    zero = jnp.zeros_like(plain_values)
    values = [
        jnp.where(lane_all < 64, plain_values, zero),
        jnp.where(lane_all >= 64, plain_values, zero),
    ]

    def first(head, t):
        q = kept[head, pl.ds(t * tile, tile), :]
        grad = ctx_grad[pl.ds(t * tile, tile), :]
        return q, grad, nt(keys[head], q), nt(values[head], grad)

    sums = {}

    def second(head, t, q, grad, score, prob_back):
        probs = jnp.exp(score)
        product = probs * prob_back
        delta = jnp.sum(product, axis=0, keepdims=True)
        score_back = (product - probs * delta).astype(BF)
        dv_part = nn(probs.astype(BF), grad)
        dk_part = nn(score_back, q)
        sums[head, "v"] = dv_part if t == 0 else sums[head, "v"] + dv_part
        sums[head, "k"] = dk_part if t == 0 else sums[head, "k"] + dk_part
        sums[head, t] = tn(score_back, plain)

    order = [(head, t) for head in range(2) for t in range(count)]
    ahead = first(*order[0])
    for n, spot in enumerate(order):
        now = ahead
        if n + 1 < len(order):
            ahead = first(*order[n + 1])
        second(*spot, *now)
    dk[...] = jnp.where(lane_all < 64, sums[0, "k"], sums[1, "k"]).astype(BF)
    dv[...] = jnp.where(lane_all < 64, sums[0, "v"], sums[1, "v"]).astype(BF)
    for t in range(count):
        both = jnp.where(lane < 64, sums[0, t], sums[1, t]) * 0.125
        dq[pl.ds(t * tile, tile), :] = both.astype(BF)


def attend_back_head(length, head, kept, key, value, ctx_grad, dq, dk, dv, tile):
    rows = key.shape[0]
    lane = lane_iota(tile) - 64 * head
    lane_all = lane_iota(rows) - 64 * head
    mine = (lane >= 0) & (lane < 64)
    mine_all = (lane_all >= 0) & (lane_all < 64)
    count = rows // tile
    plain = key[...]
    keys = jnp.where(mine_all, plain, key_extra(rows, length, 64 - 64 * head))
    values = jnp.where(mine_all, value[...], jnp.zeros_like(plain))

    def first(t):
        q = kept[pl.ds(t * tile, tile), :]
        grad = ctx_grad[pl.ds(t * tile, tile), :]
        return q, grad, nt(keys, q), nt(values, grad)

    dv_sum = dk_sum = None
    ahead = first(0)
    for t in range(count):
        q, grad, score, prob_back = ahead
        if t + 1 < count:
            ahead = first(t + 1)
        probs = jnp.exp(score)
        product = probs * prob_back
        delta = jnp.sum(product, axis=0, keepdims=True)
        score_back = (product - probs * delta).astype(BF)
        dv_part = nn(probs.astype(BF), grad)
        dk_part = nn(score_back, q)
        dv_sum = dv_part if t == 0 else dv_sum + dv_part
        dk_sum = dk_part if t == 0 else dk_sum + dk_part
        part = pl.ds(t * tile, tile)
        dq[part, :] = jnp.where(mine, (tn(score_back, plain) * 0.125).astype(BF), dq[part, :])
    dk[...] = jnp.where(mine_all, dk_sum.astype(BF), dk[...])
    dv[...] = jnp.where(mine_all, dv_sum.astype(BF), dv[...])


def attend_back_kernel(length, kept, key, value, ctx_grad, dq, dk, dv, *, tile):
    attend_back_pair(length[0], kept, key.at[0], value.at[0], ctx_grad, dq, dk, dv, tile)


def run_attend_back(length, kept, mixed, ctx_grad, tile=128):
    groups, rows, _ = mixed.shape
    pairs = groups // 3
    width = pairs * 128
    spec = pl.BlockSpec((rows, 128), lambda p: (0, p))
    return pl.pallas_call(
        functools.partial(attend_back_kernel, tile=tile),
        grid=(pairs,),
        in_specs=[
            pl.BlockSpec(memory_space=pltpu.SMEM),
            pl.BlockSpec((2, rows, 128), lambda p: (p, 0, 0)),
            pl.BlockSpec((1, rows, 128), lambda p: (pairs + p, 0, 0)),
            pl.BlockSpec((1, rows, 128), lambda p: (2 * pairs + p, 0, 0)),
            spec,
        ],
        out_specs=[spec, spec, spec],
        out_shape=[jax.ShapeDtypeStruct((rows, width), BF)] * 3,
        compiler_params=params(),
        name="attend_back",
    )(length, kept, mixed, mixed, ctx_grad)


def gelu_pair(v):
    cdf = 0.5 * (1.0 + lax.erf(v * 0.7071067811865476))
    return v * cdf, cdf + v * jnp.exp(-0.5 * v * v) * 0.3989422804014327


def feed_start(
    length, context, tokens, marks, vectors, proj, cotangent, middle, normed, bound, out_sum, back_sum, tile
):
    @pl.loop(0, tokens.shape[0] // tile)
    def _(t):
        part = pl.ds(pl.multiple_of(t * tile, tile), tile)
        start = tokens[part, :].astype(F32) + tn(marks[:, part], vectors[...].astype(BF))
        mid = start + nn(context[part, :], proj)
        middle[part, :] = mid
        out_sum[part, :] = jnp.zeros_like(mid)
        back_sum[part, :] = jnp.zeros_like(mid)
        normal, _ = normalise(mid)
        normed[part, :] = (normal * vectors[2:3, :] + vectors[3:4, :]).astype(BF)
        row = t * tile + lax.broadcasted_iota(jnp.int32, (tile, 1), 0)
        kept = jnp.where(row < length, cotangent[part, :].astype(F32), 0.0)
        bound[part, :] = kept.astype(BF)


def feed_chunk(expand, shrink, normed, bound, active, inner_back, out_sum, back_sum, tile, between=None):
    @pl.loop(0, normed.shape[0] // tile // 2)
    def _(pair):
        for k in range(2):
            part = pl.ds(pl.multiple_of((pair * 2 + k) * tile, tile), tile)
            inner = nn(normed[part, :], expand)
            act_back = nt(bound[part, :], shrink)
            act, slope = gelu_pair(inner)
            act = act.astype(BF)
            active[part, :] = act
            back = (act_back * slope).astype(BF)
            inner_back[part, :] = back
            out_sum[part, :] += nn(act, shrink)
            back_sum[part, :] += nt(back, expand)
        if between is not None:

            @pl.when(pair == 0)
            def _():
                between()


def feed_finish(
    vectors, proj, middle, normed, bound, out_sum, back_sum, output, middle_back, ctx_back, gain_grads, tile
):
    gain_grads[...] = jnp.zeros_like(gain_grads)

    @pl.loop(0, middle.shape[0] // tile)
    def _(t):
        part = pl.ds(pl.multiple_of(t * tile, tile), tile)
        mid = middle[part, :]
        output[part, :] = (mid + out_sum[part, :]).astype(BF)
        normal, inverse = normalise(mid)
        grad = back_sum[part, :]
        gain_grads[0:1, :] += jnp.sum(grad * normal, axis=0, keepdims=True)
        gain_grads[1:2, :] += jnp.sum(grad, axis=0, keepdims=True)
        back = bound[part, :].astype(F32) + norm_back(grad, normal, inverse, vectors[2:3, :])
        middle_back[part, :] = back
        low = back.astype(BF)
        normed[part, :] = low
        ctx_back[part, :] = nt(low, proj).astype(BF)


def feed_kernel(
    length, context, tokens, marks, vectors, proj, expand, shrink, cotangent,
    output, middle_back, ctx_back, gain_grads, proj_grad, expand_grad, shrink_grad,
    middle, normed, bound, out_sum, active, inner_back, *, tile
):
    j = pl.program_id(0)

    @pl.when(j == 0)
    def _():
        feed_start(
            length[0], context, tokens, marks, vectors, proj[...], cotangent, middle, normed, bound,
            out_sum, middle_back, tile,
        )

    feed_chunk(
        expand[...], shrink[...], normed, bound, active, inner_back, out_sum, middle_back, tile
    )
    expand_grad[...] = tn(normed[...], inner_back[...])
    shrink_grad[...] = tn(active[...], bound[...])

    @pl.when(j == pl.num_programs(0) - 1)
    def _():
        feed_finish(
            vectors, proj[...], middle, normed, bound, out_sum, middle_back,
            output, middle_back, ctx_back, gain_grads, tile,
        )
        proj_grad[...] = tn(context[...], normed[...])


def run_feed(length, context, tokens, marks, vectors, proj, expand, shrink, cotangent, tile=256):
    rows, width = tokens.shape
    inner = expand.shape[1]
    chunk = width
    wide = pl.BlockSpec((width, chunk), lambda j: (0, j))
    tall = pl.BlockSpec((chunk, width), lambda j: (j, 0))
    return pl.pallas_call(
        functools.partial(feed_kernel, tile=tile),
        grid=(inner // chunk,),
        in_specs=[
            SCALARS, fixed(rows, width), fixed(rows, width), fixed(16, rows), fixed(16, width),
            fixed(width, width), wide, tall, fixed(rows, width),
        ],
        out_specs=[
            fixed(rows, width), fixed(rows, width), fixed(rows, width), fixed(8, width),
            fixed(width, width), wide, tall,
        ],
        out_shape=shapes(
            ((rows, width), BF), ((rows, width), F32), ((rows, width), BF), ((8, width), F32),
            ((width, width), F32), ((width, inner), F32), ((inner, width), F32),
        ),
        scratch_shapes=[
            pltpu.VMEM((rows, width), F32),
            pltpu.VMEM((rows, width), BF),
            pltpu.VMEM((rows, width), BF),
            pltpu.VMEM((rows, width), F32),
            pltpu.VMEM((rows, chunk), BF),
            pltpu.VMEM((rows, chunk), BF),
        ],
        compiler_params=params(),
        name="feed",
    )(length, context, tokens, marks, vectors, proj, expand, shrink, cotangent)


def feed_send_kernel(
    length, context, tokens, marks, vectors, proj, expand, shrink, cotangent,
    output_out, middle_out, ctx_out, gain_grads, proj_box, near_e, near_s, rest_s, got_e, got_s,
    output, middle_back, ctx_back, middle, normed, bound, out_sum, active, inner_back,
    results, box_e, box_s, pair_e, pair_s, out_e, out_s,
    pair_sem, pair_got, first_e_sem, first_e_got, first_s_sem, first_s_got, *, tile
):
    j = pl.program_id(0)
    spot = Spot()
    c = spot.c

    peers = [spot.core, spot.first]
    leaving = [
        pltpu.make_async_copy(src, dst, results.at[k])
        for k, (src, dst) in enumerate(
            ((output, output_out), (middle_back, middle_out), (ctx_back, ctx_out))
        )
    ]

    def pair_copy(step, g):
        slot = step % 2
        src, dst = (box_e, pair_e) if g == 0 else (box_s, pair_s)
        return link(
            src.at[1, slot], dst.at[step], pair_sem.at[g, slot], pair_got.at[g, step], spot.core
        )

    def first_e(p2):
        return link(
            out_e.at[p2], got_e.at[p2], first_e_sem.at[p2], first_e_got.at[p2], spot.first
        )

    def first_s(p2, r):
        return link(
            out_s.at[p2, r], got_s.at[p2, r], first_s_sem.at[p2, r], first_s_got.at[p2, r], spot.first
        )

    def keep_e(step, p2):
        @pl.loop(0, 4)
        def _(r):
            near_e[p2, r] = total_of(box_e[0, step % 2, r], pair_e[step, r]).astype(BF)

    def push_e(step, p2):
        @pl.loop(0, 4)
        def _(r):
            out_e[p2, r] = total_of(box_e[0, step % 2, r], pair_e[step, r]).astype(BF)

        first_e(p2).start()

    def to_first(step):
        slot = step % 2
        pair_copy(step, 0).wait_recv()
        if step == 0:
            push_e(0, 1)
        elif step == 3:
            keep_e(3, 0)
        else:

            @pl.when(c == step - 1)
            def _():
                push_e(step, 0)

            @pl.when(c != step - 1)
            def _():
                keep_e(step, 1)

        pair_copy(step, 1).wait_recv()
        r = spot.rel_z(spot.order[step])
        for p2, q in enumerate((spot.qs[1], spot.qs[3])):
            value = total_of(box_s[0, slot, q], pair_s[step, q]).astype(BF)
            if step < 3:
                out_s[p2, r] = value
                first_s(p2, r).start()
            else:
                rest_s[p2] = value
        for p2, q in enumerate((spot.qs[0], spot.qs[2])):
            near_s[p2, r] = total_of(box_s[0, slot, q], pair_s[step, q]).astype(BF)

    @pl.when(j == 0)
    def _():
        greet(peers)
        feed_start(
            length[0], context, tokens, marks, vectors, rows_of(proj), cotangent,
            middle, normed, bound, out_sum, middle_back, tile,
        )

    def between():
        @pl.when(j == 0)
        def _():
            greeted(peers)

        for step in range(3):

            @pl.when(j == step + 1)
            def _():
                to_first(step)

    feed_chunk(
        rows_of(expand), rows_of(shrink), normed, bound, active, inner_back,
        out_sum, middle_back, tile, between,
    )
    slot = j % 2

    @pl.when(j >= 2)
    def _():
        pair_copy(j - 2, 0).wait_send()
        pair_copy(j - 2, 1).wait_send()

    grad_e = tn(normed[...], inner_back[...])
    for z in range(4):
        r = spot.rel_z(z)
        for cc in range(2):
            piece = grad_e[(2 * z + cc) * 96 : (2 * z + cc + 1) * 96, :]
            box_e[spot.other(cc), slot, r] = piece.astype(BF)
    pair_copy(j, 0).start()
    grad_s = tn(active[...], bound[...])
    for cc in range(2):
        for q in range(4):
            piece = grad_s[(cc * 4 + q) * 96 : (cc * 4 + q + 1) * 96, :]
            box_s[spot.other(cc), slot, q] = piece.astype(BF)
    pair_copy(j, 1).start()

    @pl.when(j == 3)
    def _():
        feed_finish(
            vectors, rows_of(proj), middle, normed, bound, out_sum, middle_back,
            output, middle_back, ctx_back, gain_grads, tile,
        )
        for copy in leaving:
            copy.start()
        grad_p = tn(context[...], normed[...])
        for z in range(4):
            r = spot.rel_z(z)
            for cc in range(2):
                piece = grad_p[(2 * z + cc) * 96 : (2 * z + cc + 1) * 96, :]
                proj_box[spot.other(cc), r] = piece.astype(BF)
        to_first(3)
        for copy in leaving:
            copy.wait()
        for step in (2, 3):
            for g in range(2):
                pair_copy(step, g).wait_send()
        first_e(0).wait_send()
        first_e(1).wait_send()
        first_e(0).wait_recv()
        first_e(1).wait_recv()
        for step in range(3):
            r = spot.rel_z(spot.order[step])
            for p2 in range(2):
                first_s(p2, r).wait_send()
        for p2 in range(2):
            for z in spot.first_order[:3]:
                first_s(p2, spot.rel_z(z)).wait_recv()


def run_feed_send(length, context, tokens, marks, vectors, a_full, b_full, c_full, cotangent, tile=256):
    rows, width = tokens.shape
    block = (96, 768)

    def chunk_at(j):
        dp = lax.axis_index("dp")
        x, y = dp % 2, dp // 2
        turn_x = jnp.where(j < 2, 1, 0)
        turn_y = jnp.where(j % 2 == 0, 1, 0) * jnp.where(j < 3, 1, 0)
        return (y + turn_y - 2 * y * turn_y) * 2 + x + turn_x - 2 * x * turn_x

    return pl.pallas_call(
        functools.partial(feed_send_kernel, tile=tile),
        grid=(4,),
        in_specs=[
            SCALARS, fixed(rows, width), fixed(rows, width), fixed(16, rows), fixed(16, width),
            pl.BlockSpec((1, 4, 2) + block, lambda j: (3, 0, 0, 0, 0), pipeline_mode=pl.Buffered(1)),
            pl.BlockSpec((1, 4, 2) + block, lambda j: (chunk_at(j), 0, 0, 0, 0)),
            pl.BlockSpec((1, 2, 4) + block, lambda j: (chunk_at(j), 0, 0, 0, 0)),
            fixed(rows, width),
        ],
        out_specs=[
            ANYWHERE, ANYWHERE, ANYWHERE, fixed(8, width),
            fixed(2, 4, *block), fixed(2, 4, *block), fixed(2, 4, *block),
            fixed(2, *block), ANYWHERE, ANYWHERE,
        ],
        out_shape=shapes(
            ((rows, width), BF), ((rows, width), F32), ((rows, width), BF), ((8, width), F32),
            *[((2, 4) + block, BF)] * 3,
            ((2,) + block, BF), *[((2, 4) + block, BF)] * 2,
        ),
        scratch_shapes=[
            pltpu.VMEM((rows, width), BF),
            pltpu.VMEM((rows, width), F32),
            pltpu.VMEM((rows, width), BF),
            pltpu.VMEM((rows, width), F32),
            pltpu.VMEM((rows, width), BF),
            pltpu.VMEM((rows, width), BF),
            pltpu.VMEM((rows, width), F32),
            pltpu.VMEM((rows, width), BF),
            pltpu.VMEM((rows, width), BF),
            pltpu.SemaphoreType.DMA((3,)),
            *[pltpu.VMEM((2, 2, 4) + block, BF)] * 2,
            *[pltpu.VMEM((4, 4) + block, BF)] * 2,
            *[pltpu.VMEM((2, 4) + block, BF)] * 2,
            pltpu.SemaphoreType.DMA((2, 2)),
            pltpu.SemaphoreType.DMA((2, 4)),
            pltpu.SemaphoreType.DMA((2,)),
            pltpu.SemaphoreType.DMA((2,)),
            pltpu.SemaphoreType.DMA((2, 4)),
            pltpu.SemaphoreType.DMA((2, 4)),
        ],
        compiler_params=params(collective_id=1, has_side_effects=True),
        name="feed",
    )(length, context, tokens, marks, vectors, a_full, b_full, c_full, cotangent)


def mix_grad_kernel(normed, dq, dk, dv, grad_out):
    j = pl.program_id(0)
    for index, source in enumerate((dq, dk, dv)):

        @pl.when(j == index)
        def _():
            grad_out[...] = tn(normed[...], source[...])


def run_mix_grad(normed, dq, dk, dv):
    rows, width = normed.shape
    return pl.pallas_call(
        mix_grad_kernel,
        grid=(3,),
        in_specs=[fixed(rows, width)] * 4,
        out_specs=pl.BlockSpec((width, width), lambda j: (0, j)),
        out_shape=jax.ShapeDtypeStruct((width, 3 * width), F32),
        compiler_params=params(),
        name="mix_grad",
    )(normed, dq, dk, dv)


def input_part(tokens, marks, vectors, weights, sources, middle_back):
    start = tokens.astype(F32) + tn(marks, vectors.astype(BF))
    normal, inverse = normalise(start)
    grad = nt(sources[0], weights[0])
    for source, weight in zip(sources[1:], weights[1:]):
        grad += nt(source, weight)
    gain = jnp.sum(grad * normal, axis=0, keepdims=True)
    shift = jnp.sum(grad, axis=0, keepdims=True)
    result = middle_back + norm_back(grad, normal, inverse, vectors[0:1, :])
    spread = tn(marks, jnp.ones(vectors.shape, BF))
    mark = jnp.sum(spread * result, axis=0, keepdims=True)
    return result, gain, shift, mark


def input_kernel(tokens, marks, vectors, weight, dq, dk, dv, middle_back, input_grad, sums):
    i = pl.program_id(0)
    width = tokens.shape[1]
    weights = [weight[:, k * width : (k + 1) * width] for k in range(3)]
    result, gain, shift, mark = input_part(
        tokens[...], marks[...], vectors[...], weights, (dq[...], dk[...], dv[...]), middle_back[...]
    )
    input_grad[...] = result
    both = jnp.concatenate([gain, shift, mark, jnp.zeros((5, width), F32)], axis=0)

    @pl.when(i == 0)
    def _():
        sums[...] = both

    @pl.when(i > 0)
    def _():
        sums[...] += both


def run_input(tokens, marks, vectors, weight, dq, dk, dv, middle_back, tile=256):
    rows, width = tokens.shape
    spec = pl.BlockSpec((tile, width), lambda i: (i, 0))
    return pl.pallas_call(
        input_kernel,
        grid=(rows // tile,),
        in_specs=[
            spec,
            pl.BlockSpec((16, tile), lambda i: (0, i)),
            fixed(16, width),
            fixed(width, 3 * width),
            spec,
            spec,
            spec,
            spec,
        ],
        out_specs=[spec, fixed(8, width)],
        out_shape=shapes(((rows, width), F32), ((8, width), F32)),
        compiler_params=params(),
        name="input_grad",
    )(tokens, marks, vectors, weight, dq, dk, dv, middle_back)


BETA = 1.0 - STEP ** (-0.8)


def back_kernel(
    length, row_flag, kept, key, value, ctx_grad, rest_s, marks, vectors, gain2, mix_rows, proj_rows, expand_rows, shrink_rows,
    near_e_in, near_s_in, normed_in, proj_box_in, got_e_in, got_s_in, tokens_in, mix_in, back_in, w_mix_in, w_proj_in, w_expand_in, w_shrink_in,
    input_grad, grads, rows_new, sums_a, sums_b, vector_sum,
    tokens, mix, back, w_mix, w_proj, w_expand, w_shrink, near_e, near_s, normed, proj_box, grads_qkv,
    got, out2b, in2b, out3b, in3b, out4b, in4b, holdb,
    box, pair, out1, in1, out2, in2, out3, in3, out4, in4, hold,
    full_a, full_b, vec_q, vec_f, slots_a, slots_b, gains, columns_old,
    loads, got_sem, late_sent, late_got, sentb, gotb,
    pair_sent, pair_got, sent1, got1, sent, landed, full_sent, full_got,
    vecq_sent, vecq_got, vecf_sent, vecf_got, slot_sent, slot_got, *, tile
):
    step = pl.program_id(0)
    spot = Spot()
    c, dp, fs = spot.c, spot.dp, spot.fs
    trio = (spot.first, spot.second, spot.diag)
    local = [
        pltpu.make_async_copy(src, dst, loads.at[k])
        for k, (src, dst) in enumerate(
            (
                (tokens_in, tokens), (mix_in.at[pl.ds(0, 3)], mix), (back_in, back),
                (w_mix_in, w_mix), (w_proj_in, w_proj), (w_expand_in, w_expand), (w_shrink_in, w_shrink),
            )
        )
    ]

    early = [
        pltpu.make_async_copy(src, dst, loads.at[8 + k])
        for k, (src, dst) in enumerate(
            ((near_e_in, near_e), (near_s_in, near_s), (normed_in, normed), (proj_box_in, proj_box))
        )
    ]

    near = (near_e, near_s)
    load_e = pltpu.make_async_copy(got_e_in, got.at[0], got_sem.at[0])

    def late_s(p2):
        r = spot.rel_z(dp)
        return link(
            rest_s.at[p2], got.at[1, p2, r], late_sent.at[p2], late_got.at[p2], spot.first
        )

    def late_s_came(p2):
        r = spot.rel_z(spot.first_order[3])
        link(
            rest_s.at[p2], got.at[1, p2, r], late_sent.at[p2], late_got.at[p2], spot.first
        ).wait_recv()

    def load_s(k):
        r = spot.rel_z(spot.first_order[k])
        return pltpu.make_async_copy(got_s_in.at[:, r], got.at[1, :, r], got_sem.at[2 + k])

    peers = [spot.core, spot.near, spot.far, (dp, spot.zs[3] * 2 + c), spot.first, spot.second, spot.diag]

    def begin():
        load_e.start()
        early[0].start()
        for k in range(3):
            load_s(k).start()
        greet(peers)
        for copy in early[1:]:
            copy.start()
        for copy in local:
            copy.start()

    def begin_copies():
        greeted(peers)
        for p2 in range(2):
            late_s(p2).start()
        load_e.wait()
        early[0].wait()
        stage2b(0)

    def late():
        for k in range(3):
            load_s(k).wait()
        for p2 in range(2):
            late_s_came(p2)

    def copyb(stage, g):
        src, dst, target = (
            (out2b, in2b, spot.second), (out3b, in3b, spot.near), (out4b, in4b, spot.far),
        )[stage]
        return link(src.at[g], dst.at[g], sentb.at[stage, g], gotb.at[stage, g], target)

    def stage2b(g):
        @pl.loop(0, 4)
        def _(r):
            out2b[g, r] = total_of(near[g][1, r], got[g, 1, r]).astype(BF)

        copyb(0, g).start()

    def stage3b(g):
        copyb(0, g).wait_recv()

        @pl.loop(0, 2)
        def _(r):
            out3b[g, r] = total_of(near[g][0, 2 + r], got[g, 0, 2 + r], in2b[g, 2 + r]).astype(BF)

        copyb(1, g).start()

        @pl.loop(0, 2)
        def _(r):
            holdb[g, r] = total_of(near[g][0, r], got[g, 0, r], in2b[g, r])


    def stage4b(g):
        copyb(1, g).wait_recv()
        out4b[g] = total_of(holdb[g, 1], in3b[g, 1]).astype(BF)
        copyb(2, g).start()
        holdb[g, 0] = total_of(holdb[g, 0], in3b[g, 0])

    def stage5b(g):
        copyb(2, g).wait_recv()
        full_b[g, dp] = total_of(holdb[g, 0], in4b[g]).astype(BF)
        for k in range(3):
            share_b(g, k).start()

    def share_b(g, k):
        place = full_b.at[g, dp]
        return link(place, place, full_sent.at[g, k], full_got.at[g, dp], trio[k])

    def share_a(h, k):
        place = full_a.at[dp, h]
        return link(place, place, full_sent.at[2 + h, k], full_got.at[2 + h, dp], trio[k])

    def shared_b(g):
        for q in spot.qs[1:]:
            place = full_b.at[g, q]
            link(place, place, full_sent.at[g, 0], full_got.at[g, q], spot.first).wait_recv()

    def shared_a(h):
        for q in spot.qs[1:]:
            place = full_a.at[q, h]
            link(place, place, full_sent.at[2 + h, 0], full_got.at[2 + h, q], spot.first).wait_recv()

    def pair_copy(h, q):
        return link(
            box.at[1, h, q], pair.at[h, q], pair_sent.at[h, q], pair_got.at[h, q], spot.core
        )

    def first_copy(h, p2):
        return link(
            out1.at[h, p2], in1.at[h, p2], sent1.at[h, p2], got1.at[h, p2], spot.first
        )

    def copy(stage, h):
        src, dst, target = (
            (out2, in2, spot.second), (out3, in3, spot.near), (out4, in4, spot.far),
        )[stage]
        return link(src.at[h], dst.at[h], sent.at[stage, h], landed.at[stage, h], target)

    def third_grad(h):
        @pl.loop(0, 4)
        def _(r):
            for side in range(2):
                for k in range(3):

                    @pl.when(h == k)
                    def _():
                        box[side, h, 3, r] = proj_box[side, r, :, k * 256 : (k + 1) * 256]

        pair_copy(h, 3).start()

        columns = pl.ds(pl.multiple_of(h * 256, 256), 256)
        sources = jnp.concatenate([grads_qkv[q, :, columns] for q in range(3)], axis=1)
        grad = tn(normed[...], sources)
        for q in range(3):
            for z in range(4):
                r = spot.rel_z(z)
                for cc in range(2):
                    piece = grad[(2 * z + cc) * 96 : (2 * z + cc + 1) * 96, q * 256 : (q + 1) * 256]
                    box[spot.other(cc), h, q, r] = piece.astype(BF)
            pair_copy(h, q).start()

    def stage1(h):
        for p2, q in enumerate((spot.qs[1], spot.qs[3])):
            pair_copy(h, q).wait_recv()

            @pl.loop(0, 4)
            def _(r):
                out1[h, p2, r] = total_of(box[0, h, q, r], pair[h, q, r]).astype(BF)

            first_copy(h, p2).start()

    def stage2(h):
        q = spot.qs[2]
        pair_copy(h, q).wait_recv()
        first_copy(h, 1).wait_recv()

        @pl.loop(0, 4)
        def _(r):
            out2[h, r] = total_of(box[0, h, q, r], pair[h, q, r], in1[h, 1, r]).astype(BF)

        copy(0, h).start()

    def stage3(h):
        pair_copy(h, dp).wait_recv()
        first_copy(h, 0).wait_recv()
        copy(0, h).wait_recv()

        @pl.loop(0, 2)
        def _(r):
            value = total_of(box[0, h, dp, 2 + r], pair[h, dp, 2 + r], in1[h, 0, 2 + r], in2[h, 2 + r])
            out3[h, r] = value.astype(BF)

        copy(1, h).start()

        @pl.loop(0, 2)
        def _(r):
            hold[h, r] = total_of(box[0, h, dp, r], pair[h, dp, r], in1[h, 0, r], in2[h, r])


    def stage4(h):
        copy(1, h).wait_recv()
        out4[h] = total_of(hold[h, 1], in3[h, 1]).astype(BF)
        copy(2, h).start()
        hold[h, 0] = total_of(hold[h, 0], in3[h, 0])

    def stage5(h):
        copy(2, h).wait_recv()
        full_a[dp, h] = total_of(hold[h, 0], in4[h]).astype(BF)
        for k in range(3):
            share_a(h, k).start()

    def input_rows(t):
        weights = [rows_of(mix.at[k]) for k in range(3)]
        part = pl.ds(pl.multiple_of(t * 256, 256), 256)
        result, gain, shift, mark = input_part(
            tokens[part, :], marks[:, part], vectors[...], weights,
            [grads_qkv[k, part, :] for k in range(3)], back[part, :],
        )
        back[part, :] = result
        gains[0:1, :] += gain
        gains[1:2, :] += shift
        gains[2:3, :] += mark

    column = (spot.near, spot.far, (dp, spot.zs[3] * 2 + c))
    result_copy = pltpu.make_async_copy(back, input_grad, loads.at[7])

    def vecq_copy(k):
        place = vec_q.at[dp]
        return link(place, place, vecq_sent.at[k], vecq_got.at[dp], trio[k])

    def vec_pair():
        place = vec_f.at[4 + c]
        return link(place, place, vecf_sent.at[3], vecf_got.at[4 + c], spot.core)

    def vecf_copy(k):
        place = vec_f.at[spot.z]
        return link(place, place, vecf_sent.at[k], vecf_got.at[spot.z], column[k])

    def vec_first():
        gain, shift, mark = (gains[k : k + 1, :] for k in range(3))
        flag = (row_flag[0] == 1).astype(F32)
        vec_q[dp] = jnp.concatenate(
            [
                gain, shift, gain2[0:2, :], mark * (1.0 - flag), mark * flag,
                jnp.zeros((2, 768), F32),
            ],
            axis=0,
        )
        for k in range(3):
            vecq_copy(k).start()

    def vec_second():
        for q in spot.qs[1:]:
            place = vec_q.at[q]
            link(place, place, vecq_sent.at[0], vecq_got.at[q], spot.first).wait_recv()
        vec_f[4 + c] = vec_q[0] + vec_q[1] + vec_q[2] + vec_q[3]
        vec_pair().start()

    def vec_spread():
        place = vec_f.at[5 - c]
        link(place, place, vecf_sent.at[3], vecf_got.at[5 - c], spot.core).wait_recv()
        vec_f[spot.z] = vec_f[4] + vec_f[5]
        for k in range(3):
            vecf_copy(k).start()

    def vec_third():
        for k in range(1, 4):
            other = spot.zs[k]
            place = vec_f.at[other]
            link(place, place, vecf_sent.at[0], vecf_got.at[other], spot.near).wait_recv()
        vector_sum[...] = vec_f[0] + vec_f[1] + vec_f[2] + vec_f[3]

    def turn_rows():
        lines = [ref[...].reshape(1, 96) for ref in (mix_rows, proj_rows, expand_rows)]
        tall = shrink_rows[...].reshape(1, 384)
        lines += [tall[:, 96 * k : 96 * (k + 1)] for k in range(4)]
        columns_old[0:96, 0:8] = jnp.concatenate(lines + lines[:1], axis=0).T
        for k in range(3, 7):
            local[k].wait()
        squares = [square_sum(w) for w in (w_mix, w_proj, w_expand, w_shrink)]
        columns_old[96:104, 0:1] = jnp.concatenate(squares + squares, axis=0)

    def old_row(index):
        return columns_old[0:96, index : index + 1]

    def wide_stats(blocks, index):
        squares = [b * b for b in blocks]
        total = jnp.sum(squares[0] + 1e-30, axis=1, keepdims=True)
        for square in squares[1:]:
            total = total + jnp.sum(square + 1e-30, axis=1, keepdims=True)
        row = BETA * old_row(index) + (1.0 - BETA) * (total / (768.0 * len(blocks)))
        rows_new[index] = jnp.broadcast_to(row, (96, 128))
        inverse = 1.0 / row
        cols = [jnp.sum(square + 1e-30, axis=0, keepdims=True) for square in squares]
        scaled = [jnp.sum(square * inverse, axis=0, keepdims=True) for square in squares]
        return jnp.sum(row, axis=0, keepdims=True), cols, scaled

    def square_sum(ref):
        value = ref[...]
        return jnp.sum(jnp.sum(value * value, axis=0, keepdims=True), axis=1, keepdims=True)

    def tiles(value):
        return [value[:, 128 * k : 128 * (k + 1)] for k in range(6)]

    def scalar_tile(values):
        column = jnp.concatenate(values + [jnp.zeros((8 - len(values), 1), F32)], axis=0)
        return jnp.broadcast_to(column, (8, 128))

    def slot_pair(kind):
        slots = (slots_a, slots_b)[kind]
        return link(
            slots.at[4 + c], slots.at[4 + c], slot_sent.at[kind, 3], slot_got.at[kind, 4 + c], spot.core
        )

    def slot_copy(kind, k):
        place = (slots_a, slots_b)[kind].at[spot.z]
        return link(place, place, slot_sent.at[kind, k], slot_got.at[kind, spot.z], column[k])

    def slot_spread(kind):
        slots = (slots_a, slots_b)[kind]
        link(
            slots.at[5 - c], slots.at[5 - c], slot_sent.at[kind, 3], slot_got.at[kind, 5 - c], spot.core
        ).wait_recv()
        slots[spot.z] = slots[4] + slots[5]
        for k in range(3):
            slot_copy(kind, k).start()

    def slot_sum(kind, out):
        slots = (slots_a, slots_b)[kind]
        for k in range(1, 4):
            other = spot.zs[k]
            place = slots.at[other]
            link(place, place, slot_sent.at[kind, 0], slot_got.at[kind, other], spot.near).wait_recv()
        out[...] = slots[0] + slots[1] + slots[2] + slots[3]

    def stats_b():
        shared_b(0)
        shared_b(1)
        for g in range(2):
            for q in range(4):
                grads[1 + g, q] = full_b[g, q]
        blocks = [full_b[0, q].astype(F32) for q in range(4)]
        total, cols, scaled = wide_stats(blocks, 2)
        total_s, cols_s, scaled_s = None, None, None
        for q in range(4):
            t, col, sc = wide_stats([full_b[1, q].astype(F32)], 3 + q)
            total_s = t if q == 0 else total_s + t
            cols_s = col[0] if q == 0 else cols_s + col[0]
            scaled_s = sc[0] if q == 0 else scaled_s + sc[0]
        slots_b[4 + c] = jnp.concatenate(
            tiles(jnp.concatenate(cols + scaled, axis=0))
            + tiles(jnp.concatenate([cols_s, scaled_s], axis=0))
            + [jnp.zeros((4, 128), F32)]
            + [
                scalar_tile([total, total_s, columns_old[98:99, 0:1], columns_old[99:100, 0:1]])
            ],
            axis=0,
        )
        slot_pair(1).start()

    def stats_a():
        blocks = [
            jnp.concatenate([full_a[q, h] for h in range(3)], axis=1) for q in range(4)
        ]
        for q in range(4):
            grads[0, q] = blocks[q]
        blocks = [b.astype(F32) for b in blocks]
        total, cols, scaled = wide_stats(blocks[:3], 0)
        total_p, cols_p, scaled_p = wide_stats(blocks[3:], 1)
        slots_a[4 + c] = jnp.concatenate(
            tiles(jnp.concatenate(cols + cols_p + scaled + scaled_p, axis=0))
            + [
                scalar_tile([total, total_p, columns_old[96:97, 0:1], columns_old[97:98, 0:1]])
            ],
            axis=0,
        )
        slot_pair(0).start()

    @pl.when(step == 0)
    def _():
        begin()

    @pl.when(step < 12)
    def _():
        columns = pl.ds(pl.multiple_of(step // 2 * 128, 128), 128)
        attend_back_head(
            length[0], step % 2, kept.at[0], key.at[0], value.at[0], ctx_grad,
            grads_qkv.at[0, :, columns], grads_qkv.at[1, :, columns], grads_qkv.at[2, :, columns], tile,
        )

    @pl.when(step == 0)
    def _():
        begin_copies()
        gains[...] = jnp.zeros((8, 768), F32)

    @pl.when(step == 1)
    def _():
        late()
        for copy in early[1:]:
            copy.wait()
        stage2b(1)

    @pl.when(step == 11)
    def _():
        stage5(0)

    @pl.when((step == 3) | (step == 7) | (step == 11))
    def _():
        third_grad(step // 4)

    for at, stage, g in (
        (2, stage3b, 0), (4, stage3b, 1), (5, stage4b, 0), (7, stage4b, 1), (7, stage5b, 0), (9, stage5b, 1),
    ):

        @pl.when(step == at)
        def _():
            stage(g)

    @pl.when((step == 4) | (step == 8))
    def _():
        stage1(step // 4 - 1)

    @pl.when((step == 6) | (step == 11))
    def _():
        stage2(step // 8)

    @pl.when(step == 8)
    def _():
        stage3(0)

    @pl.when(step == 10)
    def _():
        stage4(0)

    @pl.when(step == 9)
    def _():
        turn_rows()

    @pl.when(step == 12)
    def _():
        stage1(2)
        for k in range(3):
            local[k].wait()

        @pl.loop(0, 4)
        def _(t):
            input_rows(t)

            @pl.when(t == 0)
            def _():
                stage3(1)

            @pl.when(t == 1)
            def _():
                stage2(2)

            @pl.when(t == 2)
            def _():
                stage4(1)
                stage3(2)

        result_copy.start()
        vec_first()
        stage4(2)
        stage5(1)
        stats_b()
        stage5(2)
        vec_second()
        slot_spread(1)
        for h in range(3):
            shared_a(h)
        stats_a()
        vec_spread()
        slot_sum(1, sums_b)
        slot_spread(0)
        for p2 in range(2):
            late_s(p2).wait_send()
        for g in range(2):
            for k in range(3):
                share_b(g, k).wait_send()
            for stage in range(3):
                copyb(stage, g).wait_send()

        @pl.loop(0, 3)
        def _(h):
            for k in range(3):
                share_a(h, k).wait_send()
            for q in range(4):
                pair_copy(h, q).wait_send()
            for p2 in range(2):
                first_copy(h, p2).wait_send()
            for stage in range(3):
                copy(stage, h).wait_send()

        for k in range(3):
            vecq_copy(k).wait_send()
        vec_pair().wait_send()
        for k in range(3):
            vecf_copy(k).wait_send()
        result_copy.wait()
        vec_third()
        slot_sum(0, sums_a)
        for kind in range(2):
            slot_pair(kind).wait_send()
            for k in range(3):
                slot_copy(kind, k).wait_send()


def run_back(length, row_flag, kept, mixed, ctx_grad, rest_s, near_e, near_s, normed, proj_box,
             marks, vectors, gain2, mix_rows, proj_rows, expand_rows, shrink_rows, got_e, got_s, tokens, a_full, middle_back,
             w_mix, w_proj, w_expand, w_shrink, tile=128):
    rows, width = normed.shape
    third = (96, 256)
    block = (96, 768)
    sem = pltpu.SemaphoreType.DMA

    def at(p):
        return jnp.minimum(p, 11)

    return pl.pallas_call(
        functools.partial(back_kernel, tile=tile),
        grid=(13,),
        in_specs=[
            SCALARS,
            SCALARS,
            pl.BlockSpec((1, rows, 128), lambda p: (at(p), 0, 0)),
            pl.BlockSpec((1, rows, 128), lambda p: (6 + at(p) // 2, 0, 0)),
            pl.BlockSpec((1, rows, 128), lambda p: (12 + at(p) // 2, 0, 0)),
            pl.BlockSpec((rows, 128), lambda p: (0, at(p) // 2)),
            fixed(2, *block), fixed(16, rows), fixed(16, width), fixed(8, width),
            fixed(96), fixed(96), fixed(96), fixed(384),
            *[ANYWHERE] * 13,
        ],
        out_specs=[
            ANYWHERE, fixed(3, 4, *block), fixed(7, 96, 128), fixed(56, 128), fixed(72, 128),
            fixed(8, width),
        ],
        out_shape=shapes(
            ((rows, width), F32), ((3, 4) + block, BF), ((7, 96, 128), F32),
            ((56, 128), F32), ((72, 128), F32), ((8, width), F32),
        ),
        scratch_shapes=[
            pltpu.VMEM((rows, width), BF),
            pltpu.VMEM((3, 4, 2) + block, BF),
            pltpu.VMEM((rows, width), F32),
            pltpu.VMEM(w_mix.shape, F32),
            pltpu.VMEM(w_proj.shape, F32),
            pltpu.VMEM(w_expand.shape, F32),
            pltpu.VMEM(w_shrink.shape, F32),
            *[pltpu.VMEM((2, 4) + block, BF)] * 2,
            pltpu.VMEM((rows, width), BF),
            pltpu.VMEM((2, 4) + block, BF),
            pltpu.VMEM((3, rows, width), BF),
            pltpu.VMEM((2, 2, 4) + block, BF),
            *[pltpu.VMEM((2, 4) + block, BF)] * 2,
            *[pltpu.VMEM((2, 2) + block, BF)] * 2,
            *[pltpu.VMEM((2,) + block, BF)] * 2,
            pltpu.VMEM((2, 2) + block, F32),
            pltpu.VMEM((2, 3, 4, 4) + third, BF),
            pltpu.VMEM((3, 4, 4) + third, BF),
            *[pltpu.VMEM((3, 2, 4) + third, BF)] * 2,
            *[pltpu.VMEM((3, 4) + third, BF)] * 2,
            *[pltpu.VMEM((3, 2) + third, BF)] * 2,
            *[pltpu.VMEM((3,) + third, BF)] * 2,
            pltpu.VMEM((3, 2) + third, F32),
            pltpu.VMEM((4, 3) + third, BF),
            pltpu.VMEM((2, 4) + block, BF),
            pltpu.VMEM((4, 8, 768), F32),
            pltpu.VMEM((6, 8, 768), F32),
            pltpu.VMEM((6, 56, 128), F32),
            pltpu.VMEM((6, 72, 128), F32),
            pltpu.VMEM((8, 768), F32),
            pltpu.VMEM((104, 128), F32),
            sem((12,)), sem((5,)), sem((2,)), sem((2,)), sem((3, 2)), sem((3, 2)),
            sem((3, 4)), sem((3, 4)), sem((3, 2)), sem((3, 2)), sem((3, 3)), sem((3, 3)),
            sem((5, 3)), sem((5, 4)),
            sem((3,)), sem((4,)), sem((4,)), sem((6,)), sem((2, 4)), sem((2, 6)),
        ],
        compiler_params=params(collective_id=2, has_side_effects=True),
        name="back",
    )(length, row_flag, kept, mixed, mixed, ctx_grad, rest_s, marks, vectors, gain2, mix_rows, proj_rows, expand_rows, shrink_rows, near_e, near_s, normed, proj_box,
      got_e, got_s, tokens, a_full, middle_back, w_mix, w_proj, w_expand, w_shrink)


def step_kernel(
    grad_a, grad_e, grad_s, w_mix, w_proj, w_expand, w_shrink, rows,
    mix_cols, proj_cols, expand_cols, shrink_cols, sums_a, sums_b, vector_sum, old, vectors, moment,
    output_in, input_grad_in,
    mix_grad, proj_grad, expand_grad, shrink_grad, mix_new, proj_new, expand_new, shrink_new,
    mix_rows_new, proj_rows_new, expand_rows_new, shrink_rows_new,
    mix_cols_new, proj_cols_new, expand_cols_new, shrink_cols_new,
    vector_grad, vector_new, moment_new, output, input_grad, cols_new, *, owners
):
    q = pl.program_id(0)
    height = 96.0 * owners
    output[...] = output_in[...]
    input_grad[...] = input_grad_in[...]

    def wide(ref, at, row, count, of):
        return jnp.concatenate(
            [ref[at + of * k + row : at + of * k + row + count, :] for k in range(6)], axis=1
        )

    def one(ref, at, k):
        return ref[at + k : at + k + 1, 0:1]

    @pl.when(q == 0)
    def _():
        def lines(ref, count):
            value = ref[...].reshape(1, 768 * count)
            return [value[:, 768 * k : 768 * (k + 1)] for k in range(count)]

        def flat(first, count):
            value = jnp.concatenate([cols_new[k : k + 1, :] for k in range(first, first + count)], axis=1)
            return value.reshape(768 * count)

        parts = [wide(sums_a, 0, 0, 4, 8), wide(sums_b, 0, 0, 4, 8)]
        before = lines(mix_cols, 3) + lines(proj_cols, 1) + lines(expand_cols, 4)
        cols_new[0:8, :] = BETA * jnp.concatenate(before, axis=0) + (1.0 - BETA) * (
            jnp.concatenate(parts, axis=0) / height
        )
        tall = BETA * lines(shrink_cols, 1)[0] + (1.0 - BETA) * (
            wide(sums_b, 48, 0, 1, 2) / (4.0 * height)
        )
        cols_new[8:16, :] = jnp.broadcast_to(tall, (8, 768))
        mix_cols_new[...] = flat(0, 3)
        proj_cols_new[...] = flat(3, 1)
        expand_cols_new[...] = flat(4, 4)
        shrink_cols_new[...] = flat(8, 1)
        turned = [rows[k].T[0:1, :] for k in range(7)]
        mix_rows_new[...] = turned[0].reshape(96)
        proj_rows_new[...] = turned[1].reshape(96)
        expand_rows_new[...] = turned[2].reshape(96)
        shrink_rows_new[...] = jnp.concatenate(turned[3:], axis=1).reshape(384)
        fs = lax.axis_index("fsdp")
        grads = vector_sum[...]
        steps, squares = 0.0, 0.0
        for owner in range(8):
            part = pltpu.roll(grads, (768 - 96 * owner) % 768, 1)[0:6, 0:96]
            change = part * lax.rsqrt(
                BETA * old[owner, 8:14, 0:96] + (1.0 - BETA) * (part * part + 1e-30)
            )
            steps += jnp.sum(change * change, axis=1, keepdims=True)
            plain = old[owner, 0:6, 0:96]
            squares += jnp.sum(plain * plain, axis=1, keepdims=True)
        grad = pltpu.roll(grads, (768 - 96 * fs) % 768, 1)[0:6, 0:96]
        vector_grad[...] = grad
        new = BETA * moment[...] + (1.0 - BETA) * (grad * grad + 1e-30)
        moment_new[...] = new
        clip = jnp.maximum(1.0, jnp.sqrt(steps / 768.0) / CLIP)
        rate = RATE * jnp.maximum(0.001, jnp.sqrt(squares / 768.0))
        vector_new[...] = vectors[...] - rate * ((grad * lax.rsqrt(new)) / clip)

    def update(grad, weight, row, col, scaled, all_cols, row_total, square, count, across):
        row_mean = row_total / count
        entries = count * across
        update_square = row_mean * jnp.sum(
            jnp.sum(scaled / all_cols, axis=1, keepdims=True), axis=0, keepdims=True
        )
        clip = jnp.maximum(1.0, jnp.sqrt(update_square / entries) / CLIP)
        rate = RATE * jnp.maximum(0.001, jnp.sqrt(square / entries))
        factor = rate / clip
        return weight - factor * (grad * lax.rsqrt(row * (col / row_mean)))

    a = grad_a[0, 0].astype(F32)
    col = cols_new[pl.ds(q, 1), :]

    @pl.when(q < 3)
    def _():
        mix_grad[...] = a
        mix_new[...] = update(
            a, w_mix[...], rows[0][:, 0:1], col, wide(sums_a, 0, 4, 3, 8), cols_new[0:3, :],
            one(sums_a, 48, 0), one(sums_a, 48, 2), height, 2304.0,
        )

    @pl.when(q == 3)
    def _():
        proj_grad[...] = a
        proj_new[...] = update(
            a, w_proj[...], rows[1][:, 0:1], col, wide(sums_a, 0, 7, 1, 8), cols_new[3:4, :],
            one(sums_a, 48, 1), one(sums_a, 48, 3), height, 768.0,
        )

    e = grad_e[0, 0].astype(F32)
    expand_grad[...] = e
    expand_new[...] = update(
        e, w_expand[...], rows[2][:, 0:1], cols_new[pl.ds(4 + q, 1), :], wide(sums_b, 0, 4, 4, 8), cols_new[4:8, :],
        one(sums_b, 64, 0), one(sums_b, 64, 2), height, 3072.0,
    )
    t = grad_s[0, 0].astype(F32)
    shrink_grad[...] = t
    shrink_new[...] = update(
        t, w_shrink[...], rows[3 + q][:, 0:1], cols_new[8:9, :], wide(sums_b, 48, 1, 1, 2), cols_new[8:9, :],
        one(sums_b, 64, 1), one(sums_b, 64, 3), 4.0 * height, 768.0,
    )

def run_step(grads, w_mix, w_proj, w_expand, w_shrink, rows, mix_cols, proj_cols, expand_cols, shrink_cols,
             sums_a, sums_b, vector_sum, old, vectors, moment, output, input_grad, owners):
    block = (96, 768)
    wide = pl.BlockSpec(block, lambda q: (0, q))
    three = pl.BlockSpec(block, lambda q: (0, jnp.minimum(q, 2)))
    tall = pl.BlockSpec(block, lambda q: (q, 0))
    part = pl.BlockSpec((output.shape[0] // 4, 768), lambda q: (q, 0))
    return pl.pallas_call(
        functools.partial(step_kernel, owners=owners),
        grid=(4,),
        in_specs=[
            pl.BlockSpec((1, 1) + block, lambda q: (0, q, 0, 0)),
            pl.BlockSpec((1, 1) + block, lambda q: (1, q, 0, 0)),
            pl.BlockSpec((1, 1) + block, lambda q: (2, q, 0, 0)),
            three, fixed(*block), wide, tall,
            fixed(7, 96, 128), fixed(2304), fixed(768), fixed(3072), fixed(768),
            fixed(56, 128), fixed(72, 128), fixed(8, 768), fixed(8, 16, 128), fixed(6, 96), fixed(6, 96),
            part, part,
        ],
        out_specs=[
            three, fixed(*block), wide, tall, three, fixed(*block), wide, tall,
            fixed(96), fixed(96), fixed(96), fixed(384), fixed(2304), fixed(768), fixed(3072), fixed(768),
            fixed(6, 96), fixed(6, 96), fixed(6, 96), part, part,
        ],
        out_shape=shapes(
            *[(w.shape, F32) for w in (w_mix, w_proj, w_expand, w_shrink)] * 2,
            *[((n,), F32) for n in (96, 96, 96, 384, 2304, 768, 3072, 768)],
            *[((6, 96), F32)] * 3, (output.shape, BF), (input_grad.shape, F32),
        ),
        scratch_shapes=[pltpu.VMEM((16, 768), F32)],
        compiler_params=params(),
        name="step",
    )(grads, grads, grads, w_mix, w_proj, w_expand, w_shrink, rows, mix_cols, proj_cols, expand_cols,
      shrink_cols, sums_a, sums_b, vector_sum, old, vectors, moment, output, input_grad)


def masks(row_flag, sentence_mask, token_mask, lengths):
    length = sentence_mask.shape[1]
    valid = (lax.broadcasted_iota(jnp.int32, (1, length), 1) < lengths[:, None]).astype(jnp.int32)
    is_token = (row_flag == 1).astype(jnp.int32)[:, None]
    return jnp.concatenate(
        [
            jnp.zeros((4, length), jnp.int32),
            sentence_mask * valid * (1 - is_token),
            token_mask * valid * is_token,
            jnp.zeros((10, length), jnp.int32),
        ]
    ).astype(BF)


def staged_body(
    tokens, cotangent, row_flag, sentence_mask, token_mask, lengths,
    mix_weight, proj_weight, expand_weight, shrink_weight, norm_vectors,
    mix_rows, proj_rows, expand_rows, shrink_rows,
    mix_cols, proj_cols, expand_cols, shrink_cols, vector_moment,
):
    length, width = tokens.shape[1:]
    tokens = tokens.reshape(length, width)
    cotangent = cotangent.reshape(length, width)
    owners = lax.axis_size("fsdp")
    a_full, b_full, c_full, vectors, old, marks, normed, mixed, context, kept = run_front(
        lengths, row_flag, tokens, sentence_mask, token_mask, norm_vectors, vector_moment,
        mix_weight, proj_weight, expand_weight, shrink_weight,
    )
    (block_output, middle_back, ctx_back, gain2, proj_box,
     near_e, near_s, rest_s, got_e, got_s) = run_feed_send(
        lengths, context, tokens, marks, vectors, a_full, b_full, c_full, cotangent
    )
    input_grad, grads, rows, sums_a, sums_b, vector_sum = run_back(
        lengths, row_flag, kept, mixed, ctx_back, rest_s, near_e, near_s, normed, proj_box,
        marks, vectors, gain2, mix_rows, proj_rows, expand_rows, shrink_rows,
        got_e, got_s, tokens, a_full, middle_back, mix_weight, proj_weight, expand_weight, shrink_weight,
    )
    (mix_grad, proj_grad, expand_grad, shrink_grad, mix_new, proj_new, expand_new, shrink_new,
     *statistics, vector_grad, vector_new, moment_new, block_output, input_grad) = run_step(
        grads, mix_weight, proj_weight, expand_weight, shrink_weight, rows,
        mix_cols, proj_cols, expand_cols, shrink_cols, sums_a, sums_b, vector_sum, old,
        norm_vectors, vector_moment, block_output, input_grad, owners,
    )
    return (
        block_output.reshape(1, length, width),
        input_grad.reshape(1, length, width),
        mix_grad, proj_grad, expand_grad, shrink_grad, vector_grad,
        mix_new, proj_new, expand_new, shrink_new, vector_new, *statistics, moment_new,
    )


def plain_body(
    tokens, cotangent, row_flag, sentence_mask, token_mask, lengths,
    mix_weight, proj_weight, expand_weight, shrink_weight, norm_vectors,
    mix_rows, proj_rows, expand_rows, shrink_rows,
    mix_cols, proj_cols, expand_cols, shrink_cols, vector_moment,
):
    length, width = tokens.shape[1:]
    tokens = tokens.reshape(length, width)
    cotangent = cotangent.reshape(length, width)
    owners = lax.axis_size("fsdp")
    marks = masks(row_flag, sentence_mask, token_mask, lengths)
    is_token = (row_flag == 1).astype(F32)[:, None]
    mix_full = lax.all_gather(mix_weight.astype(BF), "fsdp", axis=0, tiled=True)
    proj_full = lax.all_gather(proj_weight.astype(BF), "fsdp", axis=0, tiled=True)
    expand_full = lax.all_gather(expand_weight.astype(BF), "fsdp", axis=0, tiled=True)
    shrink_full = lax.all_gather(shrink_weight.astype(BF), "fsdp", axis=0, tiled=True)
    vectors = lax.all_gather(norm_vectors.astype(BF), "fsdp", axis=1, tiled=True).astype(F32)
    vectors = jnp.concatenate([vectors, jnp.zeros((10, width), F32)])
    normed, mixed = run_mixed(tokens, marks, vectors, mix_full)
    context, kept = run_attend(lengths, mixed)
    block_output, middle_back, ctx_back, gain2, proj_local, expand_local, shrink_local = run_feed(
        lengths, context, tokens, marks, vectors, proj_full, expand_full, shrink_full, cotangent
    )
    dq, dk, dv = run_attend_back(lengths, kept, mixed, ctx_back)
    mix_local = run_mix_grad(normed, dq, dk, dv)
    input_grad, gain1 = run_input(tokens, marks, vectors, mix_full, dq, dk, dv, middle_back)
    vector_local = jnp.concatenate(
        [gain1[0:2], gain2[0:2], gain1[2:3] * (1.0 - is_token), gain1[2:3] * is_token]
    )
    local = (mix_local, proj_local, expand_local, shrink_local)
    shards = [lax.psum_scatter(g, "fsdp", scatter_dimension=0, tiled=True) for g in local]
    shards.append(lax.psum_scatter(vector_local, "fsdp", scatter_dimension=1, tiled=True))
    mix_grad, proj_grad, expand_grad, shrink_grad, vector_grad = lax.psum(tuple(shards), "dp")

    grads = (mix_grad, proj_grad, expand_grad, shrink_grad)
    weights = (mix_weight, proj_weight, expand_weight, shrink_weight)
    old_rows = (mix_rows, proj_rows, expand_rows, shrink_rows)
    old_cols = (mix_cols, proj_cols, expand_cols, shrink_cols)
    rows_new, col_parts, scaled_parts = [], [], []
    for g, r in zip(grads, old_rows):
        square = g * g + 1e-30
        row = BETA * r + (1.0 - BETA) * jnp.mean(square, axis=1)
        rows_new.append(row)
        col_parts.append(jnp.sum(square, axis=0))
        scaled_parts.append(jnp.sum(g * g * (1.0 / row)[:, None], axis=0))
    moment_new = BETA * vector_moment + (1.0 - BETA) * (vector_grad * vector_grad + 1e-30)
    vector_step = vector_grad * lax.rsqrt(moment_new)
    small = jnp.concatenate(
        [
            jnp.stack([jnp.sum(r) for r in rows_new]),
            jnp.stack([jnp.sum(w * w) for w in weights]),
            jnp.sum(vector_step * vector_step, axis=1),
            jnp.sum(norm_vectors * norm_vectors, axis=1),
        ]
    )
    packed = lax.psum(jnp.concatenate(col_parts + scaled_parts + [small]), "fsdp")
    offset = 0
    total_cols = sum(col.shape[0] for col in old_cols)
    small = packed[2 * total_cols :]
    cols_new, new_weights = [], []
    for index in range(4):
        count = grads[index].shape[0] * owners
        wide = old_cols[index].shape[0]
        entries = count * wide
        col = BETA * old_cols[index] + (1.0 - BETA) * packed[offset : offset + wide] / count
        scaled = packed[total_cols + offset : total_cols + offset + wide]
        offset += wide
        cols_new.append(col)
        row_mean = small[index] / count
        update_square = row_mean * jnp.sum(scaled / col)
        clip_factor = jnp.maximum(1.0, jnp.sqrt(update_square / entries) / CLIP)
        rate = RATE * jnp.maximum(0.001, jnp.sqrt(small[4 + index] / entries))
        approx = rows_new[index][:, None] * col[None, :] / row_mean
        step = grads[index] * lax.rsqrt(approx)
        new_weights.append(weights[index] - (rate / clip_factor) * step)
    vector_clip = jnp.maximum(1.0, jnp.sqrt(small[8:14] / width) / CLIP)
    vector_rate = RATE * jnp.maximum(0.001, jnp.sqrt(small[14:20] / width))
    vector_new = norm_vectors - vector_rate[:, None] * (vector_step / vector_clip[:, None])
    return (
        block_output.reshape(1, length, width),
        input_grad.reshape(1, length, width),
        mix_grad, proj_grad, expand_grad, shrink_grad, vector_grad,
        *new_weights, vector_new, *rows_new, *cols_new, moment_new,
    )


def solution(mesh):
    sequence = P(AXES, None, None)
    ins = (
        sequence, sequence, P(AXES), P(AXES, None), P(AXES, None), P(AXES),
        P("fsdp", None), P("fsdp", None), P("fsdp", None), P("fsdp", None), P(None, "fsdp"),
        P("fsdp"), P("fsdp"), P("fsdp"), P("fsdp"), P(), P(), P(), P(), P(None, "fsdp"),
    )
    outs = (
        sequence, sequence,
        P("fsdp", None), P("fsdp", None), P("fsdp", None), P("fsdp", None), P(None, "fsdp"),
        P("fsdp", None), P("fsdp", None), P("fsdp", None), P("fsdp", None), P(None, "fsdp"),
        P("fsdp"), P("fsdp"), P("fsdp"), P("fsdp"), P(), P(), P(), P(), P(None, "fsdp"),
    )
    staged = (mesh.shape["dp"], mesh.shape["fsdp"]) == (4, 8)
    body = staged_body if staged else plain_body
    return jax.shard_map(body, mesh=mesh, in_specs=ins, out_specs=outs, check_vma=False)
```
